32 devices in a mesh: expert: 4 (over y, x), context: 2 (over core), dp: 4 (over z).
Axes of the slice: x: 2, y: 2, z: 4, core: 2. Of those that a mesh axis runs over, the one named last changes fastest.
Arguments:
- tokens: bfloat16 [16, 2048, 768], P(('expert', 'dp'), 'context'), may hold values from -6 to 6
- segments: int32 [16, 2048], P(('expert', 'dp'), 'context'), may hold values from 0 to 4, as said below
- routes: int32 [16, 2048, 2], P(('expert', 'dp'), 'context'), may hold values from 0 to 7, all different within a row
- prev_logits: float32 [16, 2048, 8], P(('expert', 'dp'), 'context'), may hold values from -3 to 3
- ranks: int32 [16, 2, 1024], P(('expert', 'dp'), 'context'), may hold values from 0 to 1023, each once within a row
- cotangent: bfloat16 [16, 2048, 768], P(('expert', 'dp'), 'context'), may hold values from -6 to 6
- norm_one: bfloat16 [768], P('dp'), may hold values from 0.099609375 to 1.8984375
- w_query: bfloat16 [768, 768], P('dp'), may hold values from -0.21875 to 0.21875
- w_key: bfloat16 [768, 768], P('dp'), may hold values from -0.21875 to 0.21875
- w_value: bfloat16 [768, 768], P('dp'), may hold values from -0.21875 to 0.21875
- w_out: bfloat16 [768, 768], P('dp'), may hold values from -0.875 to 0.875
- norm_two: bfloat16 [768], P('dp'), may hold values from 0.099609375 to 1.8984375
- router: bfloat16 [768, 8], P('dp'), may hold values from -0.15625 to 0.15625
- w_res: bfloat16 [8, 8], replicated, may hold values from -2 to 2
- const_mix: bfloat16 [768, 4], P('dp'), may hold values from -0.21875 to 0.21875
- const_vec: bfloat16 [768, 2], P('dp'), may hold values from -5 to 5
- w_gate: bfloat16 [4, 768, 2048], P('expert', 'dp'), may hold values from -0.21875 to 0.21875
- w_up: bfloat16 [4, 768, 2048], P('expert', 'dp'), may hold values from -0.21875 to 0.21875
- w_down: bfloat16 [4, 2048, 768], P('expert', 'dp'), may hold values from -0.75 to 0.75
Outputs:
- output: bfloat16 [16, 2048, 768], P(('expert', 'dp'), 'context')
- grad_tokens: float32 [16, 2048, 768], P(('expert', 'dp'), 'context')
- grad_norm_one: float32 [768], P('dp')
- grad_w_query: float32 [768, 768], P('dp')
- grad_w_key: float32 [768, 768], P('dp')
- grad_w_value: float32 [768, 768], P('dp')
- grad_w_out: float32 [768, 768], P('dp')
- grad_norm_two: float32 [768], P('dp')
- grad_router: float32 [768, 8], P('dp')
- grad_w_res: float32 [8, 8], replicated
- grad_const_mix: float32 [768, 4], P('dp')
- grad_const_vec: float32 [768, 2], P('dp')
- grad_w_gate: float32 [4, 768, 2048], P('expert', 'dp')
- grad_w_up: float32 [4, 768, 2048], P('expert', 'dp')
- grad_w_down: float32 [4, 2048, 768], P('expert', 'dp')
The draws below stay inside these ranges and needn't reach their ends.
Inputs may be any that keep to these rules, and one draw needn't show every extreme that they name: `segments`: segment numbers never fall along a sequence; the tokens with one number form one document. `routes`: each token names two different experts. In each block of 1024 consecutive tokens of a sequence the ranks are a permutation.
All inputs are finite; a program needn't handle non-finite values.
Results may differ from the reference program's by a relative error of at most 0.015.
Values may be sent and summed in bfloat16 or wider, within the bound.
A program may use at most 256 MiB of HBM per device.

```python
from functools import partial
import jax
import jax.numpy as jnp
from jax import lax

D = 768
HEADS = 12
HEAD_DIM = 64
FF = 2048
WIN = 1024
QB = 512
TOK_DEV = 1024
NE = 4
NALL = 8
CAP = 288
SEQ_LEN = 2048
SEQS = 16
N_CONTEXT = 2


def draw_segments(key, part):
    key = jax.random.fold_in(key, 17)
    key_lower, key_upper = jax.random.split(key)
    middle = SEQ_LEN // 2
    lower_cut = jax.random.randint(key_lower, (SEQS, 2), 1, middle - WIN // 4, dtype=jnp.int32)
    upper_cut = jax.random.randint(key_upper, (SEQS, 2), middle + WIN // 4, SEQ_LEN, dtype=jnp.int32)
    bounds = jnp.concatenate([lower_cut, upper_cut], axis=1)
    places = jnp.arange(SEQ_LEN, dtype=jnp.int32)
    return jnp.sum((places[None, :, None] >= bounds[:, None, :]).astype(jnp.int32), axis=-1).astype(jnp.int32)


def block_scale(stream_key, shape, cuts, least, largest):
    loudness, own = 1.0, jax.random.fold_in(stream_key, 6)
    for position, shards_of in cuts:
        steps = jnp.exp(jax.random.uniform(jax.random.fold_in(own, position), (shards_of,), jnp.float32, least / len(cuts), largest / len(cuts)))
        loudness = loudness * jnp.repeat(steps, shape[position] // shards_of).reshape([-1 if axis == position else 1 for axis in range(len(shape))])
    return loudness


def distinct(rng, rows, amount, top, lift):
    sequence = jax.random.permutation(jax.random.fold_in(rng, 1), amount)
    favour = sequence
    for power in range(3):
        favour = favour * favour // amount
    favour = favour * lift // amount
    tickets = jax.random.randint(jax.random.fold_in(rng, 2), (rows, amount), 0, 4096) + favour
    holders = jax.random.permutation(jax.random.fold_in(rng, 3), rows)[jnp.arange(amount) % rows]
    tickets = jnp.where(jnp.arange(rows)[:, None] == holders[None, :], 1 << 14, tickets)
    score = tickets * amount + jnp.arange(amount)
    return lax.top_k(score.astype(jnp.int32), top)[1].astype(jnp.int32)


def scatter_about(own_key, shape, deviation, reach, cuts=(), held_as=jnp.bfloat16):
    values = jax.random.normal(own_key, shape, jnp.float32) * deviation
    if len(cuts) > 0:
        values = block_scale(own_key, shape, cuts, -0.22, 0.18) * values
    return jnp.clip(values, min=-reach, max=reach).astype(held_as)


def setup_inputs(seed: int = 0) -> dict:
    key_of = jax.random.split(jax.random.key(seed), 20)
    tokens = scatter_about(key_of[0], (SEQS, SEQ_LEN, D), 1.0, 6.0, ((0, 16), (1, 2)))
    segments = draw_segments(jax.random.fold_in(key_of[19], 71), 0)
    routes = distinct(key_of[2], SEQS * SEQ_LEN, NALL, 2, 2048).reshape((SEQS, SEQ_LEN, 2))
    prev_logits = scatter_about(key_of[3], (SEQS, SEQ_LEN, NALL), 0.5, 3.0, ((0, 16), (1, 2)), jnp.float32)
    ranks = jax.vmap(lambda own: jax.random.permutation(own, TOK_DEV))(jax.random.split(key_of[4], SEQS * N_CONTEXT)).reshape((SEQS, N_CONTEXT, TOK_DEV)).astype(jnp.int32)
    cotangent = scatter_about(key_of[5], (SEQS, SEQ_LEN, D), 1.0, 6.0, ((0, 16), (1, 2)))
    norm_one = jnp.clip(1.0 + 0.18 * jax.random.normal(key_of[6], (D,), jnp.float32), 0.099609375, 1.8984375).astype(jnp.bfloat16)
    w_query = scatter_about(key_of[7], (D, D), D ** -0.5, 0.21875, ((0, 4),))
    w_key = scatter_about(key_of[8], (D, D), D ** -0.5, 0.21875, ((0, 4),))
    w_value = scatter_about(key_of[9], (D, D), D ** -0.5, 0.21875, ((0, 4),))
    w_out = scatter_about(key_of[10], (D, D), (D // 16) ** -0.5, 0.875, ((0, 4),))
    norm_two = jnp.clip(1.0 + 0.18 * jax.random.normal(key_of[11], (D,), jnp.float32), 0.099609375, 1.8984375).astype(jnp.bfloat16)
    router = scatter_about(key_of[12], (D, NALL), (2 * D) ** -0.5, 0.15625, ((0, 4),))
    w_res = scatter_about(key_of[13], (NALL, NALL), NALL ** -0.5, 2.0)
    const_mix = scatter_about(key_of[14], (D, 4), D ** -0.5, 0.21875, ((0, 4),))
    const_vec = scatter_about(key_of[15], (D, 2), 1.0, 5.0, ((0, 4),))
    w_gate = scatter_about(key_of[16], (NE, D, FF), D ** -0.5, 0.21875, ((0, 4), (1, 4)))
    w_up = scatter_about(key_of[17], (NE, D, FF), D ** -0.5, 0.21875, ((0, 4), (1, 4)))
    w_down = scatter_about(key_of[18], (NE, FF, D), (FF // 32) ** -0.5, 0.75, ((0, 4), (1, 4)))
    return dict(tokens=tokens, segments=segments, routes=routes, prev_logits=prev_logits, ranks=ranks, cotangent=cotangent, norm_one=norm_one, w_query=w_query, w_key=w_key, w_value=w_value, w_out=w_out, norm_two=norm_two, router=router, w_res=w_res, const_mix=const_mix, const_vec=const_vec, w_gate=w_gate, w_up=w_up, w_down=w_down)


EPS = 1e-05
HIGH = lax.Precision.HIGHEST
MASKED = -1000000000.0

@jax.custom_vjp
def low(v):
    return lax.optimization_barrier(v.astype(jnp.bfloat16)).astype(jnp.float32)

@jax.custom_vjp
def low_back(v):
    return v

def low_keep(v):
    return (low(v), None)

def low_pass(kept, grad):
    return (grad,)

def back_keep(v):
    return (v, None)

def back_low(kept, grad):
    return (low(grad),)
low.defvjp(low_keep, low_pass)
low_back.defvjp(back_keep, back_low)

def rms_norm(values, gain_vec):
    return values * lax.rsqrt(lax.optimization_barrier(jnp.mean(values * values, axis=-1, keepdims=True)) + EPS) * gain_vec

def rotary(tensor, positions):
    half_dim = HEAD_DIM // 2
    frequency = 10000.0 ** (-jnp.arange(half_dim, dtype=jnp.float32) * 2.0 / HEAD_DIM)
    angles = positions.astype(jnp.float32)[:, None] * frequency[None, :]
    cos_table = jnp.cos(angles)[:, None, :]
    sin_table = jnp.sin(angles)[:, None, :]
    shaped = tensor.reshape(tensor.shape[0], HEADS, HEAD_DIM)
    first_half = shaped[..., :half_dim]
    second_half = shaped[..., half_dim:]
    turned = jnp.concatenate([first_half * cos_table - second_half * sin_table, first_half * sin_table + second_half * cos_table], axis=-1)
    return turned.reshape(tensor.shape)

def place_pairs(route_blk, rank_blk, experts, capacity):
    row_count = rank_blk.shape[0]
    token_ids = jnp.arange(row_count, dtype=jnp.int32)
    rank_order = jnp.zeros((row_count,), jnp.int32).at[rank_blk].set(token_ids)
    ordered = route_blk[rank_order].reshape(-1)
    onehot = (ordered[:, None] == jnp.arange(experts, dtype=jnp.int32)[None, :]).astype(jnp.int32)
    before = (jnp.cumsum(onehot, axis=0).astype(jnp.int32) - onehot).astype(jnp.int32)
    slot_ord = lax.optimization_barrier(jnp.sum(before * onehot, axis=1)).astype(jnp.int32).reshape(row_count, 2)
    slot_tok = slot_ord[rank_blk]
    kept_pair = (route_blk < experts) & (slot_tok < capacity)
    flat_index = jnp.where(kept_pair, route_blk * capacity + slot_tok, experts * capacity).astype(jnp.int32)
    pair_ids = jnp.arange(2 * row_count, dtype=jnp.int32)
    holder = jnp.full((experts * capacity + 1,), 2 * row_count, jnp.int32).at[flat_index.reshape(-1)].set(pair_ids)
    return (flat_index, holder[:experts * capacity])

def take_rows(table, where_index):
    return table[where_index]

def forward_sequence(param_all, packed):
    gain_one, query_w, key_w, value_w, out_w, gain_two, router_w, res_w, mix_w, vec_w, gate_w, up_w, down_w = param_all
    hidden_in, seg_ids, route_ids, prev_logit, rank_ids = packed
    scale_factor = HEAD_DIM ** (-0.5)
    positions = jnp.arange(SEQ_LEN, dtype=jnp.int32)
    normed = rms_norm(hidden_in, gain_one)
    normed_low = low(normed)
    queries = low(rotary(low_back(jnp.dot(normed_low, query_w, precision=HIGH)), positions))
    keys_rot = low(rotary(low_back(jnp.dot(normed_low, key_w, precision=HIGH)), positions))
    values_low = low(low_back(jnp.dot(normed_low, value_w, precision=HIGH)))
    pad_keys = jnp.concatenate([jnp.zeros((WIN, D), jnp.float32), keys_rot], axis=0)
    pad_values = jnp.concatenate([jnp.zeros((WIN, D), jnp.float32), values_low], axis=0)
    pad_segs = jnp.concatenate([jnp.zeros((WIN,), jnp.int32), seg_ids], axis=0)

    def attend_block(block_id):
        row_start = block_id * QB
        query_blk = lax.dynamic_slice_in_dim(queries, row_start, QB, 0).reshape(QB, HEADS, HEAD_DIM)
        key_blk = lax.dynamic_slice_in_dim(pad_keys, row_start, WIN + QB, 0).reshape(WIN + QB, HEADS, HEAD_DIM)
        value_blk = lax.dynamic_slice_in_dim(pad_values, row_start, WIN + QB, 0).reshape(WIN + QB, HEADS, HEAD_DIM)
        query_pos = row_start + jnp.arange(QB, dtype=jnp.int32)
        key_pos = row_start - WIN + jnp.arange(WIN + QB, dtype=jnp.int32)
        query_seg = lax.dynamic_slice_in_dim(seg_ids, row_start, QB, 0)
        key_seg = lax.dynamic_slice_in_dim(pad_segs, row_start, WIN + QB, 0)
        distance = query_pos[:, None] - key_pos[None, :]
        allowed = (key_pos[None, :] >= 0) & (distance >= 0) & (distance < WIN) & (query_seg[:, None] == key_seg[None, :])
        raw_scores = low_back(jnp.einsum('qhd,khd->hqk', query_blk, key_blk, precision=HIGH))
        scores = jnp.where(allowed[None], raw_scores * scale_factor, MASKED)
        row_peak = lax.optimization_barrier(jnp.max(scores, axis=-1, keepdims=True))
        exp_scores = jnp.exp(scores - row_peak)
        weights = low(exp_scores / lax.optimization_barrier(jnp.sum(exp_scores, axis=-1, keepdims=True)))
        return jnp.einsum('hqk,khd->qhd', weights, value_blk, precision=HIGH).reshape(QB, D)
    attended = lax.map(jax.checkpoint(attend_block), jnp.arange(SEQ_LEN // QB, dtype=jnp.int32)).reshape(SEQ_LEN, D)
    attn_low = low(low_back(attended))
    residual = hidden_in + low_back(jnp.dot(attn_low, out_w, precision=HIGH))
    normed_two = rms_norm(residual, gain_two)
    low_two = low(normed_two)
    logits = low_back(jnp.dot(low_two, router_w, precision=HIGH)) + jnp.dot(prev_logit, res_w, precision=HIGH)
    mix_logit = low_back(jnp.dot(low_two, mix_w, precision=HIGH)).reshape(SEQ_LEN, 2, 2)
    router_probs = jax.nn.softmax(logits, axis=-1)
    choose_hot = (route_ids[:, :, None] == jnp.arange(NALL, dtype=jnp.int32)[None, None, :]).astype(jnp.float32)
    gate_values = lax.optimization_barrier(jnp.sum(choose_hot * router_probs[:, None, :], axis=-1))
    placer = jax.vmap(partial(place_pairs, experts=NE, capacity=CAP))
    flat_index, holder = placer(route_ids.reshape(N_CONTEXT, TOK_DEV, 2), rank_ids)
    token_src = jnp.where(holder < 2 * TOK_DEV, holder // 2, TOK_DEV).astype(jnp.int32)
    low_blocks = jnp.concatenate([low_two.reshape(N_CONTEXT, TOK_DEV, D), jnp.zeros((N_CONTEXT, 1, D), jnp.float32)], axis=1)
    gathered = low_back(jax.vmap(take_rows)(low_blocks, token_src))
    expert_in = gathered.reshape(N_CONTEXT, NE, CAP, D).transpose(1, 0, 2, 3).reshape(NE, N_CONTEXT * CAP, D)
    gate_pre = low_back(jnp.einsum('erd,edf->erf', expert_in, gate_w, precision=HIGH))
    up_pre = low_back(jnp.einsum('erd,edf->erf', expert_in, up_w, precision=HIGH))
    hidden_low = low(jax.nn.silu(gate_pre) * up_pre)
    expert_rows = low_back(low(jnp.einsum('erf,efd->erd', hidden_low, down_w, precision=HIGH)))
    back_blocks = expert_rows.reshape(NE, N_CONTEXT, CAP, D).transpose(1, 0, 2, 3).reshape(N_CONTEXT, NE * CAP, D)
    back_blocks = jnp.concatenate([back_blocks, jnp.zeros((N_CONTEXT, 1, D), jnp.float32)], axis=1)
    ffn_out = jax.vmap(take_rows)(back_blocks, flat_index).reshape(SEQ_LEN, 2, D)
    mix_prob = jax.nn.softmax(mix_logit, axis=-1)
    const_out = mix_prob[:, :, 0:1] * normed_two[:, None, :] + mix_prob[:, :, 1:2] * vec_w.T[None, :, :]
    chosen = route_ids[:, :, None]
    expert_out = jnp.where(chosen < NE, ffn_out, 0.0) + jnp.where(chosen == NE + 1, normed_two[:, None, :], 0.0) + jnp.where(chosen == NE + 2, const_out[:, 0:1, :], 0.0) + jnp.where(chosen == NE + 3, const_out[:, 1:2, :], 0.0)
    return residual + lax.optimization_barrier(jnp.sum(gate_values[:, :, None] * expert_out, axis=1))

def reference(tokens, segments, routes, prev_logits, ranks, cotangent, norm_one, w_query, w_key, w_value, w_out, norm_two, router, w_res, const_mix, const_vec, w_gate, w_up, w_down):
    params = (norm_one.astype(jnp.float32), w_query.astype(jnp.float32), w_key.astype(jnp.float32), w_value.astype(jnp.float32), w_out.astype(jnp.float32), norm_two.astype(jnp.float32), router.astype(jnp.float32), w_res.astype(jnp.float32), const_mix.astype(jnp.float32), const_vec.astype(jnp.float32), w_gate.astype(jnp.float32), w_up.astype(jnp.float32), w_down.astype(jnp.float32))

    def whole(hidden_all, param_all):

        def one_sequence(packed):
            return forward_sequence(param_all, packed)
        return lax.map(jax.checkpoint(one_sequence), (hidden_all, segments, routes, prev_logits.astype(jnp.float32), ranks))
    result, pullback = jax.vjp(whole, tokens.astype(jnp.float32), params)
    grad_in, grads = pullback(cotangent.astype(jnp.float32))
    return (result.astype(jnp.bfloat16), grad_in, grads[0], grads[1], grads[2], grads[3], grads[4], grads[5], grads[6], grads[7], grads[8], grads[9], grads[10], grads[11], grads[12])
```

```python
import functools

import jax
import jax.numpy as jnp
import numpy as np
from jax import lax
from jax.experimental import pallas as pl
from jax.experimental.pallas import tpu as pltpu
from jax.sharding import PartitionSpec as P

HEADS = 12
HEAD_DIM = 64
WIN = 1024
NZ = 4
TQ = 256
TB = 256
FC = 256
LANES = 128
EPS = 1e-05
MASKED = -1000000000.0
HIGH = lax.Precision.HIGHEST
F32 = jnp.float32
BF16 = jnp.bfloat16
MIB = 1024 * 1024


def params(mib):
    return pltpu.CompilerParams(vmem_limit_bytes=mib * MIB)


def cost(flops, nbytes, trans=0):
    return pl.CostEstimate(flops=int(flops), bytes_accessed=int(nbytes), transcendentals=int(trans))


def dot(left, right):
    return jnp.dot(left, right, preferred_element_type=F32)


def dot_nt(left, right):
    return lax.dot_general(left, right, (((1,), (1,)), ((), ())), preferred_element_type=F32)


def dot_tn(left, right):
    return lax.dot_general(left, right, (((0,), (0,)), ((), ())), preferred_element_type=F32)


def iota(shape, axis):
    return lax.broadcasted_iota(jnp.int32, shape, axis)


def rope_tables(seq):
    half = HEAD_DIM // 2
    frequency = np.float32(10000.0) ** (
        -np.arange(half, dtype=np.float32) * np.float32(2.0) / np.float32(HEAD_DIM)
    )
    angles = np.arange(seq, dtype=np.float32)[:, None] * frequency.astype(np.float32)[None, :]
    cos = np.cos(angles.astype(np.float64)).astype(np.float32)
    sin = np.sin(angles.astype(np.float64)).astype(np.float32)
    return np.concatenate([cos] * 4, axis=1), np.concatenate([-sin, sin, -sin, sin], axis=1)


def swap_halves(chunk):
    lane = iota(chunk.shape, 1)
    return jnp.where(
        lane % HEAD_DIM < HEAD_DIM // 2, pltpu.roll(chunk, 96, 1), pltpu.roll(chunk, 32, 1)
    )


def place_kernel(experts, cap, routes_ref, rank_col_ref, rank_row_ref, flat_ref, flat_t_ref):
    rows = routes_ref.shape[0]
    lane = iota((rows, LANES), 1)
    first, second = routes_ref[:, 0:1], routes_ref[:, 1:2]
    hot_first, hot_second = first == lane, second == lane
    hot = (hot_first.astype(F32) + hot_second.astype(F32)).astype(BF16)
    earlier = jnp.where(rank_row_ref[...] < rank_col_ref[...], 1.0, 0.0).astype(BF16)
    counts = dot(earlier, hot)

    def flat(hit, route):
        slot = jnp.sum(jnp.where(hit, counts, 0.0), axis=1, keepdims=True).astype(jnp.int32)
        return jnp.where((route < experts) & (slot < cap), route * cap + slot, experts * cap)

    out = jnp.where(
        lane == 0, flat(hot_first, first), jnp.where(lane == 1, flat(hot_second, second), 0)
    )
    flat_ref[...] = out
    flat_t_ref[...] = out.astype(F32).T[:8]


def place(routes, ranks, experts, cap):
    rows = routes.shape[0]
    return pl.pallas_call(
        functools.partial(place_kernel, experts, cap),
        out_shape=(
            jax.ShapeDtypeStruct((rows, LANES), jnp.int32),
            jax.ShapeDtypeStruct((8, rows), F32),
        ),
        compiler_params=params(32),
        cost_estimate=cost(2 * rows * rows * LANES, 8 * rows * LANES),
        name="place",
    )(routes, ranks.reshape(rows, 1), ranks.reshape(1, rows))


def qkv_kernel(ctx_ref, x_ref, gain_ref, w_ref, cos_ref, sin_ref, out_ref, aone_ref):
    width = x_ref.shape[1]
    values = x_ref[...].astype(F32)
    scale = lax.rsqrt(jnp.mean(values * values, axis=-1, keepdims=True) + EPS)
    normed = (values * scale * gain_ref[...]).astype(BF16)
    aone_ref[...] = normed
    cos, sin = cos_ref[...], sin_ref[...]
    pairs = width // LANES
    for which in range(3):
        product = dot(normed, w_ref[which])
        for pair in range(pairs):
            chunk = product[:, pair * LANES : (pair + 1) * LANES]
            if which < 2:
                chunk = chunk * cos + swap_halves(chunk) * sin
            if which == 0:
                chunk = chunk * HEAD_DIM ** (-0.5)
            side, place_in = pair // (pairs // 2), pair % (pairs // 2)
            out_ref[side, which, :, place_in * LANES : (place_in + 1) * LANES] = chunk.astype(BF16)


def project(ctx, x, gain, w_qkv, cos, sin):
    rows, width = x.shape
    blocks = rows // TB
    return pl.pallas_call(
        qkv_kernel,
        grid_spec=pltpu.PrefetchScalarGridSpec(
            num_scalar_prefetch=1,
            grid=(blocks,),
            in_specs=[
                pl.BlockSpec((TB, width), lambda i, c: (i, 0)),
                pl.BlockSpec((1, width), lambda i, c: (0, 0)),
                pl.BlockSpec((3, width, width), lambda i, c: (0, 0, 0)),
                pl.BlockSpec((TB, LANES), lambda i, c: (c[0] * blocks + i, 0)),
                pl.BlockSpec((TB, LANES), lambda i, c: (c[0] * blocks + i, 0)),
            ],
            out_specs=[
                pl.BlockSpec((2, 3, TB, width // 2), lambda i, c: (0, 0, i, 0)),
                pl.BlockSpec((TB, width), lambda i, c: (i, 0)),
            ],
        ),
        out_shape=(
            jax.ShapeDtypeStruct((2, 3, rows, width // 2), BF16),
            jax.ShapeDtypeStruct((rows, width), BF16),
        ),
        compiler_params=params(40),
        cost_estimate=cost(6 * rows * width * width, 6 * width * width + 12 * rows * width),
        name="project",
    )(ctx, x, gain, w_qkv, cos, sin)


def head_masks():
    lane = iota((TQ, LANES), 1)
    low = jnp.where(lane < HEAD_DIM, 1.0, 0.0).astype(BF16)
    return low, (1.0 - low.astype(F32)).astype(BF16)


def attend_kernel(first_ref, q_ref, k_ref, v_ref, lo_ref, o_ref, lse_ref, vt_ref):
    per = q_ref.shape[2] // TQ
    count = 2 * per
    masks = head_masks()
    sub = iota((TQ, TQ), 0)
    diagonal = sub <= iota((TQ, TQ), 1)

    def turn(tile, carry):
        vt_ref[tile] = v_ref[tile // per, 0, pl.ds((tile % per) * TQ, TQ), :].T
        return carry

    lax.fori_loop(0, count, turn, 0)

    def q_step(qi, carry):
        rows = pl.ds((qi % per) * TQ, TQ)
        query = q_ref[qi // per, 0, rows, :]
        queries = [query * mask for mask in masks]
        low = lo_ref[qi]
        keys = k_ref[qi // per, 0, rows, :]
        turned = vt_ref[qi]
        ok = diagonal & (sub >= low - qi * TQ)
        state = []
        for head in range(2):
            scores = jnp.where(ok, dot_nt(keys, queries[head]), MASKED)
            peak = jnp.max(scores, axis=0, keepdims=True)
            probs = jnp.exp(scores - peak)
            total = jnp.sum(probs, axis=0, keepdims=True)
            mixed = dot(turned[head * HEAD_DIM : (head + 1) * HEAD_DIM], probs.astype(BF16))
            state += [peak, total, mixed]

        def k_step(ki, state):
            keys = k_ref[ki // per, 0, pl.ds((ki % per) * TQ, TQ), :]
            turned = vt_ref[ki]
            ok = sub >= low - ki * TQ
            new = []
            for head in range(2):
                peak, total, mixed = state[3 * head : 3 * head + 3]
                scores = jnp.where(ok, dot_nt(keys, queries[head]), MASKED)
                top = jnp.maximum(peak, jnp.max(scores, axis=0, keepdims=True))
                shrink = jnp.exp(peak - top)
                probs = jnp.exp(scores - top)
                total = total * shrink + jnp.sum(probs, axis=0, keepdims=True)
                part = dot(turned[head * HEAD_DIM : (head + 1) * HEAD_DIM], probs.astype(BF16))
                new += [top, total, mixed * shrink + part]
            return tuple(new)

        state = lax.fori_loop(first_ref[qi], qi, k_step, tuple(state))
        out = jnp.concatenate([state[2] / state[1], state[5] / state[4]], axis=0)
        o_ref[qi // per, rows, :] = out.T.astype(BF16)
        lse_ref[0, qi, 0:1, :] = state[0] + jnp.log(state[1])
        lse_ref[0, qi, 1:2, :] = state[3] + jnp.log(state[4])
        return carry

    lax.fori_loop(0, count, q_step, 0)


def part_spec(which, rows):
    return pl.BlockSpec((2, 1, rows, LANES), lambda p, first, which=which: (0, which, 0, p))


def attend(first, qkv, low):
    _, _, rows, half = qkv.shape
    pairs = half // LANES
    tiles = 2 * rows // TQ
    return pl.pallas_call(
        attend_kernel,
        grid_spec=pltpu.PrefetchScalarGridSpec(
            num_scalar_prefetch=1,
            grid=(pairs,),
            in_specs=[
                part_spec(0, rows),
                part_spec(1, rows),
                part_spec(2, rows),
                pl.BlockSpec((tiles, 1, TQ), lambda p, first: (0, 0, 0)),
            ],
            out_specs=[
                pl.BlockSpec((2, rows, LANES), lambda p, first: (0, 0, p)),
                pl.BlockSpec((1, tiles, 8, TQ), lambda p, first: (p, 0, 0, 0)),
            ],
            scratch_shapes=[pltpu.VMEM((tiles, LANES, TQ), BF16)],
        ),
        out_shape=(
            jax.ShapeDtypeStruct((2, rows, half), BF16),
            jax.ShapeDtypeStruct((pairs, tiles, 8, TQ), F32),
        ),
        compiler_params=params(40),
        cost_estimate=cost(40e9, 16 * rows * half, 12e6),
        name="attend",
    )(first, qkv, qkv, qkv, low)


def attend_back_kernel(
    first_ref,
    q_ref,
    k_ref,
    v_ref,
    do_ref,
    o_ref,
    lse_ref,
    lo_ref,
    cos_ref,
    sin_ref,
    g_ref,
    kt_ref,
    delta_ref,
    dk_ref,
    dv_ref,
):
    per = q_ref.shape[2] // TQ
    count = 2 * per
    masks = head_masks()
    sub = iota((TQ, TQ), 0)
    diagonal = sub <= iota((TQ, TQ), 1)

    def prepare(tile, carry):
        rows = pl.ds((tile % per) * TQ, TQ)
        kt_ref[tile] = k_ref[tile // per, 0, rows, :].T
        both = o_ref[tile // per, rows, :].astype(F32) * do_ref[tile // per, rows, :].astype(F32)
        both = both.T
        delta_ref[tile, 0:1, :] = jnp.sum(both[:HEAD_DIM], axis=0, keepdims=True)
        delta_ref[tile, 1:2, :] = jnp.sum(both[HEAD_DIM:], axis=0, keepdims=True)
        dk_ref[tile] = jnp.zeros((TQ, LANES), F32)
        dv_ref[tile] = jnp.zeros((TQ, LANES), F32)
        return carry

    lax.fori_loop(0, count, prepare, 0)

    def q_step(qi, carry):
        rows = pl.ds((qi % per) * TQ, TQ)
        query = q_ref[qi // per, 0, rows, :]
        grad = do_ref[qi // per, rows, :]
        queries = [query * mask for mask in masks]
        grads = [grad * mask for mask in masks]
        both_queries = jnp.concatenate(queries, axis=0)
        both_grads = jnp.concatenate(grads, axis=0)
        low = lo_ref[qi]
        lse = [lse_ref[0, qi, h : h + 1, :] for h in range(2)]
        delta = [delta_ref[qi, h : h + 1, :] for h in range(2)]

        def tile(ki, ok, sums):
            at = pl.ds((ki % per) * TQ, TQ)
            keys = k_ref[ki // per, 0, at, :]
            values = v_ref[ki // per, 0, at, :]
            turned = kt_ref[ki]
            all_probs, all_scores, new = [], [], []
            for h in range(2):
                scores = jnp.where(ok, dot_nt(keys, queries[h]), MASKED)
                probs = jnp.exp(scores - lse[h])
                grad_probs = dot_nt(values, grads[h])
                grad_scores = (probs * (grad_probs - delta[h])).astype(BF16)
                new.append(
                    sums[h] + dot(turned[h * HEAD_DIM : (h + 1) * HEAD_DIM], grad_scores)
                )
                all_probs.append(probs.astype(BF16))
                all_scores.append(grad_scores)
            dv_ref[ki] += dot(jnp.concatenate(all_probs, axis=1), both_grads)
            dk_ref[ki] += dot(jnp.concatenate(all_scores, axis=1), both_queries)
            return tuple(new)

        start = jnp.zeros((HEAD_DIM, TQ), F32)
        sums = tile(qi, diagonal & (sub >= low - qi * TQ), (start, start))
        sums = lax.fori_loop(
            first_ref[qi], qi, lambda ki, s: tile(ki, sub >= low - ki * TQ, s), sums
        )
        grad_query = jnp.concatenate(sums, axis=0).T * HEAD_DIM ** (-0.5)
        cos, sin = cos_ref[qi // per, rows, :], sin_ref[qi // per, rows, :]
        g_ref[qi // per, 0, rows, :] = (grad_query * cos - swap_halves(grad_query) * sin).astype(
            BF16
        )
        return carry

    lax.fori_loop(0, count, q_step, 0)

    def finish(tile, carry):
        rows = pl.ds((tile % per) * TQ, TQ)
        cos, sin = cos_ref[tile // per, rows, :], sin_ref[tile // per, rows, :]
        grad_key = dk_ref[tile]
        g_ref[tile // per, 1, rows, :] = (grad_key * cos - swap_halves(grad_key) * sin).astype(BF16)
        g_ref[tile // per, 2, rows, :] = dv_ref[tile].astype(BF16)
        return carry

    lax.fori_loop(0, count, finish, 0)


def attend_back(first, qkv, grad_o, o, lse, low, cos, sin):
    _, _, rows, half = qkv.shape
    pairs = half // LANES
    tiles = 2 * rows // TQ
    side = pl.BlockSpec((2, rows, LANES), lambda p, first: (0, 0, p))
    table = pl.BlockSpec((2, rows, LANES), lambda p, first: (0, 0, 0))
    return pl.pallas_call(
        attend_back_kernel,
        grid_spec=pltpu.PrefetchScalarGridSpec(
            num_scalar_prefetch=1,
            grid=(pairs,),
            in_specs=[
                part_spec(0, rows),
                part_spec(1, rows),
                part_spec(2, rows),
                side,
                side,
                pl.BlockSpec((1, tiles, 8, TQ), lambda p, first: (p, 0, 0, 0)),
                pl.BlockSpec((tiles, 1, TQ), lambda p, first: (0, 0, 0)),
                table,
                table,
            ],
            out_specs=pl.BlockSpec((2, 3, rows, LANES), lambda p, first: (0, 0, 0, p)),
            scratch_shapes=[
                pltpu.VMEM((tiles, LANES, TQ), BF16),
                pltpu.VMEM((tiles, 8, TQ), F32),
                pltpu.VMEM((tiles, TQ, LANES), F32),
                pltpu.VMEM((tiles, TQ, LANES), F32),
            ],
        ),
        out_shape=jax.ShapeDtypeStruct((2, 3, rows, half), BF16),
        compiler_params=params(48),
        cost_estimate=cost(100e9, 32 * rows * half, 12e6),
        name="attend_back",
    )(first, qkv, qkv, qkv, grad_o, o, lse, low, cos, sin)


def middle_kernel(
    total, x_ref, o_ref, w_ref, gain_ref, route_ref, prev_ref, routes_ref, hres_ref, atwo_ref, stat_ref
):
    half = o_ref.shape[2]
    hres = (
        x_ref[...].astype(F32) + dot(o_ref[0], w_ref[:half]) + dot(o_ref[1], w_ref[half:])
    )
    hres_ref[...] = hres
    scale = lax.rsqrt(jnp.mean(hres * hres, axis=-1, keepdims=True) + EPS)
    atwo = (hres * scale * gain_ref[...]).astype(BF16)
    atwo_ref[...] = atwo
    logits = dot(atwo, route_ref[...]) + prev_ref[...]
    lane = iota(logits.shape, 1)

    def soft(inside):
        peak = jnp.max(jnp.where(inside, logits, -jnp.inf), axis=1, keepdims=True)
        powers = jnp.where(inside, jnp.exp(jnp.where(inside, logits - peak, 0.0)), 0.0)
        return powers / jnp.sum(powers, axis=1, keepdims=True)

    probs = soft(lane < total)
    stat = probs
    for j in range(2):
        start = total + 2 * j
        stat = stat + soft((lane >= start) & (lane < start + 2))
    stat = jnp.where(lane == total + 4, scale, stat)
    for k in range(2):
        gate = jnp.sum(
            jnp.where(lane == routes_ref[:, k : k + 1], probs, 0.0), axis=1, keepdims=True
        )
        stat = jnp.where(lane == total + 5 + k, gate, stat)
    stat_ref[...] = stat


def middle(total, x, o, w_out, gain, route_w, prev, routes):
    rows, width = x.shape
    token = lambda i: (i, 0)
    whole = lambda i: (0, 0)
    return pl.pallas_call(
        functools.partial(middle_kernel, total),
        grid=(rows // TB,),
        in_specs=[
            pl.BlockSpec((TB, width), token),
            pl.BlockSpec((2, TB, width // 2), lambda i: (0, i, 0)),
            pl.BlockSpec((width, width), whole),
            pl.BlockSpec((1, width), whole),
            pl.BlockSpec((width, LANES), whole),
            pl.BlockSpec((TB, LANES), token),
            pl.BlockSpec((TB, 2), token),
        ],
        out_specs=[
            pl.BlockSpec((TB, width), token),
            pl.BlockSpec((TB, width), token),
            pl.BlockSpec((TB, LANES), token),
        ],
        out_shape=(
            jax.ShapeDtypeStruct((rows, width), F32),
            jax.ShapeDtypeStruct((rows, width), BF16),
            jax.ShapeDtypeStruct((rows, LANES), F32),
        ),
        compiler_params=params(40),
        cost_estimate=cost(2 * rows * width * width, 2 * width * width + 10 * rows * width),
        name="middle",
    )(x, o, w_out, gain, route_w, prev, routes)


def dispatch_kernel(total, flat_ref, atwo_ref, dy_ref, stat_ref, rows_ref, grads_ref):
    cap = rows_ref.shape[1]
    tokens = atwo_ref.shape[0]
    slot = (iota((cap, tokens), 0) + pl.program_id(0) * cap).astype(F32)
    gates = stat_ref[...].T
    first, second = flat_ref[0:1, :] == slot, flat_ref[1:2, :] == slot
    hot = jnp.where(first | second, 1.0, 0.0).astype(BF16)
    gate = jnp.sum(
        jnp.where(first, gates[total + 5 : total + 6], 0.0)
        + jnp.where(second, gates[total + 6 : total + 7], 0.0),
        axis=1,
        keepdims=True,
    )
    rows_ref[0] = dot(hot, atwo_ref[...]).astype(BF16)
    grads_ref[0] = (dot(hot, dy_ref[...]) * gate).astype(BF16)


def dispatch(total, experts, cap, flat_t, atwo, dy, stat):
    rows, width = atwo.shape
    whole = lambda e: (0, 0)
    return pl.pallas_call(
        functools.partial(dispatch_kernel, total),
        grid=(experts,),
        in_specs=[
            pl.BlockSpec((8, rows), whole),
            pl.BlockSpec((rows, width), whole),
            pl.BlockSpec((rows, width), whole),
            pl.BlockSpec((rows, LANES), whole),
        ],
        out_specs=[pl.BlockSpec((1, cap, width), lambda e: (e, 0, 0))] * 2,
        out_shape=(jax.ShapeDtypeStruct((experts, cap, width), BF16),) * 2,
        compiler_params=params(40),
        cost_estimate=cost(4 * experts * cap * rows * width, 8 * rows * width),
        name="dispatch",
    )(flat_t, atwo, dy, stat)


def up_kernel(x_ref, wg_ref, wu_ref, wd_ref, flow_ref, z_ref, a_ref, b_ref, acc_ref):
    step = pl.program_id(0)
    rows = x_ref[...]
    gate = dot(rows, wg_ref[0])
    up = dot(rows, wu_ref[0])
    sig = 1.0 / (1.0 + jnp.exp(-gate))
    swish = gate * sig
    hidden = (swish * up).astype(BF16)
    z_ref[...] = hidden
    a_ref[...] = (up * sig * (1.0 + gate * (1.0 - sig))).astype(BF16)
    b_ref[...] = swish.astype(BF16)
    part = dot(hidden, jnp.concatenate([wd_ref[0], wd_ref[1]], axis=1))

    @pl.when(step == 0)
    def _():
        acc_ref[...] = part

    @pl.when(step > 0)
    def _():
        acc_ref[...] += part

    @pl.when(step == pl.num_programs(0) - 1)
    def _():
        flow_ref[...] = acc_ref[...].astype(BF16)


def weight_specs(width, hidden):
    chunks = hidden // 2 // FC
    wide = pl.BlockSpec((1, width, FC), lambda f: (f // chunks, 0, f % chunks))
    down = pl.BlockSpec((2, FC, width // 2), lambda f: (0, f, 0))
    return wide, down


def expert_up(x, wg, wu, wd):
    rows, width = x.shape
    hidden = wd.shape[1]
    wide, down = weight_specs(width, hidden)
    whole = pl.BlockSpec((rows, width), lambda f: (0, 0))
    chunk = pl.BlockSpec((rows, FC), lambda f: (0, f))
    return pl.pallas_call(
        up_kernel,
        grid=(hidden // FC,),
        in_specs=[whole, wide, wide, down],
        out_specs=[whole, chunk, chunk, chunk],
        out_shape=(
            jax.ShapeDtypeStruct((rows, width), BF16),
            jax.ShapeDtypeStruct((rows, hidden), BF16),
            jax.ShapeDtypeStruct((rows, hidden), BF16),
            jax.ShapeDtypeStruct((rows, hidden), BF16),
        ),
        scratch_shapes=[pltpu.VMEM((rows, width), F32)],
        compiler_params=params(48),
        cost_estimate=cost(6 * rows * width * hidden, 6 * width * hidden + 6 * rows * hidden, rows * hidden),
        name="expert_up",
    )(x, wg, wu, wd)


def down_kernel(dflow_ref, wg_ref, wu_ref, wd_ref, a_ref, b_ref, drow_ref, dg_ref, du_ref, acc_ref):
    step = pl.program_id(0)
    dz = dot_nt(dflow_ref[...], jnp.concatenate([wd_ref[0], wd_ref[1]], axis=1))
    dg = (dz * a_ref[...].astype(F32)).astype(BF16)
    du = (dz * b_ref[...].astype(F32)).astype(BF16)
    dg_ref[...] = dg
    du_ref[...] = du
    part = dot_nt(dg, wg_ref[0]) + dot_nt(du, wu_ref[0])

    @pl.when(step == 0)
    def _():
        acc_ref[...] = part

    @pl.when(step > 0)
    def _():
        acc_ref[...] += part

    @pl.when(step == pl.num_programs(0) - 1)
    def _():
        drow_ref[...] = acc_ref[...].astype(BF16)


def expert_down(dflow, wg, wu, wd, a, b):
    rows, width = dflow.shape
    hidden = wd.shape[1]
    wide, down = weight_specs(width, hidden)
    whole = pl.BlockSpec((rows, width), lambda f: (0, 0))
    chunk = pl.BlockSpec((rows, FC), lambda f: (0, f))
    return pl.pallas_call(
        down_kernel,
        grid=(hidden // FC,),
        in_specs=[whole, wide, wide, down, chunk, chunk],
        out_specs=[whole, chunk, chunk],
        out_shape=(
            jax.ShapeDtypeStruct((rows, width), BF16),
            jax.ShapeDtypeStruct((rows, hidden), BF16),
            jax.ShapeDtypeStruct((rows, hidden), BF16),
        ),
        scratch_shapes=[pltpu.VMEM((rows, width), F32)],
        compiler_params=params(48),
        cost_estimate=cost(6 * rows * width * hidden, 6 * width * hidden + 8 * rows * hidden),
        name="expert_down",
    )(dflow, wg, wu, wd, a, b)


def wgrad_kernel(x_ref, dflow_ref, z_ref, dg_ref, du_ref, gg_ref, gu_ref, gd_ref, xt_ref):
    @pl.when(pl.program_id(0) == 0)
    def _():
        xt_ref[...] = x_ref[...].T

    turned = xt_ref[...]
    gg_ref[0] = dot(turned, dg_ref[...]).astype(BF16)
    gu_ref[0] = dot(turned, du_ref[...]).astype(BF16)
    down = dot(z_ref[...].T, dflow_ref[...]).astype(BF16)
    half = down.shape[1] // 2
    gd_ref[0] = down[:, :half]
    gd_ref[1] = down[:, half:]


def expert_wgrad(x, dflow, z, dg, du):
    rows, width = x.shape
    hidden = z.shape[1]
    wide, down = weight_specs(width, hidden)
    whole = pl.BlockSpec((rows, width), lambda f: (0, 0))
    chunk = pl.BlockSpec((rows, FC), lambda f: (0, f))
    return pl.pallas_call(
        wgrad_kernel,
        grid=(hidden // FC,),
        in_specs=[whole, whole, chunk, chunk, chunk],
        out_specs=[wide, wide, down],
        out_shape=(
            jax.ShapeDtypeStruct((2, width, hidden // 2), BF16),
            jax.ShapeDtypeStruct((2, width, hidden // 2), BF16),
            jax.ShapeDtypeStruct((2, hidden, width // 2), BF16),
        ),
        scratch_shapes=[pltpu.VMEM((width, rows), BF16)],
        compiler_params=params(48),
        cost_estimate=cost(6 * rows * width * hidden, 6 * width * hidden + 6 * rows * hidden),
        name="expert_wgrad",
    )(x, dflow, z, dg, du)


def combine_kernel(
    experts,
    total,
    flow_ref,
    drow_ref,
    flat_ref,
    stat_ref,
    routes_ref,
    hres_ref,
    atwo_ref,
    dy_ref,
    o_ref,
    vec_ref,
    gain_ref,
    route_ref,
    w_ref,
    out_ref,
    dh_ref,
    dolow_ref,
    dlogit_ref,
    gw_ref,
    small_ref,
):
    step = pl.program_id(0)
    slots = flow_ref.shape[0]
    half = o_ref.shape[2]
    gain = gain_ref[...]
    stat = stat_ref[...]
    hres = hres_ref[...]
    dy = dy_ref[...].astype(F32)
    scale = stat[:, total + 4 : total + 5]
    gates = [stat[:, total + 5 + k : total + 6 + k] for k in range(2)]
    ntwo = hres * scale * gain
    spread = iota((TB, slots), 1)
    hots = [flat_ref[:, k : k + 1] == spread for k in range(2)]
    returned = flow_ref[...]
    mixes = [[stat[:, total + 2 * j + i : total + 2 * j + i + 1] for i in range(2)] for j in range(2)]
    vecs = [vec_ref[j : j + 1, :] for j in range(2)]
    moe = jnp.zeros_like(hres)
    lane = iota((TB, LANES), 1)
    dpgate = jnp.zeros((TB, LANES), F32)
    weight = jnp.zeros((TB, 1), F32)
    const_weights = [jnp.zeros((TB, 1), F32)] * 2
    for k in range(2):
        route = routes_ref[:, k : k + 1]
        epair = dot(jnp.where(hots[k], 1.0, 0.0).astype(BF16), returned)
        share = jnp.where(route == experts + 1, 1.0, 0.0)
        weight = weight + share * gates[k]
        for j in range(2):
            chosen = jnp.where(route == experts + 2 + j, 1.0, 0.0)
            share = share + chosen * mixes[j][0]
            epair = epair + (chosen * mixes[j][1]) * vecs[j]
            const_weights[j] = const_weights[j] + chosen * gates[k]
        epair = epair + share * ntwo
        moe = moe + gates[k] * epair
        dgate = jnp.sum(dy * epair, axis=1, keepdims=True)
        dpgate = dpgate + jnp.where(lane == route, dgate, 0.0)
    out_ref[...] = (hres + moe).astype(BF16)

    pgate = jnp.where(lane < total, stat, 0.0)
    dlogit = pgate * (dpgate - jnp.sum(pgate * dpgate, axis=1, keepdims=True))
    dlogit_ref[...] = dlogit
    dot_normed = jnp.sum(dy * ntwo, axis=1, keepdims=True)
    droute = dlogit
    vec_rows = []
    for j in range(2):
        dot_vec = jnp.sum(dy * vecs[j], axis=1, keepdims=True)
        grads = [const_weights[j] * dot_normed, const_weights[j] * dot_vec]
        inner = mixes[j][0] * grads[0] + mixes[j][1] * grads[1]
        for i in range(2):
            droute = jnp.where(
                lane == total + 2 * j + i, mixes[j][i] * (grads[i] - inner), droute
            )
        weight = weight + const_weights[j] * mixes[j][0]
        vec_rows.append(jnp.sum((const_weights[j] * mixes[j][1]) * dy, axis=0, keepdims=True))
    droute = droute.astype(BF16)
    hot_any = jnp.where(hots[0] | hots[1], 1.0, 0.0).astype(BF16)
    dntwo = weight * dy + dot_nt(droute, route_ref[...]) + dot(hot_any, drow_ref[...])
    turned = dntwo * gain
    inner = jnp.mean(hres * turned, axis=1, keepdims=True)
    dh = dy + scale * turned - hres * (scale * scale * scale * inner)
    dh_ref[...] = dh
    dhlow = dh.astype(BF16)
    dolow = dot_nt(dhlow, w_ref[...]).astype(BF16)
    dolow_ref[0] = dolow[:, :half]
    dolow_ref[1] = dolow[:, half:]
    gain_row = jnp.sum(dntwo * hres * scale, axis=0, keepdims=True)
    route_rows = dot(droute.T, atwo_ref[...])
    fill = small_ref.shape[0] - total - 7
    small = jnp.concatenate(
        [route_rows[: total + 4], gain_row, vec_rows[0], vec_rows[1], jnp.zeros((fill, hres.shape[1]), F32)],
        axis=0,
    )
    parts = [dot(o_ref[i].T, dhlow) for i in range(2)]

    @pl.when(step == 0)
    def _():
        small_ref[...] = small
        gw_ref[:half] = parts[0]
        gw_ref[half:] = parts[1]

    @pl.when(step > 0)
    def _():
        small_ref[...] += small
        gw_ref[:half] += parts[0]
        gw_ref[half:] += parts[1]


def combine(experts, total, flow, drow, flat, stat, routes, hres, atwo, dy, o, vec, gain, route_w, w_out):
    rows, width = hres.shape
    slots = flow.shape[0]
    token = lambda i: (i, 0)
    whole = lambda i: (0, 0)
    side = pl.BlockSpec((2, TB, width // 2), lambda i: (0, i, 0))
    small_rows = -(-(total + 7) // 8) * 8
    return pl.pallas_call(
        functools.partial(combine_kernel, experts, total),
        grid=(rows // TB,),
        in_specs=[
            pl.BlockSpec((slots, width), whole),
            pl.BlockSpec((slots, width), whole),
            pl.BlockSpec((TB, LANES), token),
            pl.BlockSpec((TB, LANES), token),
            pl.BlockSpec((TB, 2), token),
            pl.BlockSpec((TB, width), token),
            pl.BlockSpec((TB, width), token),
            pl.BlockSpec((TB, width), token),
            side,
            pl.BlockSpec((2, width), whole),
            pl.BlockSpec((1, width), whole),
            pl.BlockSpec((width, LANES), whole),
            pl.BlockSpec((width, width), whole),
        ],
        out_specs=[
            pl.BlockSpec((TB, width), token),
            pl.BlockSpec((TB, width), token),
            side,
            pl.BlockSpec((TB, LANES), token),
            pl.BlockSpec((width, width), whole),
            pl.BlockSpec((small_rows, width), whole),
        ],
        out_shape=(
            jax.ShapeDtypeStruct((rows, width), BF16),
            jax.ShapeDtypeStruct((rows, width), F32),
            jax.ShapeDtypeStruct((2, rows, width // 2), BF16),
            jax.ShapeDtypeStruct((rows, LANES), F32),
            jax.ShapeDtypeStruct((width, width), F32),
            jax.ShapeDtypeStruct((small_rows, width), F32),
        ),
        compiler_params=params(56),
        cost_estimate=cost(
            6 * rows * slots * width + 4 * rows * width * width, 30 * rows * width + 8 * width * width
        ),
        name="combine",
    )(flow, drow, flat, stat, routes, hres, atwo, dy, o, vec, gain, route_w, w_out)


def project_back_kernel(g_ref, w_ref, x_ref, aone_ref, dh_ref, gain_ref, out_ref, gw_ref, gain_out_ref):
    step = pl.program_id(0)
    half = g_ref.shape[3]
    turned = aone_ref[...].T
    dnone = None
    for which in range(3):
        grad = jnp.concatenate([g_ref[0, which], g_ref[1, which]], axis=1)
        part = dot_nt(grad, w_ref[which])
        dnone = part if dnone is None else dnone + part
        weight = dot(turned, grad)

        @pl.when(step == 0)
        def _():
            gw_ref[which] = weight

        @pl.when(step > 0)
        def _():
            gw_ref[which] += weight

    values = x_ref[...].astype(F32)
    scale = lax.rsqrt(jnp.mean(values * values, axis=-1, keepdims=True) + EPS)
    scaled = dnone * gain_ref[...]
    inner = jnp.mean(values * scaled, axis=1, keepdims=True)
    out_ref[...] = dh_ref[...] + scale * scaled - values * (scale * scale * scale * inner)
    row = jnp.sum(dnone * values * scale, axis=0, keepdims=True)

    @pl.when(step == 0)
    def _():
        gain_out_ref[...] = row

    @pl.when(step > 0)
    def _():
        gain_out_ref[...] += row


def project_back(grad, w_qkv, x, aone, dh, gain):
    rows, width = x.shape
    token = lambda i: (i, 0)
    whole = lambda i: (0, 0)
    return pl.pallas_call(
        project_back_kernel,
        grid=(rows // TB,),
        in_specs=[
            pl.BlockSpec((2, 3, TB, width // 2), lambda i: (0, 0, i, 0)),
            pl.BlockSpec((3, width, width), lambda i: (0, 0, 0)),
            pl.BlockSpec((TB, width), token),
            pl.BlockSpec((TB, width), token),
            pl.BlockSpec((TB, width), token),
            pl.BlockSpec((1, width), whole),
        ],
        out_specs=[
            pl.BlockSpec((TB, width), token),
            pl.BlockSpec((3, width, width), lambda i: (0, 0, 0)),
            pl.BlockSpec((1, width), whole),
        ],
        out_shape=(
            jax.ShapeDtypeStruct((rows, width), F32),
            jax.ShapeDtypeStruct((3, width, width), F32),
            jax.ShapeDtypeStruct((1, width), F32),
        ),
        compiler_params=params(56),
        cost_estimate=cost(12 * rows * width * width, 18 * width * width + 20 * rows * width),
        name="project_back",
    )(grad, w_qkv, x, aone, dh, gain)


def swap_cores(value):
    return lax.all_to_all(value, "context", split_axis=0, concat_axis=0, tiled=True)


def swap_experts(value):
    return lax.all_to_all(value, "expert", split_axis=0, concat_axis=0, tiled=True)


def gather_half(shard, width):
    core = lax.axis_index("context")
    mine = lax.dynamic_slice_in_dim(shard, core * width, width, 1)
    whole = lax.all_gather(mine, ("context", "dp"), axis=0)
    dp = lax.axis_size("dp")
    return whole.reshape(2, dp * mine.shape[0], width)


def on_device(
    tokens,
    segments,
    routes,
    prev_logits,
    ranks,
    cotangent,
    norm_one,
    w_query,
    w_key,
    w_value,
    w_out,
    norm_two,
    router,
    w_res,
    const_mix,
    const_vec,
    w_gate,
    w_up,
    w_down,
):
    experts = lax.axis_size("expert")
    dp = lax.axis_size("dp")
    total = experts + NZ
    _, rows, width = tokens.shape
    hidden = w_gate.shape[2]
    cap = (18 * rows + 8 * total - 1) // (8 * total)
    seq = 2 * rows
    tiles = seq // TQ
    core = lax.axis_index("context")
    mesh_axes = ("expert", "context", "dp")

    w_qkv = lax.all_gather(jnp.stack([w_query, w_key, w_value]), "dp", axis=1, tiled=True)
    extra = jnp.concatenate(
        [
            norm_one.astype(BF16)[:, None],
            norm_two.astype(BF16)[:, None],
            const_vec,
            router,
            const_mix,
        ],
        axis=1,
    )
    extra = jnp.pad(extra, ((0, 0), (0, LANES - extra.shape[1])))
    out_and_extra = lax.all_gather(
        jnp.concatenate([w_out, extra], axis=1), "dp", axis=0, tiled=True
    )
    out_w = out_and_extra[:, :width]
    extra = out_and_extra[:, width:]
    extra_t = extra[:, :4].astype(F32).T
    gain_one, gain_two, vec = extra_t[0:1], extra_t[1:2], extra_t[2:4]
    route_w = jnp.pad(extra[:, 4 : 8 + total], ((0, 0), (0, LANES - total - 4)))

    gate_w = gather_half(w_gate[0], hidden // 2)
    up_w = gather_half(w_up[0], hidden // 2)
    down_w = gather_half(w_down[0], width // 2)

    flat, flat_t = place(routes[0], ranks[0, 0], experts, cap)
    segs = lax.all_gather(segments[0], "context", axis=0, tiled=True)
    places = jnp.arange(seq, dtype=jnp.int32)
    starts = jnp.sum((segs[None, :] < segs[:, None]).astype(jnp.int32), axis=1)
    low = jnp.maximum(starts, places - (WIN - 1)).reshape(tiles, 1, TQ)
    first = low[:, 0, 0] // TQ
    cos, sin = rope_tables(seq)
    cos, sin = jnp.asarray(cos), jnp.asarray(sin)
    prev_term = jnp.pad(
        jnp.dot(prev_logits[0], w_res.astype(F32), precision=HIGH),
        ((0, 0), (0, LANES - total)),
    )

    x = tokens[0]
    dy = cotangent[0]
    sent, aone = project(core.reshape(1), x, gain_one, w_qkv, cos, sin)
    qkv = swap_cores(sent)
    o_heads, lse = attend(first, qkv, low)
    o = swap_cores(o_heads)
    hres, atwo, stat = middle(total, x, o, out_w, gain_two, route_w, prev_term, routes[0])
    sent_rows, sent_grads = dispatch(total, experts, cap, flat_t, atwo, dy, stat)
    in_rows = swap_experts(sent_rows).reshape(experts * cap, width)
    in_grads = swap_experts(sent_grads).reshape(experts * cap, width)
    flow, z, a, b = expert_up(in_rows, gate_w, up_w, down_w)
    flow_back = swap_experts(flow.reshape(experts, cap, width)).reshape(experts * cap, width)
    drow, dg, du = expert_down(in_grads, gate_w, up_w, down_w, a, b)
    drow_back = swap_experts(drow.reshape(experts, cap, width)).reshape(experts * cap, width)
    grad_gate, grad_up, grad_down = expert_wgrad(in_rows, in_grads, z, dg, du)

    def scatter_half(grad):
        shape = grad.shape
        share = lax.psum_scatter(
            grad.reshape(2 * shape[1], shape[2]), ("context", "dp"), scatter_dimension=0, tiled=True
        )
        both = lax.all_gather(share, "context", axis=1, tiled=True)
        return both.astype(F32)[None]

    total_gate, total_up, total_down = (
        scatter_half(grad_gate),
        scatter_half(grad_up),
        scatter_half(grad_down),
    )

    output, dh, dolow, dlogit, grad_out_w, small = combine(
        experts,
        total,
        flow_back,
        drow_back,
        flat,
        stat,
        routes[0],
        hres,
        atwo,
        dy,
        o,
        vec,
        gain_two,
        route_w,
        out_w,
    )
    grad_o = swap_cores(dolow)
    grads_sent = attend_back(
        first,
        qkv,
        grad_o,
        o_heads,
        lse,
        low,
        cos.reshape(2, rows, LANES),
        sin.reshape(2, rows, LANES),
    )
    grads = swap_cores(grads_sent)
    grad_tokens, grad_qkv, grad_gain_one = project_back(grads, w_qkv, x, aone, dh, gain_one)

    grad_res = lax.dot_general(
        prev_logits[0],
        dlogit[:, :total],
        (((0,), (0,)), ((), ())),
        precision=HIGH,
        preferred_element_type=F32,
    )
    res_row = jnp.pad(grad_res.reshape(1, -1), ((0, 0), (0, width - total * total)))
    small = jnp.concatenate([small, grad_gain_one, res_row], axis=0)
    small = lax.psum(small, mesh_axes)
    rank = lax.axis_index("dp")
    part = width // dp
    mine = lax.dynamic_slice_in_dim(small, rank * part, part, 1)
    grad_res_total = small[-1, : total * total].reshape(total, total)

    shared = jnp.concatenate([grad_qkv, grad_out_w[None]], axis=0).astype(BF16)
    shared = lax.psum_scatter(shared, "dp", scatter_dimension=1, tiled=True)
    shared = lax.psum(shared, ("expert", "context")).astype(F32)
    return (
        output[None],
        grad_tokens[None],
        mine[-2],
        shared[0],
        shared[1],
        shared[2],
        shared[3],
        mine[total + 4],
        mine[:total].T,
        grad_res_total,
        mine[total : total + 4].T,
        mine[total + 5 : total + 7].T,
        total_gate,
        total_up,
        total_down,
    )


def solution(mesh):
    token = P(("expert", "dp"), "context", None)
    rows = P("dp", None)
    expert = P("expert", "dp", None)
    in_specs = (
        token,
        P(("expert", "dp"), "context"),
        token,
        token,
        token,
        token,
        P("dp"),
        rows,
        rows,
        rows,
        rows,
        P("dp"),
        rows,
        P(),
        rows,
        rows,
        expert,
        expert,
        expert,
    )
    out_specs = (
        token,
        token,
        P("dp"),
        rows,
        rows,
        rows,
        rows,
        P("dp"),
        rows,
        P(),
        rows,
        rows,
        expert,
        expert,
        expert,
    )
    return jax.shard_map(
        on_device, mesh=mesh, in_specs=in_specs, out_specs=out_specs, check_vma=False
    )
```

```python
import functools

import jax
import jax.numpy as jnp
import numpy as np
from jax import lax
from jax.experimental import pallas as pl
from jax.experimental.pallas import tpu as pltpu
from jax.sharding import PartitionSpec as P

HEADS = 12
HEAD_DIM = 64
WIN = 1024
NZ = 4
TQ = 256
TB = 256
FC = 256
LANES = 128
EPS = 1e-05
MASKED = -1000000000.0
HIGH = lax.Precision.HIGHEST
F32 = jnp.float32
BF16 = jnp.bfloat16
MIB = 1024 * 1024


def params(mib):
    return pltpu.CompilerParams(vmem_limit_bytes=mib * MIB)


def cost(flops, nbytes, trans=0):
    return pl.CostEstimate(flops=int(flops), bytes_accessed=int(nbytes), transcendentals=int(trans))


def dot(left, right):
    return jnp.dot(left, right, preferred_element_type=F32)


def dot_nt(left, right):
    return lax.dot_general(left, right, (((1,), (1,)), ((), ())), preferred_element_type=F32)


def dot_tn(left, right):
    return lax.dot_general(left, right, (((0,), (0,)), ((), ())), preferred_element_type=F32)


def iota(shape, axis):
    return lax.broadcasted_iota(jnp.int32, shape, axis)


def rope_tables(seq):
    half = HEAD_DIM // 2
    frequency = np.float32(10000.0) ** (
        -np.arange(half, dtype=np.float32) * np.float32(2.0) / np.float32(HEAD_DIM)
    )
    angles = np.arange(seq, dtype=np.float32)[:, None] * frequency.astype(np.float32)[None, :]
    cos = np.cos(angles.astype(np.float64)).astype(np.float32)
    sin = np.sin(angles.astype(np.float64)).astype(np.float32)
    return np.concatenate([cos] * 4, axis=1), np.concatenate([-sin, sin, -sin, sin], axis=1)


def swap_halves(chunk):
    lane = iota(chunk.shape, 1)
    return jnp.where(
        lane % HEAD_DIM < HEAD_DIM // 2, pltpu.roll(chunk, 96, 1), pltpu.roll(chunk, 32, 1)
    )


def place_kernel(experts, cap, routes_ref, rank_col_ref, rank_row_ref, flat_ref, flat_t_ref):
    rows = routes_ref.shape[0]
    lane = iota((rows, LANES), 1)
    first, second = routes_ref[:, 0:1], routes_ref[:, 1:2]
    hot_first, hot_second = first == lane, second == lane
    hot = (hot_first.astype(F32) + hot_second.astype(F32)).astype(BF16)
    earlier = jnp.where(rank_row_ref[...] < rank_col_ref[...], 1.0, 0.0).astype(BF16)
    counts = dot(earlier, hot)

    def flat(hit, route):
        slot = jnp.sum(jnp.where(hit, counts, 0.0), axis=1, keepdims=True).astype(jnp.int32)
        return jnp.where((route < experts) & (slot < cap), route * cap + slot, experts * cap)

    out = jnp.where(
        lane == 0, flat(hot_first, first), jnp.where(lane == 1, flat(hot_second, second), 0)
    )
    flat_ref[...] = out
    flat_t_ref[...] = out.astype(F32).T[:8]


def place(routes, ranks, experts, cap):
    rows = routes.shape[0]
    return pl.pallas_call(
        functools.partial(place_kernel, experts, cap),
        out_shape=(
            jax.ShapeDtypeStruct((rows, LANES), jnp.int32),
            jax.ShapeDtypeStruct((8, rows), F32),
        ),
        compiler_params=params(32),
        cost_estimate=cost(2 * rows * rows * LANES, 8 * rows * LANES),
        name="place",
    )(routes, ranks.reshape(rows, 1), ranks.reshape(1, rows))


def qkv_kernel(ctx_ref, x_ref, gain_ref, w_ref, cos_ref, sin_ref, out_ref, aone_ref):
    width = x_ref.shape[1]
    half = width // 2
    values = x_ref[...].astype(F32)
    scale = lax.rsqrt(jnp.mean(values * values, axis=-1, keepdims=True) + EPS)
    gain = gain_ref[0].astype(F32).T[0:1]
    normed = (values * scale * gain).astype(BF16)
    aone_ref[...] = normed
    cos, sin = cos_ref[...], sin_ref[...]
    for side in range(2):
        product = dot(normed, w_ref[side])
        for which in range(3):
            for pair in range(half // LANES):
                at = which * half + pair * LANES
                chunk = product[:, at : at + LANES]
                if which < 2:
                    chunk = chunk * cos + swap_halves(chunk) * sin
                if which == 0:
                    chunk = chunk * HEAD_DIM ** (-0.5)
                out_ref[side, which, :, pair * LANES : (pair + 1) * LANES] = chunk.astype(BF16)


def project(ctx, x, w_qkv, cos, sin):
    rows, width = x.shape
    blocks = rows // TB
    return pl.pallas_call(
        qkv_kernel,
        grid_spec=pltpu.PrefetchScalarGridSpec(
            num_scalar_prefetch=1,
            grid=(blocks,),
            in_specs=[
                pl.BlockSpec((TB, width), lambda i, c: (i, 0)),
                pl.BlockSpec((1, width, LANES), lambda i, c: (0, 0, 3 * width // 2 // LANES)),
                pl.BlockSpec((2, width, 3 * width // 2), lambda i, c: (0, 0, 0)),
                pl.BlockSpec((TB, LANES), lambda i, c: (c[0] * blocks + i, 0)),
                pl.BlockSpec((TB, LANES), lambda i, c: (c[0] * blocks + i, 0)),
            ],
            out_specs=[
                pl.BlockSpec((2, 3, TB, width // 2), lambda i, c: (0, 0, i, 0)),
                pl.BlockSpec((TB, width), lambda i, c: (i, 0)),
            ],
        ),
        out_shape=(
            jax.ShapeDtypeStruct((2, 3, rows, width // 2), BF16),
            jax.ShapeDtypeStruct((rows, width), BF16),
        ),
        compiler_params=params(40),
        cost_estimate=cost(6 * rows * width * width, 6 * width * width + 12 * rows * width),
        name="project",
    )(ctx, x, w_qkv, w_qkv, cos, sin)


def head_masks():
    lane = iota((TQ, LANES), 1)
    low = jnp.where(lane < HEAD_DIM, 1.0, 0.0).astype(BF16)
    return low, (1.0 - low.astype(F32)).astype(BF16)


def attend_kernel(first_ref, q_ref, k_ref, v_ref, lo_ref, o_ref, lse_ref, vt_ref):
    per = q_ref.shape[2] // TQ
    count = 2 * per
    masks = head_masks()
    sub = iota((TQ, TQ), 0)
    diagonal = sub <= iota((TQ, TQ), 1)

    def turn(tile, carry):
        vt_ref[tile] = v_ref[tile // per, 0, pl.ds((tile % per) * TQ, TQ), :].T
        return carry

    lax.fori_loop(0, count, turn, 0)

    def q_step(qi, carry):
        rows = pl.ds((qi % per) * TQ, TQ)
        query = q_ref[qi // per, 0, rows, :]
        queries = [query * mask for mask in masks]
        low = lo_ref[qi]
        keys = k_ref[qi // per, 0, rows, :]
        turned = vt_ref[qi]
        ok = diagonal & (sub >= low - qi * TQ)
        state = []
        for head in range(2):
            scores = jnp.where(ok, dot_nt(keys, queries[head]), MASKED)
            peak = jnp.max(scores, axis=0, keepdims=True)
            probs = jnp.exp(scores - peak)
            total = jnp.sum(probs, axis=0, keepdims=True)
            mixed = dot(turned[head * HEAD_DIM : (head + 1) * HEAD_DIM], probs.astype(BF16))
            state += [peak, total, mixed]

        def k_step(ki, state):
            keys = k_ref[ki // per, 0, pl.ds((ki % per) * TQ, TQ), :]
            turned = vt_ref[ki]
            ok = sub >= low - ki * TQ
            new = []
            for head in range(2):
                peak, total, mixed = state[3 * head : 3 * head + 3]
                scores = jnp.where(ok, dot_nt(keys, queries[head]), MASKED)
                top = jnp.maximum(peak, jnp.max(scores, axis=0, keepdims=True))
                shrink = jnp.exp(peak - top)
                probs = jnp.exp(scores - top)
                total = total * shrink + jnp.sum(probs, axis=0, keepdims=True)
                part = dot(turned[head * HEAD_DIM : (head + 1) * HEAD_DIM], probs.astype(BF16))
                new += [top, total, mixed * shrink + part]
            return tuple(new)

        state = lax.fori_loop(first_ref[qi], qi, k_step, tuple(state))
        out = jnp.concatenate([state[2] / state[1], state[5] / state[4]], axis=0)
        o_ref[qi // per, rows, :] = out.T.astype(BF16)
        lse_ref[0, qi, 0:1, :] = state[0] + jnp.log(state[1])
        lse_ref[0, qi, 1:2, :] = state[3] + jnp.log(state[4])
        return carry

    lax.fori_loop(0, count, q_step, 0)


def part_spec(which, rows):
    return pl.BlockSpec((2, 1, rows, LANES), lambda p, first, which=which: (0, which, 0, p))


def attend(first, qkv, low):
    _, _, rows, half = qkv.shape
    pairs = half // LANES
    tiles = 2 * rows // TQ
    return pl.pallas_call(
        attend_kernel,
        grid_spec=pltpu.PrefetchScalarGridSpec(
            num_scalar_prefetch=1,
            grid=(pairs,),
            in_specs=[
                part_spec(0, rows),
                part_spec(1, rows),
                part_spec(2, rows),
                pl.BlockSpec((tiles, 1, TQ), lambda p, first: (0, 0, 0)),
            ],
            out_specs=[
                pl.BlockSpec((2, rows, LANES), lambda p, first: (0, 0, p)),
                pl.BlockSpec((1, tiles, 8, TQ), lambda p, first: (p, 0, 0, 0)),
            ],
            scratch_shapes=[pltpu.VMEM((tiles, LANES, TQ), BF16)],
        ),
        out_shape=(
            jax.ShapeDtypeStruct((2, rows, half), BF16),
            jax.ShapeDtypeStruct((pairs, tiles, 8, TQ), F32),
        ),
        compiler_params=params(40),
        cost_estimate=cost(40e9, 16 * rows * half, 12e6),
        name="attend",
    )(first, qkv, qkv, qkv, low)


def attend_back_kernel(
    first_ref,
    q_ref,
    k_ref,
    v_ref,
    do_ref,
    o_ref,
    lse_ref,
    lo_ref,
    cos_ref,
    sin_ref,
    g_ref,
    kt_ref,
    delta_ref,
    dk_ref,
    dv_ref,
):
    per = q_ref.shape[2] // TQ
    count = 2 * per
    masks = head_masks()
    sub = iota((TQ, TQ), 0)
    diagonal = sub <= iota((TQ, TQ), 1)

    def prepare(tile, carry):
        rows = pl.ds((tile % per) * TQ, TQ)
        kt_ref[tile] = k_ref[tile // per, 0, rows, :].T
        both = o_ref[tile // per, rows, :].astype(F32) * do_ref[tile // per, rows, :].astype(F32)
        both = both.T
        delta_ref[tile, 0:1, :] = jnp.sum(both[:HEAD_DIM], axis=0, keepdims=True)
        delta_ref[tile, 1:2, :] = jnp.sum(both[HEAD_DIM:], axis=0, keepdims=True)
        dk_ref[tile] = jnp.zeros((TQ, LANES), F32)
        dv_ref[tile] = jnp.zeros((TQ, LANES), F32)
        return carry

    lax.fori_loop(0, count, prepare, 0)

    def q_step(qi, carry):
        rows = pl.ds((qi % per) * TQ, TQ)
        query = q_ref[qi // per, 0, rows, :]
        grad = do_ref[qi // per, rows, :]
        queries = [query * mask for mask in masks]
        grads = [grad * mask for mask in masks]
        both_queries = jnp.concatenate(queries, axis=0)
        both_grads = jnp.concatenate(grads, axis=0)
        low = lo_ref[qi]
        lse = [lse_ref[0, qi, h : h + 1, :] for h in range(2)]
        delta = [delta_ref[qi, h : h + 1, :] for h in range(2)]

        def tile(ki, ok, sums):
            at = pl.ds((ki % per) * TQ, TQ)
            keys = k_ref[ki // per, 0, at, :]
            values = v_ref[ki // per, 0, at, :]
            turned = kt_ref[ki]
            all_probs, all_scores, new = [], [], []
            for h in range(2):
                scores = jnp.where(ok, dot_nt(keys, queries[h]), MASKED)
                probs = jnp.exp(scores - lse[h])
                grad_probs = dot_nt(values, grads[h])
                grad_scores = (probs * (grad_probs - delta[h])).astype(BF16)
                new.append(
                    sums[h] + dot(turned[h * HEAD_DIM : (h + 1) * HEAD_DIM], grad_scores)
                )
                all_probs.append(probs.astype(BF16))
                all_scores.append(grad_scores)
            dv_ref[ki] += dot(jnp.concatenate(all_probs, axis=1), both_grads)
            dk_ref[ki] += dot(jnp.concatenate(all_scores, axis=1), both_queries)
            return tuple(new)

        start = jnp.zeros((HEAD_DIM, TQ), F32)
        sums = tile(qi, diagonal & (sub >= low - qi * TQ), (start, start))
        sums = lax.fori_loop(
            first_ref[qi], qi, lambda ki, s: tile(ki, sub >= low - ki * TQ, s), sums
        )
        grad_query = jnp.concatenate(sums, axis=0).T * HEAD_DIM ** (-0.5)
        cos, sin = cos_ref[qi // per, rows, :], sin_ref[qi // per, rows, :]
        g_ref[qi // per, 0, rows, :] = (grad_query * cos - swap_halves(grad_query) * sin).astype(
            BF16
        )
        return carry

    lax.fori_loop(0, count, q_step, 0)

    def finish(tile, carry):
        rows = pl.ds((tile % per) * TQ, TQ)
        cos, sin = cos_ref[tile // per, rows, :], sin_ref[tile // per, rows, :]
        grad_key = dk_ref[tile]
        g_ref[tile // per, 1, rows, :] = (grad_key * cos - swap_halves(grad_key) * sin).astype(BF16)
        g_ref[tile // per, 2, rows, :] = dv_ref[tile].astype(BF16)
        return carry

    lax.fori_loop(0, count, finish, 0)


def attend_back(first, qkv, grad_o, o, lse, low, cos, sin):
    _, _, rows, half = qkv.shape
    pairs = half // LANES
    tiles = 2 * rows // TQ
    side = pl.BlockSpec((2, rows, LANES), lambda p, first: (0, 0, p))
    table = pl.BlockSpec((2, rows, LANES), lambda p, first: (0, 0, 0))
    return pl.pallas_call(
        attend_back_kernel,
        grid_spec=pltpu.PrefetchScalarGridSpec(
            num_scalar_prefetch=1,
            grid=(pairs,),
            in_specs=[
                part_spec(0, rows),
                part_spec(1, rows),
                part_spec(2, rows),
                side,
                side,
                pl.BlockSpec((1, tiles, 8, TQ), lambda p, first: (p, 0, 0, 0)),
                pl.BlockSpec((tiles, 1, TQ), lambda p, first: (0, 0, 0)),
                table,
                table,
            ],
            out_specs=pl.BlockSpec((2, 3, rows, LANES), lambda p, first: (0, 0, 0, p)),
            scratch_shapes=[
                pltpu.VMEM((tiles, LANES, TQ), BF16),
                pltpu.VMEM((tiles, 8, TQ), F32),
                pltpu.VMEM((tiles, TQ, LANES), F32),
                pltpu.VMEM((tiles, TQ, LANES), F32),
            ],
        ),
        out_shape=jax.ShapeDtypeStruct((2, 3, rows, half), BF16),
        compiler_params=params(48),
        cost_estimate=cost(100e9, 32 * rows * half, 12e6),
        name="attend_back",
    )(first, qkv, qkv, qkv, grad_o, o, lse, low, cos, sin)


def middle_kernel(
    total, x_ref, o_ref, w_ref, extra_ref, prev_ref, res_ref, routes_ref, hres_ref, atwo_ref, stat_ref
):
    attended = jnp.concatenate([o_ref[0], o_ref[1]], axis=1)
    hres = x_ref[...].astype(F32) + jnp.concatenate(
        [dot(attended, w_ref[0]), dot(attended, w_ref[1])], axis=1
    )
    hres_ref[...] = hres
    scale = lax.rsqrt(jnp.mean(hres * hres, axis=-1, keepdims=True) + EPS)
    extra = extra_ref[0]
    gain = extra.astype(F32).T[total + 4 : total + 5]
    atwo = (hres * scale * gain).astype(BF16)
    atwo_ref[...] = atwo
    logits = dot(atwo, extra)
    for j in range(total):
        logits = logits + prev_ref[:, j : j + 1] * res_ref[j : j + 1, :]
    lane = iota(logits.shape, 1)

    def soft(inside):
        peak = jnp.max(jnp.where(inside, logits, -jnp.inf), axis=1, keepdims=True)
        powers = jnp.where(inside, jnp.exp(jnp.where(inside, logits - peak, 0.0)), 0.0)
        return powers / jnp.sum(powers, axis=1, keepdims=True)

    probs = soft(lane < total)
    stat = probs
    for j in range(2):
        start = total + 2 * j
        stat = stat + soft((lane >= start) & (lane < start + 2))
    stat = jnp.where(lane == total + 4, scale, stat)
    for k in range(2):
        gate = jnp.sum(
            jnp.where(lane == routes_ref[:, k : k + 1], probs, 0.0), axis=1, keepdims=True
        )
        stat = jnp.where(lane == total + 5 + k, gate, stat)
    stat_ref[...] = stat


def middle(total, x, o, w_out, prev, res, routes):
    rows, width = x.shape
    token = lambda i: (i, 0)
    whole = lambda i: (0, 0)
    return pl.pallas_call(
        functools.partial(middle_kernel, total),
        grid=(rows // TB,),
        in_specs=[
            pl.BlockSpec((TB, width), token),
            pl.BlockSpec((2, TB, width // 2), lambda i: (0, i, 0)),
            pl.BlockSpec((2, width, width // 2), lambda i: (0, 0, 0)),
            pl.BlockSpec((1, width, LANES), lambda i: (0, 0, width // 2 // LANES)),
            pl.BlockSpec((TB, total), token),
            pl.BlockSpec((total, LANES), whole),
            pl.BlockSpec((TB, 2), token),
        ],
        out_specs=[
            pl.BlockSpec((TB, width), token),
            pl.BlockSpec((TB, width), token),
            pl.BlockSpec((TB, LANES), token),
        ],
        out_shape=(
            jax.ShapeDtypeStruct((rows, width), F32),
            jax.ShapeDtypeStruct((rows, width), BF16),
            jax.ShapeDtypeStruct((rows, LANES), F32),
        ),
        compiler_params=params(40),
        cost_estimate=cost(2 * rows * width * width, 2 * width * width + 10 * rows * width),
        name="middle",
    )(x, o, w_out, w_out, prev, res, routes)


def dispatch_kernel(total, flat_ref, atwo_ref, dy_ref, stat_ref, rows_ref, grads_ref):
    cap = rows_ref.shape[1]
    tokens = atwo_ref.shape[0]
    slot = (iota((cap, tokens), 0) + pl.program_id(0) * cap).astype(F32)
    gates = stat_ref[...].T
    first, second = flat_ref[0:1, :] == slot, flat_ref[1:2, :] == slot
    hot = jnp.where(first | second, 1.0, 0.0).astype(BF16)
    gate = jnp.sum(
        jnp.where(first, gates[total + 5 : total + 6], 0.0)
        + jnp.where(second, gates[total + 6 : total + 7], 0.0),
        axis=1,
        keepdims=True,
    )
    rows_ref[0] = dot(hot, atwo_ref[...]).astype(BF16)
    grads_ref[0] = (dot(hot, dy_ref[...]) * gate).astype(BF16)


def dispatch(total, experts, cap, flat_t, atwo, dy, stat):
    rows, width = atwo.shape
    whole = lambda e: (0, 0)
    return pl.pallas_call(
        functools.partial(dispatch_kernel, total),
        grid=(experts,),
        in_specs=[
            pl.BlockSpec((8, rows), whole),
            pl.BlockSpec((rows, width), whole),
            pl.BlockSpec((rows, width), whole),
            pl.BlockSpec((rows, LANES), whole),
        ],
        out_specs=[pl.BlockSpec((1, cap, width), lambda e: (e, 0, 0))] * 2,
        out_shape=(jax.ShapeDtypeStruct((experts, cap, width), BF16),) * 2,
        compiler_params=params(40),
        cost_estimate=cost(4 * experts * cap * rows * width, 8 * rows * width),
        name="dispatch",
    )(flat_t, atwo, dy, stat)


def up_kernel(x_ref, wg_ref, wu_ref, wd_ref, flow_ref, z_ref, a_ref, b_ref, acc_ref):
    step = pl.program_id(0)
    rows = x_ref[...]
    gate = dot(rows, wg_ref[0])
    up = dot(rows, wu_ref[0])
    sig = 1.0 / (1.0 + jnp.exp(-gate))
    swish = gate * sig
    hidden = (swish * up).astype(BF16)
    z_ref[...] = hidden
    a_ref[...] = (up * sig * (1.0 + gate * (1.0 - sig))).astype(BF16)
    b_ref[...] = swish.astype(BF16)
    part = dot(hidden, jnp.concatenate([wd_ref[0], wd_ref[1]], axis=1))

    @pl.when(step == 0)
    def _():
        acc_ref[...] = part

    @pl.when(step > 0)
    def _():
        acc_ref[...] += part

    @pl.when(step == pl.num_programs(0) - 1)
    def _():
        flow_ref[...] = acc_ref[...].astype(BF16)


def weight_specs(width, hidden):
    chunks = hidden // 2 // FC
    wide = pl.BlockSpec((1, width, FC), lambda f: (f // chunks, 0, f % chunks))
    down = pl.BlockSpec((2, FC, width // 2), lambda f: (0, f, 0))
    return wide, down


def expert_up(x, wg, wu, wd):
    rows, width = x.shape
    hidden = wd.shape[1]
    wide, down = weight_specs(width, hidden)
    whole = pl.BlockSpec((rows, width), lambda f: (0, 0))
    chunk = pl.BlockSpec((rows, FC), lambda f: (0, f))
    return pl.pallas_call(
        up_kernel,
        grid=(hidden // FC,),
        in_specs=[whole, wide, wide, down],
        out_specs=[whole, chunk, chunk, chunk],
        out_shape=(
            jax.ShapeDtypeStruct((rows, width), BF16),
            jax.ShapeDtypeStruct((rows, hidden), BF16),
            jax.ShapeDtypeStruct((rows, hidden), BF16),
            jax.ShapeDtypeStruct((rows, hidden), BF16),
        ),
        scratch_shapes=[pltpu.VMEM((rows, width), F32)],
        compiler_params=params(48),
        cost_estimate=cost(6 * rows * width * hidden, 6 * width * hidden + 6 * rows * hidden, rows * hidden),
        name="expert_up",
    )(x, wg, wu, wd)


def down_kernel(dflow_ref, wg_ref, wu_ref, wd_ref, a_ref, b_ref, drow_ref, dg_ref, du_ref, acc_ref):
    step = pl.program_id(0)
    dz = dot_nt(dflow_ref[...], jnp.concatenate([wd_ref[0], wd_ref[1]], axis=1))
    dg = (dz * a_ref[...].astype(F32)).astype(BF16)
    du = (dz * b_ref[...].astype(F32)).astype(BF16)
    dg_ref[...] = dg
    du_ref[...] = du
    part = dot_nt(dg, wg_ref[0]) + dot_nt(du, wu_ref[0])

    @pl.when(step == 0)
    def _():
        acc_ref[...] = part

    @pl.when(step > 0)
    def _():
        acc_ref[...] += part

    @pl.when(step == pl.num_programs(0) - 1)
    def _():
        drow_ref[...] = acc_ref[...].astype(BF16)


def expert_down(dflow, wg, wu, wd, a, b):
    rows, width = dflow.shape
    hidden = wd.shape[1]
    wide, down = weight_specs(width, hidden)
    whole = pl.BlockSpec((rows, width), lambda f: (0, 0))
    chunk = pl.BlockSpec((rows, FC), lambda f: (0, f))
    return pl.pallas_call(
        down_kernel,
        grid=(hidden // FC,),
        in_specs=[whole, wide, wide, down, chunk, chunk],
        out_specs=[whole, chunk, chunk],
        out_shape=(
            jax.ShapeDtypeStruct((rows, width), BF16),
            jax.ShapeDtypeStruct((rows, hidden), BF16),
            jax.ShapeDtypeStruct((rows, hidden), BF16),
        ),
        scratch_shapes=[pltpu.VMEM((rows, width), F32)],
        compiler_params=params(48),
        cost_estimate=cost(6 * rows * width * hidden, 6 * width * hidden + 8 * rows * hidden),
        name="expert_down",
    )(dflow, wg, wu, wd, a, b)


def wgrad_kernel(x_ref, dflow_ref, z_ref, dg_ref, du_ref, gg_ref, gu_ref, gd_ref, xt_ref):
    @pl.when(pl.program_id(0) == 0)
    def _():
        xt_ref[...] = x_ref[...].T

    turned = xt_ref[...]
    gg_ref[0] = dot(turned, dg_ref[...]).astype(BF16)
    gu_ref[0] = dot(turned, du_ref[...]).astype(BF16)
    down = dot(z_ref[...].T, dflow_ref[...]).astype(BF16)
    half = down.shape[1] // 2
    gd_ref[0] = down[:, :half]
    gd_ref[1] = down[:, half:]


def expert_wgrad(x, dflow, z, dg, du):
    rows, width = x.shape
    hidden = z.shape[1]
    wide, down = weight_specs(width, hidden)
    whole = pl.BlockSpec((rows, width), lambda f: (0, 0))
    chunk = pl.BlockSpec((rows, FC), lambda f: (0, f))
    return pl.pallas_call(
        wgrad_kernel,
        grid=(hidden // FC,),
        in_specs=[whole, whole, chunk, chunk, chunk],
        out_specs=[wide, wide, down],
        out_shape=(
            jax.ShapeDtypeStruct((2, width, hidden // 2), BF16),
            jax.ShapeDtypeStruct((2, width, hidden // 2), BF16),
            jax.ShapeDtypeStruct((2, hidden, width // 2), BF16),
        ),
        scratch_shapes=[pltpu.VMEM((width, rows), BF16)],
        compiler_params=params(48),
        cost_estimate=cost(6 * rows * width * hidden, 6 * width * hidden + 6 * rows * hidden),
        name="expert_wgrad",
    )(x, dflow, z, dg, du)


def combine_kernel(
    experts,
    total,
    flow_ref,
    drow_ref,
    flat_ref,
    stat_ref,
    routes_ref,
    hres_ref,
    atwo_ref,
    dy_ref,
    o_ref,
    extra_ref,
    w_ref,
    prev_ref,
    out_ref,
    dh_ref,
    dolow_ref,
    gw_ref,
    small_ref,
    acc_ref,
):
    step = pl.program_id(0)
    slots = flow_ref.shape[0]
    half = o_ref.shape[2]
    extra = extra_ref[0]
    rows = extra.astype(F32).T
    gain = rows[total + 4 : total + 5]
    stat = stat_ref[...]
    hres = hres_ref[...]
    dy = dy_ref[...].astype(F32)
    scale = stat[:, total + 4 : total + 5]
    gates = [stat[:, total + 5 + k : total + 6 + k] for k in range(2)]
    ntwo = hres * scale * gain
    spread = iota((TB, slots), 1)
    hots = [flat_ref[:, k : k + 1] == spread for k in range(2)]
    returned = flow_ref[...]
    mixes = [[stat[:, total + 2 * j + i : total + 2 * j + i + 1] for i in range(2)] for j in range(2)]
    vecs = [rows[total + 5 + j : total + 6 + j] for j in range(2)]
    moe = jnp.zeros_like(hres)
    lane = iota((TB, LANES), 1)
    dpgate = jnp.zeros((TB, LANES), F32)
    weight = jnp.zeros((TB, 1), F32)
    const_weights = [jnp.zeros((TB, 1), F32)] * 2
    for k in range(2):
        route = routes_ref[:, k : k + 1]
        epair = dot(jnp.where(hots[k], 1.0, 0.0).astype(BF16), returned)
        share = jnp.where(route == experts + 1, 1.0, 0.0)
        weight = weight + share * gates[k]
        for j in range(2):
            chosen = jnp.where(route == experts + 2 + j, 1.0, 0.0)
            share = share + chosen * mixes[j][0]
            epair = epair + (chosen * mixes[j][1]) * vecs[j]
            const_weights[j] = const_weights[j] + chosen * gates[k]
        epair = epair + share * ntwo
        moe = moe + gates[k] * epair
        dgate = jnp.sum(dy * epair, axis=1, keepdims=True)
        dpgate = dpgate + jnp.where(lane == route, dgate, 0.0)
    out_ref[...] = (hres + moe).astype(BF16)

    pgate = jnp.where(lane < total, stat, 0.0)
    dlogit = pgate * (dpgate - jnp.sum(pgate * dpgate, axis=1, keepdims=True))
    dot_normed = jnp.sum(dy * ntwo, axis=1, keepdims=True)
    droute = dlogit
    vec_rows = []
    for j in range(2):
        dot_vec = jnp.sum(dy * vecs[j], axis=1, keepdims=True)
        grads = [const_weights[j] * dot_normed, const_weights[j] * dot_vec]
        inner = mixes[j][0] * grads[0] + mixes[j][1] * grads[1]
        for i in range(2):
            droute = jnp.where(
                lane == total + 2 * j + i, mixes[j][i] * (grads[i] - inner), droute
            )
        weight = weight + const_weights[j] * mixes[j][0]
        vec_rows.append(jnp.sum((const_weights[j] * mixes[j][1]) * dy, axis=0, keepdims=True))
    droute = droute.astype(BF16)
    hot_any = jnp.where(hots[0] | hots[1], 1.0, 0.0).astype(BF16)
    dntwo = weight * dy + dot_nt(droute, extra) + dot(hot_any, drow_ref[...])
    turned = dntwo * gain
    inner = jnp.mean(hres * turned, axis=1, keepdims=True)
    dh = dy + scale * turned - hres * (scale * scale * scale * inner)
    dh_ref[...] = dh
    dhlow = dh.astype(BF16)
    dolow = (dot_nt(dhlow[:, :half], w_ref[0]) + dot_nt(dhlow[:, half:], w_ref[1])).astype(BF16)
    dolow_ref[0] = dolow[:, :half]
    dolow_ref[1] = dolow[:, half:]
    gain_row = jnp.sum(dntwo * hres * scale, axis=0, keepdims=True)
    route_rows = dot(droute.T, atwo_ref[...])
    res_rows = lax.dot_general(
        prev_ref[...],
        dlogit,
        (((0,), (0,)), ((), ())),
        precision=HIGH,
        preferred_element_type=F32,
    )
    width = hres.shape[1]
    res_rows = jnp.concatenate([res_rows, jnp.zeros((total, width - LANES), F32)], axis=1)
    small = jnp.concatenate(
        [route_rows[: total + 4], gain_row, vec_rows[0], vec_rows[1], jnp.zeros((1, width), F32), res_rows],
        axis=0,
    )
    part = dot(jnp.concatenate([o_ref[0], o_ref[1]], axis=1).T, dhlow)

    @pl.when(step == 0)
    def _():
        small_ref[...] = small
        acc_ref[...] = part

    @pl.when(step > 0)
    def _():
        small_ref[...] += small
        acc_ref[...] += part

    @pl.when(step == pl.num_programs(0) - 1)
    def _():
        for side in range(2):
            gw_ref[side] = acc_ref[:, side * half : (side + 1) * half].astype(BF16)


def combine(experts, total, flow, drow, flat, stat, routes, hres, atwo, dy, o, w_out, prev):
    rows, width = hres.shape
    slots = flow.shape[0]
    half = width // 2
    token = lambda i: (i, 0)
    whole = lambda i: (0, 0)
    side = pl.BlockSpec((2, TB, half), lambda i: (0, i, 0))
    weight = pl.BlockSpec((2, width, half), lambda i: (0, 0, 0))
    small_rows = 2 * total + 8
    return pl.pallas_call(
        functools.partial(combine_kernel, experts, total),
        grid=(rows // TB,),
        in_specs=[
            pl.BlockSpec((slots, width), whole),
            pl.BlockSpec((slots, width), whole),
            pl.BlockSpec((TB, LANES), token),
            pl.BlockSpec((TB, LANES), token),
            pl.BlockSpec((TB, 2), token),
            pl.BlockSpec((TB, width), token),
            pl.BlockSpec((TB, width), token),
            pl.BlockSpec((TB, width), token),
            side,
            pl.BlockSpec((1, width, LANES), lambda i: (0, 0, half // LANES)),
            weight,
            pl.BlockSpec((TB, total), token),
        ],
        out_specs=[
            pl.BlockSpec((TB, width), token),
            pl.BlockSpec((TB, width), token),
            side,
            weight,
            pl.BlockSpec((small_rows, width), whole),
        ],
        out_shape=(
            jax.ShapeDtypeStruct((rows, width), BF16),
            jax.ShapeDtypeStruct((rows, width), F32),
            jax.ShapeDtypeStruct((2, rows, half), BF16),
            jax.ShapeDtypeStruct((2, width, half), BF16),
            jax.ShapeDtypeStruct((small_rows, width), F32),
        ),
        scratch_shapes=[pltpu.VMEM((width, width), F32)],
        compiler_params=params(56),
        cost_estimate=cost(
            6 * rows * slots * width + 4 * rows * width * width, 30 * rows * width + 8 * width * width
        ),
        name="combine",
    )(flow, drow, flat, stat, routes, hres, atwo, dy, o, w_out, w_out, prev)


def project_back_kernel(
    g_ref, w_ref, gain_ref, x_ref, aone_ref, dh_ref, gwo_ref, out_ref, gw_ref, gain_out_ref, acc_ref
):
    step = pl.program_id(0)
    half = g_ref.shape[3]
    turned = aone_ref[...].T
    dnone = None
    for side in range(2):
        grad = jnp.concatenate([g_ref[side, which] for which in range(3)], axis=1)
        part = dot_nt(grad, w_ref[side])
        dnone = part if dnone is None else dnone + part
        weight = dot(turned, grad)

        @pl.when(step == 0)
        def _():
            acc_ref[side] = weight

        @pl.when(step > 0)
        def _():
            acc_ref[side] += weight

    values = x_ref[...].astype(F32)
    scale = lax.rsqrt(jnp.mean(values * values, axis=-1, keepdims=True) + EPS)
    scaled = dnone * gain_ref[0].astype(F32).T[0:1]
    inner = jnp.mean(values * scaled, axis=1, keepdims=True)
    out_ref[...] = dh_ref[...] + scale * scaled - values * (scale * scale * scale * inner)
    row = jnp.sum(dnone * values * scale, axis=0, keepdims=True)

    @pl.when(step == 0)
    def _():
        gain_out_ref[...] = row

    @pl.when(step > 0)
    def _():
        gain_out_ref[...] += row

    @pl.when(step == pl.num_programs(0) - 1)
    def _():
        for side in range(2):
            for which in range(3):
                at = which * half
                gw_ref[side, which] = acc_ref[side, :, at : at + half].astype(BF16)
            gw_ref[side, 3] = gwo_ref[side]


def project_back(grad, w_qkv, x, aone, dh, grad_out_w):
    rows, width = x.shape
    half = width // 2
    token = lambda i: (i, 0)
    whole = lambda i: (0, 0)
    return pl.pallas_call(
        project_back_kernel,
        grid=(rows // TB,),
        in_specs=[
            pl.BlockSpec((2, 3, TB, half), lambda i: (0, 0, i, 0)),
            pl.BlockSpec((2, width, 3 * half), lambda i: (0, 0, 0)),
            pl.BlockSpec((1, width, LANES), lambda i: (0, 0, 3 * half // LANES)),
            pl.BlockSpec((TB, width), token),
            pl.BlockSpec((TB, width), token),
            pl.BlockSpec((TB, width), token),
            pl.BlockSpec((2, width, half), lambda i: (0, 0, 0)),
        ],
        out_specs=[
            pl.BlockSpec((TB, width), token),
            pl.BlockSpec((2, 4, width, half), lambda i: (0, 0, 0, 0)),
            pl.BlockSpec((1, width), whole),
        ],
        out_shape=(
            jax.ShapeDtypeStruct((rows, width), F32),
            jax.ShapeDtypeStruct((2, 4, width, half), BF16),
            jax.ShapeDtypeStruct((1, width), F32),
        ),
        scratch_shapes=[pltpu.VMEM((2, width, 3 * half), F32)],
        compiler_params=params(56),
        cost_estimate=cost(12 * rows * width * width, 18 * width * width + 20 * rows * width),
        name="project_back",
    )(grad, w_qkv, w_qkv, x, aone, dh, grad_out_w)


def loop(count, body):
    if count <= 4:
        for step in range(count):
            body(step)
    else:
        lax.fori_loop(0, count, lambda step, carry: (body(step), carry)[1], 0)


def reduce_kernel(
    gain_at,
    grads_ref,
    small_ref,
    gain_ref,
    out_ref,
    small_out_ref,
    core_in,
    plane_out,
    plane_in,
    slab_out,
    slab_in,
    final,
    own_ref,
    small_own,
    small_core,
    small_plane,
    small_slab,
    core_sems,
    plane_sems,
    slab_sems,
    final_sems,
    pass_sems,
    small_core_sems,
    small_plane_sems,
    small_slab_sems,
):
    experts = lax.axis_size("expert")
    slabs = lax.axis_size("dp")
    me, core, slab = lax.axis_index("expert"), lax.axis_index("context"), lax.axis_index("dp")
    other = 1 - core

    barrier = pltpu.get_barrier_semaphore()
    pl.semaphore_signal(
        barrier, inc=1, device_id={"context": other}, device_id_type=pl.DeviceIdType.MESH
    )
    for j in range(1, experts):
        pl.semaphore_signal(
            barrier,
            inc=1,
            device_id={"expert": lax.rem(me + j, experts)},
            device_id_type=pl.DeviceIdType.MESH,
        )

    def greet(k):
        pl.semaphore_signal(
            barrier,
            inc=1,
            device_id={"dp": lax.rem(slab + k + 1, slabs)},
            device_id_type=pl.DeviceIdType.MESH,
        )

    loop(slabs - 1, greet)
    pl.semaphore_wait(barrier, experts + slabs - 1)

    def send(src, dst, sems, index, where):
        return pltpu.make_async_remote_copy(
            src_ref=src,
            dst_ref=dst,
            send_sem=sems.at[(0,) + index],
            recv_sem=sems.at[(1,) + index],
            device_id=where,
            device_id_type=pl.DeviceIdType.MESH,
        )

    order = list(range(1, experts)) + [0]
    core_copies = {}
    for j in order:
        core_copies[j] = send(
            grads_ref.at[other, lax.rem(me + j, experts)],
            core_in.at[j],
            core_sems,
            (j,),
            {"context": other},
        )
        core_copies[j].start()
    row = iota(small_ref.shape, 0)
    small_own[...] = small_ref[...] + jnp.where(row == gain_at, gain_ref[...], 0.0)
    small_copy = send(small_own, small_core, small_core_sems, (0,), {"context": other})
    small_copy.start()

    def plane_copy(j, at):
        return send(
            plane_out.at[j - 1, at],
            plane_in.at[j - 1, at],
            plane_sems,
            (j - 1, at),
            {"expert": lax.rem(me + j, experts)},
        )

    for j in range(1, experts):
        core_copies[j].wait_recv()
        which = lax.rem(me + j, experts)

        def pass_on(k, j=j, which=which):
            at = lax.rem(slab + k + 1, slabs)
            plane_out[j - 1, at] = (
                grads_ref[core, which, at].astype(F32) + core_in[j, at].astype(F32)
            ).astype(BF16)
            plane_copy(j, at).start()

        loop(slabs, pass_on)
    core_copies[0].wait_recv()

    small_copy.wait()
    small_plane[me] = small_own[...] + small_core[...]
    small_plane_copies = []
    for j in range(1, experts):
        small_plane_copies.append(
            send(
                small_plane.at[me],
                small_plane.at[me],
                small_plane_sems,
                (j,),
                {"expert": lax.rem(me + j, experts)},
            )
        )
        small_plane_copies[-1].start()

    def gathered(at):
        value = grads_ref[core, me, at].astype(F32) + core_in[0, at].astype(F32)
        for j in range(1, experts):
            plane_copy(j, at).wait_recv()
            value = value + plane_in[j - 1, at].astype(F32)
        return value

    def slab_copy(k):
        return send(
            slab_out.at[k],
            slab_in.at[k],
            slab_sems,
            (k,),
            {"dp": lax.rem(slab + k + 1, slabs)},
        )

    def scatter(k):
        slab_out[k] = gathered(lax.rem(slab + k + 1, slabs)).astype(BF16)
        slab_copy(k).start()

    loop(slabs - 1, scatter)

    for copy in small_plane_copies:
        copy.wait()
    value = small_plane[0]
    for j in range(1, experts):
        value = value + small_plane[j]
    small_slab[slab] = value

    def small_slab_copy(k):
        return send(
            small_slab.at[slab],
            small_slab.at[slab],
            small_slab_sems,
            (k,),
            {"dp": lax.rem(slab + k + 1, slabs)},
        )

    loop(slabs - 1, lambda k: small_slab_copy(k).start())

    own_ref[...] = gathered(slab)

    def collect(k):
        slab_copy(k).wait_recv()
        own_ref[...] += slab_in[k].astype(F32)

    loop(slabs - 1, collect)
    final[core, me] = own_ref[...].astype(BF16)
    final_copies, pass_copies = [], []
    for j in range(1, experts):
        final_copies.append(
            send(
                final.at[core, me],
                final.at[core, me],
                final_sems,
                (j,),
                {"expert": lax.rem(me + j, experts)},
            )
        )
        final_copies[-1].start()
    for j in range(experts):
        source = lax.rem(me + experts - j, experts)
        if j > 0:
            final_copies[j - 1].wait_recv()
        pass_copies.append(
            send(
                final.at[core, source],
                final.at[core, source],
                pass_sems,
                (j,),
                {"context": other},
            )
        )
        pass_copies[-1].start()

    loop(slabs - 1, lambda k: small_slab_copy(k).wait())
    small_out_ref[...] = small_slab[0]

    def add_small(k):
        small_out_ref[...] += small_slab[k + 1]

    loop(slabs - 1, add_small)

    for copy in pass_copies:
        copy.wait_recv()
    half = final.shape[3]
    for which in range(experts):
        for side in range(2):
            out_ref[which, :, side * half : (side + 1) * half] = final[side, which].astype(F32)

    for j in range(experts):
        core_copies[j].wait_send()
    for j in range(1, experts):

        def sent(k, j=j):
            plane_copy(j, k).wait_send()

        loop(slabs, sent)
    loop(slabs - 1, lambda k: slab_copy(k).wait_send())
    for copy in final_copies + pass_copies:
        copy.wait_send()


def reduce_shared(mesh_sizes, grads, small, gain_row, gain_at):
    experts, slabs = mesh_sizes
    _, _, _, rows, half = grads.shape
    small_shape = small.shape
    vmem = pl.BlockSpec(memory_space=pltpu.VMEM)
    dma = pltpu.SemaphoreType.DMA
    return pl.pallas_call(
        functools.partial(reduce_kernel, gain_at),
        in_specs=[vmem] * 3,
        out_specs=[vmem] * 2,
        out_shape=(
            jax.ShapeDtypeStruct((experts, rows, 2 * half), F32),
            jax.ShapeDtypeStruct(small_shape, F32),
        ),
        scratch_shapes=[
            pltpu.VMEM((experts, slabs, rows, half), BF16),
            pltpu.VMEM((experts - 1, slabs, rows, half), BF16),
            pltpu.VMEM((experts - 1, slabs, rows, half), BF16),
            pltpu.VMEM((slabs - 1, rows, half), BF16),
            pltpu.VMEM((slabs - 1, rows, half), BF16),
            pltpu.VMEM((2, experts, rows, half), BF16),
            pltpu.VMEM((rows, half), F32),
            pltpu.VMEM(small_shape, F32),
            pltpu.VMEM(small_shape, F32),
            pltpu.VMEM((experts,) + small_shape, F32),
            pltpu.VMEM((slabs,) + small_shape, F32),
            dma((2, experts)),
            dma((2, experts - 1, slabs)),
            dma((2, slabs - 1)),
            dma((2, experts)),
            dma((2, experts)),
            dma((2, 1)),
            dma((2, experts)),
            dma((2, slabs - 1)),
        ],
        compiler_params=pltpu.CompilerParams(
            collective_id=0, has_side_effects=True, vmem_limit_bytes=56 * MIB
        ),
        cost_estimate=cost(1e6, 2 * grads.size),
        name="reduce_shared",
    )(grads, small, gain_row)


def swap_cores(value):
    return lax.all_to_all(value, "context", split_axis=0, concat_axis=0, tiled=True)


def swap_experts(value):
    return lax.all_to_all(value, "expert", split_axis=0, concat_axis=0, tiled=True)


def on_device(
    tokens,
    segments,
    routes,
    prev_logits,
    ranks,
    cotangent,
    norm_one,
    w_query,
    w_key,
    w_value,
    w_out,
    norm_two,
    router,
    w_res,
    const_mix,
    const_vec,
    w_gate,
    w_up,
    w_down,
):
    experts = lax.axis_size("expert")
    dp = lax.axis_size("dp")
    total = experts + NZ
    _, rows, width = tokens.shape
    hidden = w_gate.shape[2]
    cap = (18 * rows + 8 * total - 1) // (8 * total)
    seq = 2 * rows
    tiles = seq // TQ
    core = lax.axis_index("context")
    half = width // 2

    def mine(shard, size):
        return lax.dynamic_slice_in_dim(shard, core * size, size, 1)

    def widened(columns):
        return jnp.pad(columns, ((0, 0), (0, LANES - columns.shape[1])))

    def gather(shard):
        return lax.all_gather(shard, ("context", "dp"), axis=0).reshape(
            2, dp * shard.shape[0], shard.shape[1]
        )

    w_qkv = gather(
        jnp.concatenate(
            [mine(w_query, half), mine(w_key, half), mine(w_value, half), widened(norm_one[:, None])],
            axis=1,
        )
    )
    extra = jnp.concatenate([router, const_mix, norm_two[:, None], const_vec], axis=1)
    out_w = gather(jnp.concatenate([mine(w_out, half), widened(extra)], axis=1))
    gate_w = gather(mine(w_gate[0], hidden // 2))
    up_w = gather(mine(w_up[0], hidden // 2))
    down_w = gather(mine(w_down[0], half))

    flat, flat_t = place(routes[0], ranks[0, 0], experts, cap)
    segs = lax.all_gather(segments[0], "context", axis=0, tiled=True)
    places = jnp.arange(seq, dtype=jnp.int32)
    starts = jnp.sum((segs[None, :] < segs[:, None]).astype(jnp.int32), axis=1)
    low = jnp.maximum(starts, places - (WIN - 1)).reshape(tiles, 1, TQ)
    first = low[:, 0, 0] // TQ
    cos, sin = rope_tables(seq)
    cos, sin = jnp.asarray(cos), jnp.asarray(sin)
    res = jnp.pad(w_res.astype(F32), ((0, 0), (0, LANES - total)))

    x = tokens[0]
    dy = cotangent[0]
    sent, aone = project(core.reshape(1), x, w_qkv, cos, sin)
    qkv = swap_cores(sent)
    o_heads, lse = attend(first, qkv, low)
    o = swap_cores(o_heads)
    hres, atwo, stat = middle(total, x, o, out_w, prev_logits[0], res, routes[0])
    sent_rows, sent_grads = dispatch(total, experts, cap, flat_t, atwo, dy, stat)
    in_rows = swap_experts(sent_rows).reshape(experts * cap, width)
    in_grads = swap_experts(sent_grads).reshape(experts * cap, width)
    flow, z, a, b = expert_up(in_rows, gate_w, up_w, down_w)
    flow_back = swap_experts(flow.reshape(experts, cap, width)).reshape(experts * cap, width)
    drow, dg, du = expert_down(in_grads, gate_w, up_w, down_w, a, b)
    drow_back = swap_experts(drow.reshape(experts, cap, width)).reshape(experts * cap, width)
    grad_gate, grad_up, grad_down = expert_wgrad(in_rows, in_grads, z, dg, du)

    def scatter_half(grad):
        kept = lax.dynamic_index_in_dim(grad, core, 0, keepdims=False)
        given = lax.dynamic_index_in_dim(grad, 1 - core, 0, keepdims=False)
        taken = lax.ppermute(given, "context", [(0, 1), (1, 0)])
        chip = (kept.astype(F32) + taken.astype(F32)).astype(BF16)
        share = lax.psum_scatter(chip, "dp", scatter_dimension=0, tiled=True)
        both = lax.all_gather(share, "context", axis=1, tiled=True)
        return both.astype(F32)[None]

    total_gate, total_up, total_down = (
        scatter_half(grad_gate),
        scatter_half(grad_up),
        scatter_half(grad_down),
    )

    output, dh, dolow, grad_out_w, small = combine(
        experts,
        total,
        flow_back,
        drow_back,
        flat,
        stat,
        routes[0],
        hres,
        atwo,
        dy,
        o,
        out_w,
        prev_logits[0],
    )
    grad_o = swap_cores(dolow)
    grads_sent = attend_back(
        first,
        qkv,
        grad_o,
        o_heads,
        lse,
        low,
        cos.reshape(2, rows, LANES),
        sin.reshape(2, rows, LANES),
    )
    grads = swap_cores(grads_sent)
    grad_tokens, grad_shared, gain_row = project_back(grads, w_qkv, x, aone, dh, grad_out_w)
    shared, small = reduce_shared(
        (experts, dp),
        grad_shared.reshape(2, 4, dp, width // dp, half),
        small,
        gain_row,
        total + 7,
    )
    part = width // dp
    owned = lax.dynamic_slice_in_dim(small, lax.axis_index("dp") * part, part, 1)
    grad_res_total = small[total + 8 :, :total]
    return (
        output[None],
        grad_tokens[None],
        owned[total + 7],
        shared[0],
        shared[1],
        shared[2],
        shared[3],
        owned[total + 4],
        owned[:total].T,
        grad_res_total,
        owned[total : total + 4].T,
        owned[total + 5 : total + 7].T,
        total_gate,
        total_up,
        total_down,
    )


def solution(mesh):
    token = P(("expert", "dp"), "context", None)
    rows = P("dp", None)
    expert = P("expert", "dp", None)
    in_specs = (
        token,
        P(("expert", "dp"), "context"),
        token,
        token,
        token,
        token,
        P("dp"),
        rows,
        rows,
        rows,
        rows,
        P("dp"),
        rows,
        P(),
        rows,
        rows,
        expert,
        expert,
        expert,
    )
    out_specs = (
        token,
        token,
        P("dp"),
        rows,
        rows,
        rows,
        rows,
        P("dp"),
        rows,
        P(),
        rows,
        rows,
        expert,
        expert,
        expert,
    )
    return jax.shard_map(
        on_device, mesh=mesh, in_specs=in_specs, out_specs=out_specs, check_vma=False
    )
```

```python
import functools

import jax
import jax.numpy as jnp
import numpy as np
from jax import lax
from jax.experimental import pallas as pl
from jax.experimental.pallas import tpu as pltpu
from jax.sharding import PartitionSpec as P

HEADS = 12
HEAD_DIM = 64
WIN = 1024
NZ = 4
GAIN_ONE, GAIN_TWO, VECS = 112, 113, 114
TQ = 256
TB = 256
FC = 256
LANES = 128
EPS = 1e-05
MASKED = -1000000000.0
HIGH = lax.Precision.HIGHEST
F32 = jnp.float32
BF16 = jnp.bfloat16
MIB = 1024 * 1024


def params(mib):
    return pltpu.CompilerParams(vmem_limit_bytes=mib * MIB)


def cost(flops, nbytes, trans=0):
    return pl.CostEstimate(flops=int(flops), bytes_accessed=int(nbytes), transcendentals=int(trans))


def dot(left, right):
    return jnp.dot(left, right, preferred_element_type=F32)


def dot_nt(left, right):
    return lax.dot_general(left, right, (((1,), (1,)), ((), ())), preferred_element_type=F32)


def dot_tn(left, right):
    return lax.dot_general(left, right, (((0,), (0,)), ((), ())), preferred_element_type=F32)


def iota(shape, axis):
    return lax.broadcasted_iota(jnp.int32, shape, axis)


def rope_tables(seq):
    half = HEAD_DIM // 2
    frequency = np.float32(10000.0) ** (
        -np.arange(half, dtype=np.float32) * np.float32(2.0) / np.float32(HEAD_DIM)
    )
    angles = np.arange(seq, dtype=np.float32)[:, None] * frequency.astype(np.float32)[None, :]
    cos = np.cos(angles.astype(np.float64)).astype(np.float32)
    sin = np.sin(angles.astype(np.float64)).astype(np.float32)
    return np.concatenate([cos] * 4, axis=1), np.concatenate([-sin, sin, -sin, sin], axis=1)


def swap_halves(chunk):
    lane = iota(chunk.shape, 1)
    return jnp.where(
        lane % HEAD_DIM < HEAD_DIM // 2, pltpu.roll(chunk, 96, 1), pltpu.roll(chunk, 32, 1)
    )


def loop(count, body):
    if count <= 4:
        for step in range(count):
            body(step)
    else:
        lax.fori_loop(0, count, lambda step, carry: (body(step), carry)[1], 0)


def remote(src, dst, sems, index, where):
    return pltpu.make_async_remote_copy(
        src_ref=src,
        dst_ref=dst,
        send_sem=sems.at[(0,) + index],
        recv_sem=sems.at[(1,) + index],
        device_id=where,
        device_id_type=pl.DeviceIdType.MESH,
    )


def greet_all(axes):
    barrier = pltpu.get_barrier_semaphore()
    total = 0
    for axis in axes:
        size = lax.axis_size(axis)
        me = lax.axis_index(axis)
        total += size - 1

        def greet(k, axis=axis, size=size, me=me):
            pl.semaphore_signal(
                barrier,
                inc=1,
                device_id={axis: lax.rem(me + k + 1, size)},
                device_id_type=pl.DeviceIdType.MESH,
            )

        loop(size - 1, greet)
    pl.semaphore_wait(barrier, total)


def spread_kernel(
    w_query_ref,
    w_key_ref,
    w_value_ref,
    w_out_ref,
    extra_ref,
    out_ref,
    extra_out_ref,
    slab_sems,
    plane_sems,
    core_sems,
    extra_sems,
):
    experts = lax.axis_size("expert")
    slabs = lax.axis_size("dp")
    me, core, slab = lax.axis_index("expert"), lax.axis_index("context"), lax.axis_index("dp")
    half = out_ref.shape[4]
    for which, ref in enumerate((w_query_ref, w_key_ref, w_value_ref, w_out_ref)):
        for side in range(2):

            @pl.when((me == which) & (core == side))
            def _():
                out_ref[which, side, slab] = ref[:, side * half : (side + 1) * half]

    extra_out_ref[slab] = extra_ref[...]
    greet_all(("context", "expert", "dp"))

    def slab_copy(k):
        piece = out_ref.at[me, core, slab]
        return remote(piece, piece, slab_sems, (k,), {"dp": lax.rem(slab + k + 1, slabs)})

    def extra_copy(k):
        piece = extra_out_ref.at[slab]
        return remote(piece, piece, extra_sems, (k,), {"dp": lax.rem(slab + k + 1, slabs)})

    def plane_copy(j, at):
        piece = out_ref.at[me, core, at]
        return remote(
            piece, piece, plane_sems, (j - 1, at), {"expert": lax.rem(me + j, experts)}
        )

    def core_copy(j, at):
        piece = out_ref.at[lax.rem(me + experts - j, experts), core, at]
        return remote(piece, piece, core_sems, (j, at), {"context": 1 - core})

    def share(at):
        for j in range(1, experts):
            plane_copy(j, at).start()
        core_copy(0, at).start()

    loop(slabs - 1, lambda k: extra_copy(k).start())
    loop(slabs - 1, lambda k: slab_copy(k).start())
    share(slab)

    def forward(k):
        slab_copy(k).wait_recv()
        share(lax.rem(slab + slabs - k - 1, slabs))

    loop(slabs - 1, forward)

    def relay(k):
        at = lax.rem(slab + slabs - k, slabs)
        for j in range(1, experts):
            plane_copy(j, at).wait_recv()
            core_copy(j, at).start()

    loop(slabs, relay)
    loop(slabs - 1, lambda k: extra_copy(k).wait())
    loop(slabs - 1, lambda k: slab_copy(k).wait_send())

    def finish(at):
        for j in range(experts):
            core_copy(j, at).wait()
        for j in range(1, experts):
            plane_copy(j, at).wait_send()

    loop(slabs, finish)


def spread(experts, slabs, w_query, w_key, w_value, w_out, extra):
    rows, width = w_query.shape
    half = width // 2
    vmem = pl.BlockSpec(memory_space=pltpu.VMEM)
    dma = pltpu.SemaphoreType.DMA
    return pl.pallas_call(
        spread_kernel,
        in_specs=[vmem] * 5,
        out_specs=[vmem] * 2,
        out_shape=(
            jax.ShapeDtypeStruct((4, 2, slabs, rows, half), BF16),
            jax.ShapeDtypeStruct((slabs,) + extra.shape, F32),
        ),
        scratch_shapes=[
            dma((2, slabs - 1)),
            dma((2, experts - 1, slabs)),
            dma((2, experts, slabs)),
            dma((2, slabs - 1)),
        ],
        compiler_params=pltpu.CompilerParams(
            collective_id=1, has_side_effects=True, vmem_limit_bytes=32 * MIB
        ),
        cost_estimate=cost(1e6, 16 * width * width),
        name="spread",
    )(w_query, w_key, w_value, w_out, extra)


def place_kernel(experts, cap, routes_ref, rank_col_ref, rank_row_ref, flat_ref, flat_t_ref):
    rows = routes_ref.shape[0]
    lane = iota((rows, LANES), 1)
    first, second = routes_ref[:, 0:1], routes_ref[:, 1:2]
    hot_first, hot_second = first == lane, second == lane
    hot = (hot_first.astype(F32) + hot_second.astype(F32)).astype(BF16)
    earlier = jnp.where(rank_row_ref[...] < rank_col_ref[...], 1.0, 0.0).astype(BF16)
    counts = dot(earlier, hot)

    def flat(hit, route):
        slot = jnp.sum(jnp.where(hit, counts, 0.0), axis=1, keepdims=True).astype(jnp.int32)
        return jnp.where((route < experts) & (slot < cap), route * cap + slot, experts * cap)

    out = jnp.where(
        lane == 0, flat(hot_first, first), jnp.where(lane == 1, flat(hot_second, second), 0)
    )
    flat_ref[...] = out
    flat_t_ref[...] = out.astype(F32).T[:8]


def place(routes, ranks, experts, cap):
    rows = routes.shape[0]
    return pl.pallas_call(
        functools.partial(place_kernel, experts, cap),
        out_shape=(
            jax.ShapeDtypeStruct((rows, LANES), jnp.int32),
            jax.ShapeDtypeStruct((8, rows), F32),
        ),
        compiler_params=params(32),
        cost_estimate=cost(2 * rows * rows * LANES, 8 * rows * LANES),
        name="place",
    )(routes, ranks.reshape(rows, 1), ranks.reshape(1, rows))


def qkv_kernel(ctx_ref, x_ref, extra_ref, w_ref, cos_ref, sin_ref, out_ref, aone_ref, whole_ref):
    half = x_ref.shape[1] // 2

    @pl.when(pl.program_id(0) == 0)
    def _():
        for which in range(3):
            whole_ref[which] = jnp.concatenate([w_ref[which, 0], w_ref[which, 1]], axis=1)

    values = x_ref[...].astype(F32)
    scale = lax.rsqrt(jnp.mean(values * values, axis=-1, keepdims=True) + EPS)
    normed = (values * scale * extra_ref[GAIN_ONE : GAIN_ONE + 1].astype(F32)).astype(BF16)
    aone_ref[...] = normed
    cos, sin = cos_ref[...], sin_ref[...]
    for which in range(3):
        product = dot(normed, whole_ref[which])
        for pair in range(2 * half // LANES):
            chunk = product[:, pair * LANES : (pair + 1) * LANES]
            if which < 2:
                chunk = chunk * cos + swap_halves(chunk) * sin
            if which == 0:
                chunk = chunk * HEAD_DIM ** (-0.5)
            side, place_in = pair // (half // LANES), pair % (half // LANES)
            out_ref[side, which, :, place_in * LANES : (place_in + 1) * LANES] = chunk.astype(BF16)


def project(ctx, x, extra, w_shared, cos, sin):
    rows, width = x.shape
    blocks = rows // TB
    return pl.pallas_call(
        qkv_kernel,
        grid_spec=pltpu.PrefetchScalarGridSpec(
            num_scalar_prefetch=1,
            grid=(blocks,),
            in_specs=[
                pl.BlockSpec((TB, width), lambda i, c: (i, 0)),
                pl.BlockSpec((LANES, width), lambda i, c: (0, 0)),
                pl.BlockSpec((3, 2, width, width // 2), lambda i, c: (0, 0, 0, 0)),
                pl.BlockSpec((TB, LANES), lambda i, c: (c[0] * blocks + i, 0)),
                pl.BlockSpec((TB, LANES), lambda i, c: (c[0] * blocks + i, 0)),
            ],
            out_specs=[
                pl.BlockSpec((2, 3, TB, width // 2), lambda i, c: (0, 0, i, 0)),
                pl.BlockSpec((TB, width), lambda i, c: (i, 0)),
            ],
            scratch_shapes=[pltpu.VMEM((3, width, width), BF16)],
        ),
        out_shape=(
            jax.ShapeDtypeStruct((2, 3, rows, width // 2), BF16),
            jax.ShapeDtypeStruct((rows, width), BF16),
        ),
        compiler_params=params(40),
        cost_estimate=cost(6 * rows * width * width, 6 * width * width + 12 * rows * width),
        name="project",
    )(ctx, x, extra, w_shared, cos, sin)


def head_masks():
    lane = iota((TQ, LANES), 1)
    low = jnp.where(lane < HEAD_DIM, 1.0, 0.0).astype(BF16)
    return low, (1.0 - low.astype(F32)).astype(BF16)


def attend_kernel(first_ref, q_ref, k_ref, v_ref, lo_ref, o_ref, lse_ref, vt_ref):
    per = q_ref.shape[2] // TQ
    count = 2 * per
    masks = head_masks()
    sub = iota((TQ, TQ), 0)
    diagonal = sub <= iota((TQ, TQ), 1)

    def turn(tile, carry):
        vt_ref[tile] = v_ref[tile // per, 0, pl.ds((tile % per) * TQ, TQ), :].T
        return carry

    lax.fori_loop(0, count, turn, 0)

    def q_step(qi, carry):
        rows = pl.ds((qi % per) * TQ, TQ)
        query = q_ref[qi // per, 0, rows, :]
        queries = [query * mask for mask in masks]
        low = lo_ref[qi]
        keys = k_ref[qi // per, 0, rows, :]
        turned = vt_ref[qi]
        ok = diagonal & (sub >= low - qi * TQ)
        state = []
        for head in range(2):
            scores = jnp.where(ok, dot_nt(keys, queries[head]), MASKED)
            peak = jnp.max(scores, axis=0, keepdims=True)
            probs = jnp.exp(scores - peak)
            total = jnp.sum(probs, axis=0, keepdims=True)
            mixed = dot(turned[head * HEAD_DIM : (head + 1) * HEAD_DIM], probs.astype(BF16))
            state += [peak, total, mixed]

        def k_step(ki, state):
            keys = k_ref[ki // per, 0, pl.ds((ki % per) * TQ, TQ), :]
            turned = vt_ref[ki]
            ok = sub >= low - ki * TQ
            new = []
            for head in range(2):
                peak, total, mixed = state[3 * head : 3 * head + 3]
                scores = jnp.where(ok, dot_nt(keys, queries[head]), MASKED)
                top = jnp.maximum(peak, jnp.max(scores, axis=0, keepdims=True))
                shrink = jnp.exp(peak - top)
                probs = jnp.exp(scores - top)
                total = total * shrink + jnp.sum(probs, axis=0, keepdims=True)
                part = dot(turned[head * HEAD_DIM : (head + 1) * HEAD_DIM], probs.astype(BF16))
                new += [top, total, mixed * shrink + part]
            return tuple(new)

        state = lax.fori_loop(first_ref[qi], qi, k_step, tuple(state))
        out = jnp.concatenate([state[2] / state[1], state[5] / state[4]], axis=0)
        o_ref[qi // per, rows, :] = out.T.astype(BF16)
        lse_ref[0, qi, 0:1, :] = state[0] + jnp.log(state[1])
        lse_ref[0, qi, 1:2, :] = state[3] + jnp.log(state[4])
        return carry

    lax.fori_loop(0, count, q_step, 0)


def part_spec(which, rows):
    return pl.BlockSpec((2, 1, rows, LANES), lambda p, first, which=which: (0, which, 0, p))


def attend(first, qkv, low):
    _, _, rows, half = qkv.shape
    pairs = half // LANES
    tiles = 2 * rows // TQ
    return pl.pallas_call(
        attend_kernel,
        grid_spec=pltpu.PrefetchScalarGridSpec(
            num_scalar_prefetch=1,
            grid=(pairs,),
            in_specs=[
                part_spec(0, rows),
                part_spec(1, rows),
                part_spec(2, rows),
                pl.BlockSpec((tiles, 1, TQ), lambda p, first: (0, 0, 0)),
            ],
            out_specs=[
                pl.BlockSpec((2, rows, LANES), lambda p, first: (0, 0, p)),
                pl.BlockSpec((1, tiles, 8, TQ), lambda p, first: (p, 0, 0, 0)),
            ],
            scratch_shapes=[pltpu.VMEM((tiles, LANES, TQ), BF16)],
        ),
        out_shape=(
            jax.ShapeDtypeStruct((2, rows, half), BF16),
            jax.ShapeDtypeStruct((pairs, tiles, 8, TQ), F32),
        ),
        compiler_params=params(40),
        cost_estimate=cost(40e9, 16 * rows * half, 12e6),
        name="attend",
    )(first, qkv, qkv, qkv, low)


def attend_back_kernel(
    first_ref,
    q_ref,
    k_ref,
    v_ref,
    do_ref,
    o_ref,
    lse_ref,
    lo_ref,
    cos_ref,
    sin_ref,
    g_ref,
    kt_ref,
    delta_ref,
    dk_ref,
    dv_ref,
):
    per = q_ref.shape[2] // TQ
    count = 2 * per
    masks = head_masks()
    sub = iota((TQ, TQ), 0)
    diagonal = sub <= iota((TQ, TQ), 1)

    def prepare(tile, carry):
        rows = pl.ds((tile % per) * TQ, TQ)
        kt_ref[tile] = k_ref[tile // per, 0, rows, :].T
        both = o_ref[tile // per, rows, :].astype(F32) * do_ref[tile // per, rows, :].astype(F32)
        both = both.T
        delta_ref[tile, 0:1, :] = jnp.sum(both[:HEAD_DIM], axis=0, keepdims=True)
        delta_ref[tile, 1:2, :] = jnp.sum(both[HEAD_DIM:], axis=0, keepdims=True)
        dk_ref[tile] = jnp.zeros((TQ, LANES), F32)
        dv_ref[tile] = jnp.zeros((TQ, LANES), F32)
        return carry

    lax.fori_loop(0, count, prepare, 0)

    def q_step(qi, carry):
        rows = pl.ds((qi % per) * TQ, TQ)
        query = q_ref[qi // per, 0, rows, :]
        grad = do_ref[qi // per, rows, :]
        queries = [query * mask for mask in masks]
        grads = [grad * mask for mask in masks]
        both_queries = jnp.concatenate(queries, axis=0)
        both_grads = jnp.concatenate(grads, axis=0)
        low = lo_ref[qi]
        lse = [lse_ref[0, qi, h : h + 1, :] for h in range(2)]
        delta = [delta_ref[qi, h : h + 1, :] for h in range(2)]

        def tile(ki, ok, sums):
            at = pl.ds((ki % per) * TQ, TQ)
            keys = k_ref[ki // per, 0, at, :]
            values = v_ref[ki // per, 0, at, :]
            turned = kt_ref[ki]
            all_probs, all_scores, new = [], [], []
            for h in range(2):
                scores = jnp.where(ok, dot_nt(keys, queries[h]), MASKED)
                probs = jnp.exp(scores - lse[h])
                grad_probs = dot_nt(values, grads[h])
                grad_scores = (probs * (grad_probs - delta[h])).astype(BF16)
                new.append(
                    sums[h] + dot(turned[h * HEAD_DIM : (h + 1) * HEAD_DIM], grad_scores)
                )
                all_probs.append(probs.astype(BF16))
                all_scores.append(grad_scores)
            dv_ref[ki] += dot(jnp.concatenate(all_probs, axis=1), both_grads)
            dk_ref[ki] += dot(jnp.concatenate(all_scores, axis=1), both_queries)
            return tuple(new)

        start = jnp.zeros((HEAD_DIM, TQ), F32)
        sums = tile(qi, diagonal & (sub >= low - qi * TQ), (start, start))
        sums = lax.fori_loop(
            first_ref[qi], qi, lambda ki, s: tile(ki, sub >= low - ki * TQ, s), sums
        )
        grad_query = jnp.concatenate(sums, axis=0).T * HEAD_DIM ** (-0.5)
        cos, sin = cos_ref[qi // per, rows, :], sin_ref[qi // per, rows, :]
        g_ref[qi // per, 0, rows, :] = (grad_query * cos - swap_halves(grad_query) * sin).astype(
            BF16
        )
        return carry

    lax.fori_loop(0, count, q_step, 0)

    def finish(tile, carry):
        rows = pl.ds((tile % per) * TQ, TQ)
        cos, sin = cos_ref[tile // per, rows, :], sin_ref[tile // per, rows, :]
        grad_key = dk_ref[tile]
        g_ref[tile // per, 1, rows, :] = (grad_key * cos - swap_halves(grad_key) * sin).astype(BF16)
        g_ref[tile // per, 2, rows, :] = dv_ref[tile].astype(BF16)
        return carry

    lax.fori_loop(0, count, finish, 0)


def attend_back(first, qkv, grad_o, o, lse, low, cos, sin):
    _, _, rows, half = qkv.shape
    pairs = half // LANES
    tiles = 2 * rows // TQ
    side = pl.BlockSpec((2, rows, LANES), lambda p, first: (0, 0, p))
    table = pl.BlockSpec((2, rows, LANES), lambda p, first: (0, 0, 0))
    return pl.pallas_call(
        attend_back_kernel,
        grid_spec=pltpu.PrefetchScalarGridSpec(
            num_scalar_prefetch=1,
            grid=(pairs,),
            in_specs=[
                part_spec(0, rows),
                part_spec(1, rows),
                part_spec(2, rows),
                side,
                side,
                pl.BlockSpec((1, tiles, 8, TQ), lambda p, first: (p, 0, 0, 0)),
                pl.BlockSpec((tiles, 1, TQ), lambda p, first: (0, 0, 0)),
                table,
                table,
            ],
            out_specs=pl.BlockSpec((2, 3, rows, LANES), lambda p, first: (0, 0, 0, p)),
            scratch_shapes=[
                pltpu.VMEM((tiles, LANES, TQ), BF16),
                pltpu.VMEM((tiles, 8, TQ), F32),
                pltpu.VMEM((tiles, TQ, LANES), F32),
                pltpu.VMEM((tiles, TQ, LANES), F32),
            ],
        ),
        out_shape=jax.ShapeDtypeStruct((2, 3, rows, half), BF16),
        compiler_params=params(48),
        cost_estimate=cost(100e9, 32 * rows * half, 12e6),
        name="attend_back",
    )(first, qkv, qkv, qkv, grad_o, o, lse, low, cos, sin)


def middle_kernel(
    total, x_ref, o_ref, w_ref, extra_ref, prev_ref, res_ref, routes_ref, hres_ref, atwo_ref, stat_ref
):
    attended = jnp.concatenate([o_ref[0], o_ref[1]], axis=1)
    hres = x_ref[...].astype(F32) + dot(
        attended, jnp.concatenate([w_ref[0, 0], w_ref[0, 1]], axis=1)
    )
    hres_ref[...] = hres
    scale = lax.rsqrt(jnp.mean(hres * hres, axis=-1, keepdims=True) + EPS)
    extra = extra_ref[...]
    gain = extra[GAIN_TWO : GAIN_TWO + 1].astype(F32)
    atwo = (hres * scale * gain).astype(BF16)
    atwo_ref[...] = atwo
    logits = dot_nt(atwo, extra)
    for j in range(total):
        logits = logits + prev_ref[:, j : j + 1] * res_ref[j : j + 1, :]
    lane = iota(logits.shape, 1)

    def soft(inside):
        peak = jnp.max(jnp.where(inside, logits, -jnp.inf), axis=1, keepdims=True)
        powers = jnp.where(inside, jnp.exp(jnp.where(inside, logits - peak, 0.0)), 0.0)
        return powers / jnp.sum(powers, axis=1, keepdims=True)

    probs = soft(lane < total)
    stat = probs
    for j in range(2):
        start = total + 2 * j
        stat = stat + soft((lane >= start) & (lane < start + 2))
    stat = jnp.where(lane == total + 4, scale, stat)
    for k in range(2):
        gate = jnp.sum(
            jnp.where(lane == routes_ref[:, k : k + 1], probs, 0.0), axis=1, keepdims=True
        )
        stat = jnp.where(lane == total + 5 + k, gate, stat)
    stat_ref[...] = stat


def middle(total, x, o, w_shared, extra, prev, res, routes):
    rows, width = x.shape
    token = lambda i: (i, 0)
    whole = lambda i: (0, 0)
    return pl.pallas_call(
        functools.partial(middle_kernel, total),
        grid=(rows // TB,),
        in_specs=[
            pl.BlockSpec((TB, width), token),
            pl.BlockSpec((2, TB, width // 2), lambda i: (0, i, 0)),
            pl.BlockSpec((1, 2, width, width // 2), lambda i: (3, 0, 0, 0)),
            pl.BlockSpec((LANES, width), whole),
            pl.BlockSpec((TB, total), token),
            pl.BlockSpec((total, LANES), whole),
            pl.BlockSpec((TB, 2), token),
        ],
        out_specs=[
            pl.BlockSpec((TB, width), token),
            pl.BlockSpec((TB, width), token),
            pl.BlockSpec((TB, LANES), token),
        ],
        out_shape=(
            jax.ShapeDtypeStruct((rows, width), F32),
            jax.ShapeDtypeStruct((rows, width), BF16),
            jax.ShapeDtypeStruct((rows, LANES), F32),
        ),
        compiler_params=params(40),
        cost_estimate=cost(2 * rows * width * width, 2 * width * width + 10 * rows * width),
        name="middle",
    )(x, o, w_shared, extra, prev, res, routes)


def expert_kernel(
    total,
    flat_ref,
    atwo_ref,
    dy_ref,
    stat_ref,
    wg_ref,
    wu_ref,
    wd_ref,
    flow_ref,
    drow_ref,
    gg_ref,
    gu_ref,
    gd_ref,
    send_x,
    send_g,
    all_x,
    all_g,
    acc_ref,
    z_ref,
    a_ref,
    b_ref,
    turned_ref,
    wide_buf,
    down_buf,
    wide_given,
    wide_taken,
    down_given,
    down_taken,
    x_sems,
    g_sems,
    flow_sems,
    drow_sems,
    local_sems,
    weight_sems,
    wide_sems,
    down_sems,
):
    experts, cap, width = all_x.shape
    slots = experts * cap
    chunks = z_ref.shape[0]
    per = chunks // 2
    half = width // 2
    tokens = atwo_ref.shape[0]
    me, core = lax.axis_index("expert"), lax.axis_index("context")

    def weights(step):
        chunk, slot = lax.rem(step, chunks), lax.rem(step, 2)
        at = pl.ds(pl.multiple_of(lax.rem(chunk, per) * FC, FC), FC)
        rows = pl.ds(pl.multiple_of(chunk * FC, FC), FC)
        return (
            pltpu.make_async_copy(
                wg_ref.at[chunk // per, :, at], wide_buf.at[slot, 0], weight_sems.at[slot, 0]
            ),
            pltpu.make_async_copy(
                wu_ref.at[chunk // per, :, at], wide_buf.at[slot, 1], weight_sems.at[slot, 1]
            ),
            pltpu.make_async_copy(
                wd_ref.at[0, rows, :], down_buf.at[slot, 0], weight_sems.at[slot, 2]
            ),
            pltpu.make_async_copy(
                wd_ref.at[1, rows, :], down_buf.at[slot, 1], weight_sems.at[slot, 3]
            ),
        )

    def next_weights(step):
        @pl.when(step + 1 < 2 * chunks)
        def _():
            for copy in weights(step + 1):
                copy.start()

        for copy in weights(step):
            copy.wait()

    for copy in weights(0):
        copy.start()
    greet_all(("context", "expert"))

    def hots(target):
        slot = (iota((cap, tokens), 0) + target * cap).astype(F32)
        return flat_ref[0:1, :] == slot, flat_ref[1:2, :] == slot

    order = list(range(1, experts)) + [0]
    x_copies, g_copies = {}, {}
    for j in order:
        target = lax.rem(me + j, experts)
        first, second = hots(target)
        rows = dot(jnp.where(first | second, 1.0, 0.0).astype(BF16), atwo_ref[...]).astype(BF16)
        if j == 0:
            all_x[0] = rows
        else:
            send_x[j - 1] = rows
            x_copies[j] = remote(
                send_x.at[j - 1], all_x.at[j], x_sems, (j - 1,), {"expert": target}
            )
            x_copies[j].start()
    gates = stat_ref[...].T
    for j in order:
        target = lax.rem(me + j, experts)
        first, second = hots(target)
        gate = jnp.sum(
            jnp.where(first, gates[total + 5 : total + 6], 0.0)
            + jnp.where(second, gates[total + 6 : total + 7], 0.0),
            axis=1,
            keepdims=True,
        )
        rows = dot(jnp.where(first | second, 1.0, 0.0).astype(BF16), dy_ref[...])
        rows = (rows * gate).astype(BF16)
        if j == 0:
            all_g[0] = rows
        else:
            send_g[j - 1] = rows
            g_copies[j] = remote(
                send_g.at[j - 1], all_g.at[j], g_sems, (j - 1,), {"expert": target}
            )
            g_copies[j].start()

    def back(buffer, dest, sems, j):
        return remote(
            buffer.at[j - 1],
            dest.at[me],
            sems,
            (j - 1,),
            {"expert": lax.rem(me + experts - j, experts)},
        )

    for j in range(1, experts):
        x_copies[j].wait()
    acc_ref[...] = jnp.zeros_like(acc_ref)

    def up(step, carry):
        next_weights(step)
        slot = lax.rem(step, 2)
        rows = all_x[...].reshape(slots, width)
        gate = dot(rows, wide_buf[slot, 0])
        lift = dot(rows, wide_buf[slot, 1])
        sig = 1.0 / (1.0 + jnp.exp(-gate))
        swish = gate * sig
        hidden = (swish * lift).astype(BF16)
        z_ref[step] = hidden
        a_ref[step] = (lift * sig * (1.0 + gate * (1.0 - sig))).astype(BF16)
        b_ref[step] = swish.astype(BF16)
        acc_ref[...] += dot(hidden, jnp.concatenate([down_buf[slot, 0], down_buf[slot, 1]], axis=1))
        return carry

    lax.fori_loop(0, chunks, up, 0)
    own = [
        pltpu.make_async_copy(all_own, dest.at[me], local_sems.at[i])
        for i, (all_own, dest) in enumerate(
            ((send_x.at[experts - 1], flow_ref), (send_g.at[experts - 1], drow_ref))
        )
    ]
    for j in range(1, experts):
        send_x[j - 1] = acc_ref[j * cap : (j + 1) * cap, :].astype(BF16)
        back(send_x, flow_ref, flow_sems, j).start()
    send_x[experts - 1] = acc_ref[:cap, :].astype(BF16)
    own[0].start()
    turned_ref[...] = all_x[...].reshape(slots, width).T
    acc_ref[...] = jnp.zeros_like(acc_ref)
    for j in range(1, experts):
        g_copies[j].wait()

    def down(step, carry):
        next_weights(step + chunks)
        slot = lax.rem(step, 2)
        whole = jnp.concatenate([down_buf[slot, 0], down_buf[slot, 1]], axis=1)
        dz = dot_nt(all_g[...].reshape(slots, width), whole)
        dg = (dz * a_ref[step].astype(F32)).astype(BF16)
        du = (dz * b_ref[step].astype(F32)).astype(BF16)
        a_ref[step] = dg
        b_ref[step] = du
        acc_ref[...] += dot_nt(dg, wide_buf[slot, 0]) + dot_nt(du, wide_buf[slot, 1])
        return carry

    lax.fori_loop(0, chunks, down, 0)
    for j in range(1, experts):
        send_g[j - 1] = acc_ref[j * cap : (j + 1) * cap, :].astype(BF16)
        back(send_g, drow_ref, drow_sems, j).start()
    send_g[experts - 1] = acc_ref[:cap, :].astype(BF16)
    own[1].start()

    def wide_copy(step):
        return remote(
            wide_given.at[step],
            wide_taken.at[step],
            wide_sems,
            (step,),
            {"context": 1 - core},
        )

    def down_copy(step):
        chunk = lax.rem((1 - core) * per + step, chunks)
        return remote(
            down_given.at[step],
            down_taken.at[chunk],
            down_sems,
            (chunk,),
            {"context": 1 - core},
        )

    def products(step):
        chunk = lax.rem((1 - core) * per + step, chunks)
        gate = dot(turned_ref[...], a_ref[chunk])
        lift = dot(turned_ref[...], b_ref[chunk])
        low = dot(z_ref[chunk].T, all_g[...].reshape(slots, width))
        left, right = low[:, :half], low[:, half:]
        down_given[step] = jnp.where(core == 0, right, left).astype(BF16)
        gd_ref[chunk] = jnp.where(core == 0, left, right).astype(BF16)
        down_copy(step).start()
        return gate, lift

    def give(step, carry):
        gate, lift = products(step)
        wide_given[step, 0] = gate.astype(BF16)
        wide_given[step, 1] = lift.astype(BF16)
        wide_copy(step).start()
        return carry

    lax.fori_loop(0, per, give, 0)

    def keep(step, carry):
        gate, lift = products(step)
        wide_copy(step - per).wait_recv()
        gg_ref[step - per] = (gate + wide_taken[step - per, 0].astype(F32)).astype(BF16)
        gu_ref[step - per] = (lift + wide_taken[step - per, 1].astype(F32)).astype(BF16)
        return carry

    lax.fori_loop(per, chunks, keep, 0)

    def settle(step, carry):
        other = lax.rem(core * per + step, chunks)
        copy = remote(
            down_given.at[step],
            down_taken.at[other],
            down_sems,
            (other,),
            {"context": 1 - core},
        )
        copy.wait_recv()
        gd_ref[other] = (gd_ref[other].astype(F32) + down_taken[other].astype(F32)).astype(BF16)
        return carry

    lax.fori_loop(0, chunks, settle, 0)

    for copy in own:
        copy.wait()
    for j in range(1, experts):
        back(send_x, flow_ref, flow_sems, j).wait()
        back(send_g, drow_ref, drow_sems, j).wait()

    def sent(step, carry):
        down_copy(step).wait_send()
        return carry

    lax.fori_loop(0, chunks, sent, 0)
    lax.fori_loop(0, per, lambda step, carry: (wide_copy(step).wait_send(), carry)[1], 0)


def run_experts(total, experts, cap, flat_t, atwo, dy, stat, wg, wu, wd):
    rows, width = atwo.shape
    hidden = wd.shape[1]
    chunks = hidden // FC
    per = chunks // 2
    half = width // 2
    slots = experts * cap
    vmem = pl.BlockSpec(memory_space=pltpu.VMEM)
    anywhere = pl.BlockSpec(memory_space=pl.ANY)
    dma = pltpu.SemaphoreType.DMA
    return pl.pallas_call(
        functools.partial(expert_kernel, total),
        in_specs=[vmem] * 4 + [anywhere] * 3,
        out_specs=[anywhere] * 2 + [vmem] * 3,
        out_shape=(
            jax.ShapeDtypeStruct((experts, cap, width), BF16),
            jax.ShapeDtypeStruct((experts, cap, width), BF16),
            jax.ShapeDtypeStruct((per, width, FC), BF16),
            jax.ShapeDtypeStruct((per, width, FC), BF16),
            jax.ShapeDtypeStruct((chunks, FC, half), BF16),
        ),
        scratch_shapes=[
            pltpu.VMEM((experts, cap, width), BF16),
            pltpu.VMEM((experts, cap, width), BF16),
            pltpu.VMEM((experts, cap, width), BF16),
            pltpu.VMEM((experts, cap, width), BF16),
            pltpu.VMEM((slots, width), F32),
            pltpu.VMEM((chunks, slots, FC), BF16),
            pltpu.VMEM((chunks, slots, FC), BF16),
            pltpu.VMEM((chunks, slots, FC), BF16),
            pltpu.VMEM((width, slots), BF16),
            pltpu.VMEM((2, 2, width, FC), BF16),
            pltpu.VMEM((2, 2, FC, half), BF16),
            pltpu.VMEM((per, 2, width, FC), BF16),
            pltpu.VMEM((per, 2, width, FC), BF16),
            pltpu.VMEM((chunks, FC, half), BF16),
            pltpu.VMEM((chunks, FC, half), BF16),
            dma((2, experts - 1)),
            dma((2, experts - 1)),
            dma((2, experts - 1)),
            dma((2, experts - 1)),
            dma((2,)),
            dma((2, 4)),
            dma((2, per)),
            dma((2, chunks)),
        ],
        compiler_params=pltpu.CompilerParams(
            collective_id=2, has_side_effects=True, vmem_limit_bytes=62 * MIB
        ),
        cost_estimate=cost(18 * slots * width * hidden, 30 * width * hidden),
        name="experts",
    )(flat_t, atwo, dy, stat, wg, wu, wd)


def combine_kernel(
    experts,
    total,
    flow_ref,
    drow_ref,
    flat_ref,
    stat_ref,
    routes_ref,
    hres_ref,
    atwo_ref,
    dy_ref,
    o_ref,
    extra_ref,
    w_ref,
    prev_ref,
    out_ref,
    dh_ref,
    dolow_ref,
    gw_ref,
    small_ref,
    acc_ref,
):
    step = pl.program_id(0)
    slots = flow_ref.shape[0]
    half = o_ref.shape[2]
    extra = extra_ref[...]
    gain = extra[GAIN_TWO : GAIN_TWO + 1].astype(F32)
    stat = stat_ref[...]
    hres = hres_ref[...]
    dy = dy_ref[...].astype(F32)
    scale = stat[:, total + 4 : total + 5]
    gates = [stat[:, total + 5 + k : total + 6 + k] for k in range(2)]
    ntwo = hres * scale * gain
    spread = iota((TB, slots), 1)
    hots = [flat_ref[:, k : k + 1] == spread for k in range(2)]
    returned = flow_ref[...]
    mixes = [[stat[:, total + 2 * j + i : total + 2 * j + i + 1] for i in range(2)] for j in range(2)]
    vecs = [extra[VECS + j : VECS + j + 1].astype(F32) for j in range(2)]
    moe = jnp.zeros_like(hres)
    lane = iota((TB, LANES), 1)
    dpgate = jnp.zeros((TB, LANES), F32)
    weight = jnp.zeros((TB, 1), F32)
    const_weights = [jnp.zeros((TB, 1), F32)] * 2
    for k in range(2):
        route = routes_ref[:, k : k + 1]
        epair = dot(jnp.where(hots[k], 1.0, 0.0).astype(BF16), returned)
        share = jnp.where(route == experts + 1, 1.0, 0.0)
        weight = weight + share * gates[k]
        for j in range(2):
            chosen = jnp.where(route == experts + 2 + j, 1.0, 0.0)
            share = share + chosen * mixes[j][0]
            epair = epair + (chosen * mixes[j][1]) * vecs[j]
            const_weights[j] = const_weights[j] + chosen * gates[k]
        epair = epair + share * ntwo
        moe = moe + gates[k] * epair
        dgate = jnp.sum(dy * epair, axis=1, keepdims=True)
        dpgate = dpgate + jnp.where(lane == route, dgate, 0.0)
    out_ref[...] = (hres + moe).astype(BF16)

    pgate = jnp.where(lane < total, stat, 0.0)
    dlogit = pgate * (dpgate - jnp.sum(pgate * dpgate, axis=1, keepdims=True))
    dot_normed = jnp.sum(dy * ntwo, axis=1, keepdims=True)
    droute = dlogit
    vec_rows = []
    for j in range(2):
        dot_vec = jnp.sum(dy * vecs[j], axis=1, keepdims=True)
        grads = [const_weights[j] * dot_normed, const_weights[j] * dot_vec]
        inner = mixes[j][0] * grads[0] + mixes[j][1] * grads[1]
        for i in range(2):
            droute = jnp.where(
                lane == total + 2 * j + i, mixes[j][i] * (grads[i] - inner), droute
            )
        weight = weight + const_weights[j] * mixes[j][0]
        vec_rows.append(jnp.sum((const_weights[j] * mixes[j][1]) * dy, axis=0, keepdims=True))
    droute = droute.astype(BF16)
    hot_any = jnp.where(hots[0] | hots[1], 1.0, 0.0).astype(BF16)
    dntwo = weight * dy + dot(droute, extra) + dot(hot_any, drow_ref[...])
    turned = dntwo * gain
    inner = jnp.mean(hres * turned, axis=1, keepdims=True)
    dh = dy + scale * turned - hres * (scale * scale * scale * inner)
    dh_ref[...] = dh
    dhlow = dh.astype(BF16)
    w_out = jnp.concatenate([w_ref[0, 0], w_ref[0, 1]], axis=1)
    dolow = dot_nt(dhlow, w_out).astype(BF16)
    dolow_ref[0] = dolow[:, :half]
    dolow_ref[1] = dolow[:, half:]
    gain_row = jnp.sum(dntwo * hres * scale, axis=0, keepdims=True)
    route_rows = dot(droute.T, atwo_ref[...])
    res_rows = lax.dot_general(
        prev_ref[...],
        dlogit,
        (((0,), (0,)), ((), ())),
        precision=HIGH,
        preferred_element_type=F32,
    )
    width = hres.shape[1]
    res_rows = jnp.concatenate([res_rows, jnp.zeros((total, width - LANES), F32)], axis=1)
    small = jnp.concatenate(
        [route_rows[: total + 4], gain_row, vec_rows[0], vec_rows[1], jnp.zeros((1, width), F32), res_rows],
        axis=0,
    )
    part = dot(jnp.concatenate([o_ref[0], o_ref[1]], axis=1).T, dhlow)

    @pl.when(step == 0)
    def _():
        small_ref[...] = small
        acc_ref[...] = part

    @pl.when(step > 0)
    def _():
        small_ref[...] += small
        acc_ref[...] += part

    @pl.when(step == pl.num_programs(0) - 1)
    def _():
        for side in range(2):
            gw_ref[side] = acc_ref[:, side * half : (side + 1) * half].astype(BF16)


def combine(experts, total, flow, drow, flat, stat, routes, hres, atwo, dy, o, w_shared, extra, prev):
    rows, width = hres.shape
    slots = flow.shape[0]
    half = width // 2
    token = lambda i: (i, 0)
    whole = lambda i: (0, 0)
    side = pl.BlockSpec((2, TB, half), lambda i: (0, i, 0))
    weight = pl.BlockSpec((2, width, half), lambda i: (0, 0, 0))
    small_rows = 2 * total + 8
    return pl.pallas_call(
        functools.partial(combine_kernel, experts, total),
        grid=(rows // TB,),
        in_specs=[
            pl.BlockSpec((slots, width), whole),
            pl.BlockSpec((slots, width), whole),
            pl.BlockSpec((TB, LANES), token),
            pl.BlockSpec((TB, LANES), token),
            pl.BlockSpec((TB, 2), token),
            pl.BlockSpec((TB, width), token),
            pl.BlockSpec((TB, width), token),
            pl.BlockSpec((TB, width), token),
            side,
            pl.BlockSpec((LANES, width), whole),
            pl.BlockSpec((1, 2, width, half), lambda i: (3, 0, 0, 0)),
            pl.BlockSpec((TB, total), token),
        ],
        out_specs=[
            pl.BlockSpec((TB, width), token),
            pl.BlockSpec((TB, width), token),
            side,
            weight,
            pl.BlockSpec((small_rows, width), whole),
        ],
        out_shape=(
            jax.ShapeDtypeStruct((rows, width), BF16),
            jax.ShapeDtypeStruct((rows, width), F32),
            jax.ShapeDtypeStruct((2, rows, half), BF16),
            jax.ShapeDtypeStruct((2, width, half), BF16),
            jax.ShapeDtypeStruct((small_rows, width), F32),
        ),
        scratch_shapes=[pltpu.VMEM((width, width), F32)],
        compiler_params=params(56),
        cost_estimate=cost(
            6 * rows * slots * width + 4 * rows * width * width, 30 * rows * width + 8 * width * width
        ),
        name="combine",
    )(flow, drow, flat, stat, routes, hres, atwo, dy, o, extra, w_shared, prev)


def project_back_kernel(
    g_ref, w_ref, extra_ref, x_ref, aone_ref, dh_ref, gwo_ref, out_ref, gw_ref, gain_out_ref, acc_ref
):
    step = pl.program_id(0)
    half = g_ref.shape[3]
    turned = aone_ref[...].T
    dnone = None
    for which in range(3):
        grad = jnp.concatenate([g_ref[0, which], g_ref[1, which]], axis=1)
        part = dot_nt(grad, jnp.concatenate([w_ref[which, 0], w_ref[which, 1]], axis=1))
        dnone = part if dnone is None else dnone + part
        weight = dot(turned, grad)

        @pl.when(step == 0)
        def _():
            acc_ref[which] = weight

        @pl.when(step > 0)
        def _():
            acc_ref[which] += weight

    values = x_ref[...].astype(F32)
    scale = lax.rsqrt(jnp.mean(values * values, axis=-1, keepdims=True) + EPS)
    scaled = dnone * extra_ref[GAIN_ONE : GAIN_ONE + 1].astype(F32)
    inner = jnp.mean(values * scaled, axis=1, keepdims=True)
    out_ref[...] = dh_ref[...] + scale * scaled - values * (scale * scale * scale * inner)
    row = jnp.sum(dnone * values * scale, axis=0, keepdims=True)

    @pl.when(step == 0)
    def _():
        gain_out_ref[...] = row

    @pl.when(step > 0)
    def _():
        gain_out_ref[...] += row

    @pl.when(step == pl.num_programs(0) - 1)
    def _():
        for side in range(2):
            for which in range(3):
                at = side * half
                gw_ref[side, which] = acc_ref[which, :, at : at + half].astype(BF16)
            gw_ref[side, 3] = gwo_ref[side]


def project_back(grad, w_shared, extra, x, aone, dh, grad_out_w):
    rows, width = x.shape
    half = width // 2
    token = lambda i: (i, 0)
    whole = lambda i: (0, 0)
    return pl.pallas_call(
        project_back_kernel,
        grid=(rows // TB,),
        in_specs=[
            pl.BlockSpec((2, 3, TB, half), lambda i: (0, 0, i, 0)),
            pl.BlockSpec((3, 2, width, half), lambda i: (0, 0, 0, 0)),
            pl.BlockSpec((LANES, width), whole),
            pl.BlockSpec((TB, width), token),
            pl.BlockSpec((TB, width), token),
            pl.BlockSpec((TB, width), token),
            pl.BlockSpec((2, width, half), lambda i: (0, 0, 0)),
        ],
        out_specs=[
            pl.BlockSpec((TB, width), token),
            pl.BlockSpec((2, 4, width, half), lambda i: (0, 0, 0, 0)),
            pl.BlockSpec((1, width), whole),
        ],
        out_shape=(
            jax.ShapeDtypeStruct((rows, width), F32),
            jax.ShapeDtypeStruct((2, 4, width, half), BF16),
            jax.ShapeDtypeStruct((1, width), F32),
        ),
        scratch_shapes=[pltpu.VMEM((3, width, width), F32)],
        compiler_params=params(56),
        cost_estimate=cost(12 * rows * width * width, 18 * width * width + 20 * rows * width),
        name="project_back",
    )(grad, w_shared, extra, x, aone, dh, grad_out_w)


def reduce_kernel(
    gain_at,
    grads_ref,
    small_ref,
    gain_ref,
    out_ref,
    small_out_ref,
    core_in,
    plane_out,
    plane_in,
    slab_out,
    slab_in,
    final,
    own_ref,
    small_own,
    small_core,
    small_plane,
    small_slab,
    core_sems,
    plane_sems,
    slab_sems,
    final_sems,
    pass_sems,
    small_core_sems,
    small_plane_sems,
    small_slab_sems,
):
    experts = lax.axis_size("expert")
    slabs = lax.axis_size("dp")
    me, core, slab = lax.axis_index("expert"), lax.axis_index("context"), lax.axis_index("dp")
    other = 1 - core

    greet_all(("context", "expert", "dp"))
    send = remote

    order = list(range(1, experts)) + [0]
    core_copies = {}
    for j in order:
        core_copies[j] = send(
            grads_ref.at[other, lax.rem(me + j, experts)],
            core_in.at[j],
            core_sems,
            (j,),
            {"context": other},
        )
        core_copies[j].start()
    row = iota(small_ref.shape, 0)
    small_own[...] = small_ref[...] + jnp.where(row == gain_at, gain_ref[...], 0.0)
    small_copy = send(small_own, small_core, small_core_sems, (0,), {"context": other})
    small_copy.start()

    def plane_copy(j, at):
        return send(
            plane_out.at[j - 1, at],
            plane_in.at[j - 1, at],
            plane_sems,
            (j - 1, at),
            {"expert": lax.rem(me + j, experts)},
        )

    for j in range(1, experts):
        core_copies[j].wait_recv()
        which = lax.rem(me + j, experts)

        def pass_on(k, j=j, which=which):
            at = lax.rem(slab + k + 1, slabs)
            plane_out[j - 1, at] = (
                grads_ref[core, which, at].astype(F32) + core_in[j, at].astype(F32)
            ).astype(BF16)
            plane_copy(j, at).start()

        loop(slabs, pass_on)
    core_copies[0].wait_recv()

    small_copy.wait()
    small_plane[me] = small_own[...] + small_core[...]
    small_plane_copies = []
    for j in range(1, experts):
        small_plane_copies.append(
            send(
                small_plane.at[me],
                small_plane.at[me],
                small_plane_sems,
                (j,),
                {"expert": lax.rem(me + j, experts)},
            )
        )
        small_plane_copies[-1].start()

    def gathered(at):
        value = grads_ref[core, me, at].astype(F32) + core_in[0, at].astype(F32)
        for j in range(1, experts):
            plane_copy(j, at).wait_recv()
            value = value + plane_in[j - 1, at].astype(F32)
        return value

    def slab_copy(k):
        return send(
            slab_out.at[k],
            slab_in.at[k],
            slab_sems,
            (k,),
            {"dp": lax.rem(slab + k + 1, slabs)},
        )

    def scatter(k):
        slab_out[k] = gathered(lax.rem(slab + k + 1, slabs)).astype(BF16)
        slab_copy(k).start()

    loop(slabs - 1, scatter)

    for copy in small_plane_copies:
        copy.wait()
    value = small_plane[0]
    for j in range(1, experts):
        value = value + small_plane[j]
    small_slab[slab] = value

    def small_slab_copy(k):
        return send(
            small_slab.at[slab],
            small_slab.at[slab],
            small_slab_sems,
            (k,),
            {"dp": lax.rem(slab + k + 1, slabs)},
        )

    loop(slabs - 1, lambda k: small_slab_copy(k).start())

    own_ref[...] = gathered(slab)

    def collect(k):
        slab_copy(k).wait_recv()
        own_ref[...] += slab_in[k].astype(F32)

    loop(slabs - 1, collect)
    final[core, me] = own_ref[...].astype(BF16)
    final_copies, pass_copies = [], []
    for j in range(1, experts):
        final_copies.append(
            send(
                final.at[core, me],
                final.at[core, me],
                final_sems,
                (j,),
                {"expert": lax.rem(me + j, experts)},
            )
        )
        final_copies[-1].start()
    for j in range(experts):
        source = lax.rem(me + experts - j, experts)
        if j > 0:
            final_copies[j - 1].wait_recv()
        pass_copies.append(
            send(
                final.at[core, source],
                final.at[core, source],
                pass_sems,
                (j,),
                {"context": other},
            )
        )
        pass_copies[-1].start()

    loop(slabs - 1, lambda k: small_slab_copy(k).wait())
    small_out_ref[...] = small_slab[0]

    def add_small(k):
        small_out_ref[...] += small_slab[k + 1]

    loop(slabs - 1, add_small)

    for copy in pass_copies:
        copy.wait_recv()
    half = final.shape[3]
    for which in range(experts):
        for side in range(2):
            out_ref[which, :, side * half : (side + 1) * half] = final[side, which].astype(F32)

    for j in range(experts):
        core_copies[j].wait_send()
    for j in range(1, experts):

        def sent(k, j=j):
            plane_copy(j, k).wait_send()

        loop(slabs, sent)
    loop(slabs - 1, lambda k: slab_copy(k).wait_send())
    for copy in final_copies + pass_copies:
        copy.wait_send()


def reduce_shared(mesh_sizes, grads, small, gain_row, gain_at):
    experts, slabs = mesh_sizes
    _, _, _, rows, half = grads.shape
    small_shape = small.shape
    vmem = pl.BlockSpec(memory_space=pltpu.VMEM)
    dma = pltpu.SemaphoreType.DMA
    return pl.pallas_call(
        functools.partial(reduce_kernel, gain_at),
        in_specs=[vmem] * 3,
        out_specs=[vmem] * 2,
        out_shape=(
            jax.ShapeDtypeStruct((experts, rows, 2 * half), F32),
            jax.ShapeDtypeStruct(small_shape, F32),
        ),
        scratch_shapes=[
            pltpu.VMEM((experts, slabs, rows, half), BF16),
            pltpu.VMEM((experts - 1, slabs, rows, half), BF16),
            pltpu.VMEM((experts - 1, slabs, rows, half), BF16),
            pltpu.VMEM((slabs - 1, rows, half), BF16),
            pltpu.VMEM((slabs - 1, rows, half), BF16),
            pltpu.VMEM((2, experts, rows, half), BF16),
            pltpu.VMEM((rows, half), F32),
            pltpu.VMEM(small_shape, F32),
            pltpu.VMEM(small_shape, F32),
            pltpu.VMEM((experts,) + small_shape, F32),
            pltpu.VMEM((slabs,) + small_shape, F32),
            dma((2, experts)),
            dma((2, experts - 1, slabs)),
            dma((2, slabs - 1)),
            dma((2, experts)),
            dma((2, experts)),
            dma((2, 1)),
            dma((2, experts)),
            dma((2, slabs - 1)),
        ],
        compiler_params=pltpu.CompilerParams(
            collective_id=0, has_side_effects=True, vmem_limit_bytes=56 * MIB
        ),
        cost_estimate=cost(1e6, 2 * grads.size),
        name="reduce_shared",
    )(grads, small, gain_row)


def swap_cores(value):
    return lax.all_to_all(value, "context", split_axis=0, concat_axis=0, tiled=True)


def on_device(
    tokens,
    segments,
    routes,
    prev_logits,
    ranks,
    cotangent,
    norm_one,
    w_query,
    w_key,
    w_value,
    w_out,
    norm_two,
    router,
    w_res,
    const_mix,
    const_vec,
    w_gate,
    w_up,
    w_down,
):
    experts = lax.axis_size("expert")
    dp = lax.axis_size("dp")
    total = experts + NZ
    _, rows, width = tokens.shape
    hidden = w_gate.shape[2]
    cap = (18 * rows + 8 * total - 1) // (8 * total)
    seq = 2 * rows
    tiles = seq // TQ
    core = lax.axis_index("context")
    half = width // 2

    def mine(shard, size):
        return lax.dynamic_slice_in_dim(shard, core * size, size, 1)

    def gather(shard):
        return lax.all_gather(shard, ("context", "dp"), axis=0).reshape(
            2, dp * shard.shape[0], shard.shape[1]
        )

    extra = jnp.concatenate(
        [router, const_mix, norm_one[:, None], norm_two[:, None], const_vec], axis=1
    )
    w_shared, extra = spread(experts, dp, w_query, w_key, w_value, w_out, extra.astype(F32).T)
    w_shared = w_shared.reshape(4, 2, width, half)
    extra = extra.transpose(1, 0, 2).reshape(total + 8, width).astype(BF16)
    extra = jnp.concatenate(
        [
            extra[: total + 4],
            jnp.zeros((GAIN_ONE - total - 4, width), BF16),
            extra[total + 4 :],
            jnp.zeros((LANES - GAIN_ONE - 4, width), BF16),
        ],
        axis=0,
    )
    gate_w = gather(mine(w_gate[0], hidden // 2))
    up_w = gather(mine(w_up[0], hidden // 2))
    down_w = gather(mine(w_down[0], half))

    flat, flat_t = place(routes[0], ranks[0, 0], experts, cap)
    segs = lax.all_gather(segments[0], "context", axis=0, tiled=True)
    places = jnp.arange(seq, dtype=jnp.int32)
    starts = jnp.sum((segs[None, :] < segs[:, None]).astype(jnp.int32), axis=1)
    low = jnp.maximum(starts, places - (WIN - 1)).reshape(tiles, 1, TQ)
    first = low[:, 0, 0] // TQ
    cos, sin = rope_tables(seq)
    cos, sin = jnp.asarray(cos), jnp.asarray(sin)
    res = jnp.pad(w_res.astype(F32), ((0, 0), (0, LANES - total)))

    x = tokens[0]
    dy = cotangent[0]
    sent, aone = project(core.reshape(1), x, extra, w_shared, cos, sin)
    qkv = swap_cores(sent)
    o_heads, lse = attend(first, qkv, low)
    o = swap_cores(o_heads)
    hres, atwo, stat = middle(total, x, o, w_shared, extra, prev_logits[0], res, routes[0])
    flow_back, drow_back, grad_gate, grad_up, grad_down = run_experts(
        total, experts, cap, flat_t, atwo, dy, stat, gate_w, up_w, down_w
    )
    flow_back = flow_back.reshape(experts * cap, width)
    drow_back = drow_back.reshape(experts * cap, width)

    def scatter_half(chip):
        share = lax.psum_scatter(chip, "dp", scatter_dimension=0, tiled=True)
        both = lax.all_gather(share, "context", axis=1, tiled=True)
        return both.astype(F32)[None]

    def columns(grad):
        return grad.transpose(1, 0, 2).reshape(width, hidden // 2)

    total_gate, total_up, total_down = (
        scatter_half(columns(grad_gate)),
        scatter_half(columns(grad_up)),
        scatter_half(grad_down.reshape(hidden, half)),
    )

    output, dh, dolow, grad_out_w, small = combine(
        experts,
        total,
        flow_back,
        drow_back,
        flat,
        stat,
        routes[0],
        hres,
        atwo,
        dy,
        o,
        w_shared,
        extra,
        prev_logits[0],
    )
    grad_o = swap_cores(dolow)
    grads_sent = attend_back(
        first,
        qkv,
        grad_o,
        o_heads,
        lse,
        low,
        cos.reshape(2, rows, LANES),
        sin.reshape(2, rows, LANES),
    )
    grads = swap_cores(grads_sent)
    grad_tokens, grad_shared, gain_row = project_back(grads, w_shared, extra, x, aone, dh, grad_out_w)
    shared, small = reduce_shared(
        (experts, dp),
        grad_shared.reshape(2, 4, dp, width // dp, half),
        small,
        gain_row,
        total + 7,
    )
    part = width // dp
    owned = lax.dynamic_slice_in_dim(small, lax.axis_index("dp") * part, part, 1)
    grad_res_total = small[total + 8 :, :total]
    return (
        output[None],
        grad_tokens[None],
        owned[total + 7],
        shared[0],
        shared[1],
        shared[2],
        shared[3],
        owned[total + 4],
        owned[:total].T,
        grad_res_total,
        owned[total : total + 4].T,
        owned[total + 5 : total + 7].T,
        total_gate,
        total_up,
        total_down,
    )


def solution(mesh):
    token = P(("expert", "dp"), "context", None)
    rows = P("dp", None)
    expert = P("expert", "dp", None)
    in_specs = (
        token,
        P(("expert", "dp"), "context"),
        token,
        token,
        token,
        token,
        P("dp"),
        rows,
        rows,
        rows,
        rows,
        P("dp"),
        rows,
        P(),
        rows,
        rows,
        expert,
        expert,
        expert,
    )
    out_specs = (
        token,
        token,
        P("dp"),
        rows,
        rows,
        rows,
        rows,
        P("dp"),
        rows,
        P(),
        rows,
        rows,
        expert,
        expert,
        expert,
    )
    return jax.shard_map(
        on_device, mesh=mesh, in_specs=in_specs, out_specs=out_specs, check_vma=False
    )
```

```python
import functools

import jax
import jax.numpy as jnp
import numpy as np
from jax import lax
from jax.experimental import pallas as pl
from jax.experimental.pallas import tpu as pltpu
from jax.sharding import PartitionSpec as P

HEADS = 12
HEAD_DIM = 64
WIN = 1024
NZ = 4
SEGMENTS = 5
GAIN_ONE, GAIN_TWO, VECS = 112, 113, 114
TQ = 256
TB = 256
FC = 256
LANES = 128
EPS = 1e-05
MASKED = -1000000000.0
HIGH = lax.Precision.HIGHEST
F32 = jnp.float32
BF16 = jnp.bfloat16
MIB = 1024 * 1024


def params(mib):
    return pltpu.CompilerParams(vmem_limit_bytes=mib * MIB)


def cost(flops, nbytes, trans=0):
    return pl.CostEstimate(flops=int(flops), bytes_accessed=int(nbytes), transcendentals=int(trans))


def dot(left, right):
    return jnp.dot(left, right, preferred_element_type=F32)


def dot_nt(left, right):
    return lax.dot_general(left, right, (((1,), (1,)), ((), ())), preferred_element_type=F32)


def dot_tn(left, right):
    return lax.dot_general(left, right, (((0,), (0,)), ((), ())), preferred_element_type=F32)


def iota(shape, axis):
    return lax.broadcasted_iota(jnp.int32, shape, axis)


def rope_tables(seq):
    half = HEAD_DIM // 2
    frequency = np.float32(10000.0) ** (
        -np.arange(half, dtype=np.float32) * np.float32(2.0) / np.float32(HEAD_DIM)
    )
    angles = np.arange(seq, dtype=np.float32)[:, None] * frequency.astype(np.float32)[None, :]
    cos = np.cos(angles.astype(np.float64)).astype(np.float32)
    sin = np.sin(angles.astype(np.float64)).astype(np.float32)
    return np.concatenate([cos] * 4, axis=1), np.concatenate([-sin, sin, -sin, sin], axis=1)


def swap_halves(chunk):
    lane = iota(chunk.shape, 1)
    return jnp.where(
        lane % HEAD_DIM < HEAD_DIM // 2, pltpu.roll(chunk, 96, 1), pltpu.roll(chunk, 32, 1)
    )


def loop(count, body):
    if count <= 4:
        for step in range(count):
            body(step)
    else:
        lax.fori_loop(0, count, lambda step, carry: (body(step), carry)[1], 0)


def remote(src, dst, sems, index, where):
    return pltpu.make_async_remote_copy(
        src_ref=src,
        dst_ref=dst,
        send_sem=sems.at[(0,) + index],
        recv_sem=sems.at[(1,) + index],
        device_id=where,
        device_id_type=pl.DeviceIdType.MESH,
    )


def greet_all(axes):
    barrier = pltpu.get_barrier_semaphore()
    total = 0
    for axis in axes:
        size = lax.axis_size(axis)
        me = lax.axis_index(axis)
        total += size - 1

        def greet(k, axis=axis, size=size, me=me):
            pl.semaphore_signal(
                barrier,
                inc=1,
                device_id={axis: lax.rem(me + k + 1, size)},
                device_id_type=pl.DeviceIdType.MESH,
            )

        loop(size - 1, greet)
    pl.semaphore_wait(barrier, total)


def place_pairs(experts, cap, routes_ref, ranks_ref, flat_ref, flat_t_ref):
    rows = routes_ref.shape[0]
    lane = iota((rows, LANES), 1)
    first, second = routes_ref[:, 0:1], routes_ref[:, 1:2]
    hot_first, hot_second = first == lane, second == lane
    hot = (hot_first.astype(F32) + hot_second.astype(F32)).astype(BF16)
    ranks = ranks_ref[...].astype(F32)
    ranks_col = jnp.broadcast_to(ranks, (LANES, rows)).T[:, 0:1]
    earlier = jnp.where(ranks < ranks_col, 1.0, 0.0).astype(BF16)
    counts = dot(earlier, hot)

    def flat(hit, route):
        slot = jnp.sum(jnp.where(hit, counts, 0.0), axis=1, keepdims=True).astype(jnp.int32)
        return jnp.where((route < experts) & (slot < cap), route * cap + slot, experts * cap)

    out = jnp.where(
        lane == 0, flat(hot_first, first), jnp.where(lane == 1, flat(hot_second, second), 0)
    )
    flat_ref[...] = out
    flat_t_ref[...] = out.astype(F32).T[:8]


def find_starts(segs_ref, low_ref, first_ref):
    rows = segs_ref.shape[2]
    per = rows // TQ
    segs = [segs_ref[side].astype(F32) for side in range(2)]
    starts = [jnp.zeros((1, rows), F32) for side in range(2)]
    for number in range(1, SEGMENTS):
        before = sum(
            jnp.sum(jnp.where(part < number, 1.0, 0.0), axis=1, keepdims=True) for part in segs
        )
        starts = [
            jnp.where(part == number, before, start) for part, start in zip(segs, starts)
        ]
    for side in range(2):
        place = (iota((1, rows), 1) + (side * rows - WIN + 1)).astype(F32)
        low = jnp.maximum(starts[side], place)
        for tile in range(per):
            part = low[:, tile * TQ : (tile + 1) * TQ]
            low_ref[side * per + tile] = part.astype(jnp.int32)
            first_ref[side * per + tile] = jnp.min(part).astype(jnp.int32) // TQ


def spread_kernel(
    cap,
    w_query_ref,
    w_key_ref,
    w_value_ref,
    w_out_ref,
    extra_ref,
    routes_ref,
    ranks_ref,
    segs_ref,
    out_ref,
    extra_out_ref,
    flat_ref,
    flat_t_ref,
    low_ref,
    first_ref,
    segs_all,
    slab_sems,
    plane_sems,
    core_sems,
    extra_sems,
    segs_sems,
):
    experts = lax.axis_size("expert")
    slabs = lax.axis_size("dp")
    me, core, slab = lax.axis_index("expert"), lax.axis_index("context"), lax.axis_index("dp")
    half = out_ref.shape[4]
    for which, ref in enumerate((w_query_ref, w_key_ref, w_value_ref, w_out_ref)):
        for side in range(2):

            @pl.when((me == which) & (core == side))
            def _():
                out_ref[which, side, slab] = ref[:, side * half : (side + 1) * half]

    extra_out_ref[slab] = extra_ref[...]
    segs_all[core] = segs_ref[...]
    greet_all(("context", "expert", "dp"))

    def slab_copy(k):
        piece = out_ref.at[me, core, slab]
        return remote(piece, piece, slab_sems, (k,), {"dp": lax.rem(slab + k + 1, slabs)})

    def extra_copy(k):
        piece = extra_out_ref.at[slab]
        return remote(piece, piece, extra_sems, (k,), {"dp": lax.rem(slab + k + 1, slabs)})

    def plane_copy(j, at):
        piece = out_ref.at[me, core, at]
        return remote(
            piece, piece, plane_sems, (j - 1, at), {"expert": lax.rem(me + j, experts)}
        )

    def core_copy(j, at):
        piece = out_ref.at[lax.rem(me + experts - j, experts), core, at]
        return remote(piece, piece, core_sems, (j, at), {"context": 1 - core})

    def share(at):
        for j in range(1, experts):
            plane_copy(j, at).start()
        core_copy(0, at).start()

    loop(slabs - 1, lambda k: extra_copy(k).start())
    loop(slabs - 1, lambda k: slab_copy(k).start())
    share(slab)
    segs_copy = remote(
        segs_all.at[core], segs_all.at[core], segs_sems, (0,), {"context": 1 - core}
    )
    segs_copy.start()
    place_pairs(experts, cap, routes_ref, ranks_ref, flat_ref, flat_t_ref)
    segs_copy.wait()
    find_starts(segs_all, low_ref, first_ref)

    def forward(k):
        slab_copy(k).wait_recv()
        share(lax.rem(slab + slabs - k - 1, slabs))

    loop(slabs - 1, forward)

    def relay(k):
        at = lax.rem(slab + slabs - k, slabs)
        for j in range(1, experts):
            plane_copy(j, at).wait_recv()
            core_copy(j, at).start()

    loop(slabs, relay)
    loop(slabs - 1, lambda k: extra_copy(k).wait())
    loop(slabs - 1, lambda k: slab_copy(k).wait_send())

    def finish(at):
        for j in range(experts):
            core_copy(j, at).wait()
        for j in range(1, experts):
            plane_copy(j, at).wait_send()

    loop(slabs, finish)


def spread(experts, slabs, cap, w_query, w_key, w_value, w_out, extra, routes, ranks, segs):
    tokens = routes.shape[0]
    tiles = 2 * tokens // TQ
    rows, width = w_query.shape
    half = width // 2
    vmem = pl.BlockSpec(memory_space=pltpu.VMEM)
    dma = pltpu.SemaphoreType.DMA
    return pl.pallas_call(
        functools.partial(spread_kernel, cap),
        in_specs=[vmem] * 8,
        out_specs=[vmem] * 5 + [pl.BlockSpec(memory_space=pltpu.SMEM)],
        out_shape=(
            jax.ShapeDtypeStruct((4, 2, slabs, rows, half), BF16),
            jax.ShapeDtypeStruct((slabs,) + extra.shape, F32),
            jax.ShapeDtypeStruct((tokens, LANES), jnp.int32),
            jax.ShapeDtypeStruct((8, tokens), F32),
            jax.ShapeDtypeStruct((tiles, 1, TQ), jnp.int32),
            jax.ShapeDtypeStruct((tiles,), jnp.int32),
        ),
        scratch_shapes=[
            pltpu.VMEM((2, 1, tokens), jnp.int32),
            dma((2, slabs - 1)),
            dma((2, experts - 1, slabs)),
            dma((2, experts, slabs)),
            dma((2, slabs - 1)),
            dma((2, 1)),
        ],
        compiler_params=pltpu.CompilerParams(
            collective_id=1, has_side_effects=True, vmem_limit_bytes=32 * MIB
        ),
        cost_estimate=cost(1e6, 16 * width * width),
        name="spread",
    )(w_query, w_key, w_value, w_out, extra, routes, ranks, segs)


def qkv_kernel(ctx_ref, x_ref, extra_ref, w_ref, cos_ref, sin_ref, out_ref, aone_ref, whole_ref):
    half = x_ref.shape[1] // 2

    @pl.when(pl.program_id(0) == 0)
    def _():
        for which in range(3):
            whole_ref[which] = jnp.concatenate([w_ref[which, 0], w_ref[which, 1]], axis=1)

    values = x_ref[...].astype(F32)
    scale = lax.rsqrt(jnp.mean(values * values, axis=-1, keepdims=True) + EPS)
    normed = (values * scale * extra_ref[GAIN_ONE : GAIN_ONE + 1].astype(F32)).astype(BF16)
    aone_ref[...] = normed
    cos, sin = cos_ref[...], sin_ref[...]
    for which in range(3):
        product = dot(normed, whole_ref[which])
        for pair in range(2 * half // LANES):
            chunk = product[:, pair * LANES : (pair + 1) * LANES]
            if which < 2:
                chunk = chunk * cos + swap_halves(chunk) * sin
            if which == 0:
                chunk = chunk * HEAD_DIM ** (-0.5)
            side, place_in = pair // (half // LANES), pair % (half // LANES)
            out_ref[side, which, :, place_in * LANES : (place_in + 1) * LANES] = chunk.astype(BF16)


def project(ctx, x, extra, w_shared, cos, sin):
    rows, width = x.shape
    blocks = rows // TB
    return pl.pallas_call(
        qkv_kernel,
        grid_spec=pltpu.PrefetchScalarGridSpec(
            num_scalar_prefetch=1,
            grid=(blocks,),
            in_specs=[
                pl.BlockSpec((TB, width), lambda i, c: (i, 0)),
                pl.BlockSpec((LANES, width), lambda i, c: (0, 0)),
                pl.BlockSpec((3, 2, width, width // 2), lambda i, c: (0, 0, 0, 0)),
                pl.BlockSpec((TB, LANES), lambda i, c: (c[0] * blocks + i, 0)),
                pl.BlockSpec((TB, LANES), lambda i, c: (c[0] * blocks + i, 0)),
            ],
            out_specs=[
                pl.BlockSpec((2, 3, TB, width // 2), lambda i, c: (0, 0, i, 0)),
                pl.BlockSpec((TB, width), lambda i, c: (i, 0)),
            ],
            scratch_shapes=[pltpu.VMEM((3, width, width), BF16)],
        ),
        out_shape=(
            jax.ShapeDtypeStruct((2, 3, rows, width // 2), BF16),
            jax.ShapeDtypeStruct((rows, width), BF16),
        ),
        compiler_params=params(40),
        cost_estimate=cost(6 * rows * width * width, 6 * width * width + 12 * rows * width),
        name="project",
    )(ctx, x, extra, w_shared, cos, sin)


def head_masks():
    lane = iota((TQ, LANES), 1)
    low = jnp.where(lane < HEAD_DIM, 1.0, 0.0).astype(BF16)
    return low, (1.0 - low.astype(F32)).astype(BF16)


def spans(tile, first, body):
    for count in range(1, WIN // TQ + 2):

        @pl.when(tile - first + 1 == count)
        def _():
            body(count)


def allowed(low, start, count):
    sub = iota((TQ, TQ), 0)
    marks = [sub >= low - (start + t * TQ) for t in range(count)]
    marks[-1] = marks[-1] & (sub <= iota((TQ, TQ), 1))
    return marks


def masked(scores, marks):
    return [
        jnp.where(mark, scores[t * TQ : (t + 1) * TQ], MASKED) for t, mark in enumerate(marks)
    ]


def attend_kernel(first_ref, q_ref, k_ref, v_ref, lo_ref, o_ref, lse_ref, keys_ref, vt_ref):
    rows = q_ref.shape[2]
    per = rows // TQ
    masks = head_masks()
    for side in range(2):
        at = slice(side * rows, (side + 1) * rows)
        keys_ref[at, :] = k_ref[side, 0]
        turned = v_ref[side, 0].T
        for head in range(2):
            vt_ref[head, :HEAD_DIM, at] = turned[head * HEAD_DIM : (head + 1) * HEAD_DIM]
            vt_ref[head, HEAD_DIM:, at] = jnp.ones((16, rows), BF16)

    def q_step(qi, carry):
        at = pl.ds(pl.multiple_of(lax.rem(qi, per) * TQ, TQ), TQ)
        query = q_ref[qi // per, 0, at, :]
        low = lo_ref[qi]

        def run(count):
            start = pl.multiple_of((qi - count + 1) * TQ, TQ)
            span = pl.ds(start, count * TQ)
            keys = keys_ref[span, :]
            marks = allowed(low, start, count)
            outs = []
            for head in range(2):
                scores = masked(dot_nt(keys, query * masks[head]), marks)
                peak = functools.reduce(
                    jnp.maximum, [jnp.max(part, axis=0, keepdims=True) for part in scores]
                )
                probs = jnp.concatenate(
                    [jnp.exp(part - peak).astype(BF16) for part in scores], axis=0
                )
                mixed = dot(vt_ref[head, :, span], probs)
                total = mixed[HEAD_DIM : HEAD_DIM + 1]
                outs.append(mixed[:HEAD_DIM] / total)
                lse_ref[0, qi, head : head + 1, :] = peak + jnp.log(total)
            o_ref[qi // per, at, :] = jnp.concatenate(outs, axis=0).T.astype(BF16)

        spans(qi, first_ref[qi], run)
        return carry

    lax.fori_loop(0, 2 * per, q_step, 0)


def part_spec(which, rows):
    return pl.BlockSpec((2, 1, rows, LANES), lambda p, first, which=which: (0, which, 0, p))


def attend(first, qkv, low):
    _, _, rows, half = qkv.shape
    pairs = half // LANES
    tiles = 2 * rows // TQ
    return pl.pallas_call(
        attend_kernel,
        grid_spec=pltpu.PrefetchScalarGridSpec(
            num_scalar_prefetch=1,
            grid=(pairs,),
            in_specs=[
                part_spec(0, rows),
                part_spec(1, rows),
                part_spec(2, rows),
                pl.BlockSpec((tiles, 1, TQ), lambda p, first: (0, 0, 0)),
            ],
            out_specs=[
                pl.BlockSpec((2, rows, LANES), lambda p, first: (0, 0, p)),
                pl.BlockSpec((1, tiles, 8, TQ), lambda p, first: (p, 0, 0, 0)),
            ],
            scratch_shapes=[
                pltpu.VMEM((2 * rows, LANES), BF16),
                pltpu.VMEM((2, HEAD_DIM + 16, 2 * rows), BF16),
            ],
        ),
        out_shape=(
            jax.ShapeDtypeStruct((2, rows, half), BF16),
            jax.ShapeDtypeStruct((pairs, tiles, 8, TQ), F32),
        ),
        compiler_params=params(40),
        cost_estimate=cost(40e9, 16 * rows * half, 12e6),
        name="attend",
    )(first, qkv, qkv, qkv, low)


def attend_back_kernel(
    first_ref,
    q_ref,
    k_ref,
    v_ref,
    do_ref,
    o_ref,
    lse_ref,
    lo_ref,
    cos_ref,
    sin_ref,
    g_ref,
    keys_ref,
    values_ref,
    kt_ref,
    delta_ref,
    dk_ref,
    dv_ref,
):
    rows = q_ref.shape[2]
    per = rows // TQ
    masks = head_masks()
    for side in range(2):
        at = slice(side * rows, (side + 1) * rows)
        keys_ref[at, :] = k_ref[side, 0]
        values_ref[at, :] = v_ref[side, 0]
        kt_ref[:, at] = k_ref[side, 0].T
    dk_ref[...] = jnp.zeros_like(dk_ref)
    dv_ref[...] = jnp.zeros_like(dv_ref)

    def prepare(tile, carry):
        at = pl.ds(pl.multiple_of(lax.rem(tile, per) * TQ, TQ), TQ)
        both = o_ref[tile // per, at, :].astype(F32) * do_ref[tile // per, at, :].astype(F32)
        both = both.T
        delta_ref[tile, 0:1, :] = jnp.sum(both[:HEAD_DIM], axis=0, keepdims=True)
        delta_ref[tile, 1:2, :] = jnp.sum(both[HEAD_DIM:], axis=0, keepdims=True)
        return carry

    lax.fori_loop(0, 2 * per, prepare, 0)

    def q_step(qi, carry):
        at = pl.ds(pl.multiple_of(lax.rem(qi, per) * TQ, TQ), TQ)
        query = q_ref[qi // per, 0, at, :]
        grad = do_ref[qi // per, at, :]
        low = lo_ref[qi]

        def run(count):
            start = pl.multiple_of((qi - count + 1) * TQ, TQ)
            span = pl.ds(start, count * TQ)
            keys, values = keys_ref[span, :], values_ref[span, :]
            marks = allowed(low, start, count)
            queries = [query * mask for mask in masks]
            grads = [grad * mask for mask in masks]
            all_probs, all_scores, sums = [], [], []
            for h in range(2):
                lse = lse_ref[0, qi, h : h + 1, :]
                delta = delta_ref[qi, h : h + 1, :]
                scores = masked(dot_nt(keys, queries[h]), marks)
                grad_probs = dot_nt(values, grads[h])
                probs = [jnp.exp(part - lse) for part in scores]
                grad_scores = [
                    (part * (grad_probs[t * TQ : (t + 1) * TQ] - delta)).astype(BF16)
                    for t, part in enumerate(probs)
                ]
                all_probs.append(jnp.concatenate([part.astype(BF16) for part in probs], axis=0))
                all_scores.append(jnp.concatenate(grad_scores, axis=0))
                sums.append(dot(kt_ref[h * HEAD_DIM : (h + 1) * HEAD_DIM, span], all_scores[h]))
            dv_ref[span, :] += dot(
                jnp.concatenate(all_probs, axis=1), jnp.concatenate(grads, axis=0)
            )
            dk_ref[span, :] += dot(
                jnp.concatenate(all_scores, axis=1), jnp.concatenate(queries, axis=0)
            )
            grad_query = jnp.concatenate(sums, axis=0).T * HEAD_DIM ** (-0.5)
            cos, sin = cos_ref[qi // per, at, :], sin_ref[qi // per, at, :]
            g_ref[qi // per, 0, at, :] = (
                grad_query * cos - swap_halves(grad_query) * sin
            ).astype(BF16)

        spans(qi, first_ref[qi], run)
        return carry

    lax.fori_loop(0, 2 * per, q_step, 0)

    def finish(tile, carry):
        at = pl.ds(pl.multiple_of(lax.rem(tile, per) * TQ, TQ), TQ)
        span = pl.ds(pl.multiple_of(tile * TQ, TQ), TQ)
        cos, sin = cos_ref[tile // per, at, :], sin_ref[tile // per, at, :]
        grad_key = dk_ref[span, :]
        g_ref[tile // per, 1, at, :] = (grad_key * cos - swap_halves(grad_key) * sin).astype(BF16)
        g_ref[tile // per, 2, at, :] = dv_ref[span, :].astype(BF16)
        return carry

    lax.fori_loop(0, 2 * per, finish, 0)


def attend_back(first, qkv, grad_o, o, lse, low, cos, sin):
    _, _, rows, half = qkv.shape
    pairs = half // LANES
    tiles = 2 * rows // TQ
    side = pl.BlockSpec((2, rows, LANES), lambda p, first: (0, 0, p))
    table = pl.BlockSpec((2, rows, LANES), lambda p, first: (0, 0, 0))
    return pl.pallas_call(
        attend_back_kernel,
        grid_spec=pltpu.PrefetchScalarGridSpec(
            num_scalar_prefetch=1,
            grid=(pairs,),
            in_specs=[
                part_spec(0, rows),
                part_spec(1, rows),
                part_spec(2, rows),
                side,
                side,
                pl.BlockSpec((1, tiles, 8, TQ), lambda p, first: (p, 0, 0, 0)),
                pl.BlockSpec((tiles, 1, TQ), lambda p, first: (0, 0, 0)),
                table,
                table,
            ],
            out_specs=pl.BlockSpec((2, 3, rows, LANES), lambda p, first: (0, 0, 0, p)),
            scratch_shapes=[
                pltpu.VMEM((2 * rows, LANES), BF16),
                pltpu.VMEM((2 * rows, LANES), BF16),
                pltpu.VMEM((LANES, 2 * rows), BF16),
                pltpu.VMEM((tiles, 8, TQ), F32),
                pltpu.VMEM((2 * rows, LANES), F32),
                pltpu.VMEM((2 * rows, LANES), F32),
            ],
        ),
        out_shape=jax.ShapeDtypeStruct((2, 3, rows, half), BF16),
        compiler_params=params(48),
        cost_estimate=cost(100e9, 32 * rows * half, 12e6),
        name="attend_back",
    )(first, qkv, qkv, qkv, grad_o, o, lse, low, cos, sin)


def middle_kernel(
    total, x_ref, o_ref, w_ref, extra_ref, prev_ref, res_ref, routes_ref, hres_ref, atwo_ref, stat_ref
):
    attended = jnp.concatenate([o_ref[0], o_ref[1]], axis=1)
    hres = x_ref[...].astype(F32) + dot(
        attended, jnp.concatenate([w_ref[0, 0], w_ref[0, 1]], axis=1)
    )
    hres_ref[...] = hres
    scale = lax.rsqrt(jnp.mean(hres * hres, axis=-1, keepdims=True) + EPS)
    extra = extra_ref[...]
    gain = extra[GAIN_TWO : GAIN_TWO + 1].astype(F32)
    atwo = (hres * scale * gain).astype(BF16)
    atwo_ref[...] = atwo
    logits = dot_nt(atwo, extra)
    for j in range(total):
        logits = logits + prev_ref[:, j : j + 1] * res_ref[j : j + 1, :]
    lane = iota(logits.shape, 1)

    def soft(inside):
        peak = jnp.max(jnp.where(inside, logits, -jnp.inf), axis=1, keepdims=True)
        powers = jnp.where(inside, jnp.exp(jnp.where(inside, logits - peak, 0.0)), 0.0)
        return powers / jnp.sum(powers, axis=1, keepdims=True)

    probs = soft(lane < total)
    stat = probs
    for j in range(2):
        start = total + 2 * j
        stat = stat + soft((lane >= start) & (lane < start + 2))
    stat = jnp.where(lane == total + 4, scale, stat)
    for k in range(2):
        gate = jnp.sum(
            jnp.where(lane == routes_ref[:, k : k + 1], probs, 0.0), axis=1, keepdims=True
        )
        stat = jnp.where(lane == total + 5 + k, gate, stat)
    stat_ref[...] = stat


def middle(total, x, o, w_shared, extra, prev, res, routes):
    rows, width = x.shape
    token = lambda i: (i, 0)
    whole = lambda i: (0, 0)
    return pl.pallas_call(
        functools.partial(middle_kernel, total),
        grid=(rows // TB,),
        in_specs=[
            pl.BlockSpec((TB, width), token),
            pl.BlockSpec((2, TB, width // 2), lambda i: (0, i, 0)),
            pl.BlockSpec((1, 2, width, width // 2), lambda i: (3, 0, 0, 0)),
            pl.BlockSpec((LANES, width), whole),
            pl.BlockSpec((TB, total), token),
            pl.BlockSpec((total, LANES), whole),
            pl.BlockSpec((TB, 2), token),
        ],
        out_specs=[
            pl.BlockSpec((TB, width), token),
            pl.BlockSpec((TB, width), token),
            pl.BlockSpec((TB, LANES), token),
        ],
        out_shape=(
            jax.ShapeDtypeStruct((rows, width), F32),
            jax.ShapeDtypeStruct((rows, width), BF16),
            jax.ShapeDtypeStruct((rows, LANES), F32),
        ),
        compiler_params=params(40),
        cost_estimate=cost(2 * rows * width * width, 2 * width * width + 10 * rows * width),
        name="middle",
    )(x, o, w_shared, extra, prev, res, routes)


def expert_kernel(
    total,
    flat_ref,
    atwo_ref,
    dy_ref,
    stat_ref,
    wg_ref,
    wu_ref,
    wd_ref,
    flow_ref,
    drow_ref,
    gw_ref,
    gd_ref,
    send_x,
    send_g,
    all_x,
    all_g,
    acc_ref,
    z_ref,
    a_ref,
    b_ref,
    turned_ref,
    wide_buf,
    down_buf,
    wide_given,
    wide_taken,
    down_given,
    down_taken,
    x_sems,
    g_sems,
    flow_sems,
    drow_sems,
    local_sems,
    weight_sems,
    wide_sems,
    down_sems,
):
    experts, cap, width = all_x.shape
    slots = experts * cap
    chunks = z_ref.shape[0]
    per = chunks // 2
    half = width // 2
    tokens = atwo_ref.shape[0]
    me, core = lax.axis_index("expert"), lax.axis_index("context")

    def weights(step):
        chunk, slot = lax.rem(step, chunks), lax.rem(step, 2)
        at = pl.ds(pl.multiple_of(lax.rem(chunk, per) * FC, FC), FC)
        rows = pl.ds(pl.multiple_of(chunk * FC, FC), FC)
        return (
            pltpu.make_async_copy(
                wg_ref.at[chunk // per, :, at], wide_buf.at[slot, 0], weight_sems.at[slot, 0]
            ),
            pltpu.make_async_copy(
                wu_ref.at[chunk // per, :, at], wide_buf.at[slot, 1], weight_sems.at[slot, 1]
            ),
            pltpu.make_async_copy(
                wd_ref.at[0, rows, :], down_buf.at[slot, 0], weight_sems.at[slot, 2]
            ),
            pltpu.make_async_copy(
                wd_ref.at[1, rows, :], down_buf.at[slot, 1], weight_sems.at[slot, 3]
            ),
        )

    def next_weights(step):
        @pl.when(step + 1 < 2 * chunks)
        def _():
            for copy in weights(step + 1):
                copy.start()

        for copy in weights(step):
            copy.wait()

    for copy in weights(0):
        copy.start()
    greet_all(("context", "expert"))

    def hots(target):
        slot = (iota((cap, tokens), 0) + target * cap).astype(F32)
        return flat_ref[0:1, :] == slot, flat_ref[1:2, :] == slot

    order = list(range(1, experts)) + [0]
    x_copies, g_copies = {}, {}
    for j in order:
        target = lax.rem(me + j, experts)
        first, second = hots(target)
        rows = dot(jnp.where(first | second, 1.0, 0.0).astype(BF16), atwo_ref[...]).astype(BF16)
        if j == 0:
            all_x[0] = rows
        else:
            send_x[j - 1] = rows
            x_copies[j] = remote(
                send_x.at[j - 1], all_x.at[j], x_sems, (j - 1,), {"expert": target}
            )
            x_copies[j].start()
    gates = stat_ref[...].T
    for j in order:
        target = lax.rem(me + j, experts)
        first, second = hots(target)
        gate = jnp.sum(
            jnp.where(first, gates[total + 5 : total + 6], 0.0)
            + jnp.where(second, gates[total + 6 : total + 7], 0.0),
            axis=1,
            keepdims=True,
        )
        rows = dot(jnp.where(first | second, 1.0, 0.0).astype(BF16), dy_ref[...])
        rows = (rows * gate).astype(BF16)
        if j == 0:
            all_g[0] = rows
        else:
            send_g[j - 1] = rows
            g_copies[j] = remote(
                send_g.at[j - 1], all_g.at[j], g_sems, (j - 1,), {"expert": target}
            )
            g_copies[j].start()

    def back(buffer, dest, sems, j):
        return remote(
            buffer.at[j - 1],
            dest.at[me],
            sems,
            (j - 1,),
            {"expert": lax.rem(me + experts - j, experts)},
        )

    for j in range(1, experts):
        x_copies[j].wait()
    acc_ref[...] = jnp.zeros_like(acc_ref)

    def up(step, carry):
        next_weights(step)
        slot = lax.rem(step, 2)
        rows = all_x[...].reshape(slots, width)
        gate = dot(rows, wide_buf[slot, 0])
        lift = dot(rows, wide_buf[slot, 1])
        sig = 1.0 / (1.0 + jnp.exp(-gate))
        swish = gate * sig
        hidden = (swish * lift).astype(BF16)
        z_ref[step] = hidden
        a_ref[step] = (lift * sig * (1.0 + gate * (1.0 - sig))).astype(BF16)
        b_ref[step] = swish.astype(BF16)
        acc_ref[...] += dot(hidden, jnp.concatenate([down_buf[slot, 0], down_buf[slot, 1]], axis=1))
        return carry

    lax.fori_loop(0, chunks, up, 0)
    own = [
        pltpu.make_async_copy(all_own, dest.at[me], local_sems.at[i])
        for i, (all_own, dest) in enumerate(
            ((send_x.at[experts - 1], flow_ref), (send_g.at[experts - 1], drow_ref))
        )
    ]
    for j in range(1, experts):
        send_x[j - 1] = acc_ref[j * cap : (j + 1) * cap, :].astype(BF16)
        back(send_x, flow_ref, flow_sems, j).start()
    send_x[experts - 1] = acc_ref[:cap, :].astype(BF16)
    own[0].start()
    turned_ref[...] = all_x[...].reshape(slots, width).T
    acc_ref[...] = jnp.zeros_like(acc_ref)
    for j in range(1, experts):
        g_copies[j].wait()

    def down(step, carry):
        next_weights(step + chunks)
        slot = lax.rem(step, 2)
        whole = jnp.concatenate([down_buf[slot, 0], down_buf[slot, 1]], axis=1)
        dz = dot_nt(all_g[...].reshape(slots, width), whole)
        dg = (dz * a_ref[step].astype(F32)).astype(BF16)
        du = (dz * b_ref[step].astype(F32)).astype(BF16)
        a_ref[step] = dg
        b_ref[step] = du
        acc_ref[...] += dot_nt(dg, wide_buf[slot, 0]) + dot_nt(du, wide_buf[slot, 1])
        return carry

    lax.fori_loop(0, chunks, down, 0)
    for j in range(1, experts):
        send_g[j - 1] = acc_ref[j * cap : (j + 1) * cap, :].astype(BF16)
        back(send_g, drow_ref, drow_sems, j).start()
    send_g[experts - 1] = acc_ref[:cap, :].astype(BF16)
    own[1].start()

    def wide_copy(step):
        return remote(
            wide_given.at[step],
            wide_taken.at[step],
            wide_sems,
            (step,),
            {"context": 1 - core},
        )

    def down_copy(step):
        chunk = lax.rem((1 - core) * per + step, chunks)
        return remote(
            down_given.at[step],
            down_taken.at[chunk],
            down_sems,
            (chunk,),
            {"context": 1 - core},
        )

    def products(step):
        chunk = lax.rem((1 - core) * per + step, chunks)
        gate = dot(turned_ref[...], a_ref[chunk])
        lift = dot(turned_ref[...], b_ref[chunk])
        low = dot(z_ref[chunk].T, all_g[...].reshape(slots, width))
        left, right = low[:, :half], low[:, half:]
        down_given[step] = jnp.where(core == 0, right, left).astype(BF16)
        gd_ref[chunk] = jnp.where(core == 0, left, right).astype(BF16)
        down_copy(step).start()
        return gate, lift

    def give(step, carry):
        gate, lift = products(step)
        wide_given[step, 0] = gate.astype(BF16)
        wide_given[step, 1] = lift.astype(BF16)
        wide_copy(step).start()
        return carry

    lax.fori_loop(0, per, give, 0)

    def keep(step, carry):
        gate, lift = products(step)
        wide_copy(step - per).wait_recv()
        for i, value in enumerate((gate, lift)):
            at = pl.ds(pl.multiple_of((i * per + step - per) * FC, FC), FC)
            gw_ref[:, at] = (value + wide_taken[step - per, i].astype(F32)).astype(BF16)
        return carry

    lax.fori_loop(per, chunks, keep, 0)

    def settle(step, carry):
        other = lax.rem(core * per + step, chunks)
        copy = remote(
            down_given.at[step],
            down_taken.at[other],
            down_sems,
            (other,),
            {"context": 1 - core},
        )
        copy.wait_recv()
        gd_ref[other] = (gd_ref[other].astype(F32) + down_taken[other].astype(F32)).astype(BF16)
        return carry

    lax.fori_loop(0, chunks, settle, 0)

    for copy in own:
        copy.wait()
    for j in range(1, experts):
        back(send_x, flow_ref, flow_sems, j).wait()
        back(send_g, drow_ref, drow_sems, j).wait()

    def sent(step, carry):
        down_copy(step).wait_send()
        return carry

    lax.fori_loop(0, chunks, sent, 0)
    lax.fori_loop(0, per, lambda step, carry: (wide_copy(step).wait_send(), carry)[1], 0)


def run_experts(total, experts, cap, flat_t, atwo, dy, stat, wg, wu, wd):
    rows, width = atwo.shape
    hidden = wd.shape[1]
    chunks = hidden // FC
    per = chunks // 2
    half = width // 2
    slots = experts * cap
    vmem = pl.BlockSpec(memory_space=pltpu.VMEM)
    anywhere = pl.BlockSpec(memory_space=pl.ANY)
    dma = pltpu.SemaphoreType.DMA
    return pl.pallas_call(
        functools.partial(expert_kernel, total),
        in_specs=[vmem] * 4 + [anywhere] * 3,
        out_specs=[anywhere] * 2 + [vmem] * 2,
        out_shape=(
            jax.ShapeDtypeStruct((experts, cap, width), BF16),
            jax.ShapeDtypeStruct((experts, cap, width), BF16),
            jax.ShapeDtypeStruct((width, hidden), BF16),
            jax.ShapeDtypeStruct((chunks, FC, half), BF16),
        ),
        scratch_shapes=[
            pltpu.VMEM((experts, cap, width), BF16),
            pltpu.VMEM((experts, cap, width), BF16),
            pltpu.VMEM((experts, cap, width), BF16),
            pltpu.VMEM((experts, cap, width), BF16),
            pltpu.VMEM((slots, width), F32),
            pltpu.VMEM((chunks, slots, FC), BF16),
            pltpu.VMEM((chunks, slots, FC), BF16),
            pltpu.VMEM((chunks, slots, FC), BF16),
            pltpu.VMEM((width, slots), BF16),
            pltpu.VMEM((2, 2, width, FC), BF16),
            pltpu.VMEM((2, 2, FC, half), BF16),
            pltpu.VMEM((per, 2, width, FC), BF16),
            pltpu.VMEM((per, 2, width, FC), BF16),
            pltpu.VMEM((chunks, FC, half), BF16),
            pltpu.VMEM((chunks, FC, half), BF16),
            dma((2, experts - 1)),
            dma((2, experts - 1)),
            dma((2, experts - 1)),
            dma((2, experts - 1)),
            dma((2,)),
            dma((2, 4)),
            dma((2, per)),
            dma((2, chunks)),
        ],
        compiler_params=pltpu.CompilerParams(
            collective_id=2, has_side_effects=True, vmem_limit_bytes=62 * MIB
        ),
        cost_estimate=cost(18 * slots * width * hidden, 30 * width * hidden),
        name="experts",
    )(flat_t, atwo, dy, stat, wg, wu, wd)


def combine_kernel(
    experts,
    total,
    flow_ref,
    drow_ref,
    flat_ref,
    stat_ref,
    routes_ref,
    hres_ref,
    atwo_ref,
    dy_ref,
    o_ref,
    extra_ref,
    w_ref,
    prev_ref,
    out_ref,
    dh_ref,
    dolow_ref,
    gw_ref,
    small_ref,
    acc_ref,
):
    step = pl.program_id(0)
    slots = flow_ref.shape[0]
    half = o_ref.shape[2]
    extra = extra_ref[...]
    gain = extra[GAIN_TWO : GAIN_TWO + 1].astype(F32)
    stat = stat_ref[...]
    hres = hres_ref[...]
    dy = dy_ref[...].astype(F32)
    scale = stat[:, total + 4 : total + 5]
    gates = [stat[:, total + 5 + k : total + 6 + k] for k in range(2)]
    ntwo = hres * scale * gain
    spread = iota((TB, slots), 1)
    hots = [flat_ref[:, k : k + 1] == spread for k in range(2)]
    returned = flow_ref[...]
    mixes = [[stat[:, total + 2 * j + i : total + 2 * j + i + 1] for i in range(2)] for j in range(2)]
    vecs = [extra[VECS + j : VECS + j + 1].astype(F32) for j in range(2)]
    moe = jnp.zeros_like(hres)
    lane = iota((TB, LANES), 1)
    dpgate = jnp.zeros((TB, LANES), F32)
    weight = jnp.zeros((TB, 1), F32)
    const_weights = [jnp.zeros((TB, 1), F32)] * 2
    for k in range(2):
        route = routes_ref[:, k : k + 1]
        epair = dot(jnp.where(hots[k], 1.0, 0.0).astype(BF16), returned)
        share = jnp.where(route == experts + 1, 1.0, 0.0)
        weight = weight + share * gates[k]
        for j in range(2):
            chosen = jnp.where(route == experts + 2 + j, 1.0, 0.0)
            share = share + chosen * mixes[j][0]
            epair = epair + (chosen * mixes[j][1]) * vecs[j]
            const_weights[j] = const_weights[j] + chosen * gates[k]
        epair = epair + share * ntwo
        moe = moe + gates[k] * epair
        dgate = jnp.sum(dy * epair, axis=1, keepdims=True)
        dpgate = dpgate + jnp.where(lane == route, dgate, 0.0)
    out_ref[...] = (hres + moe).astype(BF16)

    pgate = jnp.where(lane < total, stat, 0.0)
    dlogit = pgate * (dpgate - jnp.sum(pgate * dpgate, axis=1, keepdims=True))
    dot_normed = jnp.sum(dy * ntwo, axis=1, keepdims=True)
    droute = dlogit
    vec_rows = []
    for j in range(2):
        dot_vec = jnp.sum(dy * vecs[j], axis=1, keepdims=True)
        grads = [const_weights[j] * dot_normed, const_weights[j] * dot_vec]
        inner = mixes[j][0] * grads[0] + mixes[j][1] * grads[1]
        for i in range(2):
            droute = jnp.where(
                lane == total + 2 * j + i, mixes[j][i] * (grads[i] - inner), droute
            )
        weight = weight + const_weights[j] * mixes[j][0]
        vec_rows.append(jnp.sum((const_weights[j] * mixes[j][1]) * dy, axis=0, keepdims=True))
    droute = droute.astype(BF16)
    hot_any = jnp.where(hots[0] | hots[1], 1.0, 0.0).astype(BF16)
    dntwo = weight * dy + dot(droute, extra) + dot(hot_any, drow_ref[...])
    turned = dntwo * gain
    inner = jnp.mean(hres * turned, axis=1, keepdims=True)
    dh = dy + scale * turned - hres * (scale * scale * scale * inner)
    dh_ref[...] = dh
    dhlow = dh.astype(BF16)
    w_out = jnp.concatenate([w_ref[0, 0], w_ref[0, 1]], axis=1)
    dolow = dot_nt(dhlow, w_out).astype(BF16)
    dolow_ref[0] = dolow[:, :half]
    dolow_ref[1] = dolow[:, half:]
    gain_row = jnp.sum(dntwo * hres * scale, axis=0, keepdims=True)
    route_rows = dot(droute.T, atwo_ref[...])
    res_rows = lax.dot_general(
        prev_ref[...],
        dlogit,
        (((0,), (0,)), ((), ())),
        precision=HIGH,
        preferred_element_type=F32,
    )
    width = hres.shape[1]
    res_rows = jnp.concatenate([res_rows, jnp.zeros((total, width - LANES), F32)], axis=1)
    small = jnp.concatenate(
        [route_rows[: total + 4], gain_row, vec_rows[0], vec_rows[1], jnp.zeros((1, width), F32), res_rows],
        axis=0,
    )
    part = dot(jnp.concatenate([o_ref[0], o_ref[1]], axis=1).T, dhlow)

    @pl.when(step == 0)
    def _():
        small_ref[...] = small
        acc_ref[...] = part

    @pl.when(step > 0)
    def _():
        small_ref[...] += small
        acc_ref[...] += part

    @pl.when(step == pl.num_programs(0) - 1)
    def _():
        for side in range(2):
            gw_ref[side] = acc_ref[:, side * half : (side + 1) * half].astype(BF16)


def combine(experts, total, flow, drow, flat, stat, routes, hres, atwo, dy, o, w_shared, extra, prev):
    rows, width = hres.shape
    slots = flow.shape[0]
    half = width // 2
    token = lambda i: (i, 0)
    whole = lambda i: (0, 0)
    side = pl.BlockSpec((2, TB, half), lambda i: (0, i, 0))
    weight = pl.BlockSpec((2, width, half), lambda i: (0, 0, 0))
    small_rows = 2 * total + 8
    return pl.pallas_call(
        functools.partial(combine_kernel, experts, total),
        grid=(rows // TB,),
        in_specs=[
            pl.BlockSpec((slots, width), whole),
            pl.BlockSpec((slots, width), whole),
            pl.BlockSpec((TB, LANES), token),
            pl.BlockSpec((TB, LANES), token),
            pl.BlockSpec((TB, 2), token),
            pl.BlockSpec((TB, width), token),
            pl.BlockSpec((TB, width), token),
            pl.BlockSpec((TB, width), token),
            side,
            pl.BlockSpec((LANES, width), whole),
            pl.BlockSpec((1, 2, width, half), lambda i: (3, 0, 0, 0)),
            pl.BlockSpec((TB, total), token),
        ],
        out_specs=[
            pl.BlockSpec((TB, width), token),
            pl.BlockSpec((TB, width), token),
            side,
            weight,
            pl.BlockSpec((small_rows, width), whole),
        ],
        out_shape=(
            jax.ShapeDtypeStruct((rows, width), BF16),
            jax.ShapeDtypeStruct((rows, width), F32),
            jax.ShapeDtypeStruct((2, rows, half), BF16),
            jax.ShapeDtypeStruct((2, width, half), BF16),
            jax.ShapeDtypeStruct((small_rows, width), F32),
        ),
        scratch_shapes=[pltpu.VMEM((width, width), F32)],
        compiler_params=params(56),
        cost_estimate=cost(
            6 * rows * slots * width + 4 * rows * width * width, 30 * rows * width + 8 * width * width
        ),
        name="combine",
    )(flow, drow, flat, stat, routes, hres, atwo, dy, o, extra, w_shared, prev)


def tail_kernel(
    gain_at,
    sent_ref,
    aone_ref,
    w_ref,
    extra_ref,
    x_ref,
    dh_ref,
    gwo_ref,
    small_ref,
    wide_ref,
    down_ref,
    out_ref,
    final,
    small_out_ref,
    wide_out,
    down_out,
    both,
    grads,
    w_buf,
    x_buf,
    dh_buf,
    out_buf,
    core_in,
    plane_out,
    plane_in,
    slab_out,
    slab_in,
    own_ref,
    small_own,
    small_core,
    small_plane,
    small_slab,
    load_sems,
    store_sems,
    both_sems,
    share_sems,
    core_sems,
    plane_sems,
    slab_sems,
    final_sems,
    pass_sems,
    small_core_sems,
    small_plane_sems,
    small_slab_sems,
):
    experts = lax.axis_size("expert")
    slabs = lax.axis_size("dp")
    me, core, slab = lax.axis_index("expert"), lax.axis_index("context"), lax.axis_index("dp")
    other = 1 - core
    tokens, width = x_buf.shape
    half = width // 2
    parts = 2
    block = tokens // parts

    mine = pltpu.make_async_copy(sent_ref.at[core], both.at[core], load_sems.at[0])
    mine.start()
    loads = [
        pltpu.make_async_copy(w_ref.at[pl.ds(0, 3)], w_buf, load_sems.at[1]),
        pltpu.make_async_copy(x_ref, x_buf, load_sems.at[2]),
        pltpu.make_async_copy(dh_ref, dh_buf, load_sems.at[3]),
    ]
    for copy in loads:
        copy.start()
    greet_all(("context", "expert", "dp"))
    theirs = [
        remote(
            sent_ref.at[other, which],
            both.at[core, which],
            both_sems,
            (which,),
            {"context": other},
        )
        for which in range(3)
    ]
    for copy in theirs:
        copy.start()

    def core_copy(which):
        return remote(
            grads.at[other, which], core_in.at[which], core_sems, (which,), {"context": other}
        )

    for side in range(2):
        grads[side, 3] = gwo_ref[side]
    core_copy(3).start()
    wide_out[core] = wide_ref[...]
    down_out[core] = down_ref[...]
    shares = [
        remote(ref.at[core], ref.at[core], share_sems, (i,), {"context": other})
        for i, ref in enumerate((wide_out, down_out))
    ]
    for copy in shares:
        copy.start()

    def plane_copy(j, at):
        return remote(
            plane_out.at[j - 1, at],
            plane_in.at[j - 1, at],
            plane_sems,
            (j - 1, at),
            {"expert": lax.rem(me + j, experts)},
        )

    def pass_on(which):
        core_copy(which).wait_recv()
        j = lax.rem(which + experts - me, experts)

        @pl.when(j != 0)
        def _():
            def one(k):
                at = lax.rem(slab + k + 1, slabs)
                plane_out[j - 1, at] = (
                    grads[core, which, at].astype(F32) + core_in[which, at].astype(F32)
                ).astype(BF16)
                plane_copy(j, at).start()

            loop(slabs, one)

    mine.wait()
    turned = aone_ref[...].T
    for which in range(3):
        theirs[which].wait_recv()
        grad = jnp.concatenate([both[0, which], both[1, which]], axis=1)
        weight = dot(turned, grad)
        for side in range(2):
            grads[side, which] = (
                weight[:, side * half : (side + 1) * half]
                .reshape(slabs, width // slabs, half)
                .astype(BF16)
            )
        core_copy(which).start()
        pass_on((which + 3) % 4)
    for copy in loads:
        copy.wait()

    gain = extra_ref[GAIN_ONE : GAIN_ONE + 1].astype(F32)
    stores = []
    gain_row = jnp.zeros((1, width), F32)
    for part in range(parts):
        at = slice(part * block, (part + 1) * block)
        dnone = None
        for which in range(3):
            grad = jnp.concatenate([both[0, which, at], both[1, which, at]], axis=1)
            whole = jnp.concatenate([w_buf[which, 0], w_buf[which, 1]], axis=1)
            product = dot_nt(grad, whole)
            dnone = product if dnone is None else dnone + product
        values = x_buf[at].astype(F32)
        scale = lax.rsqrt(jnp.mean(values * values, axis=-1, keepdims=True) + EPS)
        scaled = dnone * gain
        inner = jnp.mean(values * scaled, axis=1, keepdims=True)
        out_buf[at] = dh_buf[at] + scale * scaled - values * (scale * scale * scale * inner)
        stores.append(
            pltpu.make_async_copy(out_buf.at[at], out_ref.at[at], store_sems.at[part])
        )
        stores[-1].start()
        gain_row = gain_row + jnp.sum(dnone * values * scale, axis=0, keepdims=True)
        if part == 0:
            pass_on(2)

    row = iota(small_ref.shape, 0)
    small_own[...] = small_ref[...] + jnp.where(row == gain_at, gain_row, 0.0)
    small_copy = remote(small_own, small_core, small_core_sems, (0,), {"context": other})
    small_copy.start()
    small_copy.wait()
    small_plane[me] = small_own[...] + small_core[...]
    small_plane_copies = []
    for j in range(1, experts):
        small_plane_copies.append(
            remote(
                small_plane.at[me],
                small_plane.at[me],
                small_plane_sems,
                (j,),
                {"expert": lax.rem(me + j, experts)},
            )
        )
        small_plane_copies[-1].start()

    def gathered(at):
        value = grads[core, me, at].astype(F32) + core_in[me, at].astype(F32)
        for j in range(1, experts):
            plane_copy(j, at).wait_recv()
            value = value + plane_in[j - 1, at].astype(F32)
        return value

    def slab_copy(k):
        return remote(
            slab_out.at[k],
            slab_in.at[k],
            slab_sems,
            (k,),
            {"dp": lax.rem(slab + k + 1, slabs)},
        )

    def scatter(k):
        slab_out[k] = gathered(lax.rem(slab + k + 1, slabs)).astype(BF16)
        slab_copy(k).start()

    loop(slabs - 1, scatter)

    for copy in small_plane_copies:
        copy.wait()
    value = small_plane[0]
    for j in range(1, experts):
        value = value + small_plane[j]
    small_slab[slab] = value

    def small_slab_copy(k):
        return remote(
            small_slab.at[slab],
            small_slab.at[slab],
            small_slab_sems,
            (k,),
            {"dp": lax.rem(slab + k + 1, slabs)},
        )

    loop(slabs - 1, lambda k: small_slab_copy(k).start())

    own_ref[...] = gathered(slab)

    def collect(k):
        slab_copy(k).wait_recv()
        own_ref[...] += slab_in[k].astype(F32)

    loop(slabs - 1, collect)
    final[core, me] = own_ref[...].astype(BF16)
    final_copies, pass_copies = [], []
    for j in range(1, experts):
        final_copies.append(
            remote(
                final.at[core, me],
                final.at[core, me],
                final_sems,
                (j,),
                {"expert": lax.rem(me + j, experts)},
            )
        )
        final_copies[-1].start()
    for j in range(experts):
        source = lax.rem(me + experts - j, experts)
        if j > 0:
            final_copies[j - 1].wait_recv()
        pass_copies.append(
            remote(
                final.at[core, source],
                final.at[core, source],
                pass_sems,
                (j,),
                {"context": other},
            )
        )
        pass_copies[-1].start()

    loop(slabs - 1, lambda k: small_slab_copy(k).wait())
    small_out_ref[...] = small_slab[0]

    def add_small(k):
        small_out_ref[...] += small_slab[k + 1]

    loop(slabs - 1, add_small)

    for copy in pass_copies + shares:
        copy.wait_recv()
    for copy in stores:
        copy.wait()
    for which in range(4):
        core_copy(which).wait_send()
    for j in range(1, experts):

        def sent(k, j=j):
            plane_copy(j, k).wait_send()

        loop(slabs, sent)
    loop(slabs - 1, lambda k: slab_copy(k).wait_send())
    for copy in theirs + shares + final_copies + pass_copies:
        copy.wait_send()


def tail(experts, slabs, gain_at, sent, aone, w_shared, extra, x, dh, gwo, small, wide, down):
    tokens, width = x.shape
    half = width // 2
    rows = width // slabs
    vmem = pl.BlockSpec(memory_space=pltpu.VMEM)
    anywhere = pl.BlockSpec(memory_space=pl.ANY)
    dma = pltpu.SemaphoreType.DMA
    return pl.pallas_call(
        functools.partial(tail_kernel, gain_at),
        in_specs=[anywhere, vmem, anywhere, vmem, anywhere, anywhere] + [vmem] * 4,
        out_specs=[anywhere] + [vmem] * 4,
        out_shape=(
            jax.ShapeDtypeStruct((tokens, width), F32),
            jax.ShapeDtypeStruct((2, experts, rows, half), BF16),
            jax.ShapeDtypeStruct(small.shape, F32),
            jax.ShapeDtypeStruct((2,) + wide.shape, BF16),
            jax.ShapeDtypeStruct((2,) + down.shape, BF16),
        ),
        scratch_shapes=[
            pltpu.VMEM((2, 3, tokens, half), BF16),
            pltpu.VMEM((2, 4, slabs, rows, half), BF16),
            pltpu.VMEM((3, 2, width, half), BF16),
            pltpu.VMEM((tokens, width), BF16),
            pltpu.VMEM((tokens, width), F32),
            pltpu.VMEM((tokens, width), F32),
            pltpu.VMEM((4, slabs, rows, half), BF16),
            pltpu.VMEM((experts - 1, slabs, rows, half), BF16),
            pltpu.VMEM((experts - 1, slabs, rows, half), BF16),
            pltpu.VMEM((slabs - 1, rows, half), BF16),
            pltpu.VMEM((slabs - 1, rows, half), BF16),
            pltpu.VMEM((rows, half), F32),
            pltpu.VMEM(small.shape, F32),
            pltpu.VMEM(small.shape, F32),
            pltpu.VMEM((experts,) + small.shape, F32),
            pltpu.VMEM((slabs,) + small.shape, F32),
            dma((4,)),
            dma((2,)),
            dma((2, 3)),
            dma((2, 2)),
            dma((2, 4)),
            dma((2, experts - 1, slabs)),
            dma((2, slabs - 1)),
            dma((2, experts)),
            dma((2, experts)),
            dma((2, 1)),
            dma((2, experts)),
            dma((2, slabs - 1)),
        ],
        compiler_params=pltpu.CompilerParams(
            collective_id=0, has_side_effects=True, vmem_limit_bytes=60 * MIB
        ),
        cost_estimate=cost(12 * tokens * width * width, 40 * tokens * width),
        name="tail",
    )(sent, aone, w_shared, extra, x, dh, gwo, small, wide, down)


def finish_kernel(
    total,
    slab_ref,
    final_ref,
    small_ref,
    wide_ref,
    down_ref,
    q_ref,
    k_ref,
    v_ref,
    o_ref,
    norm_one_ref,
    norm_two_ref,
    router_ref,
    mix_ref,
    vec_ref,
    res_ref,
    gate_ref,
    up_ref,
    gd_ref,
    turned_ref,
):
    rows, half = final_ref.shape[2:]
    wide = wide_ref.shape[2] // 2
    for which, ref in enumerate((q_ref, k_ref, v_ref, o_ref)):
        for side in range(2):
            ref[:, side * half : (side + 1) * half] = final_ref[side, which].astype(F32)
    for side in range(2):
        at = slice(side * wide, (side + 1) * wide)
        gate_ref[0, :, at] = wide_ref[side, :, :wide].astype(F32)
        up_ref[0, :, at] = wide_ref[side, :, wide:].astype(F32)
        gd_ref[0, :, side * half : (side + 1) * half] = down_ref[side].astype(F32)
    small = small_ref[...]
    fill = jnp.zeros((LANES - small.shape[0], small.shape[1]), F32)
    turned_ref[...] = jnp.concatenate([small, fill], axis=0).T
    own = turned_ref[pl.ds(pl.multiple_of(slab_ref[0] * rows, 8), rows), :]
    router_ref[...] = own[:, :total]
    mix_ref[...] = own[:, total : total + 4]
    norm_two_ref[...] = own[:, total + 4 : total + 5]
    vec_ref[...] = own[:, total + 5 : total + 7]
    norm_one_ref[...] = own[:, total + 7 : total + 8]
    res_ref[...] = small[total + 8 :, :total]


def finish(total, slab, final, small, wide, down):
    rows, half = final.shape[2:]
    width = 2 * half
    vmem = pl.BlockSpec(memory_space=pltpu.VMEM)
    shape = lambda *dims: jax.ShapeDtypeStruct(dims, F32)
    return pl.pallas_call(
        functools.partial(finish_kernel, total),
        in_specs=[pl.BlockSpec(memory_space=pltpu.SMEM)] + [vmem] * 4,
        out_specs=[vmem] * 13,
        out_shape=(
            shape(rows, width),
            shape(rows, width),
            shape(rows, width),
            shape(rows, width),
            shape(rows, 1),
            shape(rows, 1),
            shape(rows, total),
            shape(rows, 4),
            shape(rows, 2),
            shape(total, total),
            shape(1, rows, wide.shape[2]),
            shape(1, rows, wide.shape[2]),
            shape(1, down.shape[1], width),
        ),
        scratch_shapes=[pltpu.VMEM((width, LANES), F32)],
        compiler_params=params(40),
        cost_estimate=cost(1e6, 20 * rows * width),
        name="finish",
    )(slab, final, small, wide, down)


def swap_cores(value):
    return lax.all_to_all(value, "context", split_axis=0, concat_axis=0, tiled=True)


def on_device(
    tokens,
    segments,
    routes,
    prev_logits,
    ranks,
    cotangent,
    norm_one,
    w_query,
    w_key,
    w_value,
    w_out,
    norm_two,
    router,
    w_res,
    const_mix,
    const_vec,
    w_gate,
    w_up,
    w_down,
):
    experts = lax.axis_size("expert")
    dp = lax.axis_size("dp")
    total = experts + NZ
    _, rows, width = tokens.shape
    hidden = w_gate.shape[2]
    cap = (18 * rows + 8 * total - 1) // (8 * total)
    seq = 2 * rows
    core = lax.axis_index("context")
    half = width // 2

    def mine(shard, size):
        return lax.dynamic_slice_in_dim(shard, core * size, size, 1)

    def gather(shard):
        return lax.all_gather(shard, ("context", "dp"), axis=0).reshape(
            2, dp * shard.shape[0], shard.shape[1]
        )

    extra = jnp.concatenate(
        [router, const_mix, norm_one[:, None], norm_two[:, None], const_vec], axis=1
    )
    w_shared, extra, flat, flat_t, low, first = spread(
        experts,
        dp,
        cap,
        w_query,
        w_key,
        w_value,
        w_out,
        extra.astype(F32).T,
        routes[0],
        ranks[0],
        segments,
    )
    w_shared = w_shared.reshape(4, 2, width, half)
    extra = extra.transpose(1, 0, 2).reshape(total + 8, width).astype(BF16)
    extra = jnp.concatenate(
        [
            extra[: total + 4],
            jnp.zeros((GAIN_ONE - total - 4, width), BF16),
            extra[total + 4 :],
            jnp.zeros((LANES - GAIN_ONE - 4, width), BF16),
        ],
        axis=0,
    )
    gate_w = gather(mine(w_gate[0], hidden // 2))
    up_w = gather(mine(w_up[0], hidden // 2))
    down_w = gather(mine(w_down[0], half))

    cos, sin = rope_tables(seq)
    cos, sin = jnp.asarray(cos), jnp.asarray(sin)
    res = jnp.pad(w_res.astype(F32), ((0, 0), (0, LANES - total)))

    x = tokens[0]
    dy = cotangent[0]
    sent, aone = project(core.reshape(1), x, extra, w_shared, cos, sin)
    qkv = swap_cores(sent)
    o_heads, lse = attend(first, qkv, low)
    o = swap_cores(o_heads)
    hres, atwo, stat = middle(total, x, o, w_shared, extra, prev_logits[0], res, routes[0])
    flow_back, drow_back, grad_wide, grad_down = run_experts(
        total, experts, cap, flat_t, atwo, dy, stat, gate_w, up_w, down_w
    )
    flow_back = flow_back.reshape(experts * cap, width)
    drow_back = drow_back.reshape(experts * cap, width)
    wide = lax.psum_scatter(grad_wide, "dp", scatter_dimension=0, tiled=True)
    down = lax.psum_scatter(
        grad_down.reshape(hidden, half), "dp", scatter_dimension=0, tiled=True
    )

    output, dh, dolow, grad_out_w, small = combine(
        experts,
        total,
        flow_back,
        drow_back,
        flat,
        stat,
        routes[0],
        hres,
        atwo,
        dy,
        o,
        w_shared,
        extra,
        prev_logits[0],
    )
    grad_o = swap_cores(dolow)
    grads_sent = attend_back(
        first,
        qkv,
        grad_o,
        o_heads,
        lse,
        low,
        cos.reshape(2, rows, LANES),
        sin.reshape(2, rows, LANES),
    )
    grad_tokens, final, small, wide, down = tail(
        experts,
        dp,
        total + 7,
        grads_sent,
        aone,
        w_shared,
        extra,
        x,
        dh,
        grad_out_w.reshape(2, dp, width // dp, half),
        small,
        wide,
        down,
    )
    (
        grad_query,
        grad_key,
        grad_value,
        grad_out,
        grad_norm_one,
        grad_norm_two,
        grad_router,
        grad_mix,
        grad_vec,
        grad_res,
        grad_gate,
        grad_up,
        grad_down,
    ) = finish(total, lax.axis_index("dp").reshape(1), final, small, wide, down)
    return (
        output[None],
        grad_tokens[None],
        grad_norm_one[:, 0],
        grad_query,
        grad_key,
        grad_value,
        grad_out,
        grad_norm_two[:, 0],
        grad_router,
        grad_res,
        grad_mix,
        grad_vec,
        grad_gate,
        grad_up,
        grad_down,
    )


def solution(mesh):
    token = P(("expert", "dp"), "context", None)
    rows = P("dp", None)
    expert = P("expert", "dp", None)
    in_specs = (
        token,
        P(("expert", "dp"), "context"),
        token,
        token,
        token,
        token,
        P("dp"),
        rows,
        rows,
        rows,
        rows,
        P("dp"),
        rows,
        P(),
        rows,
        rows,
        expert,
        expert,
        expert,
    )
    out_specs = (
        token,
        token,
        P("dp"),
        rows,
        rows,
        rows,
        rows,
        P("dp"),
        rows,
        P(),
        rows,
        rows,
        expert,
        expert,
        expert,
    )
    return jax.shard_map(
        on_device, mesh=mesh, in_specs=in_specs, out_specs=out_specs, check_vma=False
    )
```

```python
import functools

import jax
import jax.numpy as jnp
import numpy as np
from jax import lax
from jax.experimental import pallas as pl
from jax.experimental.pallas import tpu as pltpu
from jax.sharding import PartitionSpec as P

HEADS = 12
HEAD_DIM = 64
WIN = 1024
NZ = 4
SEGMENTS = 5
GAIN_ONE, GAIN_TWO, VECS = 112, 113, 114
TQ = 256
TB = 256
RC = 64
FC = 512
LANES = 128
EPS = 1e-05
MASKED = -1000000000.0
HIGH = lax.Precision.HIGHEST
F32 = jnp.float32
BF16 = jnp.bfloat16
MIB = 1024 * 1024


def params(mib):
    return pltpu.CompilerParams(vmem_limit_bytes=mib * MIB)


def cost(flops, nbytes, trans=0):
    return pl.CostEstimate(flops=int(flops), bytes_accessed=int(nbytes), transcendentals=int(trans))


def dot(left, right):
    return jnp.dot(left, right, preferred_element_type=F32)


def dot_nt(left, right):
    return lax.dot_general(left, right, (((1,), (1,)), ((), ())), preferred_element_type=F32)


def dot_tn(left, right):
    return lax.dot_general(left, right, (((0,), (0,)), ((), ())), preferred_element_type=F32)


def iota(shape, axis):
    return lax.broadcasted_iota(jnp.int32, shape, axis)


def rope_tables(seq):
    half = HEAD_DIM // 2
    frequency = np.float32(10000.0) ** (
        -np.arange(half, dtype=np.float32) * np.float32(2.0) / np.float32(HEAD_DIM)
    )
    angles = np.arange(seq, dtype=np.float32)[:, None] * frequency.astype(np.float32)[None, :]
    cos = np.cos(angles.astype(np.float64)).astype(np.float32)
    sin = np.sin(angles.astype(np.float64)).astype(np.float32)
    return np.concatenate([cos] * 4, axis=1), np.concatenate([-sin, sin, -sin, sin], axis=1)


def swap_halves(chunk):
    lane = iota(chunk.shape, 1)
    return jnp.where(
        lane % HEAD_DIM < HEAD_DIM // 2, pltpu.roll(chunk, 96, 1), pltpu.roll(chunk, 32, 1)
    )


def loop(count, body):
    if count <= 4:
        for step in range(count):
            body(step)
    else:
        lax.fori_loop(0, count, lambda step, carry: (body(step), carry)[1], 0)


def remote(src, dst, sems, index, where):
    return pltpu.make_async_remote_copy(
        src_ref=src,
        dst_ref=dst,
        send_sem=sems.at[(0,) + index],
        recv_sem=sems.at[(1,) + index],
        device_id=where,
        device_id_type=pl.DeviceIdType.MESH,
    )


def greet_all(axes):
    barrier = pltpu.get_barrier_semaphore()
    total = 0
    for axis in axes:
        size = lax.axis_size(axis)
        me = lax.axis_index(axis)
        total += size - 1

        def greet(k, axis=axis, size=size, me=me):
            pl.semaphore_signal(
                barrier,
                inc=1,
                device_id={axis: lax.rem(me + k + 1, size)},
                device_id_type=pl.DeviceIdType.MESH,
            )

        loop(size - 1, greet)
    pl.semaphore_wait(barrier, total)


def place_pairs(experts, cap, routes_ref, ranks_ref, flat_ref, flat_t_ref):
    rows = routes_ref.shape[0]
    lane = iota((rows, LANES), 1)
    first, second = routes_ref[:, 0:1], routes_ref[:, 1:2]
    hot_first, hot_second = first == lane, second == lane
    hot = (hot_first.astype(F32) + hot_second.astype(F32)).astype(BF16)
    ranks = ranks_ref[...].astype(F32)
    ranks_col = jnp.broadcast_to(ranks, (LANES, rows)).T[:, 0:1]
    earlier = jnp.where(ranks < ranks_col, 1.0, 0.0).astype(BF16)
    counts = dot(earlier, hot)

    def flat(hit, route):
        slot = jnp.sum(jnp.where(hit, counts, 0.0), axis=1, keepdims=True).astype(jnp.int32)
        return jnp.where((route < experts) & (slot < cap), route * cap + slot, experts * cap)

    columns = (flat(hot_first, first), flat(hot_second, second), first, second)
    out = jnp.zeros((rows, LANES), jnp.int32)
    for i, column in enumerate(columns):
        out = jnp.where(lane == i, column, out)
    flat_ref[...] = out
    flat_t_ref[...] = out.astype(F32).T[:8]


def find_starts(segs_ref, low_ref, first_ref):
    rows = segs_ref.shape[2]
    per = rows // TQ
    segs = [segs_ref[side].astype(F32) for side in range(2)]
    starts = [jnp.zeros((1, rows), F32) for side in range(2)]
    for number in range(1, SEGMENTS):
        before = sum(
            jnp.sum(jnp.where(part < number, 1.0, 0.0), axis=1, keepdims=True) for part in segs
        )
        starts = [
            jnp.where(part == number, before, start) for part, start in zip(segs, starts)
        ]
    for side in range(2):
        place = (iota((1, rows), 1) + (side * rows - WIN + 1)).astype(F32)
        low = jnp.maximum(starts[side], place)
        for tile in range(per):
            part = low[:, tile * TQ : (tile + 1) * TQ]
            low_ref[side * per + tile] = part.astype(jnp.int32)
            first_ref[side * per + tile] = jnp.min(part).astype(jnp.int32) // TQ


def spread_kernel(
    cap,
    w_query_ref,
    w_key_ref,
    w_value_ref,
    w_out_ref,
    extra_ref,
    routes_ref,
    ranks_ref,
    segs_ref,
    x_ref,
    cos_ref,
    sin_ref,
    shared_ref,
    extra_out_ref,
    flat_ref,
    flat_t_ref,
    low_ref,
    first_ref,
    qkv_ref,
    aone_ref,
    out_ref,
    segs_all,
    stage_ref,
    slab_sems,
    plane_sems,
    core_sems,
    extra_sems,
    segs_sems,
    shared_sem,
    own_sems,
    qkv_sems,
):
    experts = lax.axis_size("expert")
    slabs = lax.axis_size("dp")
    me, core, slab = lax.axis_index("expert"), lax.axis_index("context"), lax.axis_index("dp")
    half = out_ref.shape[4]
    for which, ref in enumerate((w_query_ref, w_key_ref, w_value_ref, w_out_ref)):
        for side in range(2):

            @pl.when((me == which) & (core == side))
            def _():
                out_ref[which, side, slab] = ref[:, side * half : (side + 1) * half]

    extra_out_ref[slab] = extra_ref[...]
    segs_all[core] = segs_ref[...]
    greet_all(("context", "expert", "dp"))

    def slab_copy(k):
        piece = out_ref.at[me, core, slab]
        return remote(piece, piece, slab_sems, (k,), {"dp": lax.rem(slab + k + 1, slabs)})

    def extra_copy(k):
        piece = extra_out_ref.at[slab]
        return remote(piece, piece, extra_sems, (k,), {"dp": lax.rem(slab + k + 1, slabs)})

    def plane_copy(j, at):
        piece = out_ref.at[me, core, at]
        return remote(
            piece, piece, plane_sems, (j - 1, at), {"expert": lax.rem(me + j, experts)}
        )

    def core_copy(j, at):
        piece = out_ref.at[lax.rem(me + experts - j, experts), core, at]
        return remote(piece, piece, core_sems, (j, at), {"context": 1 - core})

    def share(at):
        for j in range(1, experts):
            plane_copy(j, at).start()
        core_copy(0, at).start()

    loop(slabs - 1, lambda k: extra_copy(k).start())
    loop(slabs - 1, lambda k: slab_copy(k).start())
    share(slab)
    segs_copy = remote(
        segs_all.at[core], segs_all.at[core], segs_sems, (0,), {"context": 1 - core}
    )
    segs_copy.start()
    place_pairs(experts, cap, routes_ref, ranks_ref, flat_ref, flat_t_ref)
    segs_copy.wait()
    find_starts(segs_all, low_ref, first_ref)
    loop(slabs - 1, lambda k: extra_copy(k).wait())
    at = extra_ref.shape[0] - 4
    gain = jnp.concatenate([extra_out_ref[z, at : at + 1, :] for z in range(slabs)], axis=1)
    tokens = x_ref.shape[0]
    for start in range(0, tokens, TB):
        values = x_ref[start : start + TB].astype(F32)
        scale = lax.rsqrt(jnp.mean(values * values, axis=-1, keepdims=True) + EPS)
        aone_ref[start : start + TB] = (values * scale * gain).astype(BF16)

    def forward(k):
        slab_copy(k).wait_recv()
        share(lax.rem(slab + slabs - k - 1, slabs))

    loop(slabs - 1, forward)

    def relay(k):
        at = lax.rem(slab + slabs - k, slabs)
        for j in range(1, experts):
            plane_copy(j, at).wait_recv()
            core_copy(j, at).start()

    loop(slabs, relay)
    loop(slabs - 1, lambda k: slab_copy(k).wait_send())

    def arrive(at):
        for j in range(experts):
            core_copy(j, at).wait()
        for j in range(1, experts):
            plane_copy(j, at).wait_send()

    loop(slabs, arrive)
    keep = pltpu.make_async_copy(out_ref, shared_ref, shared_sem)
    keep.start()

    width = 2 * half
    wholes = [
        jnp.concatenate(
            [out_ref[which, side].reshape(width, half) for side in range(2)], axis=1
        )
        for which in range(3)
    ]
    copies = []
    for block in range(tokens // TB):
        span = slice(block * TB, (block + 1) * TB)
        cos, sin = cos_ref[core, span], sin_ref[core, span]
        for which in range(3):
            product = dot(aone_ref[span], wholes[which])
            for pair in range(width // LANES):
                chunk = product[:, pair * LANES : (pair + 1) * LANES]
                if which < 2:
                    chunk = chunk * cos + swap_halves(chunk) * sin
                if which == 0:
                    chunk = chunk * HEAD_DIM ** (-0.5)
                side, place_in = pair // (half // LANES), pair % (half // LANES)
                stage_ref[side, which, span, place_in * LANES : (place_in + 1) * LANES] = (
                    chunk.astype(BF16)
                )
        copies.append(
            pltpu.make_async_copy(
                stage_ref.at[core, :, span], qkv_ref.at[core, :, span], own_sems.at[block]
            )
        )
        copies.append(
            remote(
                stage_ref.at[1 - core, :, span],
                qkv_ref.at[core, :, span],
                qkv_sems,
                (block,),
                {"context": 1 - core},
            )
        )
        for copy in copies[-2:]:
            copy.start()
    for copy in copies:
        copy.wait()
    keep.wait()


def spread(
    experts, slabs, cap, w_query, w_key, w_value, w_out, extra, routes, ranks, segs, x, cos, sin
):
    tokens = routes.shape[0]
    tiles = 2 * tokens // TQ
    rows, width = w_query.shape
    half = width // 2
    vmem = pl.BlockSpec(memory_space=pltpu.VMEM)
    anywhere = pl.BlockSpec(memory_space=pl.ANY)
    dma = pltpu.SemaphoreType.DMA
    return pl.pallas_call(
        functools.partial(spread_kernel, cap),
        in_specs=[vmem] * 11,
        out_specs=[anywhere]
        + [vmem] * 4
        + [pl.BlockSpec(memory_space=pltpu.SMEM), anywhere, vmem],
        out_shape=(
            jax.ShapeDtypeStruct((4, 2, slabs, rows, half), BF16),
            jax.ShapeDtypeStruct((slabs,) + extra.shape, F32),
            jax.ShapeDtypeStruct((tokens, LANES), jnp.int32),
            jax.ShapeDtypeStruct((8, tokens), F32),
            jax.ShapeDtypeStruct((tiles, 1, TQ), jnp.int32),
            jax.ShapeDtypeStruct((tiles,), jnp.int32),
            jax.ShapeDtypeStruct((2, 3, tokens, half), BF16),
            jax.ShapeDtypeStruct((tokens, width), BF16),
        ),
        scratch_shapes=[
            pltpu.VMEM((4, 2, slabs, rows, half), BF16),
            pltpu.VMEM((2, 1, tokens), jnp.int32),
            pltpu.VMEM((2, 3, tokens, half), BF16),
            dma((2, slabs - 1)),
            dma((2, experts - 1, slabs)),
            dma((2, experts, slabs)),
            dma((2, slabs - 1)),
            dma((2, 1)),
            dma,
            dma((tokens // TB,)),
            dma((2, tokens // TB)),
        ],
        compiler_params=pltpu.CompilerParams(
            collective_id=1, has_side_effects=True, vmem_limit_bytes=48 * MIB
        ),
        cost_estimate=cost(1e6, 16 * width * width),
        name="spread",
    )(w_query, w_key, w_value, w_out, extra, routes, ranks, segs, x, cos, sin)


def head_masks():
    lane = iota((TQ, LANES), 1)
    low = jnp.where(lane < HEAD_DIM, 1.0, 0.0).astype(BF16)
    return low, (1.0 - low.astype(F32)).astype(BF16)


def spans(tile, first, body):
    for count in range(1, WIN // TQ + 2):

        @pl.when(tile - first + 1 == count)
        def _():
            body(count)


def allowed(low, start, count):
    sub = iota((TQ, TQ), 0)
    marks = [sub >= low - (start + t * TQ) for t in range(count)]
    marks[-1] = marks[-1] & (sub <= iota((TQ, TQ), 1))
    return marks


def masked(scores, marks):
    return [
        jnp.where(mark, scores[t * TQ : (t + 1) * TQ], MASKED) for t, mark in enumerate(marks)
    ]


def attend_kernel(first_ref, q_ref, k_ref, v_ref, lo_ref, o_ref, lse_ref, keys_ref, vt_ref):
    rows = q_ref.shape[2]
    per = rows // TQ
    masks = head_masks()
    for side in range(2):
        at = slice(side * rows, (side + 1) * rows)
        keys_ref[at, :] = k_ref[side, 0]
        turned = v_ref[side, 0].T
        for head in range(2):
            vt_ref[head, :HEAD_DIM, at] = turned[head * HEAD_DIM : (head + 1) * HEAD_DIM]
            vt_ref[head, HEAD_DIM:, at] = jnp.ones((16, rows), BF16)

    def q_step(qi, carry):
        at = pl.ds(pl.multiple_of(lax.rem(qi, per) * TQ, TQ), TQ)
        query = q_ref[qi // per, 0, at, :]
        low = lo_ref[qi]

        def run(count):
            start = pl.multiple_of((qi - count + 1) * TQ, TQ)
            span = pl.ds(start, count * TQ)
            keys = keys_ref[span, :]
            marks = allowed(low, start, count)
            outs = []
            for head in range(2):
                scores = masked(dot_nt(keys, query * masks[head]), marks)
                peak = functools.reduce(
                    jnp.maximum, [jnp.max(part, axis=0, keepdims=True) for part in scores]
                )
                probs = jnp.concatenate(
                    [jnp.exp(part - peak).astype(BF16) for part in scores], axis=0
                )
                mixed = dot(vt_ref[head, :, span], probs)
                total = mixed[HEAD_DIM : HEAD_DIM + 1]
                outs.append(mixed[:HEAD_DIM] / total)
                lse_ref[0, qi, head : head + 1, :] = peak + jnp.log(total)
            o_ref[qi // per, at, :] = jnp.concatenate(outs, axis=0).T.astype(BF16)

        spans(qi, first_ref[qi], run)
        return carry

    lax.fori_loop(0, 2 * per, q_step, 0)


def part_spec(which, rows):
    return pl.BlockSpec((2, 1, rows, LANES), lambda p, first, which=which: (0, which, 0, p))


def attend(first, qkv, low):
    _, _, rows, half = qkv.shape
    pairs = half // LANES
    tiles = 2 * rows // TQ
    return pl.pallas_call(
        attend_kernel,
        grid_spec=pltpu.PrefetchScalarGridSpec(
            num_scalar_prefetch=1,
            grid=(pairs,),
            in_specs=[
                part_spec(0, rows),
                part_spec(1, rows),
                part_spec(2, rows),
                pl.BlockSpec((tiles, 1, TQ), lambda p, first: (0, 0, 0)),
            ],
            out_specs=[
                pl.BlockSpec((2, rows, LANES), lambda p, first: (0, 0, p)),
                pl.BlockSpec((1, tiles, 8, TQ), lambda p, first: (p, 0, 0, 0)),
            ],
            scratch_shapes=[
                pltpu.VMEM((2 * rows, LANES), BF16),
                pltpu.VMEM((2, HEAD_DIM + 16, 2 * rows), BF16),
            ],
        ),
        out_shape=(
            jax.ShapeDtypeStruct((2, rows, half), BF16),
            jax.ShapeDtypeStruct((pairs, tiles, 8, TQ), F32),
        ),
        compiler_params=params(40),
        cost_estimate=cost(40e9, 16 * rows * half, 12e6),
        name="attend",
    )(first, qkv, qkv, qkv, low)


def attend_back_kernel(
    first_ref,
    q_ref,
    k_ref,
    v_ref,
    do_ref,
    o_ref,
    lse_ref,
    lo_ref,
    cos_ref,
    sin_ref,
    g_ref,
    keys_ref,
    values_ref,
    kt_ref,
    delta_ref,
    dk_ref,
    dv_ref,
):
    rows = q_ref.shape[2]
    per = rows // TQ
    masks = head_masks()
    for side in range(2):
        at = slice(side * rows, (side + 1) * rows)
        keys_ref[at, :] = k_ref[side, 0]
        values_ref[at, :] = v_ref[side, 0]
        kt_ref[:, at] = k_ref[side, 0].T
    dk_ref[...] = jnp.zeros_like(dk_ref)
    dv_ref[...] = jnp.zeros_like(dv_ref)

    def prepare(tile, carry):
        at = pl.ds(pl.multiple_of(lax.rem(tile, per) * TQ, TQ), TQ)
        both = o_ref[tile // per, at, :].astype(F32) * do_ref[tile // per, at, :].astype(F32)
        both = both.T
        delta_ref[tile, 0:1, :] = jnp.sum(both[:HEAD_DIM], axis=0, keepdims=True)
        delta_ref[tile, 1:2, :] = jnp.sum(both[HEAD_DIM:], axis=0, keepdims=True)
        return carry

    lax.fori_loop(0, 2 * per, prepare, 0)

    def q_step(qi, carry):
        at = pl.ds(pl.multiple_of(lax.rem(qi, per) * TQ, TQ), TQ)
        query = q_ref[qi // per, 0, at, :]
        grad = do_ref[qi // per, at, :]
        low = lo_ref[qi]

        def run(count):
            start = pl.multiple_of((qi - count + 1) * TQ, TQ)
            span = pl.ds(start, count * TQ)
            keys, values = keys_ref[span, :], values_ref[span, :]
            marks = allowed(low, start, count)
            queries = [query * mask for mask in masks]
            grads = [grad * mask for mask in masks]
            all_probs, all_scores, sums = [], [], []
            for h in range(2):
                lse = lse_ref[0, qi, h : h + 1, :]
                delta = delta_ref[qi, h : h + 1, :]
                scores = masked(dot_nt(keys, queries[h]), marks)
                grad_probs = dot_nt(values, grads[h])
                probs = [jnp.exp(part - lse) for part in scores]
                grad_scores = [
                    (part * (grad_probs[t * TQ : (t + 1) * TQ] - delta)).astype(BF16)
                    for t, part in enumerate(probs)
                ]
                all_probs.append(jnp.concatenate([part.astype(BF16) for part in probs], axis=0))
                all_scores.append(jnp.concatenate(grad_scores, axis=0))
                sums.append(dot(kt_ref[h * HEAD_DIM : (h + 1) * HEAD_DIM, span], all_scores[h]))
            dv_ref[span, :] += dot(
                jnp.concatenate(all_probs, axis=1), jnp.concatenate(grads, axis=0)
            )
            dk_ref[span, :] += dot(
                jnp.concatenate(all_scores, axis=1), jnp.concatenate(queries, axis=0)
            )
            grad_query = jnp.concatenate(sums, axis=0).T * HEAD_DIM ** (-0.5)
            cos, sin = cos_ref[qi // per, at, :], sin_ref[qi // per, at, :]
            g_ref[qi // per, 0, at, :] = (
                grad_query * cos - swap_halves(grad_query) * sin
            ).astype(BF16)

        spans(qi, first_ref[qi], run)
        return carry

    lax.fori_loop(0, 2 * per, q_step, 0)

    def finish(tile, carry):
        at = pl.ds(pl.multiple_of(lax.rem(tile, per) * TQ, TQ), TQ)
        span = pl.ds(pl.multiple_of(tile * TQ, TQ), TQ)
        cos, sin = cos_ref[tile // per, at, :], sin_ref[tile // per, at, :]
        grad_key = dk_ref[span, :]
        g_ref[tile // per, 1, at, :] = (grad_key * cos - swap_halves(grad_key) * sin).astype(BF16)
        g_ref[tile // per, 2, at, :] = dv_ref[span, :].astype(BF16)
        return carry

    lax.fori_loop(0, 2 * per, finish, 0)


def attend_back(first, qkv, grad_o, o, lse, low, cos, sin):
    _, _, rows, half = qkv.shape
    pairs = half // LANES
    tiles = 2 * rows // TQ
    side = pl.BlockSpec((2, rows, LANES), lambda p, first: (0, 0, p))
    table = pl.BlockSpec((2, rows, LANES), lambda p, first: (0, 0, 0))
    return pl.pallas_call(
        attend_back_kernel,
        grid_spec=pltpu.PrefetchScalarGridSpec(
            num_scalar_prefetch=1,
            grid=(pairs,),
            in_specs=[
                part_spec(0, rows),
                part_spec(1, rows),
                part_spec(2, rows),
                side,
                side,
                pl.BlockSpec((1, tiles, 8, TQ), lambda p, first: (p, 0, 0, 0)),
                pl.BlockSpec((tiles, 1, TQ), lambda p, first: (0, 0, 0)),
                table,
                table,
            ],
            out_specs=pl.BlockSpec((2, 3, rows, LANES), lambda p, first: (0, 0, 0, p)),
            scratch_shapes=[
                pltpu.VMEM((2 * rows, LANES), BF16),
                pltpu.VMEM((2 * rows, LANES), BF16),
                pltpu.VMEM((LANES, 2 * rows), BF16),
                pltpu.VMEM((tiles, 8, TQ), F32),
                pltpu.VMEM((2 * rows, LANES), F32),
                pltpu.VMEM((2 * rows, LANES), F32),
            ],
        ),
        out_shape=jax.ShapeDtypeStruct((2, 3, rows, half), BF16),
        compiler_params=params(48),
        cost_estimate=cost(100e9, 32 * rows * half, 12e6),
        name="attend_back",
    )(first, qkv, qkv, qkv, grad_o, o, lse, low, cos, sin)


def middle_kernel(
    total, x_ref, o_ref, w_ref, extra_ref, prev_ref, res_ref, routes_ref, hres_ref, atwo_ref, stat_ref
):
    attended = jnp.concatenate([o_ref[0], o_ref[1]], axis=1)
    hres = x_ref[...].astype(F32) + dot(
        attended, jnp.concatenate([w_ref[0, 0], w_ref[0, 1]], axis=1)
    )
    hres_ref[...] = hres
    scale = lax.rsqrt(jnp.mean(hres * hres, axis=-1, keepdims=True) + EPS)
    extra = extra_ref[...]
    gain = extra[GAIN_TWO : GAIN_TWO + 1].astype(F32)
    atwo = (hres * scale * gain).astype(BF16)
    atwo_ref[...] = atwo
    logits = dot_nt(atwo, extra)
    for j in range(total):
        logits = logits + prev_ref[:, j : j + 1] * res_ref[j : j + 1, :]
    lane = iota(logits.shape, 1)

    def soft(inside):
        peak = jnp.max(jnp.where(inside, logits, -jnp.inf), axis=1, keepdims=True)
        powers = jnp.where(inside, jnp.exp(jnp.where(inside, logits - peak, 0.0)), 0.0)
        return powers / jnp.sum(powers, axis=1, keepdims=True)

    probs = soft(lane < total)
    stat = probs
    for j in range(2):
        start = total + 2 * j
        stat = stat + soft((lane >= start) & (lane < start + 2))
    stat = jnp.where(lane == total + 4, scale, stat)
    for k in range(2):
        gate = jnp.sum(
            jnp.where(lane == routes_ref[:, k : k + 1], probs, 0.0), axis=1, keepdims=True
        )
        stat = jnp.where(lane == total + 5 + k, gate, stat)
    stat_ref[...] = stat


def middle(total, x, o, w_shared, extra, prev, res, routes):
    rows, width = x.shape
    token = lambda i: (i, 0)
    whole = lambda i: (0, 0)
    return pl.pallas_call(
        functools.partial(middle_kernel, total),
        grid=(rows // TB,),
        in_specs=[
            pl.BlockSpec((TB, width), token),
            pl.BlockSpec((2, TB, width // 2), lambda i: (0, i, 0)),
            pl.BlockSpec((1, 2, width, width // 2), lambda i: (3, 0, 0, 0)),
            pl.BlockSpec((LANES, width), whole),
            pl.BlockSpec((TB, total), token),
            pl.BlockSpec((total, LANES), whole),
            pl.BlockSpec((TB, 2), token),
        ],
        out_specs=[
            pl.BlockSpec((TB, width), token),
            pl.BlockSpec((TB, width), token),
            pl.BlockSpec((TB, LANES), token),
        ],
        out_shape=(
            jax.ShapeDtypeStruct((rows, width), F32),
            jax.ShapeDtypeStruct((rows, width), BF16),
            jax.ShapeDtypeStruct((rows, LANES), F32),
        ),
        compiler_params=params(40),
        cost_estimate=cost(2 * rows * width * width, 2 * width * width + 10 * rows * width),
        name="middle",
    )(x, o, w_shared, extra, prev, res, routes)


def expert_kernel(
    total,
    flat_ref,
    atwo_ref,
    dy_ref,
    stat_ref,
    wide_ref,
    wd_ref,
    flow_ref,
    drow_ref,
    gw_ref,
    send_x,
    send_g,
    all_x,
    all_g,
    acc_ref,
    z_ref,
    a_ref,
    b_ref,
    turned_ref,
    turned_g,
    kept_ref,
    wide_buf,
    down_buf,
    wide_given,
    wide_taken,
    down_given,
    down_taken,
    x_sems,
    g_sems,
    flow_sems,
    drow_sems,
    local_sems,
    weight_sems,
    wide_sems,
    down_sems,
):
    experts, cap, width = all_x.shape
    slots = experts * cap
    chunks = z_ref.shape[0]
    per = chunks // 2
    half = width // 2
    slabs, rows_out = gw_ref.shape[:2]
    deep = chunks * FC // slabs
    tokens = atwo_ref.shape[0]
    me, core = lax.axis_index("expert"), lax.axis_index("context")

    def weights(step):
        chunk, slot = lax.rem(step, chunks), lax.rem(step, 2)
        gate_at = pl.ds(pl.multiple_of(lax.rem(chunk, per) * FC, FC), FC)
        up_at = pl.ds(pl.multiple_of((per + lax.rem(chunk, per)) * FC, FC), FC)
        rows = pl.ds(pl.multiple_of(chunk * FC, FC), FC)
        return (
            pltpu.make_async_copy(
                wide_ref.at[chunk // per, :, gate_at], wide_buf.at[slot, 0], weight_sems.at[slot, 0]
            ),
            pltpu.make_async_copy(
                wide_ref.at[chunk // per, :, up_at], wide_buf.at[slot, 1], weight_sems.at[slot, 1]
            ),
            pltpu.make_async_copy(
                wd_ref.at[0, rows, :], down_buf.at[slot, 0], weight_sems.at[slot, 2]
            ),
            pltpu.make_async_copy(
                wd_ref.at[1, rows, :], down_buf.at[slot, 1], weight_sems.at[slot, 3]
            ),
        )

    def next_weights(step):
        @pl.when(step + 1 < 3 * chunks)
        def _():
            for copy in weights(step + 1):
                copy.start()

        for copy in weights(step):
            copy.wait()

    for copy in weights(0):
        copy.start()
    greet_all(("context", "expert"))

    def hots(target):
        slot = (iota((cap, tokens), 0) + target * cap).astype(F32)
        return flat_ref[0:1, :] == slot, flat_ref[1:2, :] == slot

    order = list(range(1, experts)) + [0]
    x_copies, g_copies = {}, {}
    for j in order:
        target = lax.rem(me + j, experts)
        first, second = hots(target)
        rows = dot(jnp.where(first | second, 1.0, 0.0).astype(BF16), atwo_ref[...]).astype(BF16)
        if j == 0:
            all_x[0] = rows
        else:
            send_x[j - 1] = rows
            x_copies[j] = remote(
                send_x.at[j - 1], all_x.at[j], x_sems, (j - 1,), {"expert": target}
            )
            x_copies[j].start()
    gates = stat_ref[...].T
    for j in order:
        target = lax.rem(me + j, experts)
        first, second = hots(target)
        gate = jnp.sum(
            jnp.where(first, gates[total + 5 : total + 6], 0.0)
            + jnp.where(second, gates[total + 6 : total + 7], 0.0),
            axis=1,
            keepdims=True,
        )
        rows = dot(jnp.where(first | second, 1.0, 0.0).astype(BF16), dy_ref[...])
        rows = (rows * gate).astype(BF16)
        if j == 0:
            all_g[0] = rows
        else:
            send_g[j - 1] = rows
            g_copies[j] = remote(
                send_g.at[j - 1], all_g.at[j], g_sems, (j - 1,), {"expert": target}
            )
            g_copies[j].start()

    def back(buffer, dest, sems, j):
        return remote(
            buffer.at[j - 1],
            dest.at[me],
            sems,
            (j - 1,),
            {"expert": lax.rem(me + experts - j, experts)},
        )

    acc_ref[...] = jnp.zeros_like(acc_ref)

    def up(first, last, at):
        span = slice(first * cap, last * cap)

        def one(step, carry):
            next_weights(step + at * chunks)
            slot = lax.rem(step + at * chunks, 2)
            rows = all_x[first:last].reshape((last - first) * cap, width)
            gate = dot(rows, wide_buf[slot, 0])
            lift = dot(rows, wide_buf[slot, 1])
            sig = 1.0 / (1.0 + jnp.exp(-gate))
            swish = gate * sig
            hidden = (swish * lift).astype(BF16)
            z_ref[step, span] = hidden
            a_ref[step, span] = (lift * sig * (1.0 + gate * (1.0 - sig))).astype(BF16)
            b_ref[step, span] = swish.astype(BF16)
            acc_ref[span, :] += dot(
                hidden, jnp.concatenate([down_buf[slot, 0], down_buf[slot, 1]], axis=1)
            )
            return carry

        lax.fori_loop(0, chunks, one, 0)

    up(0, 1, 0)
    for j in range(1, experts):
        x_copies[j].wait()
    up(1, experts, 1)
    own = [
        pltpu.make_async_copy(all_own, dest.at[me], local_sems.at[i])
        for i, (all_own, dest) in enumerate(
            ((send_x.at[experts - 1], flow_ref), (send_g.at[experts - 1], drow_ref))
        )
    ]
    for j in range(1, experts):
        send_x[j - 1] = acc_ref[j * cap : (j + 1) * cap, :].astype(BF16)
        back(send_x, flow_ref, flow_sems, j).start()
    send_x[experts - 1] = acc_ref[:cap, :].astype(BF16)
    own[0].start()
    turned_ref[...] = all_x[...].reshape(slots, width).T
    acc_ref[...] = jnp.zeros_like(acc_ref)
    for j in range(1, experts):
        g_copies[j].wait()
    turned_g[...] = all_g[...].reshape(slots, width).T

    def down(step, carry):
        next_weights(step + 2 * chunks)
        slot = lax.rem(step + 2 * chunks, 2)
        whole = jnp.concatenate([down_buf[slot, 0], down_buf[slot, 1]], axis=1)
        dz = dot_nt(all_g[...].reshape(slots, width), whole)
        dg = (dz * a_ref[step].astype(F32)).astype(BF16)
        du = (dz * b_ref[step].astype(F32)).astype(BF16)
        a_ref[step] = dg
        b_ref[step] = du
        acc_ref[...] += dot_nt(dg, wide_buf[slot, 0]) + dot_nt(du, wide_buf[slot, 1])
        return carry

    lax.fori_loop(0, chunks, down, 0)
    for j in range(1, experts):
        send_g[j - 1] = acc_ref[j * cap : (j + 1) * cap, :].astype(BF16)
        back(send_g, drow_ref, drow_sems, j).start()
    send_g[experts - 1] = acc_ref[:cap, :].astype(BF16)
    own[1].start()

    def wide_copy(step):
        return remote(
            wide_given.at[step],
            wide_taken.at[step],
            wide_sems,
            (step,),
            {"context": 1 - core},
        )

    def down_copy(step):
        chunk = lax.rem((1 - core) * per + step, chunks)
        return remote(
            down_given.at[step],
            down_taken.at[chunk],
            down_sems,
            (chunk,),
            {"context": 1 - core},
        )

    def products(step):
        chunk = lax.rem((1 - core) * per + step, chunks)
        gate = dot(turned_ref[...], a_ref[chunk])
        lift = dot(turned_ref[...], b_ref[chunk])
        low = dot(turned_g[...], z_ref[chunk])
        top, bottom = low[:half], low[half:]
        down_given[step] = jnp.where(core == 0, bottom, top).astype(BF16)
        kept_ref[chunk] = jnp.where(core == 0, top, bottom).astype(BF16)
        down_copy(step).start()
        return gate, lift

    def give(step, carry):
        gate, lift = products(step)
        wide_given[step, 0] = gate.astype(BF16)
        wide_given[step, 1] = lift.astype(BF16)
        wide_copy(step).start()
        return carry

    lax.fori_loop(0, per, give, 0)

    def keep(step, carry):
        gate, lift = products(step)
        wide_copy(step - per).wait_recv()
        for i, value in enumerate((gate, lift)):
            at = pl.ds(pl.multiple_of((i * per + step - per) * FC, FC), FC)
            value = value + wide_taken[step - per, i].astype(F32)
            gw_ref[:, :, at] = value.reshape(slabs, rows_out, FC).astype(BF16)
        return carry

    lax.fori_loop(per, chunks, keep, 0)

    def settle(step, carry):
        other = lax.rem(core * per + step, chunks)
        copy = remote(
            down_given.at[step],
            down_taken.at[other],
            down_sems,
            (other,),
            {"context": 1 - core},
        )
        copy.wait_recv()
        value = kept_ref[other].astype(F32) + down_taken[other].astype(F32)
        for b in range(half // rows_out):
            part = value[b * rows_out : (b + 1) * rows_out]
            start = 2 * per * FC + b * deep
            if FC <= deep:
                inside = lax.rem(other, deep // FC) * FC
                at = pl.ds(pl.multiple_of(start + inside, FC), FC)
                gw_ref[other // (deep // FC), :, at] = part.astype(BF16)
            else:
                for i in range(FC // deep):
                    gw_ref[other * (FC // deep) + i, :, start : start + deep] = part[
                        :, i * deep : (i + 1) * deep
                    ].astype(BF16)
        return carry

    lax.fori_loop(0, chunks, settle, 0)

    for copy in own:
        copy.wait()
    for j in range(1, experts):
        back(send_x, flow_ref, flow_sems, j).wait()
        back(send_g, drow_ref, drow_sems, j).wait()

    def sent(step, carry):
        down_copy(step).wait_send()
        return carry

    lax.fori_loop(0, chunks, sent, 0)
    lax.fori_loop(0, per, lambda step, carry: (wide_copy(step).wait_send(), carry)[1], 0)


def run_experts(total, experts, slabs, cap, flat_t, atwo, dy, stat, wide, wd):
    rows, width = atwo.shape
    hidden = wd.shape[1]
    chunks = hidden // FC
    per = chunks // 2
    half = width // 2
    slots = experts * cap
    vmem = pl.BlockSpec(memory_space=pltpu.VMEM)
    anywhere = pl.BlockSpec(memory_space=pl.ANY)
    dma = pltpu.SemaphoreType.DMA
    return pl.pallas_call(
        functools.partial(expert_kernel, total),
        in_specs=[vmem] * 4 + [anywhere] * 2,
        out_specs=[anywhere] * 2 + [vmem],
        out_shape=(
            jax.ShapeDtypeStruct((experts, cap, width), BF16),
            jax.ShapeDtypeStruct((experts, cap, width), BF16),
            jax.ShapeDtypeStruct((slabs, width // slabs, 3 * hidden // 2), BF16),
        ),
        scratch_shapes=[
            pltpu.VMEM((experts, cap, width), BF16),
            pltpu.VMEM((experts, cap, width), BF16),
            pltpu.VMEM((experts, cap, width), BF16),
            pltpu.VMEM((experts, cap, width), BF16),
            pltpu.VMEM((slots, width), F32),
            pltpu.VMEM((chunks, slots, FC), BF16),
            pltpu.VMEM((chunks, slots, FC), BF16),
            pltpu.VMEM((chunks, slots, FC), BF16),
            pltpu.VMEM((width, slots), BF16),
            pltpu.VMEM((width, slots), BF16),
            pltpu.VMEM((chunks, half, FC), BF16),
            pltpu.VMEM((2, 2, width, FC), BF16),
            pltpu.VMEM((2, 2, FC, half), BF16),
            pltpu.VMEM((per, 2, width, FC), BF16),
            pltpu.VMEM((per, 2, width, FC), BF16),
            pltpu.VMEM((chunks, half, FC), BF16),
            pltpu.VMEM((chunks, half, FC), BF16),
            dma((2, experts - 1)),
            dma((2, experts - 1)),
            dma((2, experts - 1)),
            dma((2, experts - 1)),
            dma((2,)),
            dma((2, 4)),
            dma((2, per)),
            dma((2, chunks)),
        ],
        compiler_params=pltpu.CompilerParams(
            collective_id=2, has_side_effects=True, vmem_limit_bytes=62 * MIB
        ),
        cost_estimate=cost(18 * slots * width * hidden, 30 * width * hidden),
        name="experts",
    )(flat_t, atwo, dy, stat, wide, wd)


def combine_kernel(
    experts,
    total,
    flow_ref,
    drow_ref,
    flat_ref,
    stat_ref,
    flat_t_ref,
    hres_ref,
    atwo_ref,
    dy_ref,
    o_ref,
    extra_ref,
    w_ref,
    prev_ref,
    out_ref,
    dh_ref,
    dolow_ref,
    gw_ref,
    small_ref,
    right_ref,
    picked_ref,
    summed_ref,
    sums_ref,
    columns_ref,
    dhlow_ref,
):
    step = pl.program_id(0)
    slots, width = flow_ref.shape
    half = width // 2
    gain = extra_ref[GAIN_TWO : GAIN_TWO + 1].astype(F32)
    vecs = [extra_ref[VECS + j : VECS + j + 1].astype(F32) for j in range(2)]

    @pl.when(step == 0)
    def _():
        right_ref[:slots] = drow_ref[...]
        right_ref[slots:] = extra_ref[...]

    spread_out = iota((TB, slots), 1)
    hots = [
        jnp.where(flat_ref[:, k : k + 1] == spread_out, 1.0, 0.0).astype(BF16) for k in range(2)
    ]
    for k in range(2):
        picked_ref[k] = dot(hots[k], flow_ref[...])
    vec_dot = dot_nt(dy_ref[...], extra_ref[...])
    lane = iota((RC, LANES), 1)
    for start in range(0, TB, RC):
        at = slice(start, start + RC)
        dy = dy_ref[at].astype(F32)
        ntwo = hres_ref[at] * stat_ref[at, total + 4 : total + 5] * gain
        sums = vec_dot[at]
        for i, part in enumerate((ntwo, picked_ref[0, at], picked_ref[1, at])):
            sums = jnp.where(lane == i, jnp.sum(dy * part, axis=1, keepdims=True), sums)
        sums_ref[at] = sums

    sums, stats = sums_ref[...].T, stat_ref[...].T
    row = lambda i: stats[i : i + 1]
    dot_normed, dot_picked = sums[0:1], [sums[1:2], sums[2:3]]
    dot_vecs = [sums[VECS + j : VECS + j + 1] for j in range(2)]
    gates = [row(total + 5 + k) for k in range(2)]
    mixes = [[row(total + 2 * j + i) for i in range(2)] for j in range(2)]
    routes = [flat_t_ref[2 + k : 3 + k] for k in range(2)]
    copies = [jnp.where(route == experts + 1, 1.0, 0.0) for route in routes]
    consts = [
        [jnp.where(route == experts + 2 + j, 1.0, 0.0) for j in range(2)] for route in routes
    ]
    pulls = [mixes[j][0] * dot_normed + mixes[j][1] * dot_vecs[j] for j in range(2)]
    sub = iota((total, TB), 0).astype(F32)
    dpgate = jnp.zeros((total, TB), F32)
    for k in range(2):
        dgate = dot_picked[k] + copies[k] * dot_normed
        dgate = dgate + consts[k][0] * pulls[0] + consts[k][1] * pulls[1]
        dpgate = dpgate + jnp.where(sub == routes[k], dgate, 0.0)
    pgate = stats[:total]
    dlogit = pgate * (dpgate - jnp.sum(pgate * dpgate, axis=0, keepdims=True))
    weight = gates[0] * copies[0] + gates[1] * copies[1]
    dmix, shares, pieces = [], [], []
    for j in range(2):
        const = gates[0] * consts[0][j] + gates[1] * consts[1][j]
        grads = [const * dot_normed, const * dot_vecs[j]]
        inner = mixes[j][0] * grads[0] + mixes[j][1] * grads[1]
        dmix += [mixes[j][i] * (grads[i] - inner) for i in range(2)]
        weight = weight + const * mixes[j][0]
        share = const * mixes[j][1]
        shares.append(share)
        for i in range(3):
            pieces.append(share.astype(BF16).astype(F32))
            share = share - pieces[-1]
    empty = jnp.zeros((1, TB), F32)
    droute_t = jnp.concatenate([dlogit] + dmix + [empty] * (12 - total), axis=0).astype(BF16)
    rows = jnp.concatenate(
        [dlogit] + dmix + [weight] + shares + [jnp.zeros((LANES - total - 7, TB), F32)], axis=0
    )
    columns_ref[...] = rows.T
    for start in range(0, TB, RC):
        at = slice(start, start + RC)
        hres = hres_ref[at]
        ntwo = hres * stat_ref[at, total + 4 : total + 5] * gain
        out = hres + columns_ref[at, total + 4 : total + 5] * ntwo
        for k in range(2):
            out = out + stat_ref[at, total + 5 + k : total + 6 + k] * picked_ref[k, at]
        for j in range(2):
            out = out + columns_ref[at, total + 5 + j : total + 6 + j] * vecs[j]
        out_ref[at] = out.astype(BF16)

    lane = iota((TB, LANES), 1)
    droute = jnp.where(lane < total + 4, columns_ref[...], 0.0).astype(BF16)
    summed_ref[...] = dot(
        jnp.concatenate([hots[0] + hots[1], droute], axis=1), right_ref[...]
    )
    gain_row = jnp.zeros((1, width), F32)
    for start in range(0, TB, RC):
        at = slice(start, start + RC)
        hres = hres_ref[at]
        dy = dy_ref[at].astype(F32)
        scale = stat_ref[at, total + 4 : total + 5]
        dntwo = columns_ref[at, total + 4 : total + 5] * dy + summed_ref[at]
        both = hres * dntwo
        inner = jnp.sum(both * gain, axis=1, keepdims=True) * (1.0 / width)
        dh = dy + dntwo * gain * scale - hres * (scale * scale * scale * inner)
        gain_row = gain_row + jnp.sum(both * scale, axis=0, keepdims=True)
        dh_ref[at] = dh
        dhlow_ref[pl.ds(pl.multiple_of(step * TB + start, RC), RC), :] = dh.astype(BF16)
    w_out = jnp.concatenate([w_ref[0, 0], w_ref[0, 1]], axis=1)
    dolow = dot_nt(dhlow_ref[pl.ds(pl.multiple_of(step * TB, TB), TB), :], w_out).astype(BF16)
    dolow_ref[0] = dolow[:, :half]
    dolow_ref[1] = dolow[:, half:]
    route_rows = dot(droute_t, atwo_ref[...])
    vec_parts = dot(
        jnp.concatenate(pieces + [empty] * 2, axis=0).astype(BF16), dy_ref[...]
    )
    vec_rows = [
        vec_parts[3 * j : 3 * j + 1] + vec_parts[3 * j + 1 : 3 * j + 2] + vec_parts[3 * j + 2 : 3 * j + 3]
        for j in range(2)
    ]
    res_rows = jnp.dot(dlogit, prev_ref[...], precision=HIGH, preferred_element_type=F32)
    res_rows = jnp.concatenate([res_rows, jnp.zeros((total, width - total), F32)], axis=1)
    small = jnp.concatenate(
        [route_rows[: total + 4], gain_row] + vec_rows + [jnp.zeros((1, width), F32), res_rows],
        axis=0,
    )

    @pl.when(step == 0)
    def _():
        small_ref[...] = small

    @pl.when(step > 0)
    def _():
        small_ref[...] += small

    @pl.when(step == pl.num_programs(0) - 1)
    def _():
        for side in range(2):
            weight = dot(o_ref[side].T, dhlow_ref[...]).astype(BF16)
            at = slice(side * half, (side + 1) * half)
            gw_ref[0, at] = weight[:, :half]
            gw_ref[1, at] = weight[:, half:]


def combine(experts, total, flow, drow, flat, stat, flat_t, hres, atwo, dy, o, w_shared, extra, prev):
    rows, width = hres.shape
    slots = flow.shape[0]
    half = width // 2
    token = lambda i: (i, 0)
    whole = lambda i: (0, 0)
    side = pl.BlockSpec((2, TB, half), lambda i: (0, i, 0))
    weight = pl.BlockSpec((2, width, half), lambda i: (0, 0, 0))
    small_rows = 2 * total + 8
    return pl.pallas_call(
        functools.partial(combine_kernel, experts, total),
        grid=(rows // TB,),
        in_specs=[
            pl.BlockSpec((slots, width), whole),
            pl.BlockSpec((slots, width), whole),
            pl.BlockSpec((TB, LANES), token),
            pl.BlockSpec((TB, LANES), token),
            pl.BlockSpec((8, TB), lambda i: (0, i)),
            pl.BlockSpec((TB, width), token),
            pl.BlockSpec((TB, width), token),
            pl.BlockSpec((TB, width), token),
            pl.BlockSpec((2, rows, half), lambda i: (0, 0, 0)),
            pl.BlockSpec((LANES, width), whole),
            pl.BlockSpec((1, 2, width, half), lambda i: (3, 0, 0, 0)),
            pl.BlockSpec((TB, total), token),
        ],
        out_specs=[
            pl.BlockSpec((TB, width), token),
            pl.BlockSpec((TB, width), token),
            side,
            weight,
            pl.BlockSpec((small_rows, width), whole),
        ],
        out_shape=(
            jax.ShapeDtypeStruct((rows, width), BF16),
            jax.ShapeDtypeStruct((rows, width), F32),
            jax.ShapeDtypeStruct((2, rows, half), BF16),
            jax.ShapeDtypeStruct((2, width, half), BF16),
            jax.ShapeDtypeStruct((small_rows, width), F32),
        ),
        scratch_shapes=[
            pltpu.VMEM((slots + LANES, width), BF16),
            pltpu.VMEM((2, TB, width), F32),
            pltpu.VMEM((TB, width), F32),
            pltpu.VMEM((TB, LANES), F32),
            pltpu.VMEM((TB, LANES), F32),
            pltpu.VMEM((rows, width), BF16),
        ],
        compiler_params=params(56),
        cost_estimate=cost(
            6 * rows * slots * width + 4 * rows * width * width, 30 * rows * width + 8 * width * width
        ),
        name="combine",
    )(flow, drow, flat, stat, flat_t, hres, atwo, dy, o, extra, w_shared, prev)


def tail_kernel(
    gain_at,
    sent_ref,
    aone_ref,
    w_ref,
    extra_ref,
    x_ref,
    dh_ref,
    gwo_ref,
    small_ref,
    out_ref,
    final,
    small_out_ref,
    both,
    grads,
    w_buf,
    x_buf,
    dh_buf,
    out_buf,
    core_in,
    plane_out,
    plane_in,
    slab_out,
    slab_in,
    own_ref,
    small_own,
    small_core,
    small_plane,
    small_slab,
    load_sems,
    store_sems,
    both_sems,
    core_sems,
    plane_sems,
    slab_sems,
    final_sems,
    pass_sems,
    small_core_sems,
    small_plane_sems,
    small_slab_sems,
):
    experts = lax.axis_size("expert")
    slabs = lax.axis_size("dp")
    me, core, slab = lax.axis_index("expert"), lax.axis_index("context"), lax.axis_index("dp")
    other = 1 - core
    tokens, width = x_buf.shape
    half = width // 2
    parts = 2
    block = tokens // parts

    mine = pltpu.make_async_copy(sent_ref.at[core], both.at[core], load_sems.at[0])
    mine.start()
    loads = [
        pltpu.make_async_copy(w_ref.at[pl.ds(0, 3)], w_buf, load_sems.at[1]),
        pltpu.make_async_copy(x_ref, x_buf, load_sems.at[2]),
        pltpu.make_async_copy(dh_ref, dh_buf, load_sems.at[3]),
    ]
    for copy in loads:
        copy.start()
    greet_all(("context", "expert", "dp"))
    theirs = [
        remote(
            sent_ref.at[other, which],
            both.at[core, which],
            both_sems,
            (which,),
            {"context": other},
        )
        for which in range(3)
    ]
    for copy in theirs:
        copy.start()

    def core_copy(which):
        return remote(
            grads.at[other, which], core_in.at[which], core_sems, (which,), {"context": other}
        )

    for side in range(2):
        grads[side, 3] = gwo_ref[side]
    core_copy(3).start()

    def plane_copy(j, at):
        return remote(
            plane_out.at[j - 1, at],
            plane_in.at[j - 1, at],
            plane_sems,
            (j - 1, at),
            {"expert": lax.rem(me + j, experts)},
        )

    def pass_on(which):
        core_copy(which).wait_recv()
        j = lax.rem(which + experts - me, experts)

        @pl.when(j != 0)
        def _():
            def one(k):
                at = lax.rem(slab + k + 1, slabs)
                plane_out[j - 1, at] = (
                    grads[core, which, at].astype(F32) + core_in[which, at].astype(F32)
                ).astype(BF16)
                plane_copy(j, at).start()

            loop(slabs, one)

    mine.wait()
    turned = aone_ref[...].T
    for which in range(3):
        theirs[which].wait_recv()
        grad = jnp.concatenate([both[0, which], both[1, which]], axis=1)
        weight = dot(turned, grad)
        for side in range(2):
            grads[side, which] = (
                weight[:, side * half : (side + 1) * half]
                .reshape(slabs, width // slabs, half)
                .astype(BF16)
            )
        core_copy(which).start()
        pass_on((which + 3) % 4)
    for copy in loads:
        copy.wait()

    gain = extra_ref[GAIN_ONE : GAIN_ONE + 1].astype(F32)
    stores = []
    gain_row = jnp.zeros((1, width), F32)
    for part in range(parts):
        at = slice(part * block, (part + 1) * block)
        dnone = None
        for which in range(3):
            grad = jnp.concatenate([both[0, which, at], both[1, which, at]], axis=1)
            whole = jnp.concatenate([w_buf[which, 0], w_buf[which, 1]], axis=1)
            product = dot_nt(grad, whole)
            dnone = product if dnone is None else dnone + product
        values = x_buf[at].astype(F32)
        scale = lax.rsqrt(jnp.mean(values * values, axis=-1, keepdims=True) + EPS)
        scaled = dnone * gain
        inner = jnp.mean(values * scaled, axis=1, keepdims=True)
        out_buf[at] = dh_buf[at] + scale * scaled - values * (scale * scale * scale * inner)
        stores.append(
            pltpu.make_async_copy(out_buf.at[at], out_ref.at[at], store_sems.at[part])
        )
        stores[-1].start()
        gain_row = gain_row + jnp.sum(dnone * values * scale, axis=0, keepdims=True)
        if part == 0:
            pass_on(2)

    row = iota(small_ref.shape, 0)
    small_own[...] = small_ref[...] + jnp.where(row == gain_at, gain_row, 0.0)
    small_copy = remote(small_own, small_core, small_core_sems, (0,), {"context": other})
    small_copy.start()
    small_copy.wait()
    small_plane[me] = small_own[...] + small_core[...]
    small_plane_copies = []
    for j in range(1, experts):
        small_plane_copies.append(
            remote(
                small_plane.at[me],
                small_plane.at[me],
                small_plane_sems,
                (j,),
                {"expert": lax.rem(me + j, experts)},
            )
        )
        small_plane_copies[-1].start()

    def gathered(at):
        value = grads[core, me, at].astype(F32) + core_in[me, at].astype(F32)
        for j in range(1, experts):
            plane_copy(j, at).wait_recv()
            value = value + plane_in[j - 1, at].astype(F32)
        return value

    def slab_copy(k):
        return remote(
            slab_out.at[k],
            slab_in.at[k],
            slab_sems,
            (k,),
            {"dp": lax.rem(slab + k + 1, slabs)},
        )

    def scatter(k):
        slab_out[k] = gathered(lax.rem(slab + k + 1, slabs)).astype(BF16)
        slab_copy(k).start()

    loop(slabs - 1, scatter)

    for copy in small_plane_copies:
        copy.wait()
    value = small_plane[0]
    for j in range(1, experts):
        value = value + small_plane[j]
    small_slab[slab] = value

    def small_slab_copy(k):
        return remote(
            small_slab.at[slab],
            small_slab.at[slab],
            small_slab_sems,
            (k,),
            {"dp": lax.rem(slab + k + 1, slabs)},
        )

    loop(slabs - 1, lambda k: small_slab_copy(k).start())

    own_ref[...] = gathered(slab)

    def collect(k):
        slab_copy(k).wait_recv()
        own_ref[...] += slab_in[k].astype(F32)

    loop(slabs - 1, collect)
    final[core, me] = own_ref[...].astype(BF16)
    final_copies, pass_copies = [], []
    for j in range(1, experts):
        final_copies.append(
            remote(
                final.at[core, me],
                final.at[core, me],
                final_sems,
                (j,),
                {"expert": lax.rem(me + j, experts)},
            )
        )
        final_copies[-1].start()
    for j in range(experts):
        source = lax.rem(me + experts - j, experts)
        if j > 0:
            final_copies[j - 1].wait_recv()
        pass_copies.append(
            remote(
                final.at[core, source],
                final.at[core, source],
                pass_sems,
                (j,),
                {"context": other},
            )
        )
        pass_copies[-1].start()

    loop(slabs - 1, lambda k: small_slab_copy(k).wait())
    small_out_ref[...] = small_slab[0]

    def add_small(k):
        small_out_ref[...] += small_slab[k + 1]

    loop(slabs - 1, add_small)

    for copy in pass_copies:
        copy.wait_recv()
    for copy in stores:
        copy.wait()
    for which in range(4):
        core_copy(which).wait_send()
    for j in range(1, experts):

        def sent(k, j=j):
            plane_copy(j, k).wait_send()

        loop(slabs, sent)
    loop(slabs - 1, lambda k: slab_copy(k).wait_send())
    for copy in theirs + final_copies + pass_copies:
        copy.wait_send()


def tail(experts, slabs, gain_at, sent, aone, w_shared, extra, x, dh, gwo, small):
    tokens, width = x.shape
    half = width // 2
    rows = width // slabs
    vmem = pl.BlockSpec(memory_space=pltpu.VMEM)
    anywhere = pl.BlockSpec(memory_space=pl.ANY)
    dma = pltpu.SemaphoreType.DMA
    return pl.pallas_call(
        functools.partial(tail_kernel, gain_at),
        in_specs=[anywhere, vmem, anywhere, vmem, anywhere, anywhere] + [vmem] * 2,
        out_specs=[anywhere] + [vmem] * 2,
        out_shape=(
            jax.ShapeDtypeStruct((tokens, width), F32),
            jax.ShapeDtypeStruct((2, experts, rows, half), BF16),
            jax.ShapeDtypeStruct(small.shape, F32),
        ),
        scratch_shapes=[
            pltpu.VMEM((2, 3, tokens, half), BF16),
            pltpu.VMEM((2, 4, slabs, rows, half), BF16),
            pltpu.VMEM((3, 2, width, half), BF16),
            pltpu.VMEM((tokens, width), BF16),
            pltpu.VMEM((tokens, width), F32),
            pltpu.VMEM((tokens, width), F32),
            pltpu.VMEM((4, slabs, rows, half), BF16),
            pltpu.VMEM((experts - 1, slabs, rows, half), BF16),
            pltpu.VMEM((experts - 1, slabs, rows, half), BF16),
            pltpu.VMEM((slabs - 1, rows, half), BF16),
            pltpu.VMEM((slabs - 1, rows, half), BF16),
            pltpu.VMEM((rows, half), F32),
            pltpu.VMEM(small.shape, F32),
            pltpu.VMEM(small.shape, F32),
            pltpu.VMEM((experts,) + small.shape, F32),
            pltpu.VMEM((slabs,) + small.shape, F32),
            dma((4,)),
            dma((2,)),
            dma((2, 3)),
            dma((2, 4)),
            dma((2, experts - 1, slabs)),
            dma((2, slabs - 1)),
            dma((2, experts)),
            dma((2, experts)),
            dma((2, 1)),
            dma((2, experts)),
            dma((2, slabs - 1)),
        ],
        compiler_params=pltpu.CompilerParams(
            collective_id=0, has_side_effects=True, vmem_limit_bytes=60 * MIB
        ),
        cost_estimate=cost(12 * tokens * width * width, 40 * tokens * width),
        name="tail",
    )(sent, aone, w_shared, extra, x, dh, gwo, small)


def finish_kernel(
    total,
    place_ref,
    final_ref,
    small_ref,
    mine_ref,
    theirs_ref,
    tokens_ref,
    q_ref,
    k_ref,
    v_ref,
    o_ref,
    norm_one_ref,
    norm_two_ref,
    router_ref,
    mix_ref,
    vec_ref,
    res_ref,
    gate_ref,
    up_ref,
    gd_ref,
    tokens_out_ref,
    turned_ref,
    copy_sem,
):
    through = pltpu.make_async_copy(tokens_ref, tokens_out_ref, copy_sem)
    through.start()
    rows, half = final_ref.shape[2:]
    wide = mine_ref.shape[1] // 3
    core = place_ref[1]
    deep = gd_ref.shape[1]
    for which, ref in enumerate((q_ref, k_ref, v_ref, o_ref)):
        for side in range(2):
            ref[:, side * half : (side + 1) * half] = final_ref[side, which].astype(F32)
    def share(ref, side):
        at = slice(side * wide, (side + 1) * wide)
        gate_ref[0, :, at] = ref[:, :wide].astype(F32)
        up_ref[0, :, at] = ref[:, wide : 2 * wide].astype(F32)
        blocks = [
            ref[:, 2 * wide + b * deep : 2 * wide + (b + 1) * deep].astype(F32)
            for b in range(half // rows)
        ]
        gd_ref[0, :, side * half : (side + 1) * half] = jnp.concatenate(blocks, axis=0).T

    for side in range(2):

        @pl.when(core == side)
        def _():
            share(mine_ref, side)
            share(theirs_ref, 1 - side)

    small = small_ref[...]
    fill = jnp.zeros((LANES - small.shape[0], small.shape[1]), F32)
    turned_ref[...] = jnp.concatenate([small, fill], axis=0).T
    own = turned_ref[pl.ds(pl.multiple_of(place_ref[0] * rows, 8), rows), :]
    router_ref[...] = own[:, :total]
    mix_ref[...] = own[:, total : total + 4]
    norm_two_ref[...] = own[:, total + 4 : total + 5]
    vec_ref[...] = own[:, total + 5 : total + 7]
    norm_one_ref[...] = own[:, total + 7 : total + 8]
    res_ref[...] = turned_ref[:total, total + 8 : 2 * total + 8]
    through.wait()


def finish(total, place, final, small, mine, theirs, tokens):
    rows, half = final.shape[2:]
    width = 2 * half
    anywhere = pl.BlockSpec(memory_space=pl.ANY)
    vmem = pl.BlockSpec(memory_space=pltpu.VMEM)
    shape = lambda *dims: jax.ShapeDtypeStruct(dims, F32)
    return pl.pallas_call(
        functools.partial(finish_kernel, total),
        in_specs=[pl.BlockSpec(memory_space=pltpu.SMEM)] + [vmem] * 4 + [anywhere],
        out_specs=[vmem] * 13 + [anywhere],
        out_shape=(
            shape(rows, width),
            shape(rows, width),
            shape(rows, width),
            shape(rows, width),
            shape(rows, 1),
            shape(rows, 1),
            shape(rows, total),
            shape(rows, 4),
            shape(rows, 2),
            shape(total, total),
            shape(1, rows, 2 * mine.shape[1] // 3),
            shape(1, rows, 2 * mine.shape[1] // 3),
            shape(1, mine.shape[1] // 3 * rows // half, width),
            shape(*tokens.shape),
        ),
        scratch_shapes=[pltpu.VMEM((width, LANES), F32), pltpu.SemaphoreType.DMA],
        compiler_params=params(40),
        cost_estimate=cost(1e6, 20 * rows * width),
        name="finish",
    )(place, final, small, mine, theirs, tokens)


def swap_cores(value):
    return lax.all_to_all(value, "context", split_axis=0, concat_axis=0, tiled=True)


def on_device(
    tokens,
    segments,
    routes,
    prev_logits,
    ranks,
    cotangent,
    norm_one,
    w_query,
    w_key,
    w_value,
    w_out,
    norm_two,
    router,
    w_res,
    const_mix,
    const_vec,
    w_gate,
    w_up,
    w_down,
):
    experts = lax.axis_size("expert")
    dp = lax.axis_size("dp")
    total = experts + NZ
    _, rows, width = tokens.shape
    hidden = w_gate.shape[2]
    cap = (18 * rows + 8 * total - 1) // (8 * total)
    seq = 2 * rows
    core = lax.axis_index("context")
    half = width // 2

    def mine(shard, size):
        return lax.dynamic_slice_in_dim(shard, core * size, size, 1)

    def gather(shard):
        return lax.all_gather(shard, ("context", "dp"), axis=0).reshape(
            2, dp * shard.shape[0], shard.shape[1]
        )

    extra = jnp.concatenate(
        [router, const_mix, norm_one[:, None], norm_two[:, None], const_vec], axis=1
    )
    cos, sin = (jnp.asarray(table).reshape(2, rows, LANES) for table in rope_tables(seq))
    x = tokens[0]
    dy = cotangent[0]
    w_shared, extra, flat, flat_t, low, first, qkv, aone = spread(
        experts,
        dp,
        cap,
        w_query,
        w_key,
        w_value,
        w_out,
        extra.astype(F32).T,
        routes[0],
        ranks[0],
        segments,
        x,
        cos,
        sin,
    )
    w_shared = w_shared.reshape(4, 2, width, half)
    extra = extra.transpose(1, 0, 2).reshape(total + 8, width).astype(BF16)
    extra = jnp.concatenate(
        [
            extra[: total + 4],
            jnp.zeros((GAIN_ONE - total - 4, width), BF16),
            extra[total + 4 :],
            jnp.zeros((LANES - GAIN_ONE - 4, width), BF16),
        ],
        axis=0,
    )
    wide_w = gather(
        jnp.concatenate([mine(w_gate[0], hidden // 2), mine(w_up[0], hidden // 2)], axis=1)
    )
    down_w = gather(mine(w_down[0], half))

    res = jnp.pad(w_res.astype(F32), ((0, 0), (0, LANES - total)))

    o_heads, lse = attend(first, qkv, low)
    o = swap_cores(o_heads)
    hres, atwo, stat = middle(total, x, o, w_shared, extra, prev_logits[0], res, routes[0])
    flow_back, drow_back, grad_wide = run_experts(
        total, experts, dp, cap, flat_t, atwo, dy, stat, wide_w, down_w
    )
    flow_back = flow_back.reshape(experts * cap, width)
    drow_back = drow_back.reshape(experts * cap, width)
    wide = lax.psum_scatter(
        grad_wide.reshape(width, 3 * hidden // 2), "dp", scatter_dimension=0, tiled=True
    )

    output, dh, dolow, grad_out_w, small = combine(
        experts,
        total,
        flow_back,
        drow_back,
        flat,
        stat,
        flat_t,
        hres,
        atwo,
        dy,
        o,
        w_shared,
        extra,
        prev_logits[0],
    )
    grad_o = swap_cores(dolow)
    grads_sent = attend_back(
        first,
        qkv,
        grad_o,
        o_heads,
        lse,
        low,
        cos,
        sin,
    )
    grad_tokens, final, small = tail(
        experts,
        dp,
        total + 7,
        grads_sent,
        aone,
        w_shared,
        extra,
        x,
        dh,
        grad_out_w.reshape(2, dp, width // dp, half),
        small,
    )
    wide, small = lax.optimization_barrier((wide, small))
    wide_other = lax.ppermute(wide, "context", [(0, 1), (1, 0)])
    (
        grad_query,
        grad_key,
        grad_value,
        grad_out,
        grad_norm_one,
        grad_norm_two,
        grad_router,
        grad_mix,
        grad_vec,
        grad_res,
        grad_gate,
        grad_up,
        grad_down,
        grad_tokens,
    ) = finish(
        total,
        jnp.stack([lax.axis_index("dp"), core]),
        final,
        small,
        wide,
        wide_other,
        grad_tokens,
    )
    return (
        output[None],
        grad_tokens[None],
        grad_norm_one[:, 0],
        grad_query,
        grad_key,
        grad_value,
        grad_out,
        grad_norm_two[:, 0],
        grad_router,
        grad_res,
        grad_mix,
        grad_vec,
        grad_gate,
        grad_up,
        grad_down,
    )


def solution(mesh):
    token = P(("expert", "dp"), "context", None)
    rows = P("dp", None)
    expert = P("expert", "dp", None)
    in_specs = (
        token,
        P(("expert", "dp"), "context"),
        token,
        token,
        token,
        token,
        P("dp"),
        rows,
        rows,
        rows,
        rows,
        P("dp"),
        rows,
        P(),
        rows,
        rows,
        expert,
        expert,
        expert,
    )
    out_specs = (
        token,
        token,
        P("dp"),
        rows,
        rows,
        rows,
        rows,
        P("dp"),
        rows,
        P(),
        rows,
        rows,
        expert,
        expert,
        expert,
    )
    return jax.shard_map(
        on_device, mesh=mesh, in_specs=in_specs, out_specs=out_specs, check_vma=False
    )
```

```python
import functools

import jax
import jax.numpy as jnp
import numpy as np
from jax import lax
from jax.experimental import pallas as pl
from jax.experimental.pallas import tpu as pltpu
from jax.sharding import PartitionSpec as P

HEADS = 12
HEAD_DIM = 64
WIN = 1024
NZ = 4
SEGMENTS = 5
GAIN_ONE, GAIN_TWO, VECS = 112, 113, 114
TQ = 256
TB = 256
RC = 64
FC = 512
LANES = 128
EPS = 1e-05
MASKED = -1000000000.0
HIGH = lax.Precision.HIGHEST
F32 = jnp.float32
BF16 = jnp.bfloat16
MIB = 1024 * 1024


def params(mib):
    return pltpu.CompilerParams(vmem_limit_bytes=mib * MIB)


def cost(flops, nbytes, trans=0):
    return pl.CostEstimate(flops=int(flops), bytes_accessed=int(nbytes), transcendentals=int(trans))


def dot(left, right):
    return jnp.dot(left, right, preferred_element_type=F32)


def dot_nt(left, right):
    return lax.dot_general(left, right, (((1,), (1,)), ((), ())), preferred_element_type=F32)


def dot_tn(left, right):
    return lax.dot_general(left, right, (((0,), (0,)), ((), ())), preferred_element_type=F32)


def iota(shape, axis):
    return lax.broadcasted_iota(jnp.int32, shape, axis)


def rope_tables(seq):
    half = HEAD_DIM // 2
    frequency = np.float32(10000.0) ** (
        -np.arange(half, dtype=np.float32) * np.float32(2.0) / np.float32(HEAD_DIM)
    )
    angles = np.arange(seq, dtype=np.float32)[:, None] * frequency.astype(np.float32)[None, :]
    cos = np.cos(angles.astype(np.float64)).astype(np.float32)
    sin = np.sin(angles.astype(np.float64)).astype(np.float32)
    return np.concatenate([cos] * 4, axis=1), np.concatenate([-sin, sin, -sin, sin], axis=1)


def swap_halves(chunk):
    lane = iota(chunk.shape, 1)
    return jnp.where(
        lane % HEAD_DIM < HEAD_DIM // 2, pltpu.roll(chunk, 96, 1), pltpu.roll(chunk, 32, 1)
    )


def loop(count, body):
    if count <= 4:
        for step in range(count):
            body(step)
    else:
        lax.fori_loop(0, count, lambda step, carry: (body(step), carry)[1], 0)


def remote(src, dst, sems, index, where):
    return pltpu.make_async_remote_copy(
        src_ref=src,
        dst_ref=dst,
        send_sem=sems.at[(0,) + index],
        recv_sem=sems.at[(1,) + index],
        device_id=where,
        device_id_type=pl.DeviceIdType.MESH,
    )


def greet_all(axes):
    barrier = pltpu.get_barrier_semaphore()
    total = 0
    for axis in axes:
        size = lax.axis_size(axis)
        me = lax.axis_index(axis)
        total += size - 1

        def greet(k, axis=axis, size=size, me=me):
            pl.semaphore_signal(
                barrier,
                inc=1,
                device_id={axis: lax.rem(me + k + 1, size)},
                device_id_type=pl.DeviceIdType.MESH,
            )

        loop(size - 1, greet)
    pl.semaphore_wait(barrier, total)


def place_pairs(experts, cap, routes_ref, ranks_ref, flat_ref, flat_t_ref):
    rows = routes_ref.shape[0]
    lane = iota((rows, LANES), 1)
    first, second = routes_ref[:, 0:1], routes_ref[:, 1:2]
    hot_first, hot_second = first == lane, second == lane
    hot = (hot_first.astype(F32) + hot_second.astype(F32)).astype(BF16)
    ranks = ranks_ref[...].astype(F32)
    ranks_col = jnp.broadcast_to(ranks, (LANES, rows)).T[:, 0:1]
    earlier = jnp.where(ranks < ranks_col, 1.0, 0.0).astype(BF16)
    counts = dot(earlier, hot)

    def flat(hit, route):
        slot = jnp.sum(jnp.where(hit, counts, 0.0), axis=1, keepdims=True).astype(jnp.int32)
        return jnp.where((route < experts) & (slot < cap), route * cap + slot, experts * cap)

    columns = (flat(hot_first, first), flat(hot_second, second), first, second)
    out = jnp.zeros((rows, LANES), jnp.int32)
    for i, column in enumerate(columns):
        out = jnp.where(lane == i, column, out)
    flat_ref[...] = out
    flat_t_ref[...] = out.astype(F32).T[:8]


def find_starts(segs_ref, low_ref, first_ref):
    rows = segs_ref.shape[2]
    per = rows // TQ
    segs = [segs_ref[side].astype(F32) for side in range(2)]
    starts = [jnp.zeros((1, rows), F32) for side in range(2)]
    for number in range(1, SEGMENTS):
        before = sum(
            jnp.sum(jnp.where(part < number, 1.0, 0.0), axis=1, keepdims=True) for part in segs
        )
        starts = [
            jnp.where(part == number, before, start) for part, start in zip(segs, starts)
        ]
    for side in range(2):
        place = (iota((1, rows), 1) + (side * rows - WIN + 1)).astype(F32)
        low = jnp.maximum(starts[side], place)
        for tile in range(per):
            part = low[:, tile * TQ : (tile + 1) * TQ]
            low_ref[side * per + tile] = part.astype(jnp.int32)
            first_ref[side * per + tile] = jnp.min(part).astype(jnp.int32) // TQ


def spread_kernel(
    cap,
    w_query_ref,
    w_key_ref,
    w_value_ref,
    w_out_ref,
    extra_ref,
    routes_ref,
    ranks_ref,
    segs_ref,
    x_ref,
    cos_ref,
    sin_ref,
    shared_ref,
    extra_out_ref,
    flat_ref,
    flat_t_ref,
    low_ref,
    first_ref,
    qkv_ref,
    aone_ref,
    out_ref,
    segs_all,
    stage_ref,
    slab_sems,
    plane_sems,
    core_sems,
    extra_sems,
    segs_sems,
    shared_sem,
    own_sems,
    qkv_sems,
):
    experts = lax.axis_size("expert")
    slabs = lax.axis_size("dp")
    me, core, slab = lax.axis_index("expert"), lax.axis_index("context"), lax.axis_index("dp")
    half = out_ref.shape[4]
    for which, ref in enumerate((w_query_ref, w_key_ref, w_value_ref, w_out_ref)):
        for side in range(2):

            @pl.when((me == which) & (core == side))
            def _():
                out_ref[which, side, slab] = ref[:, side * half : (side + 1) * half]

    extra_out_ref[slab] = extra_ref[...]
    segs_all[core] = segs_ref[...]
    greet_all(("context", "expert", "dp"))

    def slab_copy(k):
        piece = out_ref.at[me, core, slab]
        return remote(piece, piece, slab_sems, (k,), {"dp": lax.rem(slab + k + 1, slabs)})

    def extra_copy(k):
        piece = extra_out_ref.at[slab]
        return remote(piece, piece, extra_sems, (k,), {"dp": lax.rem(slab + k + 1, slabs)})

    def plane_copy(j, at):
        piece = out_ref.at[me, core, at]
        return remote(
            piece, piece, plane_sems, (j - 1, at), {"expert": lax.rem(me + j, experts)}
        )

    def core_copy(j, at):
        piece = out_ref.at[lax.rem(me + experts - j, experts), core, at]
        return remote(piece, piece, core_sems, (j, at), {"context": 1 - core})

    def share(at):
        for j in range(1, experts):
            plane_copy(j, at).start()
        core_copy(0, at).start()

    loop(slabs - 1, lambda k: extra_copy(k).start())
    loop(slabs - 1, lambda k: slab_copy(k).start())
    share(slab)
    segs_copy = remote(
        segs_all.at[core], segs_all.at[core], segs_sems, (0,), {"context": 1 - core}
    )
    segs_copy.start()
    place_pairs(experts, cap, routes_ref, ranks_ref, flat_ref, flat_t_ref)
    segs_copy.wait()
    find_starts(segs_all, low_ref, first_ref)
    loop(slabs - 1, lambda k: extra_copy(k).wait())
    at = extra_ref.shape[0] - 4
    gain = jnp.concatenate([extra_out_ref[z, at : at + 1, :] for z in range(slabs)], axis=1)
    tokens = x_ref.shape[0]
    for start in range(0, tokens, TB):
        values = x_ref[start : start + TB].astype(F32)
        scale = lax.rsqrt(jnp.mean(values * values, axis=-1, keepdims=True) + EPS)
        aone_ref[start : start + TB] = (values * scale * gain).astype(BF16)

    def forward(k):
        slab_copy(k).wait_recv()
        share(lax.rem(slab + slabs - k - 1, slabs))

    loop(slabs - 1, forward)

    def relay(k):
        at = lax.rem(slab + slabs - k, slabs)
        for j in range(1, experts):
            plane_copy(j, at).wait_recv()
            core_copy(j, at).start()

    loop(slabs, relay)
    loop(slabs - 1, lambda k: slab_copy(k).wait_send())

    def arrive(at):
        for j in range(experts):
            core_copy(j, at).wait()
        for j in range(1, experts):
            plane_copy(j, at).wait_send()

    loop(slabs, arrive)
    keep = pltpu.make_async_copy(out_ref, shared_ref, shared_sem)
    keep.start()

    width = 2 * half
    wholes = [
        jnp.concatenate(
            [out_ref[which, side].reshape(width, half) for side in range(2)], axis=1
        )
        for which in range(3)
    ]
    copies = []
    for block in range(tokens // TB):
        span = slice(block * TB, (block + 1) * TB)
        cos, sin = cos_ref[core, span], sin_ref[core, span]
        for which in range(3):
            product = dot(aone_ref[span], wholes[which])
            for pair in range(width // LANES):
                chunk = product[:, pair * LANES : (pair + 1) * LANES]
                if which < 2:
                    chunk = chunk * cos + swap_halves(chunk) * sin
                if which == 0:
                    chunk = chunk * HEAD_DIM ** (-0.5)
                side, place_in = pair // (half // LANES), pair % (half // LANES)
                stage_ref[side, which, span, place_in * LANES : (place_in + 1) * LANES] = (
                    chunk.astype(BF16)
                )
        copies.append(
            pltpu.make_async_copy(
                stage_ref.at[core, :, span], qkv_ref.at[core, :, span], own_sems.at[block]
            )
        )
        copies.append(
            remote(
                stage_ref.at[1 - core, :, span],
                qkv_ref.at[core, :, span],
                qkv_sems,
                (block,),
                {"context": 1 - core},
            )
        )
        for copy in copies[-2:]:
            copy.start()
    for copy in copies:
        copy.wait()
    keep.wait()


def spread(
    experts, slabs, cap, w_query, w_key, w_value, w_out, extra, routes, ranks, segs, x, cos, sin
):
    tokens = routes.shape[0]
    tiles = 2 * tokens // TQ
    rows, width = w_query.shape
    half = width // 2
    vmem = pl.BlockSpec(memory_space=pltpu.VMEM)
    anywhere = pl.BlockSpec(memory_space=pl.ANY)
    dma = pltpu.SemaphoreType.DMA
    return pl.pallas_call(
        functools.partial(spread_kernel, cap),
        in_specs=[vmem] * 11,
        out_specs=[anywhere]
        + [vmem] * 4
        + [pl.BlockSpec(memory_space=pltpu.SMEM), anywhere, vmem],
        out_shape=(
            jax.ShapeDtypeStruct((4, 2, slabs, rows, half), BF16),
            jax.ShapeDtypeStruct((slabs,) + extra.shape, F32),
            jax.ShapeDtypeStruct((tokens, LANES), jnp.int32),
            jax.ShapeDtypeStruct((8, tokens), F32),
            jax.ShapeDtypeStruct((tiles, 1, TQ), jnp.int32),
            jax.ShapeDtypeStruct((tiles,), jnp.int32),
            jax.ShapeDtypeStruct((2, 3, tokens, half), BF16),
            jax.ShapeDtypeStruct((tokens, width), BF16),
        ),
        scratch_shapes=[
            pltpu.VMEM((4, 2, slabs, rows, half), BF16),
            pltpu.VMEM((2, 1, tokens), jnp.int32),
            pltpu.VMEM((2, 3, tokens, half), BF16),
            dma((2, slabs - 1)),
            dma((2, experts - 1, slabs)),
            dma((2, experts, slabs)),
            dma((2, slabs - 1)),
            dma((2, 1)),
            dma,
            dma((tokens // TB,)),
            dma((2, tokens // TB)),
        ],
        compiler_params=pltpu.CompilerParams(
            collective_id=1, has_side_effects=True, vmem_limit_bytes=48 * MIB
        ),
        cost_estimate=cost(1e6, 16 * width * width),
        name="spread",
    )(w_query, w_key, w_value, w_out, extra, routes, ranks, segs, x, cos, sin)


def head_masks():
    lane = iota((TQ, LANES), 1)
    low = jnp.where(lane < HEAD_DIM, 1.0, 0.0).astype(BF16)
    return low, (1.0 - low.astype(F32)).astype(BF16)


def spans(tile, first, body):
    for count in range(1, WIN // TQ + 2):

        @pl.when(tile - first + 1 == count)
        def _():
            body(count)


def masked(scores, low, start, count):
    shape = (TQ, 2 * TQ)
    sub, lane = iota(shape, 0), lax.rem(iota(shape, 1), TQ)
    low = jnp.concatenate([low, low], axis=1)
    parts = []
    for t in range(count):
        mark = sub >= low - (start + t * TQ)
        if t == count - 1:
            mark = mark & (sub <= lane)
        parts.append(jnp.where(mark, scores[t * TQ : (t + 1) * TQ], MASKED))
    return parts


def own_blocks(both):
    return jnp.concatenate([both[:HEAD_DIM, :TQ], both[HEAD_DIM:LANES, TQ:]], axis=0)


def attend_kernel(first_ref, q_ref, k_ref, v_ref, lo_ref, o_ref, lse_ref, keys_ref, vt_ref):
    rows = q_ref.shape[2]
    per = rows // TQ
    masks = head_masks()
    for side in range(2):
        at = slice(side * rows, (side + 1) * rows)
        keys_ref[at, :] = k_ref[side, 0]
        vt_ref[:LANES, at] = v_ref[side, 0].T
        vt_ref[LANES:, at] = jnp.ones((16, rows), BF16)

    def q_step(qi, carry):
        at = pl.ds(pl.multiple_of(lax.rem(qi, per) * TQ, TQ), TQ)
        query = q_ref[qi // per, 0, at, :]
        low = lo_ref[qi]

        def run(count):
            start = pl.multiple_of((qi - count + 1) * TQ, TQ)
            span = pl.ds(start, count * TQ)
            both = jnp.concatenate([query * mask for mask in masks], axis=0)
            scores = masked(dot_nt(keys_ref[span, :], both), low, start, count)
            peak = functools.reduce(
                jnp.maximum, [jnp.max(part, axis=0, keepdims=True) for part in scores]
            )
            probs = jnp.concatenate([jnp.exp(part - peak).astype(BF16) for part in scores], axis=0)
            mixed = dot(vt_ref[:, span], probs)
            total = mixed[LANES : LANES + 1]
            lse_ref[0, qi, 0:1, :] = peak + jnp.log(total)
            o_ref[qi // per, at, :] = own_blocks(mixed[:LANES] / total).T.astype(BF16)

        spans(qi, first_ref[qi], run)
        return carry

    lax.fori_loop(0, 2 * per, q_step, 0)


def part_spec(which, rows):
    return pl.BlockSpec((2, 1, rows, LANES), lambda p, first, which=which: (0, which, 0, p))


def attend(first, qkv, low):
    _, _, rows, half = qkv.shape
    pairs = half // LANES
    tiles = 2 * rows // TQ
    return pl.pallas_call(
        attend_kernel,
        grid_spec=pltpu.PrefetchScalarGridSpec(
            num_scalar_prefetch=1,
            grid=(pairs,),
            in_specs=[
                part_spec(0, rows),
                part_spec(1, rows),
                part_spec(2, rows),
                pl.BlockSpec((tiles, 1, TQ), lambda p, first: (0, 0, 0)),
            ],
            out_specs=[
                pl.BlockSpec((2, rows, LANES), lambda p, first: (0, 0, p)),
                pl.BlockSpec((1, tiles, 8, 2 * TQ), lambda p, first: (p, 0, 0, 0)),
            ],
            scratch_shapes=[
                pltpu.VMEM((2 * rows, LANES), BF16),
                pltpu.VMEM((LANES + 16, 2 * rows), BF16),
            ],
        ),
        out_shape=(
            jax.ShapeDtypeStruct((2, rows, half), BF16),
            jax.ShapeDtypeStruct((pairs, tiles, 8, 2 * TQ), F32),
        ),
        compiler_params=params(40),
        cost_estimate=cost(40e9, 16 * rows * half, 12e6),
        name="attend",
    )(first, qkv, qkv, qkv, low)


def attend_back_kernel(
    first_ref,
    q_ref,
    k_ref,
    v_ref,
    do_ref,
    o_ref,
    lse_ref,
    lo_ref,
    cos_ref,
    sin_ref,
    g_ref,
    keys_ref,
    values_ref,
    kt_ref,
    delta_ref,
    dk_ref,
    dv_ref,
):
    rows = q_ref.shape[2]
    per = rows // TQ
    masks = head_masks()
    for side in range(2):
        at = slice(side * rows, (side + 1) * rows)
        keys_ref[at, :] = k_ref[side, 0]
        values_ref[at, :] = v_ref[side, 0]
        kt_ref[:, at] = k_ref[side, 0].T
    dk_ref[...] = jnp.zeros_like(dk_ref)
    dv_ref[...] = jnp.zeros_like(dv_ref)

    def prepare(tile, carry):
        at = pl.ds(pl.multiple_of(lax.rem(tile, per) * TQ, TQ), TQ)
        both = o_ref[tile // per, at, :].astype(F32) * do_ref[tile // per, at, :].astype(F32)
        both = both.T
        delta_ref[tile, 0:1, :TQ] = jnp.sum(both[:HEAD_DIM], axis=0, keepdims=True)
        delta_ref[tile, 0:1, TQ:] = jnp.sum(both[HEAD_DIM:], axis=0, keepdims=True)
        return carry

    lax.fori_loop(0, 2 * per, prepare, 0)

    def q_step(qi, carry):
        at = pl.ds(pl.multiple_of(lax.rem(qi, per) * TQ, TQ), TQ)
        query = q_ref[qi // per, 0, at, :]
        grad = do_ref[qi // per, at, :]
        low = lo_ref[qi]

        def run(count):
            start = pl.multiple_of((qi - count + 1) * TQ, TQ)
            span = pl.ds(start, count * TQ)
            queries = jnp.concatenate([query * mask for mask in masks], axis=0)
            grads = jnp.concatenate([grad * mask for mask in masks], axis=0)
            lse, delta = lse_ref[0, qi, 0:1, :], delta_ref[qi, 0:1, :]
            scores = masked(dot_nt(keys_ref[span, :], queries), low, start, count)
            grad_probs = dot_nt(values_ref[span, :], grads)
            probs = [jnp.exp(part - lse) for part in scores]
            grad_scores = jnp.concatenate(
                [
                    (part * (grad_probs[t * TQ : (t + 1) * TQ] - delta)).astype(BF16)
                    for t, part in enumerate(probs)
                ],
                axis=0,
            )
            probs = jnp.concatenate([part.astype(BF16) for part in probs], axis=0)
            dv_ref[span, :] += dot(probs, grads)
            dk_ref[span, :] += dot(grad_scores, queries)
            turned = own_blocks(dot(kt_ref[:, span], grad_scores))
            grad_query = turned.T * HEAD_DIM ** (-0.5)
            cos, sin = cos_ref[qi // per, at, :], sin_ref[qi // per, at, :]
            g_ref[qi // per, 0, at, :] = (
                grad_query * cos - swap_halves(grad_query) * sin
            ).astype(BF16)

        spans(qi, first_ref[qi], run)
        return carry

    lax.fori_loop(0, 2 * per, q_step, 0)

    def finish(tile, carry):
        at = pl.ds(pl.multiple_of(lax.rem(tile, per) * TQ, TQ), TQ)
        span = pl.ds(pl.multiple_of(tile * TQ, TQ), TQ)
        cos, sin = cos_ref[tile // per, at, :], sin_ref[tile // per, at, :]
        grad_key = dk_ref[span, :]
        g_ref[tile // per, 1, at, :] = (grad_key * cos - swap_halves(grad_key) * sin).astype(BF16)
        g_ref[tile // per, 2, at, :] = dv_ref[span, :].astype(BF16)
        return carry

    lax.fori_loop(0, 2 * per, finish, 0)


def attend_back(first, qkv, grad_o, o, lse, low, cos, sin):
    _, _, rows, half = qkv.shape
    pairs = half // LANES
    tiles = 2 * rows // TQ
    side = pl.BlockSpec((2, rows, LANES), lambda p, first: (0, 0, p))
    table = pl.BlockSpec((2, rows, LANES), lambda p, first: (0, 0, 0))
    return pl.pallas_call(
        attend_back_kernel,
        grid_spec=pltpu.PrefetchScalarGridSpec(
            num_scalar_prefetch=1,
            grid=(pairs,),
            in_specs=[
                part_spec(0, rows),
                part_spec(1, rows),
                part_spec(2, rows),
                side,
                side,
                pl.BlockSpec((1, tiles, 8, 2 * TQ), lambda p, first: (p, 0, 0, 0)),
                pl.BlockSpec((tiles, 1, TQ), lambda p, first: (0, 0, 0)),
                table,
                table,
            ],
            out_specs=pl.BlockSpec((2, 3, rows, LANES), lambda p, first: (0, 0, 0, p)),
            scratch_shapes=[
                pltpu.VMEM((2 * rows, LANES), BF16),
                pltpu.VMEM((2 * rows, LANES), BF16),
                pltpu.VMEM((LANES, 2 * rows), BF16),
                pltpu.VMEM((tiles, 8, 2 * TQ), F32),
                pltpu.VMEM((2 * rows, LANES), F32),
                pltpu.VMEM((2 * rows, LANES), F32),
            ],
        ),
        out_shape=jax.ShapeDtypeStruct((2, 3, rows, half), BF16),
        compiler_params=params(48),
        cost_estimate=cost(100e9, 32 * rows * half, 12e6),
        name="attend_back",
    )(first, qkv, qkv, qkv, grad_o, o, lse, low, cos, sin)


def middle_kernel(
    total, x_ref, o_ref, w_ref, extra_ref, prev_ref, res_ref, routes_ref, hres_ref, atwo_ref, stat_ref
):
    attended = jnp.concatenate([o_ref[0], o_ref[1]], axis=1)
    hres = x_ref[...].astype(F32) + dot(
        attended, jnp.concatenate([w_ref[0, 0], w_ref[0, 1]], axis=1)
    )
    hres_ref[...] = hres
    scale = lax.rsqrt(jnp.mean(hres * hres, axis=-1, keepdims=True) + EPS)
    extra = extra_ref[...]
    gain = extra[GAIN_TWO : GAIN_TWO + 1].astype(F32)
    atwo = (hres * scale * gain).astype(BF16)
    atwo_ref[...] = atwo
    logits = dot_nt(atwo, extra)
    for j in range(total):
        logits = logits + prev_ref[:, j : j + 1] * res_ref[j : j + 1, :]
    lane = iota(logits.shape, 1)

    def soft(inside):
        peak = jnp.max(jnp.where(inside, logits, -jnp.inf), axis=1, keepdims=True)
        powers = jnp.where(inside, jnp.exp(jnp.where(inside, logits - peak, 0.0)), 0.0)
        return powers / jnp.sum(powers, axis=1, keepdims=True)

    probs = soft(lane < total)
    stat = probs
    for j in range(2):
        start = total + 2 * j
        stat = stat + soft((lane >= start) & (lane < start + 2))
    stat = jnp.where(lane == total + 4, scale, stat)
    for k in range(2):
        gate = jnp.sum(
            jnp.where(lane == routes_ref[:, k : k + 1], probs, 0.0), axis=1, keepdims=True
        )
        stat = jnp.where(lane == total + 5 + k, gate, stat)
    stat_ref[...] = stat


def middle(total, x, o, w_shared, extra, prev, res, routes):
    rows, width = x.shape
    token = lambda i: (i, 0)
    whole = lambda i: (0, 0)
    return pl.pallas_call(
        functools.partial(middle_kernel, total),
        grid=(rows // TB,),
        in_specs=[
            pl.BlockSpec((TB, width), token),
            pl.BlockSpec((2, TB, width // 2), lambda i: (0, i, 0)),
            pl.BlockSpec((1, 2, width, width // 2), lambda i: (3, 0, 0, 0)),
            pl.BlockSpec((LANES, width), whole),
            pl.BlockSpec((TB, total), token),
            pl.BlockSpec((total, LANES), whole),
            pl.BlockSpec((TB, 2), token),
        ],
        out_specs=[
            pl.BlockSpec((TB, width), token),
            pl.BlockSpec((TB, width), token),
            pl.BlockSpec((TB, LANES), token),
        ],
        out_shape=(
            jax.ShapeDtypeStruct((rows, width), F32),
            jax.ShapeDtypeStruct((rows, width), BF16),
            jax.ShapeDtypeStruct((rows, LANES), F32),
        ),
        compiler_params=params(40),
        cost_estimate=cost(2 * rows * width * width, 2 * width * width + 10 * rows * width),
        name="middle",
    )(x, o, w_shared, extra, prev, res, routes)


def expert_kernel(
    total,
    flat_ref,
    atwo_ref,
    dy_ref,
    stat_ref,
    wide_ref,
    wd_ref,
    flow_ref,
    drow_ref,
    gw_ref,
    send_x,
    send_g,
    all_x,
    all_g,
    acc_ref,
    z_ref,
    a_ref,
    b_ref,
    turned_ref,
    turned_g,
    kept_ref,
    wide_buf,
    down_buf,
    wide_given,
    wide_taken,
    down_given,
    down_taken,
    x_sems,
    g_sems,
    flow_sems,
    drow_sems,
    local_sems,
    weight_sems,
    wide_sems,
    down_sems,
):
    experts, cap, width = all_x.shape
    slots = experts * cap
    chunks = z_ref.shape[0]
    per = chunks // 2
    half = width // 2
    slabs, rows_out = gw_ref.shape[:2]
    deep = chunks * FC // slabs
    tokens = atwo_ref.shape[0]
    me, core = lax.axis_index("expert"), lax.axis_index("context")

    def down_pieces(chunk):
        if deep == FC:
            rows = pl.ds(pl.multiple_of(chunk * rows_out, rows_out), rows_out)
            return [
                (
                    wd_ref.at[side, rows, 2 * per * FC + b * deep : 2 * per * FC + (b + 1) * deep],
                    side * half + b * rows_out,
                    rows_out,
                )
                for side in range(2)
                for b in range(half // rows_out)
            ]
        at = pl.ds(pl.multiple_of(chunk * FC, FC), FC)
        return [(wd_ref.at[side, :, at], side * half, half) for side in range(2)]

    def weights(step):
        chunk, slot = lax.rem(step, chunks), lax.rem(step, 2)
        gate_at = pl.ds(pl.multiple_of(lax.rem(chunk, per) * FC, FC), FC)
        up_at = pl.ds(pl.multiple_of((per + lax.rem(chunk, per)) * FC, FC), FC)
        return (
            pltpu.make_async_copy(
                wide_ref.at[chunk // per, :, gate_at], wide_buf.at[slot, 0], weight_sems.at[slot, 0]
            ),
            pltpu.make_async_copy(
                wide_ref.at[chunk // per, :, up_at], wide_buf.at[slot, 1], weight_sems.at[slot, 1]
            ),
        ) + tuple(
            pltpu.make_async_copy(
                source, down_buf.at[slot, at : at + size, :], weight_sems.at[slot, 2 + i]
            )
            for i, (source, at, size) in enumerate(down_pieces(chunk))
        )

    def next_weights(step):
        @pl.when(step + 1 < 3 * chunks)
        def _():
            for copy in weights(step + 1):
                copy.start()

        for copy in weights(step):
            copy.wait()

    for copy in weights(0):
        copy.start()
    greet_all(("context", "expert"))

    def hots(target):
        slot = (iota((cap, tokens), 0) + target * cap).astype(F32)
        return flat_ref[0:1, :] == slot, flat_ref[1:2, :] == slot

    order = list(range(1, experts)) + [0]
    x_copies, g_copies = {}, {}
    for j in order:
        target = lax.rem(me + j, experts)
        first, second = hots(target)
        rows = dot(jnp.where(first | second, 1.0, 0.0).astype(BF16), atwo_ref[...]).astype(BF16)
        if j == 0:
            all_x[0] = rows
        else:
            send_x[j - 1] = rows
            x_copies[j] = remote(
                send_x.at[j - 1], all_x.at[j], x_sems, (j - 1,), {"expert": target}
            )
            x_copies[j].start()
    gates = stat_ref[...].T
    for j in order:
        target = lax.rem(me + j, experts)
        first, second = hots(target)
        gate = jnp.sum(
            jnp.where(first, gates[total + 5 : total + 6], 0.0)
            + jnp.where(second, gates[total + 6 : total + 7], 0.0),
            axis=1,
            keepdims=True,
        )
        rows = dot(jnp.where(first | second, 1.0, 0.0).astype(BF16), dy_ref[...])
        rows = (rows * gate).astype(BF16)
        if j == 0:
            all_g[0] = rows
        else:
            send_g[j - 1] = rows
            g_copies[j] = remote(
                send_g.at[j - 1], all_g.at[j], g_sems, (j - 1,), {"expert": target}
            )
            g_copies[j].start()

    def back(buffer, dest, sems, j):
        return remote(
            buffer.at[j - 1],
            dest.at[me],
            sems,
            (j - 1,),
            {"expert": lax.rem(me + experts - j, experts)},
        )

    acc_ref[...] = jnp.zeros_like(acc_ref)

    def up(first, last, at):
        span = slice(first * cap, last * cap)

        def one(step, carry):
            next_weights(step + at * chunks)
            slot = lax.rem(step + at * chunks, 2)
            rows = all_x[first:last].reshape((last - first) * cap, width)
            gate = dot(rows, wide_buf[slot, 0])
            lift = dot(rows, wide_buf[slot, 1])
            sig = 1.0 / (1.0 + jnp.exp(-gate))
            swish = gate * sig
            hidden = (swish * lift).astype(BF16)
            z_ref[step, span] = hidden
            a_ref[step, span] = (lift * sig * (1.0 + gate * (1.0 - sig))).astype(BF16)
            b_ref[step, span] = swish.astype(BF16)
            acc_ref[span, :] += dot_nt(hidden, down_buf[slot])
            return carry

        lax.fori_loop(0, chunks, one, 0)

    up(0, 1, 0)
    for j in range(1, experts):
        x_copies[j].wait()
    up(1, experts, 1)
    own = [
        pltpu.make_async_copy(all_own, dest.at[me], local_sems.at[i])
        for i, (all_own, dest) in enumerate(
            ((send_x.at[experts - 1], flow_ref), (send_g.at[experts - 1], drow_ref))
        )
    ]
    for j in range(1, experts):
        send_x[j - 1] = acc_ref[j * cap : (j + 1) * cap, :].astype(BF16)
        back(send_x, flow_ref, flow_sems, j).start()
    send_x[experts - 1] = acc_ref[:cap, :].astype(BF16)
    own[0].start()
    turned_ref[...] = all_x[...].reshape(slots, width).T
    acc_ref[...] = jnp.zeros_like(acc_ref)
    for j in range(1, experts):
        g_copies[j].wait()
    turned_g[...] = all_g[...].reshape(slots, width).T

    def down(step, carry):
        next_weights(step + 2 * chunks)
        slot = lax.rem(step + 2 * chunks, 2)
        dz = dot(all_g[...].reshape(slots, width), down_buf[slot])
        dg = (dz * a_ref[step].astype(F32)).astype(BF16)
        du = (dz * b_ref[step].astype(F32)).astype(BF16)
        a_ref[step] = dg
        b_ref[step] = du
        acc_ref[...] += dot_nt(dg, wide_buf[slot, 0]) + dot_nt(du, wide_buf[slot, 1])
        return carry

    lax.fori_loop(0, chunks, down, 0)
    for j in range(1, experts):
        send_g[j - 1] = acc_ref[j * cap : (j + 1) * cap, :].astype(BF16)
        back(send_g, drow_ref, drow_sems, j).start()
    send_g[experts - 1] = acc_ref[:cap, :].astype(BF16)
    own[1].start()

    def wide_copy(step):
        return remote(
            wide_given.at[step],
            wide_taken.at[step],
            wide_sems,
            (step,),
            {"context": 1 - core},
        )

    def down_copy(step):
        chunk = lax.rem((1 - core) * per + step, chunks)
        return remote(
            down_given.at[step],
            down_taken.at[chunk],
            down_sems,
            (chunk,),
            {"context": 1 - core},
        )

    def products(step):
        chunk = lax.rem((1 - core) * per + step, chunks)
        gate = dot(turned_ref[...], a_ref[chunk])
        lift = dot(turned_ref[...], b_ref[chunk])
        low = dot(turned_g[...], z_ref[chunk])
        top, bottom = low[:half], low[half:]
        down_given[step] = jnp.where(core == 0, bottom, top).astype(BF16)
        kept_ref[chunk] = jnp.where(core == 0, top, bottom).astype(BF16)
        down_copy(step).start()
        return gate, lift

    def give(step, carry):
        gate, lift = products(step)
        wide_given[step, 0] = gate.astype(BF16)
        wide_given[step, 1] = lift.astype(BF16)
        wide_copy(step).start()
        return carry

    lax.fori_loop(0, per, give, 0)

    def keep(step, carry):
        gate, lift = products(step)
        wide_copy(step - per).wait_recv()
        for i, value in enumerate((gate, lift)):
            at = pl.ds(pl.multiple_of((i * per + step - per) * FC, FC), FC)
            value = value + wide_taken[step - per, i].astype(F32)
            gw_ref[:, :, at] = value.reshape(slabs, rows_out, FC).astype(BF16)
        return carry

    lax.fori_loop(per, chunks, keep, 0)

    def settle(step, carry):
        other = lax.rem(core * per + step, chunks)
        copy = remote(
            down_given.at[step],
            down_taken.at[other],
            down_sems,
            (other,),
            {"context": 1 - core},
        )
        copy.wait_recv()
        value = kept_ref[other].astype(F32) + down_taken[other].astype(F32)
        for b in range(half // rows_out):
            part = value[b * rows_out : (b + 1) * rows_out]
            start = 2 * per * FC + b * deep
            if FC <= deep:
                inside = lax.rem(other, deep // FC) * FC
                at = pl.ds(pl.multiple_of(start + inside, FC), FC)
                gw_ref[other // (deep // FC), :, at] = part.astype(BF16)
            else:
                for i in range(FC // deep):
                    gw_ref[other * (FC // deep) + i, :, start : start + deep] = part[
                        :, i * deep : (i + 1) * deep
                    ].astype(BF16)
        return carry

    lax.fori_loop(0, chunks, settle, 0)

    for copy in own:
        copy.wait()
    for j in range(1, experts):
        back(send_x, flow_ref, flow_sems, j).wait()
        back(send_g, drow_ref, drow_sems, j).wait()

    def sent(step, carry):
        down_copy(step).wait_send()
        return carry

    lax.fori_loop(0, chunks, sent, 0)
    lax.fori_loop(0, per, lambda step, carry: (wide_copy(step).wait_send(), carry)[1], 0)


def run_experts(total, experts, slabs, hidden, cap, flat_t, atwo, dy, stat, wide, wd):
    rows, width = atwo.shape
    chunks = hidden // FC
    per = chunks // 2
    half = width // 2
    slots = experts * cap
    vmem = pl.BlockSpec(memory_space=pltpu.VMEM)
    anywhere = pl.BlockSpec(memory_space=pl.ANY)
    dma = pltpu.SemaphoreType.DMA
    return pl.pallas_call(
        functools.partial(expert_kernel, total),
        in_specs=[vmem] * 4 + [anywhere] * 2,
        out_specs=[anywhere] * 2 + [vmem],
        out_shape=(
            jax.ShapeDtypeStruct((experts, cap, width), BF16),
            jax.ShapeDtypeStruct((experts, cap, width), BF16),
            jax.ShapeDtypeStruct((slabs, width // slabs, 3 * hidden // 2), BF16),
        ),
        scratch_shapes=[
            pltpu.VMEM((experts, cap, width), BF16),
            pltpu.VMEM((experts, cap, width), BF16),
            pltpu.VMEM((experts, cap, width), BF16),
            pltpu.VMEM((experts, cap, width), BF16),
            pltpu.VMEM((slots, width), F32),
            pltpu.VMEM((chunks, slots, FC), BF16),
            pltpu.VMEM((chunks, slots, FC), BF16),
            pltpu.VMEM((chunks, slots, FC), BF16),
            pltpu.VMEM((width, slots), BF16),
            pltpu.VMEM((width, slots), BF16),
            pltpu.VMEM((chunks, half, FC), BF16),
            pltpu.VMEM((2, 2, width, FC), BF16),
            pltpu.VMEM((2, width, FC), BF16),
            pltpu.VMEM((per, 2, width, FC), BF16),
            pltpu.VMEM((per, 2, width, FC), BF16),
            pltpu.VMEM((chunks, half, FC), BF16),
            pltpu.VMEM((chunks, half, FC), BF16),
            dma((2, experts - 1)),
            dma((2, experts - 1)),
            dma((2, experts - 1)),
            dma((2, experts - 1)),
            dma((2,)),
            dma((2, 6)),
            dma((2, per)),
            dma((2, chunks)),
        ],
        compiler_params=pltpu.CompilerParams(
            collective_id=2, has_side_effects=True, vmem_limit_bytes=62 * MIB
        ),
        cost_estimate=cost(18 * slots * width * hidden, 30 * width * hidden),
        name="experts",
    )(flat_t, atwo, dy, stat, wide, wd)


def combine_kernel(
    experts,
    total,
    flow_ref,
    drow_ref,
    flat_ref,
    stat_ref,
    flat_t_ref,
    hres_ref,
    atwo_ref,
    dy_ref,
    o_ref,
    extra_ref,
    w_ref,
    prev_ref,
    out_ref,
    dh_ref,
    dolow_ref,
    gw_ref,
    small_ref,
    right_ref,
    picked_ref,
    summed_ref,
    sums_ref,
    columns_ref,
    dhlow_ref,
    stage_ref,
    own_sems,
    dolow_sems,
):
    step = pl.program_id(0)
    core = lax.axis_index("context")

    @pl.when(step == 0)
    def _():
        greet_all(("context",))

    def dolow_copies(block):
        rows = pl.ds(pl.multiple_of(block * TB, TB), TB)
        return (
            pltpu.make_async_copy(
                stage_ref.at[core, rows], dolow_ref.at[core, rows], own_sems.at[block]
            ),
            remote(
                stage_ref.at[1 - core, rows],
                dolow_ref.at[core, rows],
                dolow_sems,
                (block,),
                {"context": 1 - core},
            ),
        )

    slots, width = flow_ref.shape
    half = width // 2
    gain = extra_ref[GAIN_TWO : GAIN_TWO + 1].astype(F32)
    vecs = [extra_ref[VECS + j : VECS + j + 1].astype(F32) for j in range(2)]

    @pl.when(step == 0)
    def _():
        right_ref[:slots] = drow_ref[...]
        right_ref[slots:] = extra_ref[...]

    spread_out = iota((TB, slots), 1)
    hots = [
        jnp.where(flat_ref[:, k : k + 1] == spread_out, 1.0, 0.0).astype(BF16) for k in range(2)
    ]
    for k in range(2):
        picked_ref[k] = dot(hots[k], flow_ref[...])
    vec_dot = dot_nt(dy_ref[...], extra_ref[...])
    lane = iota((RC, LANES), 1)
    for start in range(0, TB, RC):
        at = slice(start, start + RC)
        dy = dy_ref[at].astype(F32)
        ntwo = hres_ref[at] * stat_ref[at, total + 4 : total + 5] * gain
        sums = vec_dot[at]
        for i, part in enumerate((ntwo, picked_ref[0, at], picked_ref[1, at])):
            sums = jnp.where(lane == i, jnp.sum(dy * part, axis=1, keepdims=True), sums)
        sums_ref[at] = sums

    sums, stats = sums_ref[...].T, stat_ref[...].T
    row = lambda i: stats[i : i + 1]
    dot_normed, dot_picked = sums[0:1], [sums[1:2], sums[2:3]]
    dot_vecs = [sums[VECS + j : VECS + j + 1] for j in range(2)]
    gates = [row(total + 5 + k) for k in range(2)]
    mixes = [[row(total + 2 * j + i) for i in range(2)] for j in range(2)]
    routes = [flat_t_ref[2 + k : 3 + k] for k in range(2)]
    copies = [jnp.where(route == experts + 1, 1.0, 0.0) for route in routes]
    consts = [
        [jnp.where(route == experts + 2 + j, 1.0, 0.0) for j in range(2)] for route in routes
    ]
    pulls = [mixes[j][0] * dot_normed + mixes[j][1] * dot_vecs[j] for j in range(2)]
    sub = iota((total, TB), 0).astype(F32)
    dpgate = jnp.zeros((total, TB), F32)
    for k in range(2):
        dgate = dot_picked[k] + copies[k] * dot_normed
        dgate = dgate + consts[k][0] * pulls[0] + consts[k][1] * pulls[1]
        dpgate = dpgate + jnp.where(sub == routes[k], dgate, 0.0)
    pgate = stats[:total]
    dlogit = pgate * (dpgate - jnp.sum(pgate * dpgate, axis=0, keepdims=True))
    weight = gates[0] * copies[0] + gates[1] * copies[1]
    dmix, shares, pieces = [], [], []
    for j in range(2):
        const = gates[0] * consts[0][j] + gates[1] * consts[1][j]
        grads = [const * dot_normed, const * dot_vecs[j]]
        inner = mixes[j][0] * grads[0] + mixes[j][1] * grads[1]
        dmix += [mixes[j][i] * (grads[i] - inner) for i in range(2)]
        weight = weight + const * mixes[j][0]
        share = const * mixes[j][1]
        shares.append(share)
        for i in range(3):
            pieces.append(share.astype(BF16).astype(F32))
            share = share - pieces[-1]
    empty = jnp.zeros((1, TB), F32)
    droute_t = jnp.concatenate([dlogit] + dmix + [empty] * (12 - total), axis=0).astype(BF16)
    rows = jnp.concatenate(
        [dlogit] + dmix + [weight] + shares + [jnp.zeros((LANES - total - 7, TB), F32)], axis=0
    )
    columns_ref[...] = rows.T
    for start in range(0, TB, RC):
        at = slice(start, start + RC)
        hres = hres_ref[at]
        ntwo = hres * stat_ref[at, total + 4 : total + 5] * gain
        out = hres + columns_ref[at, total + 4 : total + 5] * ntwo
        for k in range(2):
            out = out + stat_ref[at, total + 5 + k : total + 6 + k] * picked_ref[k, at]
        for j in range(2):
            out = out + columns_ref[at, total + 5 + j : total + 6 + j] * vecs[j]
        out_ref[at] = out.astype(BF16)

    lane = iota((TB, LANES), 1)
    droute = jnp.where(lane < total + 4, columns_ref[...], 0.0).astype(BF16)
    summed_ref[...] = dot(
        jnp.concatenate([hots[0] + hots[1], droute], axis=1), right_ref[...]
    )
    gain_row = jnp.zeros((1, width), F32)
    for start in range(0, TB, RC):
        at = slice(start, start + RC)
        hres = hres_ref[at]
        dy = dy_ref[at].astype(F32)
        scale = stat_ref[at, total + 4 : total + 5]
        dntwo = columns_ref[at, total + 4 : total + 5] * dy + summed_ref[at]
        both = hres * dntwo
        inner = jnp.sum(both * gain, axis=1, keepdims=True) * (1.0 / width)
        dh = dy + dntwo * gain * scale - hres * (scale * scale * scale * inner)
        gain_row = gain_row + jnp.sum(both * scale, axis=0, keepdims=True)
        dh_ref[at] = dh
        dhlow_ref[pl.ds(pl.multiple_of(step * TB + start, RC), RC), :] = dh.astype(BF16)
    w_out = jnp.concatenate([w_ref[0, 0], w_ref[0, 1]], axis=1)
    dolow = dot_nt(dhlow_ref[pl.ds(pl.multiple_of(step * TB, TB), TB), :], w_out).astype(BF16)
    rows_at = pl.ds(pl.multiple_of(step * TB, TB), TB)
    stage_ref[0, rows_at] = dolow[:, :half]
    stage_ref[1, rows_at] = dolow[:, half:]
    for copy in dolow_copies(step):
        copy.start()
    route_rows = dot(droute_t, atwo_ref[...])
    vec_parts = dot(
        jnp.concatenate(pieces + [empty] * 2, axis=0).astype(BF16), dy_ref[...]
    )
    vec_rows = [
        vec_parts[3 * j : 3 * j + 1] + vec_parts[3 * j + 1 : 3 * j + 2] + vec_parts[3 * j + 2 : 3 * j + 3]
        for j in range(2)
    ]
    res_rows = jnp.dot(dlogit, prev_ref[...], precision=HIGH, preferred_element_type=F32)
    res_rows = jnp.concatenate([res_rows, jnp.zeros((total, width - total), F32)], axis=1)
    small = jnp.concatenate(
        [route_rows[: total + 4], gain_row] + vec_rows + [jnp.zeros((1, width), F32), res_rows],
        axis=0,
    )

    @pl.when(step == 0)
    def _():
        small_ref[...] = small

    @pl.when(step > 0)
    def _():
        small_ref[...] += small

    @pl.when(step == pl.num_programs(0) - 1)
    def _():
        for side in range(2):
            weight = dot(o_ref[side].T, dhlow_ref[...]).astype(BF16)
            at = slice(side * half, (side + 1) * half)
            gw_ref[0, at] = weight[:, :half]
            gw_ref[1, at] = weight[:, half:]
        for block in range(dhlow_ref.shape[0] // TB):
            for copy in dolow_copies(block):
                copy.wait()


def combine(experts, total, flow, drow, flat, stat, flat_t, hres, atwo, dy, o, w_shared, extra, prev):
    rows, width = hres.shape
    slots = flow.shape[0]
    half = width // 2
    token = lambda i: (i, 0)
    whole = lambda i: (0, 0)
    weight = pl.BlockSpec((2, width, half), lambda i: (0, 0, 0))
    small_rows = 2 * total + 8
    return pl.pallas_call(
        functools.partial(combine_kernel, experts, total),
        grid=(rows // TB,),
        in_specs=[
            pl.BlockSpec((slots, width), whole),
            pl.BlockSpec((slots, width), whole),
            pl.BlockSpec((TB, LANES), token),
            pl.BlockSpec((TB, LANES), token),
            pl.BlockSpec((8, TB), lambda i: (0, i)),
            pl.BlockSpec((TB, width), token),
            pl.BlockSpec((TB, width), token),
            pl.BlockSpec((TB, width), token),
            pl.BlockSpec((2, rows, half), lambda i: (0, 0, 0)),
            pl.BlockSpec((LANES, width), whole),
            pl.BlockSpec((1, 2, width, half), lambda i: (3, 0, 0, 0)),
            pl.BlockSpec((TB, total), token),
        ],
        out_specs=[
            pl.BlockSpec((TB, width), token),
            pl.BlockSpec((TB, width), token),
            pl.BlockSpec(memory_space=pl.ANY),
            weight,
            pl.BlockSpec((small_rows, width), whole),
        ],
        out_shape=(
            jax.ShapeDtypeStruct((rows, width), BF16),
            jax.ShapeDtypeStruct((rows, width), F32),
            jax.ShapeDtypeStruct((2, rows, half), BF16),
            jax.ShapeDtypeStruct((2, width, half), BF16),
            jax.ShapeDtypeStruct((small_rows, width), F32),
        ),
        scratch_shapes=[
            pltpu.VMEM((slots + LANES, width), BF16),
            pltpu.VMEM((2, TB, width), F32),
            pltpu.VMEM((TB, width), F32),
            pltpu.VMEM((TB, LANES), F32),
            pltpu.VMEM((TB, LANES), F32),
            pltpu.VMEM((rows, width), BF16),
            pltpu.VMEM((2, rows, half), BF16),
            pltpu.SemaphoreType.DMA((rows // TB,)),
            pltpu.SemaphoreType.DMA((2, rows // TB)),
        ],
        compiler_params=pltpu.CompilerParams(
            collective_id=3, has_side_effects=True, vmem_limit_bytes=56 * MIB
        ),
        cost_estimate=cost(
            6 * rows * slots * width + 4 * rows * width * width, 30 * rows * width + 8 * width * width
        ),
        name="combine",
    )(flow, drow, flat, stat, flat_t, hres, atwo, dy, o, extra, w_shared, prev)


def tail_kernel(
    gain_at,
    sent_ref,
    aone_ref,
    w_ref,
    extra_ref,
    x_ref,
    dh_ref,
    gwo_ref,
    small_ref,
    out_ref,
    final,
    small_out_ref,
    both,
    grads,
    w_buf,
    x_buf,
    dh_buf,
    out_buf,
    core_in,
    plane_out,
    plane_in,
    slab_out,
    slab_in,
    own_ref,
    small_own,
    small_core,
    small_plane,
    small_slab,
    load_sems,
    store_sems,
    both_sems,
    core_sems,
    plane_sems,
    slab_sems,
    final_sems,
    pass_sems,
    small_core_sems,
    small_plane_sems,
    small_slab_sems,
):
    experts = lax.axis_size("expert")
    slabs = lax.axis_size("dp")
    me, core, slab = lax.axis_index("expert"), lax.axis_index("context"), lax.axis_index("dp")
    other = 1 - core
    tokens, width = x_buf.shape
    half = width // 2
    parts = 2
    block = tokens // parts

    mine = pltpu.make_async_copy(sent_ref.at[core], both.at[core], load_sems.at[0])
    mine.start()
    loads = [
        pltpu.make_async_copy(w_ref.at[pl.ds(0, 3)], w_buf, load_sems.at[1]),
        pltpu.make_async_copy(x_ref, x_buf, load_sems.at[2]),
        pltpu.make_async_copy(dh_ref, dh_buf, load_sems.at[3]),
    ]
    for copy in loads:
        copy.start()
    greet_all(("context", "expert", "dp"))
    theirs = [
        remote(
            sent_ref.at[other, which],
            both.at[core, which],
            both_sems,
            (which,),
            {"context": other},
        )
        for which in range(3)
    ]
    for copy in theirs:
        copy.start()

    def core_copy(which):
        return remote(
            grads.at[other, which], core_in.at[which], core_sems, (which,), {"context": other}
        )

    for side in range(2):
        grads[side, 3] = gwo_ref[side]
    core_copy(3).start()

    def plane_copy(j, at):
        return remote(
            plane_out.at[j - 1, at],
            plane_in.at[j - 1, at],
            plane_sems,
            (j - 1, at),
            {"expert": lax.rem(me + j, experts)},
        )

    def pass_on(which):
        core_copy(which).wait_recv()
        j = lax.rem(which + experts - me, experts)

        @pl.when(j != 0)
        def _():
            def one(k):
                at = lax.rem(slab + k + 1, slabs)
                plane_out[j - 1, at] = (
                    grads[core, which, at].astype(F32) + core_in[which, at].astype(F32)
                ).astype(BF16)
                plane_copy(j, at).start()

            loop(slabs, one)

    mine.wait()
    turned = aone_ref[...].T
    for which in range(3):
        theirs[which].wait_recv()
        grad = jnp.concatenate([both[0, which], both[1, which]], axis=1)
        weight = dot(turned, grad)
        for side in range(2):
            grads[side, which] = (
                weight[:, side * half : (side + 1) * half]
                .reshape(slabs, width // slabs, half)
                .astype(BF16)
            )
        core_copy(which).start()
        pass_on((which + 3) % 4)
    for copy in loads:
        copy.wait()

    gain = extra_ref[GAIN_ONE : GAIN_ONE + 1].astype(F32)
    stores = []
    gain_row = jnp.zeros((1, width), F32)
    for part in range(parts):
        at = slice(part * block, (part + 1) * block)
        dnone = None
        for which in range(3):
            grad = jnp.concatenate([both[0, which, at], both[1, which, at]], axis=1)
            whole = jnp.concatenate([w_buf[which, 0], w_buf[which, 1]], axis=1)
            product = dot_nt(grad, whole)
            dnone = product if dnone is None else dnone + product
        values = x_buf[at].astype(F32)
        scale = lax.rsqrt(jnp.mean(values * values, axis=-1, keepdims=True) + EPS)
        scaled = dnone * gain
        inner = jnp.mean(values * scaled, axis=1, keepdims=True)
        out_buf[at] = dh_buf[at] + scale * scaled - values * (scale * scale * scale * inner)
        stores.append(
            pltpu.make_async_copy(out_buf.at[at], out_ref.at[at], store_sems.at[part])
        )
        stores[-1].start()
        gain_row = gain_row + jnp.sum(dnone * values * scale, axis=0, keepdims=True)
        if part == 0:
            pass_on(2)

    row = iota(small_ref.shape, 0)
    small_own[...] = small_ref[...] + jnp.where(row == gain_at, gain_row, 0.0)
    small_copy = remote(small_own, small_core, small_core_sems, (0,), {"context": other})
    small_copy.start()
    small_copy.wait()
    small_plane[me] = small_own[...] + small_core[...]
    small_plane_copies = []
    for j in range(1, experts):
        small_plane_copies.append(
            remote(
                small_plane.at[me],
                small_plane.at[me],
                small_plane_sems,
                (j,),
                {"expert": lax.rem(me + j, experts)},
            )
        )
        small_plane_copies[-1].start()

    def gathered(at):
        value = grads[core, me, at].astype(F32) + core_in[me, at].astype(F32)
        for j in range(1, experts):
            plane_copy(j, at).wait_recv()
            value = value + plane_in[j - 1, at].astype(F32)
        return value

    def slab_copy(k):
        return remote(
            slab_out.at[k],
            slab_in.at[k],
            slab_sems,
            (k,),
            {"dp": lax.rem(slab + k + 1, slabs)},
        )

    def scatter(k):
        slab_out[k] = gathered(lax.rem(slab + k + 1, slabs)).astype(BF16)
        slab_copy(k).start()

    loop(slabs - 1, scatter)

    for copy in small_plane_copies:
        copy.wait()
    value = small_plane[0]
    for j in range(1, experts):
        value = value + small_plane[j]
    small_slab[slab] = value

    def small_slab_copy(k):
        return remote(
            small_slab.at[slab],
            small_slab.at[slab],
            small_slab_sems,
            (k,),
            {"dp": lax.rem(slab + k + 1, slabs)},
        )

    loop(slabs - 1, lambda k: small_slab_copy(k).start())

    own_ref[...] = gathered(slab)

    def collect(k):
        slab_copy(k).wait_recv()
        own_ref[...] += slab_in[k].astype(F32)

    loop(slabs - 1, collect)
    final[core, me] = own_ref[...].astype(BF16)
    final_copies, pass_copies = [], []
    for j in range(1, experts):
        final_copies.append(
            remote(
                final.at[core, me],
                final.at[core, me],
                final_sems,
                (j,),
                {"expert": lax.rem(me + j, experts)},
            )
        )
        final_copies[-1].start()
    for j in range(experts):
        source = lax.rem(me + experts - j, experts)
        if j > 0:
            final_copies[j - 1].wait_recv()
        pass_copies.append(
            remote(
                final.at[core, source],
                final.at[core, source],
                pass_sems,
                (j,),
                {"context": other},
            )
        )
        pass_copies[-1].start()

    loop(slabs - 1, lambda k: small_slab_copy(k).wait())
    small_out_ref[...] = small_slab[0]

    def add_small(k):
        small_out_ref[...] += small_slab[k + 1]

    loop(slabs - 1, add_small)

    for copy in pass_copies:
        copy.wait_recv()
    for copy in stores:
        copy.wait()
    for which in range(4):
        core_copy(which).wait_send()
    for j in range(1, experts):

        def sent(k, j=j):
            plane_copy(j, k).wait_send()

        loop(slabs, sent)
    loop(slabs - 1, lambda k: slab_copy(k).wait_send())
    for copy in theirs + final_copies + pass_copies:
        copy.wait_send()


def tail(experts, slabs, gain_at, sent, aone, w_shared, extra, x, dh, gwo, small):
    tokens, width = x.shape
    half = width // 2
    rows = width // slabs
    vmem = pl.BlockSpec(memory_space=pltpu.VMEM)
    anywhere = pl.BlockSpec(memory_space=pl.ANY)
    dma = pltpu.SemaphoreType.DMA
    return pl.pallas_call(
        functools.partial(tail_kernel, gain_at),
        in_specs=[anywhere, vmem, anywhere, vmem, anywhere, anywhere] + [vmem] * 2,
        out_specs=[anywhere] + [vmem] * 2,
        out_shape=(
            jax.ShapeDtypeStruct((tokens, width), F32),
            jax.ShapeDtypeStruct((2, experts, rows, half), BF16),
            jax.ShapeDtypeStruct(small.shape, F32),
        ),
        scratch_shapes=[
            pltpu.VMEM((2, 3, tokens, half), BF16),
            pltpu.VMEM((2, 4, slabs, rows, half), BF16),
            pltpu.VMEM((3, 2, width, half), BF16),
            pltpu.VMEM((tokens, width), BF16),
            pltpu.VMEM((tokens, width), F32),
            pltpu.VMEM((tokens, width), F32),
            pltpu.VMEM((4, slabs, rows, half), BF16),
            pltpu.VMEM((experts - 1, slabs, rows, half), BF16),
            pltpu.VMEM((experts - 1, slabs, rows, half), BF16),
            pltpu.VMEM((slabs - 1, rows, half), BF16),
            pltpu.VMEM((slabs - 1, rows, half), BF16),
            pltpu.VMEM((rows, half), F32),
            pltpu.VMEM(small.shape, F32),
            pltpu.VMEM(small.shape, F32),
            pltpu.VMEM((experts,) + small.shape, F32),
            pltpu.VMEM((slabs,) + small.shape, F32),
            dma((4,)),
            dma((2,)),
            dma((2, 3)),
            dma((2, 4)),
            dma((2, experts - 1, slabs)),
            dma((2, slabs - 1)),
            dma((2, experts)),
            dma((2, experts)),
            dma((2, 1)),
            dma((2, experts)),
            dma((2, slabs - 1)),
        ],
        compiler_params=pltpu.CompilerParams(
            collective_id=0, has_side_effects=True, vmem_limit_bytes=60 * MIB
        ),
        cost_estimate=cost(12 * tokens * width * width, 40 * tokens * width),
        name="tail",
    )(sent, aone, w_shared, extra, x, dh, gwo, small)


def finish_kernel(
    total,
    place_ref,
    small_ref,
    final_ref,
    mine_ref,
    theirs_ref,
    tokens_ref,
    norm_one_ref,
    norm_two_ref,
    router_ref,
    mix_ref,
    vec_ref,
    res_ref,
    q_ref,
    k_ref,
    v_ref,
    o_ref,
    gate_ref,
    up_ref,
    gd_ref,
    tokens_out_ref,
    final_buf,
    share_buf,
    square_buf,
    gate_buf,
    up_buf,
    gd_buf,
    turned_ref,
    load_sems,
    store_sems,
):
    rows, half = final_buf.shape[2:]
    wide = share_buf.shape[2] // 3
    deep = gd_buf.shape[0]
    core = place_ref[1]
    loads = [
        pltpu.make_async_copy(mine_ref, share_buf.at[0], load_sems.at[0]),
        pltpu.make_async_copy(theirs_ref, share_buf.at[1], load_sems.at[1]),
        pltpu.make_async_copy(final_ref, final_buf, load_sems.at[2]),
        pltpu.make_async_copy(tokens_ref, tokens_out_ref, load_sems.at[3]),
    ]
    for copy in loads:
        copy.start()
    small = small_ref[...]
    fill = jnp.zeros((LANES - small.shape[0], small.shape[1]), F32)
    turned_ref[...] = jnp.concatenate([small, fill], axis=0).T
    own = turned_ref[pl.ds(pl.multiple_of(place_ref[0] * rows, 8), rows), :]
    router_ref[...] = own[:, :total]
    mix_ref[...] = own[:, total : total + 4]
    norm_two_ref[...] = own[:, total + 4 : total + 5]
    vec_ref[...] = own[:, total + 5 : total + 7]
    norm_one_ref[...] = own[:, total + 7 : total + 8]
    res_ref[...] = turned_ref[:total, total + 8 : 2 * total + 8]

    stores = []

    def store(buffer, ref):
        stores.append(pltpu.make_async_copy(buffer, ref, store_sems.at[len(stores)]))
        stores[-1].start()

    def sides(buffer, size, left, right):
        buffer[:, :size] = left
        buffer[:, size:] = right

    def ordered(get):
        first, second = get(share_buf.at[0]), get(share_buf.at[1])
        swap = core != 0
        return jnp.where(swap, second, first), jnp.where(swap, first, second)

    for copy in loads[:2]:
        copy.wait()
    sides(gate_buf, wide, *ordered(lambda ref: ref[:, :wide].astype(F32)))
    store(gate_buf, gate_ref.at[0])
    sides(up_buf, wide, *ordered(lambda ref: ref[:, wide : 2 * wide].astype(F32)))
    store(up_buf, up_ref.at[0])

    def down(ref):
        blocks = [
            ref[:, 2 * wide + b * deep : 2 * wide + (b + 1) * deep].astype(F32)
            for b in range(half // rows)
        ]
        return jnp.concatenate(blocks, axis=0).T

    sides(gd_buf, half, *ordered(down))
    store(gd_buf, gd_ref.at[0])
    loads[2].wait()
    for which, ref in enumerate((q_ref, k_ref, v_ref, o_ref)):
        sides(
            square_buf.at[which],
            half,
            final_buf[0, which].astype(F32),
            final_buf[1, which].astype(F32),
        )
        store(square_buf.at[which], ref)
    loads[3].wait()
    for copy in stores:
        copy.wait()


def finish(total, place, final, small, mine, theirs, tokens):
    rows, half = final.shape[2:]
    width = 2 * half
    wide = mine.shape[1] // 3
    deep = wide * rows // half
    anywhere = pl.BlockSpec(memory_space=pl.ANY)
    vmem = pl.BlockSpec(memory_space=pltpu.VMEM)
    shape = lambda *dims: jax.ShapeDtypeStruct(dims, F32)
    return pl.pallas_call(
        functools.partial(finish_kernel, total),
        in_specs=[pl.BlockSpec(memory_space=pltpu.SMEM), vmem] + [anywhere] * 4,
        out_specs=[vmem] * 6 + [anywhere] * 8,
        out_shape=(
            shape(rows, 1),
            shape(rows, 1),
            shape(rows, total),
            shape(rows, 4),
            shape(rows, 2),
            shape(total, total),
            shape(rows, width),
            shape(rows, width),
            shape(rows, width),
            shape(rows, width),
            shape(1, rows, 2 * wide),
            shape(1, rows, 2 * wide),
            shape(1, deep, width),
            shape(*tokens.shape),
        ),
        scratch_shapes=[
            pltpu.VMEM(final.shape, BF16),
            pltpu.VMEM((2,) + mine.shape, BF16),
            pltpu.VMEM((4, rows, width), F32),
            pltpu.VMEM((rows, 2 * wide), F32),
            pltpu.VMEM((rows, 2 * wide), F32),
            pltpu.VMEM((deep, width), F32),
            pltpu.VMEM((width, LANES), F32),
            pltpu.SemaphoreType.DMA((4,)),
            pltpu.SemaphoreType.DMA((7,)),
        ],
        compiler_params=params(40),
        cost_estimate=cost(1e6, 20 * rows * width),
        name="finish",
    )(place, small, final, mine, theirs, tokens)


def swap_cores(value):
    return lax.all_to_all(value, "context", split_axis=0, concat_axis=0, tiled=True)


def on_device(
    tokens,
    segments,
    routes,
    prev_logits,
    ranks,
    cotangent,
    norm_one,
    w_query,
    w_key,
    w_value,
    w_out,
    norm_two,
    router,
    w_res,
    const_mix,
    const_vec,
    w_gate,
    w_up,
    w_down,
):
    experts = lax.axis_size("expert")
    dp = lax.axis_size("dp")
    total = experts + NZ
    _, rows, width = tokens.shape
    hidden = w_gate.shape[2]
    cap = (18 * rows + 8 * total - 1) // (8 * total)
    seq = 2 * rows
    core = lax.axis_index("context")
    half = width // 2

    def mine(shard, size):
        return lax.dynamic_slice_in_dim(shard, core * size, size, 1)

    def gather(shard):
        return lax.all_gather(shard, ("context", "dp"), axis=0).reshape(
            2, dp * shard.shape[0], shard.shape[1]
        )

    extra = jnp.concatenate(
        [router, const_mix, norm_one[:, None], norm_two[:, None], const_vec], axis=1
    )
    cos, sin = (jnp.asarray(table).reshape(2, rows, LANES) for table in rope_tables(seq))
    x = tokens[0]
    dy = cotangent[0]
    w_shared, extra, flat, flat_t, low, first, qkv, aone = spread(
        experts,
        dp,
        cap,
        w_query,
        w_key,
        w_value,
        w_out,
        extra.astype(F32).T,
        routes[0],
        ranks[0],
        segments,
        x,
        cos,
        sin,
    )
    w_shared = w_shared.reshape(4, 2, width, half)
    extra = extra.transpose(1, 0, 2).reshape(total + 8, width).astype(BF16)
    extra = jnp.concatenate(
        [
            extra[: total + 4],
            jnp.zeros((GAIN_ONE - total - 4, width), BF16),
            extra[total + 4 :],
            jnp.zeros((LANES - GAIN_ONE - 4, width), BF16),
        ],
        axis=0,
    )
    wide_mine = [mine(w_gate[0], hidden // 2), mine(w_up[0], hidden // 2)]
    down_mine = mine(w_down[0], half)
    deep = hidden // dp
    if deep == FC:
        turned = down_mine.T.reshape(-1, width // dp, deep).transpose(1, 0, 2)
        wide_w = gather(jnp.concatenate(wide_mine + [turned.reshape(width // dp, -1)], axis=1))
        down_w = wide_w
    else:
        wide_w = gather(jnp.concatenate(wide_mine, axis=1))
        down_w = gather(down_mine).transpose(0, 2, 1)

    res = jnp.pad(w_res.astype(F32), ((0, 0), (0, LANES - total)))

    o_heads, lse = attend(first, qkv, low)
    o = swap_cores(o_heads)
    hres, atwo, stat = middle(total, x, o, w_shared, extra, prev_logits[0], res, routes[0])
    flow_back, drow_back, grad_wide = run_experts(
        total, experts, dp, hidden, cap, flat_t, atwo, dy, stat, wide_w, down_w
    )
    flow_back = flow_back.reshape(experts * cap, width)
    drow_back = drow_back.reshape(experts * cap, width)
    wide = lax.psum_scatter(
        grad_wide.reshape(width, 3 * hidden // 2), "dp", scatter_dimension=0, tiled=True
    )

    output, dh, grad_o, grad_out_w, small = combine(
        experts,
        total,
        flow_back,
        drow_back,
        flat,
        stat,
        flat_t,
        hres,
        atwo,
        dy,
        o,
        w_shared,
        extra,
        prev_logits[0],
    )
    grads_sent = attend_back(
        first,
        qkv,
        grad_o,
        o_heads,
        lse,
        low,
        cos,
        sin,
    )
    grad_tokens, final, small = tail(
        experts,
        dp,
        total + 7,
        grads_sent,
        aone,
        w_shared,
        extra,
        x,
        dh,
        grad_out_w.reshape(2, dp, width // dp, half),
        small,
    )
    wide, small = lax.optimization_barrier((wide, small))
    wide_other = lax.ppermute(wide, "context", [(0, 1), (1, 0)])
    (
        grad_norm_one,
        grad_norm_two,
        grad_router,
        grad_mix,
        grad_vec,
        grad_res,
        grad_query,
        grad_key,
        grad_value,
        grad_out,
        grad_gate,
        grad_up,
        grad_down,
        grad_tokens,
    ) = finish(
        total,
        jnp.stack([lax.axis_index("dp"), core]),
        final,
        small,
        wide,
        wide_other,
        grad_tokens,
    )
    return (
        output[None],
        grad_tokens[None],
        grad_norm_one[:, 0],
        grad_query,
        grad_key,
        grad_value,
        grad_out,
        grad_norm_two[:, 0],
        grad_router,
        grad_res,
        grad_mix,
        grad_vec,
        grad_gate,
        grad_up,
        grad_down,
    )


def solution(mesh):
    token = P(("expert", "dp"), "context", None)
    rows = P("dp", None)
    expert = P("expert", "dp", None)
    in_specs = (
        token,
        P(("expert", "dp"), "context"),
        token,
        token,
        token,
        token,
        P("dp"),
        rows,
        rows,
        rows,
        rows,
        P("dp"),
        rows,
        P(),
        rows,
        rows,
        expert,
        expert,
        expert,
    )
    out_specs = (
        token,
        token,
        P("dp"),
        rows,
        rows,
        rows,
        rows,
        P("dp"),
        rows,
        P(),
        rows,
        rows,
        expert,
        expert,
        expert,
    )
    return jax.shard_map(
        on_device, mesh=mesh, in_specs=in_specs, out_specs=out_specs, check_vma=False
    )
```

```python
import functools

import jax
import jax.numpy as jnp
import numpy as np
from jax import lax
from jax.experimental import pallas as pl
from jax.experimental.pallas import tpu as pltpu
from jax.sharding import PartitionSpec as P

HEADS = 12
HEAD_DIM = 64
WIN = 1024
NZ = 4
SEGMENTS = 5
GAIN_ONE, GAIN_TWO, VECS = 112, 113, 114
TQ = 256
TB = 256
RC = 64
FC = 512
LANES = 128
EPS = 1e-05
MASKED = -1000000000.0
HIGH = lax.Precision.HIGHEST
F32 = jnp.float32
BF16 = jnp.bfloat16
MIB = 1024 * 1024


def params(mib):
    return pltpu.CompilerParams(vmem_limit_bytes=mib * MIB)


def cost(flops, nbytes, trans=0):
    return pl.CostEstimate(flops=int(flops), bytes_accessed=int(nbytes), transcendentals=int(trans))


def dot(left, right):
    return jnp.dot(left, right, preferred_element_type=F32)


def dot_nt(left, right):
    return lax.dot_general(left, right, (((1,), (1,)), ((), ())), preferred_element_type=F32)


def dot_tn(left, right):
    return lax.dot_general(left, right, (((0,), (0,)), ((), ())), preferred_element_type=F32)


def iota(shape, axis):
    return lax.broadcasted_iota(jnp.int32, shape, axis)


def rope_tables(seq):
    half = HEAD_DIM // 2
    frequency = np.float32(10000.0) ** (
        -np.arange(half, dtype=np.float32) * np.float32(2.0) / np.float32(HEAD_DIM)
    )
    angles = np.arange(seq, dtype=np.float32)[:, None] * frequency.astype(np.float32)[None, :]
    cos = np.cos(angles.astype(np.float64)).astype(np.float32)
    sin = np.sin(angles.astype(np.float64)).astype(np.float32)
    return np.concatenate([cos] * 4, axis=1), np.concatenate([-sin, sin, -sin, sin], axis=1)


def swap_halves(chunk):
    lane = iota(chunk.shape, 1)
    return jnp.where(
        lane % HEAD_DIM < HEAD_DIM // 2, pltpu.roll(chunk, 96, 1), pltpu.roll(chunk, 32, 1)
    )


def loop(count, body):
    if count <= 4:
        for step in range(count):
            body(step)
    else:
        lax.fori_loop(0, count, lambda step, carry: (body(step), carry)[1], 0)


def remote(src, dst, sems, index, where):
    return pltpu.make_async_remote_copy(
        src_ref=src,
        dst_ref=dst,
        send_sem=sems.at[(0,) + index],
        recv_sem=sems.at[(1,) + index],
        device_id=where,
        device_id_type=pl.DeviceIdType.MESH,
    )


def greet_all(axes):
    barrier = pltpu.get_barrier_semaphore()
    total = 0
    for axis in axes:
        size = lax.axis_size(axis)
        me = lax.axis_index(axis)
        total += size - 1

        def greet(k, axis=axis, size=size, me=me):
            pl.semaphore_signal(
                barrier,
                inc=1,
                device_id={axis: lax.rem(me + k + 1, size)},
                device_id_type=pl.DeviceIdType.MESH,
            )

        loop(size - 1, greet)
    pl.semaphore_wait(barrier, total)


def place_pairs(experts, cap, routes_ref, ranks_ref, flat_ref, flat_t_ref):
    rows = routes_ref.shape[0]
    lane = iota((rows, LANES), 1)
    first, second = routes_ref[:, 0:1], routes_ref[:, 1:2]
    hot_first, hot_second = first == lane, second == lane
    hot = (hot_first.astype(F32) + hot_second.astype(F32)).astype(BF16)
    ranks = ranks_ref[...].astype(F32)
    ranks_col = jnp.broadcast_to(ranks, (LANES, rows)).T[:, 0:1]
    earlier = jnp.where(ranks < ranks_col, 1.0, 0.0).astype(BF16)
    counts = dot(earlier, hot)

    def flat(hit, route):
        slot = jnp.sum(jnp.where(hit, counts, 0.0), axis=1, keepdims=True).astype(jnp.int32)
        return jnp.where((route < experts) & (slot < cap), route * cap + slot, experts * cap)

    columns = (flat(hot_first, first), flat(hot_second, second), first, second)
    out = jnp.zeros((rows, LANES), jnp.int32)
    for i, column in enumerate(columns):
        out = jnp.where(lane == i, column, out)
    flat_ref[...] = out
    flat_t_ref[...] = out.astype(F32).T[:8]


def find_starts(segs_ref, low_ref, first_ref):
    rows = segs_ref.shape[2]
    per = rows // TQ
    segs = [segs_ref[side].astype(F32) for side in range(2)]
    starts = [jnp.zeros((1, rows), F32) for side in range(2)]
    for number in range(1, SEGMENTS):
        before = sum(
            jnp.sum(jnp.where(part < number, 1.0, 0.0), axis=1, keepdims=True) for part in segs
        )
        starts = [
            jnp.where(part == number, before, start) for part, start in zip(segs, starts)
        ]
    for side in range(2):
        place = (iota((1, rows), 1) + (side * rows - WIN + 1)).astype(F32)
        low = jnp.maximum(starts[side], place)
        for tile in range(per):
            part = low[:, tile * TQ : (tile + 1) * TQ]
            low_ref[side * per + tile] = part.astype(jnp.int32)
            first_ref[side * per + tile] = jnp.min(part).astype(jnp.int32) // TQ
    first_ref[2 * per] = lax.axis_index("context")


def hot_slots(flat_ref, cap, target):
    slot = (iota((cap, flat_ref.shape[1]), 0) + target * cap).astype(F32)
    return flat_ref[0:1, :] == slot, flat_ref[1:2, :] == slot


def spread_kernel(
    cap,
    w_query_ref,
    w_key_ref,
    w_value_ref,
    w_out_ref,
    extra_ref,
    routes_ref,
    ranks_ref,
    segs_ref,
    x_ref,
    dy_ref,
    cos_ref,
    sin_ref,
    shared_ref,
    extra_out_ref,
    flat_ref,
    flat_t_ref,
    low_ref,
    first_ref,
    qkv_ref,
    aone_ref,
    dy_rows_ref,
    out_ref,
    segs_all,
    stage_ref,
    slab_sems,
    plane_sems,
    core_sems,
    extra_sems,
    segs_sems,
    shared_sem,
    own_sems,
    qkv_sems,
):
    experts = lax.axis_size("expert")
    slabs = lax.axis_size("dp")
    me, core, slab = lax.axis_index("expert"), lax.axis_index("context"), lax.axis_index("dp")
    half = out_ref.shape[4]
    for which, ref in enumerate((w_query_ref, w_key_ref, w_value_ref, w_out_ref)):
        for side in range(2):

            @pl.when((me == which) & (core == side))
            def _():
                out_ref[which, side, slab] = ref[:, side * half : (side + 1) * half]

    extra_out_ref[slab] = extra_ref[...]
    segs_all[core] = segs_ref[...]
    greet_all(("context", "expert", "dp"))

    def slab_copy(k):
        piece = out_ref.at[me, core, slab]
        return remote(piece, piece, slab_sems, (k,), {"dp": lax.rem(slab + k + 1, slabs)})

    def extra_copy(k):
        piece = extra_out_ref.at[slab]
        return remote(piece, piece, extra_sems, (k,), {"dp": lax.rem(slab + k + 1, slabs)})

    def plane_copy(j, at):
        piece = out_ref.at[me, core, at]
        return remote(
            piece, piece, plane_sems, (j - 1, at), {"expert": lax.rem(me + j, experts)}
        )

    def core_copy(j, at):
        piece = out_ref.at[lax.rem(me + experts - j, experts), core, at]
        return remote(piece, piece, core_sems, (j, at), {"context": 1 - core})

    def share(at):
        for j in range(1, experts):
            plane_copy(j, at).start()
        core_copy(0, at).start()

    loop(slabs - 1, lambda k: extra_copy(k).start())
    loop(slabs - 1, lambda k: slab_copy(k).start())
    share(slab)
    segs_copy = remote(
        segs_all.at[core], segs_all.at[core], segs_sems, (0,), {"context": 1 - core}
    )
    segs_copy.start()
    place_pairs(experts, cap, routes_ref, ranks_ref, flat_ref, flat_t_ref)
    segs_copy.wait()
    find_starts(segs_all, low_ref, first_ref)
    loop(slabs - 1, lambda k: extra_copy(k).wait())
    at = extra_ref.shape[0] - 4
    gain = jnp.concatenate([extra_out_ref[z, at : at + 1, :] for z in range(slabs)], axis=1)
    tokens = x_ref.shape[0]
    for start in range(0, tokens, TB):
        values = x_ref[start : start + TB].astype(F32)
        scale = lax.rsqrt(jnp.mean(values * values, axis=-1, keepdims=True) + EPS)
        aone_ref[start : start + TB] = (values * scale * gain).astype(BF16)

    def forward(k):
        slab_copy(k).wait_recv()
        share(lax.rem(slab + slabs - k - 1, slabs))

    loop(slabs - 1, forward)
    for target in range(experts):
        first, second = hot_slots(flat_t_ref, cap, target)
        hot = jnp.where(first | second, 1.0, 0.0).astype(BF16)
        dy_rows_ref[target] = dot(hot, dy_ref[...]).astype(BF16)

    def relay(k):
        at = lax.rem(slab + slabs - k, slabs)
        for j in range(1, experts):
            plane_copy(j, at).wait_recv()
            core_copy(j, at).start()

    loop(slabs, relay)
    loop(slabs - 1, lambda k: slab_copy(k).wait_send())

    def arrive(at):
        for j in range(experts):
            core_copy(j, at).wait()
        for j in range(1, experts):
            plane_copy(j, at).wait_send()

    loop(slabs, arrive)
    keep = pltpu.make_async_copy(out_ref, shared_ref, shared_sem)
    keep.start()

    width = 2 * half
    wholes = [
        jnp.concatenate(
            [out_ref[which, side].reshape(width, half) for side in range(2)], axis=1
        )
        for which in range(3)
    ]
    copies = []
    for block in range(tokens // TB):
        span = slice(block * TB, (block + 1) * TB)
        cos, sin = cos_ref[core, span], sin_ref[core, span]
        for which in range(3):
            product = dot(aone_ref[span], wholes[which])
            for pair in range(width // LANES):
                chunk = product[:, pair * LANES : (pair + 1) * LANES]
                if which < 2:
                    chunk = chunk * cos + swap_halves(chunk) * sin
                if which == 0:
                    chunk = chunk * HEAD_DIM ** (-0.5)
                side, place_in = pair // (half // LANES), pair % (half // LANES)
                stage_ref[side, which, span, place_in * LANES : (place_in + 1) * LANES] = (
                    chunk.astype(BF16)
                )
        copies.append(
            pltpu.make_async_copy(
                stage_ref.at[core, :, span], qkv_ref.at[core, :, span], own_sems.at[block]
            )
        )
        copies.append(
            remote(
                stage_ref.at[1 - core, :, span],
                qkv_ref.at[core, :, span],
                qkv_sems,
                (block,),
                {"context": 1 - core},
            )
        )
        for copy in copies[-2:]:
            copy.start()
    for copy in copies:
        copy.wait()
    keep.wait()


def spread(
    experts, slabs, cap, w_query, w_key, w_value, w_out, extra, routes, ranks, segs, x, dy, cos, sin
):
    tokens = routes.shape[0]
    tiles = 2 * tokens // TQ
    rows, width = w_query.shape
    half = width // 2
    vmem = pl.BlockSpec(memory_space=pltpu.VMEM)
    anywhere = pl.BlockSpec(memory_space=pl.ANY)
    dma = pltpu.SemaphoreType.DMA
    return pl.pallas_call(
        functools.partial(spread_kernel, cap),
        in_specs=[vmem] * 12,
        out_specs=[anywhere]
        + [vmem] * 4
        + [pl.BlockSpec(memory_space=pltpu.SMEM), anywhere, vmem, vmem],
        out_shape=(
            jax.ShapeDtypeStruct((4, 2, slabs, rows, half), BF16),
            jax.ShapeDtypeStruct((slabs,) + extra.shape, F32),
            jax.ShapeDtypeStruct((tokens, LANES), jnp.int32),
            jax.ShapeDtypeStruct((8, tokens), F32),
            jax.ShapeDtypeStruct((tiles, 1, TQ), jnp.int32),
            jax.ShapeDtypeStruct((tiles + 1,), jnp.int32),
            jax.ShapeDtypeStruct((2, 3, tokens, half), BF16),
            jax.ShapeDtypeStruct((tokens, width), BF16),
            jax.ShapeDtypeStruct((experts, cap, width), BF16),
        ),
        scratch_shapes=[
            pltpu.VMEM((4, 2, slabs, rows, half), BF16),
            pltpu.VMEM((2, 1, tokens), jnp.int32),
            pltpu.VMEM((2, 3, tokens, half), BF16),
            dma((2, slabs - 1)),
            dma((2, experts - 1, slabs)),
            dma((2, experts, slabs)),
            dma((2, slabs - 1)),
            dma((2, 1)),
            dma,
            dma((tokens // TB,)),
            dma((2, tokens // TB)),
        ],
        compiler_params=pltpu.CompilerParams(
            collective_id=1, has_side_effects=True, vmem_limit_bytes=62 * MIB
        ),
        cost_estimate=cost(1e6, 16 * width * width),
        name="spread",
    )(w_query, w_key, w_value, w_out, extra, routes, ranks, segs, x, dy, cos, sin)


def head_masks():
    lane = iota((TQ, LANES), 1)
    low = jnp.where(lane < HEAD_DIM, 1.0, 0.0).astype(BF16)
    return low, (1.0 - low.astype(F32)).astype(BF16)


def spans(tile, first, body):
    for count in range(1, WIN // TQ + 2):

        @pl.when(tile - first + 1 == count)
        def _():
            body(count)


def masked(scores, low, start, count):
    shape = (TQ, 2 * TQ)
    sub, lane = iota(shape, 0), lax.rem(iota(shape, 1), TQ)
    low = jnp.concatenate([low, low], axis=1)
    parts = []
    for t in range(count):
        mark = sub >= low - (start + t * TQ)
        if t == count - 1:
            mark = mark & (sub <= lane)
        parts.append(jnp.where(mark, scores[t * TQ : (t + 1) * TQ], MASKED))
    return parts


def own_blocks(both):
    return jnp.concatenate([both[:HEAD_DIM, :TQ], both[HEAD_DIM:LANES, TQ:]], axis=0)


def attend_kernel(first_ref, q_ref, k_ref, v_ref, lo_ref, o_ref, lse_ref, keys_ref, vt_ref):
    rows = q_ref.shape[2]
    per = rows // TQ
    masks = head_masks()
    for side in range(2):
        at = slice(side * rows, (side + 1) * rows)
        keys_ref[at, :] = k_ref[side, 0]
        vt_ref[:LANES, at] = v_ref[side, 0].T
        vt_ref[LANES:, at] = jnp.ones((16, rows), BF16)

    def q_step(qi, carry):
        at = pl.ds(pl.multiple_of(lax.rem(qi, per) * TQ, TQ), TQ)
        query = q_ref[qi // per, 0, at, :]
        low = lo_ref[qi]

        def run(count):
            start = pl.multiple_of((qi - count + 1) * TQ, TQ)
            span = pl.ds(start, count * TQ)
            both = jnp.concatenate([query * mask for mask in masks], axis=0)
            scores = masked(dot_nt(keys_ref[span, :], both), low, start, count)
            peak = functools.reduce(
                jnp.maximum, [jnp.max(part, axis=0, keepdims=True) for part in scores]
            )
            probs = jnp.concatenate([jnp.exp(part - peak).astype(BF16) for part in scores], axis=0)
            mixed = dot(vt_ref[:, span], probs)
            total = mixed[LANES : LANES + 1]
            lse_ref[0, qi, 0:1, :] = peak + jnp.log(total)
            mine = jnp.where(qi // per == first_ref[2 * per], 1, 0)
            o_ref[mine, at, :] = own_blocks(mixed[:LANES] / total).T.astype(BF16)

        spans(qi, first_ref[qi], run)
        return carry

    lax.fori_loop(0, 2 * per, q_step, 0)


def part_spec(which, rows):
    return pl.BlockSpec((2, 1, rows, LANES), lambda p, first, which=which: (0, which, 0, p))


def attend(first, qkv, low):
    _, _, rows, half = qkv.shape
    pairs = half // LANES
    tiles = 2 * rows // TQ
    return pl.pallas_call(
        attend_kernel,
        grid_spec=pltpu.PrefetchScalarGridSpec(
            num_scalar_prefetch=1,
            grid=(pairs,),
            in_specs=[
                part_spec(0, rows),
                part_spec(1, rows),
                part_spec(2, rows),
                pl.BlockSpec((tiles, 1, TQ), lambda p, first: (0, 0, 0)),
            ],
            out_specs=[
                pl.BlockSpec((2, rows, LANES), lambda p, first: (0, 0, p)),
                pl.BlockSpec((1, tiles, 8, 2 * TQ), lambda p, first: (p, 0, 0, 0)),
            ],
            scratch_shapes=[
                pltpu.VMEM((2 * rows, LANES), BF16),
                pltpu.VMEM((LANES + 16, 2 * rows), BF16),
            ],
        ),
        out_shape=(
            jax.ShapeDtypeStruct((2, rows, half), BF16),
            jax.ShapeDtypeStruct((pairs, tiles, 8, 2 * TQ), F32),
        ),
        compiler_params=params(62),
        cost_estimate=cost(40e9, 16 * rows * half, 12e6),
        name="attend",
    )(first, qkv, qkv, qkv, low)


def attend_back_kernel(
    first_ref,
    q_ref,
    k_ref,
    v_ref,
    do_ref,
    o_ref,
    lse_ref,
    lo_ref,
    cos_ref,
    sin_ref,
    g_ref,
    keys_ref,
    values_ref,
    kt_ref,
    delta_ref,
    dk_ref,
    dv_ref,
):
    rows = q_ref.shape[2]
    per = rows // TQ
    masks = head_masks()
    for side in range(2):
        at = slice(side * rows, (side + 1) * rows)
        keys_ref[at, :] = k_ref[side, 0]
        values_ref[at, :] = v_ref[side, 0]
        kt_ref[:, at] = k_ref[side, 0].T
    dk_ref[...] = jnp.zeros_like(dk_ref)
    dv_ref[...] = jnp.zeros_like(dv_ref)

    def prepare(tile, carry):
        at = pl.ds(pl.multiple_of(lax.rem(tile, per) * TQ, TQ), TQ)
        mine = jnp.where(tile // per == first_ref[2 * per], 1, 0)
        both = o_ref[mine, at, :].astype(F32) * do_ref[tile // per, at, :].astype(F32)
        both = both.T
        delta_ref[tile, 0:1, :TQ] = jnp.sum(both[:HEAD_DIM], axis=0, keepdims=True)
        delta_ref[tile, 0:1, TQ:] = jnp.sum(both[HEAD_DIM:], axis=0, keepdims=True)
        return carry

    lax.fori_loop(0, 2 * per, prepare, 0)

    def q_step(qi, carry):
        at = pl.ds(pl.multiple_of(lax.rem(qi, per) * TQ, TQ), TQ)
        query = q_ref[qi // per, 0, at, :]
        grad = do_ref[qi // per, at, :]
        low = lo_ref[qi]

        def run(count):
            start = pl.multiple_of((qi - count + 1) * TQ, TQ)
            span = pl.ds(start, count * TQ)
            queries = jnp.concatenate([query * mask for mask in masks], axis=0)
            grads = jnp.concatenate([grad * mask for mask in masks], axis=0)
            lse, delta = lse_ref[0, qi, 0:1, :], delta_ref[qi, 0:1, :]
            scores = masked(dot_nt(keys_ref[span, :], queries), low, start, count)
            grad_probs = dot_nt(values_ref[span, :], grads)
            probs = [jnp.exp(part - lse) for part in scores]
            grad_scores = jnp.concatenate(
                [
                    (part * (grad_probs[t * TQ : (t + 1) * TQ] - delta)).astype(BF16)
                    for t, part in enumerate(probs)
                ],
                axis=0,
            )
            probs = jnp.concatenate([part.astype(BF16) for part in probs], axis=0)
            dv_ref[span, :] += dot(probs, grads)
            dk_ref[span, :] += dot(grad_scores, queries)
            turned = own_blocks(dot(kt_ref[:, span], grad_scores))
            grad_query = turned.T * HEAD_DIM ** (-0.5)
            cos, sin = cos_ref[qi // per, at, :], sin_ref[qi // per, at, :]
            g_ref[qi // per, 0, at, :] = (
                grad_query * cos - swap_halves(grad_query) * sin
            ).astype(BF16)

        spans(qi, first_ref[qi], run)
        return carry

    lax.fori_loop(0, 2 * per, q_step, 0)

    def finish(tile, carry):
        at = pl.ds(pl.multiple_of(lax.rem(tile, per) * TQ, TQ), TQ)
        span = pl.ds(pl.multiple_of(tile * TQ, TQ), TQ)
        cos, sin = cos_ref[tile // per, at, :], sin_ref[tile // per, at, :]
        grad_key = dk_ref[span, :]
        g_ref[tile // per, 1, at, :] = (grad_key * cos - swap_halves(grad_key) * sin).astype(BF16)
        g_ref[tile // per, 2, at, :] = dv_ref[span, :].astype(BF16)
        return carry

    lax.fori_loop(0, 2 * per, finish, 0)


def attend_back(first, qkv, grad_o, o, lse, low, cos, sin):
    _, _, rows, half = qkv.shape
    pairs = half // LANES
    tiles = 2 * rows // TQ
    side = pl.BlockSpec((2, rows, LANES), lambda p, first: (0, 0, p))
    table = pl.BlockSpec((2, rows, LANES), lambda p, first: (0, 0, 0))
    return pl.pallas_call(
        attend_back_kernel,
        grid_spec=pltpu.PrefetchScalarGridSpec(
            num_scalar_prefetch=1,
            grid=(pairs,),
            in_specs=[
                part_spec(0, rows),
                part_spec(1, rows),
                part_spec(2, rows),
                side,
                side,
                pl.BlockSpec((1, tiles, 8, 2 * TQ), lambda p, first: (p, 0, 0, 0)),
                pl.BlockSpec((tiles, 1, TQ), lambda p, first: (0, 0, 0)),
                table,
                table,
            ],
            out_specs=pl.BlockSpec((2, 3, rows, LANES), lambda p, first: (0, 0, 0, p)),
            scratch_shapes=[
                pltpu.VMEM((2 * rows, LANES), BF16),
                pltpu.VMEM((2 * rows, LANES), BF16),
                pltpu.VMEM((LANES, 2 * rows), BF16),
                pltpu.VMEM((tiles, 8, 2 * TQ), F32),
                pltpu.VMEM((2 * rows, LANES), F32),
                pltpu.VMEM((2 * rows, LANES), F32),
            ],
        ),
        out_shape=jax.ShapeDtypeStruct((2, 3, rows, half), BF16),
        compiler_params=params(62),
        cost_estimate=cost(100e9, 32 * rows * half, 12e6),
        name="attend_back",
    )(first, qkv, qkv, qkv, grad_o, o, lse, low, cos, sin)


def middle_kernel(
    total,
    first_ref,
    x_ref,
    mine_ref,
    theirs_ref,
    w_ref,
    extra_ref,
    prev_ref,
    res_ref,
    routes_ref,
    hres_ref,
    atwo_ref,
    stat_ref,
    attended_ref,
):
    mine, theirs = mine_ref[0], theirs_ref[...]
    swap = first_ref[first_ref.shape[0] - 1] != 0
    attended = jnp.concatenate(
        [jnp.where(swap, theirs, mine), jnp.where(swap, mine, theirs)], axis=1
    )
    attended_ref[...] = attended
    hres = x_ref[...].astype(F32) + dot(
        attended, jnp.concatenate([w_ref[0, 0], w_ref[0, 1]], axis=1)
    )
    hres_ref[...] = hres
    scale = lax.rsqrt(jnp.mean(hres * hres, axis=-1, keepdims=True) + EPS)
    extra = extra_ref[...]
    gain = extra[GAIN_TWO : GAIN_TWO + 1].astype(F32)
    atwo = (hres * scale * gain).astype(BF16)
    atwo_ref[...] = atwo
    logits = dot_nt(atwo, extra)
    for j in range(total):
        logits = logits + prev_ref[:, j : j + 1] * res_ref[j : j + 1, :]
    lane = iota(logits.shape, 1)

    def soft(inside):
        peak = jnp.max(jnp.where(inside, logits, -jnp.inf), axis=1, keepdims=True)
        powers = jnp.where(inside, jnp.exp(jnp.where(inside, logits - peak, 0.0)), 0.0)
        return powers / jnp.sum(powers, axis=1, keepdims=True)

    probs = soft(lane < total)
    stat = probs
    for j in range(2):
        start = total + 2 * j
        stat = stat + soft((lane >= start) & (lane < start + 2))
    stat = jnp.where(lane == total + 4, scale, stat)
    for k in range(2):
        gate = jnp.sum(
            jnp.where(lane == routes_ref[:, k : k + 1], probs, 0.0), axis=1, keepdims=True
        )
        stat = jnp.where(lane == total + 5 + k, gate, stat)
    stat_ref[...] = stat


def middle(total, first, x, o, theirs, w_shared, extra, prev, res, routes):
    rows, width = x.shape
    token = lambda i: (i, 0)
    whole = lambda i: (0, 0)
    return pl.pallas_call(
        functools.partial(middle_kernel, total),
        grid=(rows // TB,),
        in_specs=[
            pl.BlockSpec(memory_space=pltpu.SMEM),
            pl.BlockSpec((TB, width), token),
            pl.BlockSpec((1, TB, width // 2), lambda i: (1, i, 0)),
            pl.BlockSpec((TB, width // 2), token),
            pl.BlockSpec((1, 2, width, width // 2), lambda i: (3, 0, 0, 0)),
            pl.BlockSpec((LANES, width), whole),
            pl.BlockSpec((TB, total), token),
            pl.BlockSpec((total, LANES), whole),
            pl.BlockSpec((TB, 2), token),
        ],
        out_specs=[
            pl.BlockSpec((TB, width), token),
            pl.BlockSpec((TB, width), token),
            pl.BlockSpec((TB, LANES), token),
            pl.BlockSpec((TB, width), token),
        ],
        out_shape=(
            jax.ShapeDtypeStruct((rows, width), F32),
            jax.ShapeDtypeStruct((rows, width), BF16),
            jax.ShapeDtypeStruct((rows, LANES), F32),
            jax.ShapeDtypeStruct((rows, width), BF16),
        ),
        compiler_params=params(62),
        cost_estimate=cost(2 * rows * width * width, 2 * width * width + 10 * rows * width),
        name="middle",
    )(first, x, o, theirs, w_shared, extra, prev, res, routes)


def expert_kernel(
    total,
    flat_ref,
    atwo_ref,
    dy_ref,
    stat_ref,
    wide_ref,
    wd_ref,
    flow_ref,
    drow_ref,
    gw_ref,
    send_x,
    send_g,
    all_x,
    all_g,
    send_gate,
    all_gate,
    acc_ref,
    z_ref,
    a_ref,
    b_ref,
    turned_ref,
    turned_g,
    kept_ref,
    wide_buf,
    down_buf,
    wide_given,
    wide_taken,
    down_given,
    down_taken,
    dy_sems,
    x_sems,
    g_sems,
    flow_sems,
    drow_sems,
    local_sems,
    weight_sems,
    wide_sems,
    down_sems,
):
    experts, cap, width = all_x.shape
    slots = experts * cap
    chunks = z_ref.shape[0]
    per = chunks // 2
    half = width // 2
    slabs, rows_out = gw_ref.shape[:2]
    deep = chunks * FC // slabs
    me, core = lax.axis_index("expert"), lax.axis_index("context")

    def down_pieces(chunk):
        if deep == FC:
            rows = pl.ds(pl.multiple_of(chunk * rows_out, rows_out), rows_out)
            return [
                (
                    wd_ref.at[side, rows, 2 * per * FC + b * deep : 2 * per * FC + (b + 1) * deep],
                    side * half + b * rows_out,
                    rows_out,
                )
                for side in range(2)
                for b in range(half // rows_out)
            ]
        at = pl.ds(pl.multiple_of(chunk * FC, FC), FC)
        return [(wd_ref.at[side, :, at], side * half, half) for side in range(2)]

    def weights(step):
        chunk, slot = lax.rem(step, chunks), lax.rem(step, 2)
        gate_at = pl.ds(pl.multiple_of(lax.rem(chunk, per) * FC, FC), FC)
        up_at = pl.ds(pl.multiple_of((per + lax.rem(chunk, per)) * FC, FC), FC)
        return (
            pltpu.make_async_copy(
                wide_ref.at[chunk // per, :, gate_at], wide_buf.at[slot, 0], weight_sems.at[slot, 0]
            ),
            pltpu.make_async_copy(
                wide_ref.at[chunk // per, :, up_at], wide_buf.at[slot, 1], weight_sems.at[slot, 1]
            ),
        ) + tuple(
            pltpu.make_async_copy(
                source, down_buf.at[slot, at : at + size, :], weight_sems.at[slot, 2 + i]
            )
            for i, (source, at, size) in enumerate(down_pieces(chunk))
        )

    def next_weights(step):
        @pl.when(step + 1 < 4 * chunks)
        def _():
            for copy in weights(step + 1):
                copy.start()

        for copy in weights(step):
            copy.wait()

    for copy in weights(0):
        copy.start()
    greet_all(("context", "expert"))

    for j in range(experts):
        pltpu.make_async_copy(
            dy_ref.at[lax.rem(me + experts - j, experts)], all_g.at[j], dy_sems.at[j]
        ).start()
    gates = stat_ref[...].T
    x_copies, g_copies = {}, {}
    for j in list(range(1, experts)) + [0]:
        target = lax.rem(me + j, experts)
        first, second = hot_slots(flat_ref, cap, target)
        rows = dot(jnp.where(first | second, 1.0, 0.0).astype(BF16), atwo_ref[...]).astype(BF16)
        gate = jnp.sum(
            jnp.where(first, gates[total + 5 : total + 6], 0.0)
            + jnp.where(second, gates[total + 6 : total + 7], 0.0),
            axis=1,
            keepdims=True,
        )
        gate = jnp.broadcast_to(gate, (cap, LANES)).T[:8]
        if j == 0:
            all_x[0] = rows
            all_gate[0] = gate
        else:
            send_gate[j - 1] = gate
            send_x[j - 1] = rows
            g_copies[j] = remote(
                send_gate.at[j - 1], all_gate.at[j], g_sems, (j - 1,), {"expert": target}
            )
            x_copies[j] = remote(
                send_x.at[j - 1], all_x.at[j], x_sems, (j - 1,), {"expert": target}
            )
            g_copies[j].start()
            x_copies[j].start()

    def weigh(j):
        pltpu.make_async_copy(
            dy_ref.at[lax.rem(me + experts - j, experts)], all_g.at[j], dy_sems.at[j]
        ).wait()
        gate = jnp.broadcast_to(all_gate[j, 0:1, :], (LANES, cap)).T[:, 0:1]
        all_g[j] = (all_g[j].astype(F32) * gate).astype(BF16)

    def back(buffer, dest, sems, j):
        return remote(
            buffer.at[j - 1],
            dest.at[me],
            sems,
            (j - 1,),
            {"expert": lax.rem(me + experts - j, experts)},
        )

    acc_ref[...] = jnp.zeros_like(acc_ref)

    def up(first, last, at):
        span = slice(first * cap, last * cap)

        def one(step, carry):
            next_weights(step + at * chunks)
            slot = lax.rem(step + at * chunks, 2)
            rows = all_x[first:last].reshape((last - first) * cap, width)
            gate = dot(rows, wide_buf[slot, 0])
            lift = dot(rows, wide_buf[slot, 1])
            sig = 1.0 / (1.0 + jnp.exp(-gate))
            swish = gate * sig
            hidden = (swish * lift).astype(BF16)
            z_ref[step, span] = hidden
            a_ref[step, span] = (lift * sig * (1.0 + gate * (1.0 - sig))).astype(BF16)
            b_ref[step, span] = swish.astype(BF16)
            acc_ref[span, :] += dot_nt(hidden, down_buf[slot])
            return carry

        lax.fori_loop(0, chunks, one, 0)

    def down(first, last, at):
        span = slice(first * cap, last * cap)

        def one(step, carry):
            next_weights(step + at * chunks)
            slot = lax.rem(step + at * chunks, 2)
            dz = dot(all_g[first:last].reshape((last - first) * cap, width), down_buf[slot])
            dg = (dz * a_ref[step, span].astype(F32)).astype(BF16)
            du = (dz * b_ref[step, span].astype(F32)).astype(BF16)
            a_ref[step, span] = dg
            b_ref[step, span] = du
            acc_ref[span, :] += dot_nt(dg, wide_buf[slot, 0]) + dot_nt(du, wide_buf[slot, 1])
            return carry

        lax.fori_loop(0, chunks, one, 0)

    def keep_own(buffer, dest, index):
        buffer[experts - 1] = acc_ref[:cap, :].astype(BF16)
        copy = pltpu.make_async_copy(
            buffer.at[experts - 1], dest.at[me], local_sems.at[index]
        )
        copy.start()
        return copy

    weigh(0)
    up(0, 1, 0)
    own = [keep_own(send_x, flow_ref, 0)]
    acc_ref[:cap, :] = jnp.zeros((cap, width), F32)
    down(0, 1, 1)
    own.append(keep_own(send_g, drow_ref, 1))
    for j in range(1, experts):
        g_copies[j].wait()
        weigh(j)
    turned_g[...] = all_g[...].reshape(slots, width).T
    for j in range(1, experts):
        x_copies[j].wait()
    up(1, experts, 2)
    for j in range(1, experts):
        send_x[j - 1] = acc_ref[j * cap : (j + 1) * cap, :].astype(BF16)
        back(send_x, flow_ref, flow_sems, j).start()
    turned_ref[...] = all_x[...].reshape(slots, width).T
    acc_ref[cap:, :] = jnp.zeros((slots - cap, width), F32)
    down(1, experts, 3)
    for j in range(1, experts):
        send_g[j - 1] = acc_ref[j * cap : (j + 1) * cap, :].astype(BF16)
        back(send_g, drow_ref, drow_sems, j).start()

    def wide_copy(step):
        return remote(
            wide_given.at[step],
            wide_taken.at[step],
            wide_sems,
            (step,),
            {"context": 1 - core},
        )

    def down_copy(step):
        chunk = lax.rem((1 - core) * per + step, chunks)
        return remote(
            down_given.at[step],
            down_taken.at[chunk],
            down_sems,
            (chunk,),
            {"context": 1 - core},
        )

    def products(step):
        chunk = lax.rem((1 - core) * per + step, chunks)
        gate = dot(turned_ref[...], a_ref[chunk])
        lift = dot(turned_ref[...], b_ref[chunk])
        low = dot(turned_g[...], z_ref[chunk])
        top, bottom = low[:half], low[half:]
        down_given[step] = jnp.where(core == 0, bottom, top).astype(BF16)
        kept_ref[chunk] = jnp.where(core == 0, top, bottom).astype(BF16)
        down_copy(step).start()
        return gate, lift

    def give(step, carry):
        gate, lift = products(step)
        wide_given[step, 0] = gate.astype(BF16)
        wide_given[step, 1] = lift.astype(BF16)
        wide_copy(step).start()
        return carry

    lax.fori_loop(0, per, give, 0)

    def keep(step, carry):
        gate, lift = products(step)
        wide_copy(step - per).wait_recv()
        for i, value in enumerate((gate, lift)):
            at = pl.ds(pl.multiple_of((i * per + step - per) * FC, FC), FC)
            value = value + wide_taken[step - per, i].astype(F32)
            gw_ref[:, :, at] = value.reshape(slabs, rows_out, FC).astype(BF16)
        return carry

    lax.fori_loop(per, chunks, keep, 0)

    def settle(step, carry):
        other = lax.rem(core * per + step, chunks)
        copy = remote(
            down_given.at[step],
            down_taken.at[other],
            down_sems,
            (other,),
            {"context": 1 - core},
        )
        copy.wait_recv()
        value = kept_ref[other].astype(F32) + down_taken[other].astype(F32)
        for b in range(half // rows_out):
            part = value[b * rows_out : (b + 1) * rows_out]
            start = 2 * per * FC + b * deep
            if FC <= deep:
                inside = lax.rem(other, deep // FC) * FC
                at = pl.ds(pl.multiple_of(start + inside, FC), FC)
                gw_ref[other // (deep // FC), :, at] = part.astype(BF16)
            else:
                for i in range(FC // deep):
                    gw_ref[other * (FC // deep) + i, :, start : start + deep] = part[
                        :, i * deep : (i + 1) * deep
                    ].astype(BF16)
        return carry

    lax.fori_loop(0, chunks, settle, 0)

    for copy in own:
        copy.wait()
    for j in range(1, experts):
        back(send_x, flow_ref, flow_sems, j).wait()
        back(send_g, drow_ref, drow_sems, j).wait()

    def sent(step, carry):
        down_copy(step).wait_send()
        return carry

    lax.fori_loop(0, chunks, sent, 0)
    lax.fori_loop(0, per, lambda step, carry: (wide_copy(step).wait_send(), carry)[1], 0)


def run_experts(total, experts, slabs, hidden, cap, flat_t, atwo, dy, stat, wide, wd):
    rows, width = atwo.shape
    chunks = hidden // FC
    per = chunks // 2
    half = width // 2
    slots = experts * cap
    vmem = pl.BlockSpec(memory_space=pltpu.VMEM)
    anywhere = pl.BlockSpec(memory_space=pl.ANY)
    dma = pltpu.SemaphoreType.DMA
    return pl.pallas_call(
        functools.partial(expert_kernel, total),
        in_specs=[vmem] * 2 + [anywhere, vmem] + [anywhere] * 2,
        out_specs=[anywhere] * 2 + [vmem],
        out_shape=(
            jax.ShapeDtypeStruct((experts, cap, width), BF16),
            jax.ShapeDtypeStruct((experts, cap, width), BF16),
            jax.ShapeDtypeStruct((slabs, width // slabs, 3 * hidden // 2), BF16),
        ),
        scratch_shapes=[
            pltpu.VMEM((experts, cap, width), BF16),
            pltpu.VMEM((experts, cap, width), BF16),
            pltpu.VMEM((experts, cap, width), BF16),
            pltpu.VMEM((experts, cap, width), BF16),
            pltpu.VMEM((experts - 1, 8, cap), F32),
            pltpu.VMEM((experts, 8, cap), F32),
            pltpu.VMEM((slots, width), F32),
            pltpu.VMEM((chunks, slots, FC), BF16),
            pltpu.VMEM((chunks, slots, FC), BF16),
            pltpu.VMEM((chunks, slots, FC), BF16),
            pltpu.VMEM((width, slots), BF16),
            pltpu.VMEM((width, slots), BF16),
            pltpu.VMEM((chunks, half, FC), BF16),
            pltpu.VMEM((2, 2, width, FC), BF16),
            pltpu.VMEM((2, width, FC), BF16),
            pltpu.VMEM((per, 2, width, FC), BF16),
            pltpu.VMEM((per, 2, width, FC), BF16),
            pltpu.VMEM((chunks, half, FC), BF16),
            pltpu.VMEM((chunks, half, FC), BF16),
            dma((experts,)),
            dma((2, experts - 1)),
            dma((2, experts - 1)),
            dma((2, experts - 1)),
            dma((2, experts - 1)),
            dma((2,)),
            dma((2, 6)),
            dma((2, per)),
            dma((2, chunks)),
        ],
        compiler_params=pltpu.CompilerParams(
            collective_id=2, has_side_effects=True, vmem_limit_bytes=62 * MIB
        ),
        cost_estimate=cost(18 * slots * width * hidden, 30 * width * hidden),
        name="experts",
    )(flat_t, atwo, dy, stat, wide, wd)


def combine_kernel(
    experts,
    total,
    flow_ref,
    drow_ref,
    flat_ref,
    stat_ref,
    flat_t_ref,
    hres_ref,
    atwo_ref,
    dy_ref,
    o_ref,
    extra_ref,
    w_ref,
    prev_ref,
    out_ref,
    dh_ref,
    dolow_ref,
    gw_ref,
    small_ref,
    right_ref,
    picked_ref,
    summed_ref,
    sums_ref,
    columns_ref,
    dhlow_ref,
    stage_ref,
    own_sems,
    dolow_sems,
):
    step = pl.program_id(0)
    core = lax.axis_index("context")

    @pl.when(step == 0)
    def _():
        greet_all(("context",))

    def dolow_copies(block):
        rows = pl.ds(pl.multiple_of(block * TB, TB), TB)
        return (
            pltpu.make_async_copy(
                stage_ref.at[core, rows], dolow_ref.at[core, rows], own_sems.at[block]
            ),
            remote(
                stage_ref.at[1 - core, rows],
                dolow_ref.at[core, rows],
                dolow_sems,
                (block,),
                {"context": 1 - core},
            ),
        )

    slots, width = flow_ref.shape
    half = width // 2
    gain = extra_ref[GAIN_TWO : GAIN_TWO + 1].astype(F32)
    vecs = [extra_ref[VECS + j : VECS + j + 1].astype(F32) for j in range(2)]

    @pl.when(step == 0)
    def _():
        right_ref[:slots] = drow_ref[...]
        right_ref[slots:] = extra_ref[...]

    spread_out = iota((TB, slots), 1)
    hots = [
        jnp.where(flat_ref[:, k : k + 1] == spread_out, 1.0, 0.0).astype(BF16) for k in range(2)
    ]
    for k in range(2):
        picked_ref[k] = dot(hots[k], flow_ref[...])
    vec_dot = dot_nt(dy_ref[...], extra_ref[...])
    lane = iota((RC, LANES), 1)
    for start in range(0, TB, RC):
        at = slice(start, start + RC)
        dy = dy_ref[at].astype(F32)
        ntwo = hres_ref[at] * stat_ref[at, total + 4 : total + 5] * gain
        sums = vec_dot[at]
        for i, part in enumerate((ntwo, picked_ref[0, at], picked_ref[1, at])):
            sums = jnp.where(lane == i, jnp.sum(dy * part, axis=1, keepdims=True), sums)
        sums_ref[at] = sums

    sums, stats = sums_ref[...].T, stat_ref[...].T
    row = lambda i: stats[i : i + 1]
    dot_normed, dot_picked = sums[0:1], [sums[1:2], sums[2:3]]
    dot_vecs = [sums[VECS + j : VECS + j + 1] for j in range(2)]
    gates = [row(total + 5 + k) for k in range(2)]
    mixes = [[row(total + 2 * j + i) for i in range(2)] for j in range(2)]
    routes = [flat_t_ref[2 + k : 3 + k] for k in range(2)]
    copies = [jnp.where(route == experts + 1, 1.0, 0.0) for route in routes]
    consts = [
        [jnp.where(route == experts + 2 + j, 1.0, 0.0) for j in range(2)] for route in routes
    ]
    pulls = [mixes[j][0] * dot_normed + mixes[j][1] * dot_vecs[j] for j in range(2)]
    sub = iota((total, TB), 0).astype(F32)
    dpgate = jnp.zeros((total, TB), F32)
    for k in range(2):
        dgate = dot_picked[k] + copies[k] * dot_normed
        dgate = dgate + consts[k][0] * pulls[0] + consts[k][1] * pulls[1]
        dpgate = dpgate + jnp.where(sub == routes[k], dgate, 0.0)
    pgate = stats[:total]
    dlogit = pgate * (dpgate - jnp.sum(pgate * dpgate, axis=0, keepdims=True))
    weight = gates[0] * copies[0] + gates[1] * copies[1]
    dmix, shares, pieces = [], [], []
    for j in range(2):
        const = gates[0] * consts[0][j] + gates[1] * consts[1][j]
        grads = [const * dot_normed, const * dot_vecs[j]]
        inner = mixes[j][0] * grads[0] + mixes[j][1] * grads[1]
        dmix += [mixes[j][i] * (grads[i] - inner) for i in range(2)]
        weight = weight + const * mixes[j][0]
        share = const * mixes[j][1]
        shares.append(share)
        for i in range(3):
            pieces.append(share.astype(BF16).astype(F32))
            share = share - pieces[-1]
    empty = jnp.zeros((1, TB), F32)
    droute_t = jnp.concatenate([dlogit] + dmix + [empty] * (12 - total), axis=0).astype(BF16)
    rows = jnp.concatenate(
        [dlogit] + dmix + [weight] + shares + [jnp.zeros((LANES - total - 7, TB), F32)], axis=0
    )
    columns_ref[...] = rows.T
    for start in range(0, TB, RC):
        at = slice(start, start + RC)
        hres = hres_ref[at]
        ntwo = hres * stat_ref[at, total + 4 : total + 5] * gain
        out = hres + columns_ref[at, total + 4 : total + 5] * ntwo
        for k in range(2):
            out = out + stat_ref[at, total + 5 + k : total + 6 + k] * picked_ref[k, at]
        for j in range(2):
            out = out + columns_ref[at, total + 5 + j : total + 6 + j] * vecs[j]
        out_ref[at] = out.astype(BF16)

    lane = iota((TB, LANES), 1)
    droute = jnp.where(lane < total + 4, columns_ref[...], 0.0).astype(BF16)
    summed_ref[...] = dot(
        jnp.concatenate([hots[0] + hots[1], droute], axis=1), right_ref[...]
    )
    gain_row = jnp.zeros((1, width), F32)
    for start in range(0, TB, RC):
        at = slice(start, start + RC)
        hres = hres_ref[at]
        dy = dy_ref[at].astype(F32)
        scale = stat_ref[at, total + 4 : total + 5]
        dntwo = columns_ref[at, total + 4 : total + 5] * dy + summed_ref[at]
        both = hres * dntwo
        inner = jnp.sum(both * gain, axis=1, keepdims=True) * (1.0 / width)
        dh = dy + dntwo * gain * scale - hres * (scale * scale * scale * inner)
        gain_row = gain_row + jnp.sum(both * scale, axis=0, keepdims=True)
        dh_ref[at] = dh
        dhlow_ref[pl.ds(pl.multiple_of(step * TB + start, RC), RC), :] = dh.astype(BF16)
    w_out = jnp.concatenate([w_ref[0, 0], w_ref[0, 1]], axis=1)
    dolow = dot_nt(dhlow_ref[pl.ds(pl.multiple_of(step * TB, TB), TB), :], w_out).astype(BF16)
    rows_at = pl.ds(pl.multiple_of(step * TB, TB), TB)
    stage_ref[0, rows_at] = dolow[:, :half]
    stage_ref[1, rows_at] = dolow[:, half:]
    for copy in dolow_copies(step):
        copy.start()
    route_rows = dot(droute_t, atwo_ref[...])
    vec_parts = dot(
        jnp.concatenate(pieces + [empty] * 2, axis=0).astype(BF16), dy_ref[...]
    )
    vec_rows = [
        vec_parts[3 * j : 3 * j + 1] + vec_parts[3 * j + 1 : 3 * j + 2] + vec_parts[3 * j + 2 : 3 * j + 3]
        for j in range(2)
    ]
    res_rows = jnp.dot(dlogit, prev_ref[...], precision=HIGH, preferred_element_type=F32)
    res_rows = jnp.concatenate([res_rows, jnp.zeros((total, width - total), F32)], axis=1)
    small = jnp.concatenate(
        [route_rows[: total + 4], gain_row] + vec_rows + [jnp.zeros((1, width), F32), res_rows],
        axis=0,
    )

    @pl.when(step == 0)
    def _():
        small_ref[...] = small

    @pl.when(step > 0)
    def _():
        small_ref[...] += small

    @pl.when(step == pl.num_programs(0) - 1)
    def _():
        for side in range(2):
            at = slice(side * half, (side + 1) * half)
            weight = dot(o_ref[:, at].T, dhlow_ref[...]).astype(BF16)
            gw_ref[0, at] = weight[:, :half]
            gw_ref[1, at] = weight[:, half:]
        for block in range(dhlow_ref.shape[0] // TB):
            for copy in dolow_copies(block):
                copy.wait()


def combine(experts, total, flow, drow, flat, stat, flat_t, hres, atwo, dy, o, w_shared, extra, prev):
    rows, width = hres.shape
    slots = flow.shape[0]
    half = width // 2
    token = lambda i: (i, 0)
    whole = lambda i: (0, 0)
    weight = pl.BlockSpec((2, width, half), lambda i: (0, 0, 0))
    small_rows = 2 * total + 8
    return pl.pallas_call(
        functools.partial(combine_kernel, experts, total),
        grid=(rows // TB,),
        in_specs=[
            pl.BlockSpec((slots, width), whole),
            pl.BlockSpec((slots, width), whole),
            pl.BlockSpec((TB, LANES), token),
            pl.BlockSpec((TB, LANES), token),
            pl.BlockSpec((8, TB), lambda i: (0, i)),
            pl.BlockSpec((TB, width), token),
            pl.BlockSpec((TB, width), token),
            pl.BlockSpec((TB, width), token),
            pl.BlockSpec((rows, width), whole),
            pl.BlockSpec((LANES, width), whole),
            pl.BlockSpec((1, 2, width, half), lambda i: (3, 0, 0, 0)),
            pl.BlockSpec((TB, total), token),
        ],
        out_specs=[
            pl.BlockSpec((TB, width), token),
            pl.BlockSpec((TB, width), token),
            pl.BlockSpec(memory_space=pl.ANY),
            weight,
            pl.BlockSpec((small_rows, width), whole),
        ],
        out_shape=(
            jax.ShapeDtypeStruct((rows, width), BF16),
            jax.ShapeDtypeStruct((rows, width), F32),
            jax.ShapeDtypeStruct((2, rows, half), BF16),
            jax.ShapeDtypeStruct((2, width, half), BF16),
            jax.ShapeDtypeStruct((small_rows, width), F32),
        ),
        scratch_shapes=[
            pltpu.VMEM((slots + LANES, width), BF16),
            pltpu.VMEM((2, TB, width), F32),
            pltpu.VMEM((TB, width), F32),
            pltpu.VMEM((TB, LANES), F32),
            pltpu.VMEM((TB, LANES), F32),
            pltpu.VMEM((rows, width), BF16),
            pltpu.VMEM((2, rows, half), BF16),
            pltpu.SemaphoreType.DMA((rows // TB,)),
            pltpu.SemaphoreType.DMA((2, rows // TB)),
        ],
        compiler_params=pltpu.CompilerParams(
            collective_id=3, has_side_effects=True, vmem_limit_bytes=62 * MIB
        ),
        cost_estimate=cost(
            6 * rows * slots * width + 4 * rows * width * width, 30 * rows * width + 8 * width * width
        ),
        name="combine",
    )(flow, drow, flat, stat, flat_t, hres, atwo, dy, o, extra, w_shared, prev)


def tail_kernel(
    gain_at,
    sent_ref,
    aone_ref,
    w_ref,
    extra_ref,
    x_ref,
    dh_ref,
    gwo_ref,
    small_ref,
    out_ref,
    final,
    small_out_ref,
    both,
    grads,
    w_buf,
    x_buf,
    dh_buf,
    out_buf,
    core_in,
    plane_out,
    plane_in,
    slab_out,
    slab_in,
    own_ref,
    small_own,
    small_core,
    small_plane,
    small_slab,
    load_sems,
    store_sems,
    both_sems,
    core_sems,
    plane_sems,
    slab_sems,
    final_sems,
    pass_sems,
    small_core_sems,
    small_plane_sems,
    small_slab_sems,
):
    experts = lax.axis_size("expert")
    slabs = lax.axis_size("dp")
    me, core, slab = lax.axis_index("expert"), lax.axis_index("context"), lax.axis_index("dp")
    other = 1 - core
    tokens, width = x_buf.shape
    half = width // 2
    parts = 2
    block = tokens // parts

    mine = pltpu.make_async_copy(sent_ref.at[core], both.at[core], load_sems.at[0])
    mine.start()
    loads = [
        pltpu.make_async_copy(w_ref.at[pl.ds(0, 3)], w_buf, load_sems.at[1]),
        pltpu.make_async_copy(x_ref, x_buf, load_sems.at[2]),
        pltpu.make_async_copy(dh_ref, dh_buf, load_sems.at[3]),
    ]
    for copy in loads:
        copy.start()
    greet_all(("context", "expert", "dp"))
    theirs = [
        remote(
            sent_ref.at[other, which],
            both.at[core, which],
            both_sems,
            (which,),
            {"context": other},
        )
        for which in range(3)
    ]
    for copy in theirs:
        copy.start()

    def core_copy(which):
        return remote(
            grads.at[other, which], core_in.at[which], core_sems, (which,), {"context": other}
        )

    for side in range(2):
        grads[side, 3] = gwo_ref[side]
    core_copy(3).start()

    def plane_copy(j, at):
        return remote(
            plane_out.at[j - 1, at],
            plane_in.at[j - 1, at],
            plane_sems,
            (j - 1, at),
            {"expert": lax.rem(me + j, experts)},
        )

    def pass_on(which):
        core_copy(which).wait_recv()
        j = lax.rem(which + experts - me, experts)

        @pl.when(j != 0)
        def _():
            def one(k):
                at = lax.rem(slab + k + 1, slabs)
                plane_out[j - 1, at] = (
                    grads[core, which, at].astype(F32) + core_in[which, at].astype(F32)
                ).astype(BF16)
                plane_copy(j, at).start()

            loop(slabs, one)

    mine.wait()
    turned = aone_ref[...].T
    for which in range(3):
        theirs[which].wait_recv()
        grad = jnp.concatenate([both[0, which], both[1, which]], axis=1)
        weight = dot(turned, grad)
        for side in range(2):
            grads[side, which] = (
                weight[:, side * half : (side + 1) * half]
                .reshape(slabs, width // slabs, half)
                .astype(BF16)
            )
        core_copy(which).start()
        pass_on((which + 3) % 4)
    for copy in loads:
        copy.wait()

    gain = extra_ref[GAIN_ONE : GAIN_ONE + 1].astype(F32)
    stores = []
    gain_row = jnp.zeros((1, width), F32)
    for part in range(parts):
        at = slice(part * block, (part + 1) * block)
        dnone = None
        for which in range(3):
            grad = jnp.concatenate([both[0, which, at], both[1, which, at]], axis=1)
            whole = jnp.concatenate([w_buf[which, 0], w_buf[which, 1]], axis=1)
            product = dot_nt(grad, whole)
            dnone = product if dnone is None else dnone + product
        values = x_buf[at].astype(F32)
        scale = lax.rsqrt(jnp.mean(values * values, axis=-1, keepdims=True) + EPS)
        scaled = dnone * gain
        inner = jnp.mean(values * scaled, axis=1, keepdims=True)
        out_buf[at] = dh_buf[at] + scale * scaled - values * (scale * scale * scale * inner)
        stores.append(
            pltpu.make_async_copy(out_buf.at[at], out_ref.at[at], store_sems.at[part])
        )
        stores[-1].start()
        gain_row = gain_row + jnp.sum(dnone * values * scale, axis=0, keepdims=True)
        if part == 0:
            pass_on(2)

    row = iota(small_ref.shape, 0)
    small_own[...] = small_ref[...] + jnp.where(row == gain_at, gain_row, 0.0)
    small_copy = remote(small_own, small_core, small_core_sems, (0,), {"context": other})
    small_copy.start()
    small_copy.wait()
    small_plane[me] = small_own[...] + small_core[...]
    small_plane_copies = []
    for j in range(1, experts):
        small_plane_copies.append(
            remote(
                small_plane.at[me],
                small_plane.at[me],
                small_plane_sems,
                (j,),
                {"expert": lax.rem(me + j, experts)},
            )
        )
        small_plane_copies[-1].start()

    def gathered(at):
        value = grads[core, me, at].astype(F32) + core_in[me, at].astype(F32)
        for j in range(1, experts):
            plane_copy(j, at).wait_recv()
            value = value + plane_in[j - 1, at].astype(F32)
        return value

    def slab_copy(k):
        return remote(
            slab_out.at[k],
            slab_in.at[k],
            slab_sems,
            (k,),
            {"dp": lax.rem(slab + k + 1, slabs)},
        )

    def scatter(k):
        slab_out[k] = gathered(lax.rem(slab + k + 1, slabs)).astype(BF16)
        slab_copy(k).start()

    loop(slabs - 1, scatter)

    for copy in small_plane_copies:
        copy.wait()
    value = small_plane[0]
    for j in range(1, experts):
        value = value + small_plane[j]
    small_slab[slab] = value

    def small_slab_copy(k):
        return remote(
            small_slab.at[slab],
            small_slab.at[slab],
            small_slab_sems,
            (k,),
            {"dp": lax.rem(slab + k + 1, slabs)},
        )

    loop(slabs - 1, lambda k: small_slab_copy(k).start())

    own_ref[...] = gathered(slab)

    def collect(k):
        slab_copy(k).wait_recv()
        own_ref[...] += slab_in[k].astype(F32)

    loop(slabs - 1, collect)
    final[core, me] = own_ref[...].astype(BF16)
    final_copies, pass_copies = [], []
    for j in range(1, experts):
        final_copies.append(
            remote(
                final.at[core, me],
                final.at[core, me],
                final_sems,
                (j,),
                {"expert": lax.rem(me + j, experts)},
            )
        )
        final_copies[-1].start()
    for j in range(experts):
        source = lax.rem(me + experts - j, experts)
        if j > 0:
            final_copies[j - 1].wait_recv()
        pass_copies.append(
            remote(
                final.at[core, source],
                final.at[core, source],
                pass_sems,
                (j,),
                {"context": other},
            )
        )
        pass_copies[-1].start()

    loop(slabs - 1, lambda k: small_slab_copy(k).wait())
    small_out_ref[...] = small_slab[0]

    def add_small(k):
        small_out_ref[...] += small_slab[k + 1]

    loop(slabs - 1, add_small)

    for copy in pass_copies:
        copy.wait_recv()
    for copy in stores:
        copy.wait()
    for which in range(4):
        core_copy(which).wait_send()
    for j in range(1, experts):

        def sent(k, j=j):
            plane_copy(j, k).wait_send()

        loop(slabs, sent)
    loop(slabs - 1, lambda k: slab_copy(k).wait_send())
    for copy in theirs + final_copies + pass_copies:
        copy.wait_send()


def tail(experts, slabs, gain_at, sent, aone, w_shared, extra, x, dh, gwo, small):
    tokens, width = x.shape
    half = width // 2
    rows = width // slabs
    vmem = pl.BlockSpec(memory_space=pltpu.VMEM)
    anywhere = pl.BlockSpec(memory_space=pl.ANY)
    dma = pltpu.SemaphoreType.DMA
    return pl.pallas_call(
        functools.partial(tail_kernel, gain_at),
        in_specs=[anywhere, vmem, anywhere, vmem, anywhere, anywhere] + [vmem] * 2,
        out_specs=[anywhere] + [vmem] * 2,
        out_shape=(
            jax.ShapeDtypeStruct((tokens, width), F32),
            jax.ShapeDtypeStruct((2, experts, rows, half), BF16),
            jax.ShapeDtypeStruct(small.shape, F32),
        ),
        scratch_shapes=[
            pltpu.VMEM((2, 3, tokens, half), BF16),
            pltpu.VMEM((2, 4, slabs, rows, half), BF16),
            pltpu.VMEM((3, 2, width, half), BF16),
            pltpu.VMEM((tokens, width), BF16),
            pltpu.VMEM((tokens, width), F32),
            pltpu.VMEM((tokens, width), F32),
            pltpu.VMEM((4, slabs, rows, half), BF16),
            pltpu.VMEM((experts - 1, slabs, rows, half), BF16),
            pltpu.VMEM((experts - 1, slabs, rows, half), BF16),
            pltpu.VMEM((slabs - 1, rows, half), BF16),
            pltpu.VMEM((slabs - 1, rows, half), BF16),
            pltpu.VMEM((rows, half), F32),
            pltpu.VMEM(small.shape, F32),
            pltpu.VMEM(small.shape, F32),
            pltpu.VMEM((experts,) + small.shape, F32),
            pltpu.VMEM((slabs,) + small.shape, F32),
            dma((4,)),
            dma((2,)),
            dma((2, 3)),
            dma((2, 4)),
            dma((2, experts - 1, slabs)),
            dma((2, slabs - 1)),
            dma((2, experts)),
            dma((2, experts)),
            dma((2, 1)),
            dma((2, experts)),
            dma((2, slabs - 1)),
        ],
        compiler_params=pltpu.CompilerParams(
            collective_id=0, has_side_effects=True, vmem_limit_bytes=62 * MIB
        ),
        cost_estimate=cost(12 * tokens * width * width, 40 * tokens * width),
        name="tail",
    )(sent, aone, w_shared, extra, x, dh, gwo, small)


def finish_kernel(
    total,
    place_ref,
    small_ref,
    final_ref,
    mine_ref,
    theirs_ref,
    tokens_ref,
    layer_ref,
    norm_one_ref,
    norm_two_ref,
    router_ref,
    mix_ref,
    vec_ref,
    res_ref,
    q_ref,
    k_ref,
    v_ref,
    o_ref,
    gate_ref,
    up_ref,
    gd_ref,
    tokens_out_ref,
    layer_out_ref,
    tokens_buf,
    layer_buf,
    final_buf,
    share_buf,
    square_buf,
    gate_buf,
    up_buf,
    gd_buf,
    turned_ref,
    load_sems,
    store_sems,
):
    rows, half = final_buf.shape[2:]
    wide = share_buf.shape[2] // 3
    deep = gd_buf.shape[0]
    core = place_ref[1]
    loads = [
        pltpu.make_async_copy(mine_ref, share_buf.at[0], load_sems.at[0]),
        pltpu.make_async_copy(theirs_ref, share_buf.at[1], load_sems.at[1]),
        pltpu.make_async_copy(final_ref, final_buf, load_sems.at[2]),
        pltpu.make_async_copy(tokens_ref, tokens_buf, load_sems.at[3]),
        pltpu.make_async_copy(layer_ref, layer_buf, load_sems.at[4]),
    ]
    for copy in loads[3:] + loads[:3]:
        copy.start()
    small = small_ref[...]
    fill = jnp.zeros((LANES - small.shape[0], small.shape[1]), F32)
    turned_ref[...] = jnp.concatenate([small, fill], axis=0).T
    own = turned_ref[pl.ds(pl.multiple_of(place_ref[0] * rows, 8), rows), :]
    own = own.T
    router_ref[...] = own[:total]
    mix_ref[...] = own[total : total + 4]
    norm_two_ref[...] = own[total + 4 : total + 5]
    vec_ref[...] = own[total + 5 : total + 7]
    norm_one_ref[...] = own[total + 7 : total + 8]
    res_ref[...] = turned_ref[:total, total + 8 : 2 * total + 8]

    stores = []

    def store(buffer, ref):
        stores.append(pltpu.make_async_copy(buffer, ref, store_sems.at[len(stores)]))
        stores[-1].start()

    def sides(buffer, size, left, right):
        buffer[:, :size] = left
        buffer[:, size:] = right

    def ordered(get):
        first, second = get(share_buf.at[0]), get(share_buf.at[1])
        swap = core != 0
        return jnp.where(swap, second, first), jnp.where(swap, first, second)

    loads[3].wait()
    store(tokens_buf, tokens_out_ref)
    loads[4].wait()
    store(layer_buf, layer_out_ref)
    for copy in loads[:2]:
        copy.wait()
    sides(gate_buf, wide, *ordered(lambda ref: ref[:, :wide].astype(F32)))
    store(gate_buf, gate_ref.at[0])
    sides(up_buf, wide, *ordered(lambda ref: ref[:, wide : 2 * wide].astype(F32)))
    store(up_buf, up_ref.at[0])

    def down(ref):
        blocks = [
            ref[:, 2 * wide + b * deep : 2 * wide + (b + 1) * deep].astype(F32)
            for b in range(half // rows)
        ]
        return jnp.concatenate(blocks, axis=0).T

    sides(gd_buf, half, *ordered(down))
    store(gd_buf, gd_ref.at[0])
    loads[2].wait()
    for which, ref in enumerate((q_ref, k_ref, v_ref, o_ref)):
        sides(
            square_buf.at[which],
            half,
            final_buf[0, which].astype(F32),
            final_buf[1, which].astype(F32),
        )
        store(square_buf.at[which], ref)
    for copy in stores:
        copy.wait()


def finish(total, place, final, small, mine, theirs, tokens, layer):
    rows, half = final.shape[2:]
    width = 2 * half
    wide = mine.shape[1] // 3
    deep = wide * rows // half
    anywhere = pl.BlockSpec(memory_space=pl.ANY)
    vmem = pl.BlockSpec(memory_space=pltpu.VMEM)
    shape = lambda *dims: jax.ShapeDtypeStruct(dims, F32)
    return pl.pallas_call(
        functools.partial(finish_kernel, total),
        in_specs=[pl.BlockSpec(memory_space=pltpu.SMEM), vmem] + [anywhere] * 5,
        out_specs=[vmem] * 6 + [anywhere] * 9,
        out_shape=(
            shape(1, rows),
            shape(1, rows),
            shape(total, rows),
            shape(4, rows),
            shape(2, rows),
            shape(total, total),
            shape(rows, width),
            shape(rows, width),
            shape(rows, width),
            shape(rows, width),
            shape(1, rows, 2 * wide),
            shape(1, rows, 2 * wide),
            shape(1, deep, width),
            shape(*tokens.shape),
            jax.ShapeDtypeStruct(layer.shape, BF16),
        ),
        scratch_shapes=[
            pltpu.VMEM(tokens.shape, F32),
            pltpu.VMEM(layer.shape, BF16),
            pltpu.VMEM(final.shape, BF16),
            pltpu.VMEM((2,) + mine.shape, BF16),
            pltpu.VMEM((4, rows, width), F32),
            pltpu.VMEM((rows, 2 * wide), F32),
            pltpu.VMEM((rows, 2 * wide), F32),
            pltpu.VMEM((deep, width), F32),
            pltpu.VMEM((width, LANES), F32),
            pltpu.SemaphoreType.DMA((5,)),
            pltpu.SemaphoreType.DMA((9,)),
        ],
        compiler_params=params(62),
        cost_estimate=cost(1e6, 20 * rows * width),
        name="finish",
    )(place, small, final, mine, theirs, tokens, layer)


def on_device(
    tokens,
    segments,
    routes,
    prev_logits,
    ranks,
    cotangent,
    norm_one,
    w_query,
    w_key,
    w_value,
    w_out,
    norm_two,
    router,
    w_res,
    const_mix,
    const_vec,
    w_gate,
    w_up,
    w_down,
):
    experts = lax.axis_size("expert")
    dp = lax.axis_size("dp")
    total = experts + NZ
    _, rows, width = tokens.shape
    hidden = w_gate.shape[2]
    cap = (18 * rows + 8 * total - 1) // (8 * total)
    seq = 2 * rows
    core = lax.axis_index("context")
    half = width // 2

    def mine(shard, size):
        return lax.dynamic_slice_in_dim(shard, core * size, size, 1)

    def gather(shard):
        return lax.all_gather(shard, ("context", "dp"), axis=0).reshape(
            2, dp * shard.shape[0], shard.shape[1]
        )

    extra = jnp.concatenate(
        [router, const_mix, norm_one[:, None], norm_two[:, None], const_vec], axis=1
    )
    cos, sin = (jnp.asarray(table).reshape(2, rows, LANES) for table in rope_tables(seq))
    x = tokens[0]
    dy = cotangent[0]
    w_shared, extra, flat, flat_t, low, first, qkv, aone, dy_rows = spread(
        experts,
        dp,
        cap,
        w_query,
        w_key,
        w_value,
        w_out,
        extra.astype(F32).T,
        routes[0],
        ranks[0],
        segments,
        x,
        dy,
        cos,
        sin,
    )
    w_shared = w_shared.reshape(4, 2, width, half)
    extra = extra.transpose(1, 0, 2).reshape(total + 8, width).astype(BF16)
    extra = jnp.concatenate(
        [
            extra[: total + 4],
            jnp.zeros((GAIN_ONE - total - 4, width), BF16),
            extra[total + 4 :],
            jnp.zeros((LANES - GAIN_ONE - 4, width), BF16),
        ],
        axis=0,
    )
    wide_mine = [mine(w_gate[0], hidden // 2), mine(w_up[0], hidden // 2)]
    down_mine = mine(w_down[0], half)
    deep = hidden // dp
    if deep == FC:
        turned = down_mine.T.reshape(-1, width // dp, deep).transpose(1, 0, 2)
        wide_w = gather(jnp.concatenate(wide_mine + [turned.reshape(width // dp, -1)], axis=1))
        down_w = wide_w
    else:
        wide_w = gather(jnp.concatenate(wide_mine, axis=1))
        down_w = gather(down_mine).transpose(0, 2, 1)

    res = jnp.pad(w_res.astype(F32), ((0, 0), (0, LANES - total)))

    dy_rows = lax.all_to_all(dy_rows, "expert", split_axis=0, concat_axis=0, tiled=True)
    o_heads, lse = attend(first, qkv, low)
    o_heads, dy_rows = lax.optimization_barrier((o_heads, dy_rows))
    o_theirs = lax.ppermute(o_heads[0], "context", [(0, 1), (1, 0)])
    hres, atwo, stat, o = middle(
        total, first, x, o_heads, o_theirs, w_shared, extra, prev_logits[0], res, routes[0]
    )
    flow_back, drow_back, grad_wide = run_experts(
        total, experts, dp, hidden, cap, flat_t, atwo, dy_rows, stat, wide_w, down_w
    )
    flow_back = flow_back.reshape(experts * cap, width)
    drow_back = drow_back.reshape(experts * cap, width)
    wide = lax.psum_scatter(
        grad_wide.reshape(width, 3 * hidden // 2), "dp", scatter_dimension=0, tiled=True
    )

    output, dh, grad_o, grad_out_w, small = combine(
        experts,
        total,
        flow_back,
        drow_back,
        flat,
        stat,
        flat_t,
        hres,
        atwo,
        dy,
        o,
        w_shared,
        extra,
        prev_logits[0],
    )
    grads_sent = attend_back(
        first,
        qkv,
        grad_o,
        o_heads,
        lse,
        low,
        cos,
        sin,
    )
    grad_tokens, final, small = tail(
        experts,
        dp,
        total + 7,
        grads_sent,
        aone,
        w_shared,
        extra,
        x,
        dh,
        grad_out_w.reshape(2, dp, width // dp, half),
        small,
    )
    wide, small = lax.optimization_barrier((wide, small))
    wide_other = lax.ppermute(wide, "context", [(0, 1), (1, 0)])
    (
        grad_norm_one,
        grad_norm_two,
        grad_router,
        grad_mix,
        grad_vec,
        grad_res,
        grad_query,
        grad_key,
        grad_value,
        grad_out,
        grad_gate,
        grad_up,
        grad_down,
        grad_tokens,
        output,
    ) = finish(
        total,
        jnp.stack([lax.axis_index("dp"), core]),
        final,
        small,
        wide,
        wide_other,
        grad_tokens,
        output,
    )
    return (
        output[None],
        grad_tokens[None],
        grad_norm_one[0],
        grad_query,
        grad_key,
        grad_value,
        grad_out,
        grad_norm_two[0],
        grad_router.T,
        grad_res,
        grad_mix.T,
        grad_vec.T,
        grad_gate,
        grad_up,
        grad_down,
    )


def solution(mesh):
    token = P(("expert", "dp"), "context", None)
    rows = P("dp", None)
    expert = P("expert", "dp", None)
    in_specs = (
        token,
        P(("expert", "dp"), "context"),
        token,
        token,
        token,
        token,
        P("dp"),
        rows,
        rows,
        rows,
        rows,
        P("dp"),
        rows,
        P(),
        rows,
        rows,
        expert,
        expert,
        expert,
    )
    out_specs = (
        token,
        token,
        P("dp"),
        rows,
        rows,
        rows,
        rows,
        P("dp"),
        rows,
        P(),
        rows,
        rows,
        expert,
        expert,
        expert,
    )
    return jax.shard_map(
        on_device, mesh=mesh, in_specs=in_specs, out_specs=out_specs, check_vma=False
    )
```

```python
import functools

import jax
import jax.numpy as jnp
import numpy as np
from jax import lax
from jax.experimental import pallas as pl
from jax.experimental.pallas import tpu as pltpu
from jax.sharding import PartitionSpec as P

HEADS = 12
HEAD_DIM = 64
WIN = 1024
NZ = 4
SEGMENTS = 5
GAIN_ONE, GAIN_TWO, VECS = 112, 113, 114
TQ = 256
TB = 256
RC = 64
FC = 512
LANES = 128
EPS = 1e-05
MASKED = -1000000000.0
HIGH = lax.Precision.HIGHEST
F32 = jnp.float32
BF16 = jnp.bfloat16
MIB = 1024 * 1024


def params(mib):
    return pltpu.CompilerParams(vmem_limit_bytes=mib * MIB)


def cost(flops, nbytes, trans=0):
    return pl.CostEstimate(flops=int(flops), bytes_accessed=int(nbytes), transcendentals=int(trans))


def dot(left, right):
    return jnp.dot(left, right, preferred_element_type=F32)


def dot_nt(left, right):
    return lax.dot_general(left, right, (((1,), (1,)), ((), ())), preferred_element_type=F32)


def dot_tn(left, right):
    return lax.dot_general(left, right, (((0,), (0,)), ((), ())), preferred_element_type=F32)


def iota(shape, axis):
    return lax.broadcasted_iota(jnp.int32, shape, axis)


def rope_tables(seq):
    half = HEAD_DIM // 2
    frequency = np.float32(10000.0) ** (
        -np.arange(half, dtype=np.float32) * np.float32(2.0) / np.float32(HEAD_DIM)
    )
    angles = np.arange(seq, dtype=np.float32)[:, None] * frequency.astype(np.float32)[None, :]
    cos = np.cos(angles.astype(np.float64)).astype(np.float32)
    sin = np.sin(angles.astype(np.float64)).astype(np.float32)
    return np.concatenate([cos] * 4, axis=1), np.concatenate([-sin, sin, -sin, sin], axis=1)


def swap_halves(chunk):
    lane = iota(chunk.shape, 1)
    return jnp.where(
        lane % HEAD_DIM < HEAD_DIM // 2, pltpu.roll(chunk, 96, 1), pltpu.roll(chunk, 32, 1)
    )


def loop(count, body):
    if count <= 4:
        for step in range(count):
            body(step)
    else:
        lax.fori_loop(0, count, lambda step, carry: (body(step), carry)[1], 0)


def remote(src, dst, sems, index, where):
    return pltpu.make_async_remote_copy(
        src_ref=src,
        dst_ref=dst,
        send_sem=sems.at[(0,) + index],
        recv_sem=sems.at[(1,) + index],
        device_id=where,
        device_id_type=pl.DeviceIdType.MESH,
    )


def greet_all(axes):
    barrier = pltpu.get_barrier_semaphore()
    total = 0
    for axis in axes:
        size = lax.axis_size(axis)
        me = lax.axis_index(axis)
        total += size - 1

        def greet(k, axis=axis, size=size, me=me):
            pl.semaphore_signal(
                barrier,
                inc=1,
                device_id={axis: lax.rem(me + k + 1, size)},
                device_id_type=pl.DeviceIdType.MESH,
            )

        loop(size - 1, greet)
    pl.semaphore_wait(barrier, total)


def place_pairs(experts, cap, routes_ref, ranks_ref, flat_ref, flat_t_ref):
    rows = routes_ref.shape[0]
    lane = iota((rows, LANES), 1)
    first, second = routes_ref[:, 0:1], routes_ref[:, 1:2]
    hot_first, hot_second = first == lane, second == lane
    hot = (hot_first.astype(F32) + hot_second.astype(F32)).astype(BF16)
    ranks = ranks_ref[...].astype(F32)
    ranks_col = jnp.broadcast_to(ranks, (LANES, rows)).T[:, 0:1]
    earlier = jnp.where(ranks < ranks_col, 1.0, 0.0).astype(BF16)
    counts = dot(earlier, hot)

    def flat(hit, route):
        slot = jnp.sum(jnp.where(hit, counts, 0.0), axis=1, keepdims=True).astype(jnp.int32)
        return jnp.where((route < experts) & (slot < cap), route * cap + slot, experts * cap)

    columns = (flat(hot_first, first), flat(hot_second, second), first, second)
    out = jnp.zeros((rows, LANES), jnp.int32)
    for i, column in enumerate(columns):
        out = jnp.where(lane == i, column, out)
    flat_ref[...] = out
    flat_t_ref[...] = out.astype(F32).T[:8]


def find_starts(segs_ref, low_ref, first_ref):
    rows = segs_ref.shape[2]
    per = rows // TQ
    segs = [segs_ref[side].astype(F32) for side in range(2)]
    starts = [jnp.zeros((1, rows), F32) for side in range(2)]
    for number in range(1, SEGMENTS):
        before = sum(
            jnp.sum(jnp.where(part < number, 1.0, 0.0), axis=1, keepdims=True) for part in segs
        )
        starts = [
            jnp.where(part == number, before, start) for part, start in zip(segs, starts)
        ]
    for side in range(2):
        place = (iota((1, rows), 1) + (side * rows - WIN + 1)).astype(F32)
        low = jnp.maximum(starts[side], place)
        for tile in range(per):
            part = low[:, tile * TQ : (tile + 1) * TQ]
            low_ref[side * per + tile] = part.astype(jnp.int32)
            first_ref[side * per + tile] = jnp.min(part).astype(jnp.int32) // TQ
    first_ref[2 * per] = lax.axis_index("context")


def hot_slots(flat_ref, cap, target):
    slot = (iota((cap, flat_ref.shape[1]), 0) + target * cap).astype(F32)
    return flat_ref[0:1, :] == slot, flat_ref[1:2, :] == slot


def spread_kernel(
    cap,
    w_query_ref,
    w_key_ref,
    w_value_ref,
    w_out_ref,
    extra_ref,
    routes_ref,
    ranks_ref,
    segs_ref,
    x_ref,
    dy_ref,
    cos_ref,
    sin_ref,
    shared_ref,
    extra_out_ref,
    flat_ref,
    flat_t_ref,
    low_ref,
    first_ref,
    qkv_ref,
    aone_ref,
    dy_rows_ref,
    out_ref,
    segs_all,
    stage_ref,
    slab_sems,
    plane_sems,
    core_sems,
    extra_sems,
    segs_sems,
    shared_sem,
    own_sems,
    qkv_sems,
):
    experts = lax.axis_size("expert")
    slabs = lax.axis_size("dp")
    me, core, slab = lax.axis_index("expert"), lax.axis_index("context"), lax.axis_index("dp")
    half = out_ref.shape[4]
    for which, ref in enumerate((w_query_ref, w_key_ref, w_value_ref, w_out_ref)):
        for side in range(2):

            @pl.when((me == which) & (core == side))
            def _():
                out_ref[which, side, slab] = ref[:, side * half : (side + 1) * half]

    extra_out_ref[slab] = extra_ref[...]
    segs_all[core] = segs_ref[...]
    greet_all(("context", "expert", "dp"))

    def slab_copy(k):
        piece = out_ref.at[me, core, slab]
        return remote(piece, piece, slab_sems, (k,), {"dp": lax.rem(slab + k + 1, slabs)})

    def extra_copy(k):
        piece = extra_out_ref.at[slab]
        return remote(piece, piece, extra_sems, (k,), {"dp": lax.rem(slab + k + 1, slabs)})

    def plane_copy(j, at):
        piece = out_ref.at[me, core, at]
        return remote(
            piece, piece, plane_sems, (j - 1, at), {"expert": lax.rem(me + j, experts)}
        )

    def core_copy(j, at):
        piece = out_ref.at[lax.rem(me + experts - j, experts), core, at]
        return remote(piece, piece, core_sems, (j, at), {"context": 1 - core})

    def share(at):
        for j in range(1, experts):
            plane_copy(j, at).start()
        core_copy(0, at).start()

    loop(slabs - 1, lambda k: extra_copy(k).start())
    loop(slabs - 1, lambda k: slab_copy(k).start())
    share(slab)
    segs_copy = remote(
        segs_all.at[core], segs_all.at[core], segs_sems, (0,), {"context": 1 - core}
    )
    segs_copy.start()
    place_pairs(experts, cap, routes_ref, ranks_ref, flat_ref, flat_t_ref)
    segs_copy.wait()
    find_starts(segs_all, low_ref, first_ref)
    loop(slabs - 1, lambda k: extra_copy(k).wait())
    at = extra_ref.shape[0] - 4
    gain = jnp.concatenate([extra_out_ref[z, at : at + 1, :] for z in range(slabs)], axis=1)
    tokens = x_ref.shape[0]
    for start in range(0, tokens, TB):
        values = x_ref[start : start + TB].astype(F32)
        scale = lax.rsqrt(jnp.mean(values * values, axis=-1, keepdims=True) + EPS)
        aone_ref[start : start + TB] = (values * scale * gain).astype(BF16)

    def forward(k):
        slab_copy(k).wait_recv()
        share(lax.rem(slab + slabs - k - 1, slabs))

    loop(slabs - 1, forward)
    for target in range(experts):
        first, second = hot_slots(flat_t_ref, cap, target)
        hot = jnp.where(first | second, 1.0, 0.0).astype(BF16)
        dy_rows_ref[target] = dot(hot, dy_ref[...]).astype(BF16)

    def relay(k):
        at = lax.rem(slab + slabs - k, slabs)
        for j in range(1, experts):
            plane_copy(j, at).wait_recv()
            core_copy(j, at).start()

    loop(slabs, relay)
    loop(slabs - 1, lambda k: slab_copy(k).wait_send())

    def arrive(at):
        for j in range(experts):
            core_copy(j, at).wait()
        for j in range(1, experts):
            plane_copy(j, at).wait_send()

    loop(slabs, arrive)
    keep = pltpu.make_async_copy(out_ref, shared_ref, shared_sem)
    keep.start()

    width = 2 * half
    wholes = [
        jnp.concatenate(
            [out_ref[which, side].reshape(width, half) for side in range(2)], axis=1
        )
        for which in range(3)
    ]
    copies = []
    for block in range(tokens // TB):
        span = slice(block * TB, (block + 1) * TB)
        cos, sin = cos_ref[core, span], sin_ref[core, span]
        for which in range(3):
            product = dot(aone_ref[span], wholes[which])
            for pair in range(width // LANES):
                chunk = product[:, pair * LANES : (pair + 1) * LANES]
                if which < 2:
                    chunk = chunk * cos + swap_halves(chunk) * sin
                if which == 0:
                    chunk = chunk * HEAD_DIM ** (-0.5)
                side, place_in = pair // (half // LANES), pair % (half // LANES)
                stage_ref[side, which, span, place_in * LANES : (place_in + 1) * LANES] = (
                    chunk.astype(BF16)
                )
        copies.append(
            pltpu.make_async_copy(
                stage_ref.at[core, :, span], qkv_ref.at[core, :, span], own_sems.at[block]
            )
        )
        copies.append(
            remote(
                stage_ref.at[1 - core, :, span],
                qkv_ref.at[core, :, span],
                qkv_sems,
                (block,),
                {"context": 1 - core},
            )
        )
        for copy in copies[-2:]:
            copy.start()
    for copy in copies:
        copy.wait()
    keep.wait()


def spread(
    experts, slabs, cap, w_query, w_key, w_value, w_out, extra, routes, ranks, segs, x, dy, cos, sin
):
    tokens = routes.shape[0]
    tiles = 2 * tokens // TQ
    rows, width = w_query.shape
    half = width // 2
    vmem = pl.BlockSpec(memory_space=pltpu.VMEM)
    anywhere = pl.BlockSpec(memory_space=pl.ANY)
    dma = pltpu.SemaphoreType.DMA
    return pl.pallas_call(
        functools.partial(spread_kernel, cap),
        in_specs=[vmem] * 12,
        out_specs=[anywhere]
        + [vmem] * 4
        + [pl.BlockSpec(memory_space=pltpu.SMEM), anywhere, vmem, vmem],
        out_shape=(
            jax.ShapeDtypeStruct((4, 2, slabs, rows, half), BF16),
            jax.ShapeDtypeStruct((slabs,) + extra.shape, F32),
            jax.ShapeDtypeStruct((tokens, LANES), jnp.int32),
            jax.ShapeDtypeStruct((8, tokens), F32),
            jax.ShapeDtypeStruct((tiles, 1, TQ), jnp.int32),
            jax.ShapeDtypeStruct((tiles + 1,), jnp.int32),
            jax.ShapeDtypeStruct((2, 3, tokens, half), BF16),
            jax.ShapeDtypeStruct((tokens, width), BF16),
            jax.ShapeDtypeStruct((experts, cap, width), BF16),
        ),
        scratch_shapes=[
            pltpu.VMEM((4, 2, slabs, rows, half), BF16),
            pltpu.VMEM((2, 1, tokens), jnp.int32),
            pltpu.VMEM((2, 3, tokens, half), BF16),
            dma((2, slabs - 1)),
            dma((2, experts - 1, slabs)),
            dma((2, experts, slabs)),
            dma((2, slabs - 1)),
            dma((2, 1)),
            dma,
            dma((tokens // TB,)),
            dma((2, tokens // TB)),
        ],
        compiler_params=pltpu.CompilerParams(
            collective_id=1, has_side_effects=True, vmem_limit_bytes=62 * MIB
        ),
        cost_estimate=cost(1e6, 16 * width * width),
        name="spread",
    )(w_query, w_key, w_value, w_out, extra, routes, ranks, segs, x, dy, cos, sin)


def head_masks():
    lane = iota((TQ, LANES), 1)
    low = jnp.where(lane < HEAD_DIM, 1.0, 0.0).astype(BF16)
    return low, (1.0 - low.astype(F32)).astype(BF16)


def spans(tile, first, body):
    for count in range(1, WIN // TQ + 2):

        @pl.when(tile - first + 1 == count)
        def _():
            body(count)


def masked(scores, low, start, count):
    shape = (TQ, 2 * TQ)
    sub, lane = iota(shape, 0), lax.rem(iota(shape, 1), TQ)
    low = jnp.concatenate([low, low], axis=1)
    parts = []
    for t in range(count):
        mark = sub >= low - (start + t * TQ)
        if t == count - 1:
            mark = mark & (sub <= lane)
        parts.append(jnp.where(mark, scores[t * TQ : (t + 1) * TQ], MASKED))
    return parts


def own_blocks(both):
    return jnp.concatenate([both[:HEAD_DIM, :TQ], both[HEAD_DIM:LANES, TQ:]], axis=0)


def attend_kernel(
    first_ref, q_ref, k_ref, v_ref, lo_ref, keep_ref, give_ref, lse_ref, keys_ref, vt_ref
):
    rows = q_ref.shape[2]
    per = rows // TQ
    masks = head_masks()
    for side in range(2):
        at = slice(side * rows, (side + 1) * rows)
        keys_ref[at, :] = k_ref[side, 0]
        vt_ref[:LANES, at] = v_ref[side, 0].T
        vt_ref[LANES:, at] = jnp.ones((16, rows), BF16)

    def q_step(qi, carry):
        at = pl.ds(pl.multiple_of(lax.rem(qi, per) * TQ, TQ), TQ)
        query = q_ref[qi // per, 0, at, :]
        low = lo_ref[qi]

        def run(count):
            start = pl.multiple_of((qi - count + 1) * TQ, TQ)
            span = pl.ds(start, count * TQ)
            both = jnp.concatenate([query * mask for mask in masks], axis=0)
            scores = masked(dot_nt(keys_ref[span, :], both), low, start, count)
            peak = functools.reduce(
                jnp.maximum, [jnp.max(part, axis=0, keepdims=True) for part in scores]
            )
            probs = jnp.concatenate([jnp.exp(part - peak).astype(BF16) for part in scores], axis=0)
            mixed = dot(vt_ref[:, span], probs)
            total = mixed[LANES : LANES + 1]
            lse_ref[0, qi, 0:1, :] = peak + jnp.log(total)
            out = own_blocks(mixed[:LANES] / total).T.astype(BF16)

            @pl.when(qi // per == first_ref[2 * per])
            def _():
                keep_ref[at, :] = out

            @pl.when(qi // per != first_ref[2 * per])
            def _():
                give_ref[at, :] = out

        spans(qi, first_ref[qi], run)
        return carry

    lax.fori_loop(0, 2 * per, q_step, 0)


def part_spec(which, rows):
    return pl.BlockSpec((2, 1, rows, LANES), lambda p, first, which=which: (0, which, 0, p))


def attend(first, qkv, low):
    _, _, rows, half = qkv.shape
    pairs = half // LANES
    tiles = 2 * rows // TQ
    return pl.pallas_call(
        attend_kernel,
        grid_spec=pltpu.PrefetchScalarGridSpec(
            num_scalar_prefetch=1,
            grid=(pairs,),
            in_specs=[
                part_spec(0, rows),
                part_spec(1, rows),
                part_spec(2, rows),
                pl.BlockSpec((tiles, 1, TQ), lambda p, first: (0, 0, 0)),
            ],
            out_specs=[
                pl.BlockSpec((rows, LANES), lambda p, first: (0, p)),
                pl.BlockSpec((rows, LANES), lambda p, first: (0, p)),
                pl.BlockSpec((1, tiles, 8, 2 * TQ), lambda p, first: (p, 0, 0, 0)),
            ],
            scratch_shapes=[
                pltpu.VMEM((2 * rows, LANES), BF16),
                pltpu.VMEM((LANES + 16, 2 * rows), BF16),
            ],
        ),
        out_shape=(
            jax.ShapeDtypeStruct((rows, half), BF16),
            jax.ShapeDtypeStruct((rows, half), BF16),
            jax.ShapeDtypeStruct((pairs, tiles, 8, 2 * TQ), F32),
        ),
        compiler_params=params(62),
        cost_estimate=cost(40e9, 16 * rows * half, 12e6),
        name="attend",
    )(first, qkv, qkv, qkv, low)


def attend_back_kernel(
    first_ref,
    q_ref,
    k_ref,
    v_ref,
    do_ref,
    keep_ref,
    give_ref,
    lse_ref,
    lo_ref,
    cos_ref,
    sin_ref,
    layer_ref,
    g_ref,
    layer_out_ref,
    keys_ref,
    values_ref,
    kt_ref,
    delta_ref,
    dk_ref,
    dv_ref,
):
    rows = q_ref.shape[2]
    per = rows // TQ
    masks = head_masks()
    for side in range(2):
        at = slice(side * rows, (side + 1) * rows)
        keys_ref[at, :] = k_ref[side, 0]
        values_ref[at, :] = v_ref[side, 0]
        kt_ref[:, at] = k_ref[side, 0].T
    layer_out_ref[...] = layer_ref[...]
    dk_ref[...] = jnp.zeros_like(dk_ref)
    dv_ref[...] = jnp.zeros_like(dv_ref)

    def prepare(tile, carry):
        at = pl.ds(pl.multiple_of(lax.rem(tile, per) * TQ, TQ), TQ)
        out = jnp.where(tile // per == first_ref[2 * per], keep_ref[at, :], give_ref[at, :])
        both = out.astype(F32) * do_ref[tile // per, at, :].astype(F32)
        both = both.T
        delta_ref[tile, 0:1, :TQ] = jnp.sum(both[:HEAD_DIM], axis=0, keepdims=True)
        delta_ref[tile, 0:1, TQ:] = jnp.sum(both[HEAD_DIM:], axis=0, keepdims=True)
        return carry

    lax.fori_loop(0, 2 * per, prepare, 0)

    def q_step(qi, carry):
        at = pl.ds(pl.multiple_of(lax.rem(qi, per) * TQ, TQ), TQ)
        query = q_ref[qi // per, 0, at, :]
        grad = do_ref[qi // per, at, :]
        low = lo_ref[qi]

        def run(count):
            start = pl.multiple_of((qi - count + 1) * TQ, TQ)
            span = pl.ds(start, count * TQ)
            queries = jnp.concatenate([query * mask for mask in masks], axis=0)
            grads = jnp.concatenate([grad * mask for mask in masks], axis=0)
            lse, delta = lse_ref[0, qi, 0:1, :], delta_ref[qi, 0:1, :]
            scores = masked(dot_nt(keys_ref[span, :], queries), low, start, count)
            grad_probs = dot_nt(values_ref[span, :], grads)
            probs = [jnp.exp(part - lse) for part in scores]
            grad_scores = jnp.concatenate(
                [
                    (part * (grad_probs[t * TQ : (t + 1) * TQ] - delta)).astype(BF16)
                    for t, part in enumerate(probs)
                ],
                axis=0,
            )
            probs = jnp.concatenate([part.astype(BF16) for part in probs], axis=0)
            dv_ref[span, :] += dot(probs, grads)
            dk_ref[span, :] += dot(grad_scores, queries)
            turned = own_blocks(dot(kt_ref[:, span], grad_scores))
            grad_query = turned.T * HEAD_DIM ** (-0.5)
            cos, sin = cos_ref[qi // per, at, :], sin_ref[qi // per, at, :]
            g_ref[qi // per, 0, at, :] = (
                grad_query * cos - swap_halves(grad_query) * sin
            ).astype(BF16)

        spans(qi, first_ref[qi], run)
        return carry

    lax.fori_loop(0, 2 * per, q_step, 0)

    def finish(tile, carry):
        at = pl.ds(pl.multiple_of(lax.rem(tile, per) * TQ, TQ), TQ)
        span = pl.ds(pl.multiple_of(tile * TQ, TQ), TQ)
        cos, sin = cos_ref[tile // per, at, :], sin_ref[tile // per, at, :]
        grad_key = dk_ref[span, :]
        g_ref[tile // per, 1, at, :] = (grad_key * cos - swap_halves(grad_key) * sin).astype(BF16)
        g_ref[tile // per, 2, at, :] = dv_ref[span, :].astype(BF16)
        return carry

    lax.fori_loop(0, 2 * per, finish, 0)


def attend_back(first, qkv, grad_o, keep, give, lse, low, cos, sin, layer):
    _, _, rows, half = qkv.shape
    pairs = half // LANES
    tiles = 2 * rows // TQ
    side = pl.BlockSpec((2, rows, LANES), lambda p, first: (0, 0, p))
    table = pl.BlockSpec((2, rows, LANES), lambda p, first: (0, 0, 0))
    return pl.pallas_call(
        attend_back_kernel,
        grid_spec=pltpu.PrefetchScalarGridSpec(
            num_scalar_prefetch=1,
            grid=(pairs,),
            in_specs=[
                part_spec(0, rows),
                part_spec(1, rows),
                part_spec(2, rows),
                side,
                pl.BlockSpec((rows, LANES), lambda p, first: (0, p)),
                pl.BlockSpec((rows, LANES), lambda p, first: (0, p)),
                pl.BlockSpec((1, tiles, 8, 2 * TQ), lambda p, first: (p, 0, 0, 0)),
                pl.BlockSpec((tiles, 1, TQ), lambda p, first: (0, 0, 0)),
                table,
                table,
                pl.BlockSpec((rows, 2 * LANES), lambda p, first: (0, p)),
            ],
            out_specs=[
                pl.BlockSpec((2, 3, rows, LANES), lambda p, first: (0, 0, 0, p)),
                pl.BlockSpec((rows, 2 * LANES), lambda p, first: (0, p)),
            ],
            scratch_shapes=[
                pltpu.VMEM((2 * rows, LANES), BF16),
                pltpu.VMEM((2 * rows, LANES), BF16),
                pltpu.VMEM((LANES, 2 * rows), BF16),
                pltpu.VMEM((tiles, 8, 2 * TQ), F32),
                pltpu.VMEM((2 * rows, LANES), F32),
                pltpu.VMEM((2 * rows, LANES), F32),
            ],
        ),
        out_shape=(
            jax.ShapeDtypeStruct((2, 3, rows, half), BF16),
            jax.ShapeDtypeStruct(layer.shape, BF16),
        ),
        compiler_params=params(62),
        cost_estimate=cost(100e9, 32 * rows * half, 12e6),
        name="attend_back",
    )(first, qkv, qkv, qkv, grad_o, keep, give, lse, low, cos, sin, layer)


def middle_kernel(
    total,
    first_ref,
    x_ref,
    mine_ref,
    theirs_ref,
    w_ref,
    extra_ref,
    prev_ref,
    res_ref,
    routes_ref,
    hres_ref,
    atwo_ref,
    stat_ref,
    attended_ref,
):
    mine, theirs = mine_ref[...], theirs_ref[...]
    swap = first_ref[first_ref.shape[0] - 1] != 0
    attended = jnp.concatenate(
        [jnp.where(swap, theirs, mine), jnp.where(swap, mine, theirs)], axis=1
    )
    attended_ref[...] = attended
    hres = x_ref[...].astype(F32) + dot(
        attended, jnp.concatenate([w_ref[0, 0], w_ref[0, 1]], axis=1)
    )
    hres_ref[...] = hres
    scale = lax.rsqrt(jnp.mean(hres * hres, axis=-1, keepdims=True) + EPS)
    extra = extra_ref[...]
    gain = extra[GAIN_TWO : GAIN_TWO + 1].astype(F32)
    atwo = (hres * scale * gain).astype(BF16)
    atwo_ref[...] = atwo
    logits = dot_nt(atwo, extra)
    for j in range(total):
        logits = logits + prev_ref[:, j : j + 1] * res_ref[j : j + 1, :]
    lane = iota(logits.shape, 1)

    def soft(inside):
        peak = jnp.max(jnp.where(inside, logits, -jnp.inf), axis=1, keepdims=True)
        powers = jnp.where(inside, jnp.exp(jnp.where(inside, logits - peak, 0.0)), 0.0)
        return powers / jnp.sum(powers, axis=1, keepdims=True)

    probs = soft(lane < total)
    stat = probs
    for j in range(2):
        start = total + 2 * j
        stat = stat + soft((lane >= start) & (lane < start + 2))
    stat = jnp.where(lane == total + 4, scale, stat)
    for k in range(2):
        gate = jnp.sum(
            jnp.where(lane == routes_ref[:, k : k + 1], probs, 0.0), axis=1, keepdims=True
        )
        stat = jnp.where(lane == total + 5 + k, gate, stat)
    stat_ref[...] = stat


def middle(total, first, x, o, theirs, w_shared, extra, prev, res, routes):
    rows, width = x.shape
    token = lambda i: (i, 0)
    whole = lambda i: (0, 0)
    return pl.pallas_call(
        functools.partial(middle_kernel, total),
        grid=(rows // TB,),
        in_specs=[
            pl.BlockSpec(memory_space=pltpu.SMEM),
            pl.BlockSpec((TB, width), token),
            pl.BlockSpec((TB, width // 2), token),
            pl.BlockSpec((TB, width // 2), token),
            pl.BlockSpec((1, 2, width, width // 2), lambda i: (3, 0, 0, 0)),
            pl.BlockSpec((LANES, width), whole),
            pl.BlockSpec((TB, total), token),
            pl.BlockSpec((total, LANES), whole),
            pl.BlockSpec((TB, 2), token),
        ],
        out_specs=[
            pl.BlockSpec((TB, width), token),
            pl.BlockSpec((TB, width), token),
            pl.BlockSpec((TB, LANES), token),
            pl.BlockSpec((TB, width), token),
        ],
        out_shape=(
            jax.ShapeDtypeStruct((rows, width), F32),
            jax.ShapeDtypeStruct((rows, width), BF16),
            jax.ShapeDtypeStruct((rows, LANES), F32),
            jax.ShapeDtypeStruct((rows, width), BF16),
        ),
        compiler_params=params(62),
        cost_estimate=cost(2 * rows * width * width, 2 * width * width + 10 * rows * width),
        name="middle",
    )(first, x, o, theirs, w_shared, extra, prev, res, routes)


def expert_kernel(
    total,
    flat_ref,
    atwo_ref,
    dy_ref,
    stat_ref,
    wide_ref,
    wd_ref,
    flow_ref,
    drow_ref,
    gw_ref,
    send_x,
    send_g,
    all_x,
    all_g,
    send_gate,
    all_gate,
    acc_ref,
    z_ref,
    a_ref,
    b_ref,
    turned_ref,
    turned_g,
    kept_ref,
    wide_buf,
    down_buf,
    wide_given,
    wide_taken,
    down_given,
    down_taken,
    dy_sems,
    x_sems,
    g_sems,
    flow_sems,
    drow_sems,
    local_sems,
    weight_sems,
    wide_sems,
    down_sems,
):
    experts, cap, width = all_x.shape
    slots = experts * cap
    chunks = z_ref.shape[0]
    per = chunks // 2
    half = width // 2
    slabs, rows_out = gw_ref.shape[:2]
    deep = chunks * FC // slabs
    me, core = lax.axis_index("expert"), lax.axis_index("context")

    def down_pieces(chunk):
        if deep == FC:
            rows = pl.ds(pl.multiple_of(chunk * rows_out, rows_out), rows_out)
            return [
                (
                    wd_ref.at[side, rows, 2 * per * FC + b * deep : 2 * per * FC + (b + 1) * deep],
                    side * half + b * rows_out,
                    rows_out,
                )
                for side in range(2)
                for b in range(half // rows_out)
            ]
        at = pl.ds(pl.multiple_of(chunk * FC, FC), FC)
        return [(wd_ref.at[side, :, at], side * half, half) for side in range(2)]

    def weights(step):
        chunk, slot = lax.rem(step, chunks), lax.rem(step, 2)
        gate_at = pl.ds(pl.multiple_of(lax.rem(chunk, per) * FC, FC), FC)
        up_at = pl.ds(pl.multiple_of((per + lax.rem(chunk, per)) * FC, FC), FC)
        return (
            pltpu.make_async_copy(
                wide_ref.at[chunk // per, :, gate_at], wide_buf.at[slot, 0], weight_sems.at[slot, 0]
            ),
            pltpu.make_async_copy(
                wide_ref.at[chunk // per, :, up_at], wide_buf.at[slot, 1], weight_sems.at[slot, 1]
            ),
        ) + tuple(
            pltpu.make_async_copy(
                source, down_buf.at[slot, at : at + size, :], weight_sems.at[slot, 2 + i]
            )
            for i, (source, at, size) in enumerate(down_pieces(chunk))
        )

    def next_weights(step):
        @pl.when(step + 1 < 4 * chunks)
        def _():
            for copy in weights(step + 1):
                copy.start()

        for copy in weights(step):
            copy.wait()

    for copy in weights(0):
        copy.start()
    greet_all(("context", "expert"))

    for j in range(experts):
        pltpu.make_async_copy(
            dy_ref.at[lax.rem(me + experts - j, experts)], all_g.at[j], dy_sems.at[j]
        ).start()
    gates = stat_ref[...].T
    x_copies, g_copies = {}, {}
    for j in list(range(1, experts)) + [0]:
        target = lax.rem(me + j, experts)
        first, second = hot_slots(flat_ref, cap, target)
        rows = dot(jnp.where(first | second, 1.0, 0.0).astype(BF16), atwo_ref[...]).astype(BF16)
        gate = jnp.sum(
            jnp.where(first, gates[total + 5 : total + 6], 0.0)
            + jnp.where(second, gates[total + 6 : total + 7], 0.0),
            axis=1,
            keepdims=True,
        )
        gate = jnp.broadcast_to(gate, (cap, LANES)).T[:8]
        if j == 0:
            all_x[0] = rows
            all_gate[0] = gate
        else:
            send_gate[j - 1] = gate
            send_x[j - 1] = rows
            g_copies[j] = remote(
                send_gate.at[j - 1], all_gate.at[j], g_sems, (j - 1,), {"expert": target}
            )
            x_copies[j] = remote(
                send_x.at[j - 1], all_x.at[j], x_sems, (j - 1,), {"expert": target}
            )
            g_copies[j].start()
            x_copies[j].start()

    def weigh(j):
        pltpu.make_async_copy(
            dy_ref.at[lax.rem(me + experts - j, experts)], all_g.at[j], dy_sems.at[j]
        ).wait()
        gate = jnp.broadcast_to(all_gate[j, 0:1, :], (LANES, cap)).T[:, 0:1]
        all_g[j] = (all_g[j].astype(F32) * gate).astype(BF16)

    def back(buffer, dest, sems, j):
        return remote(
            buffer.at[j - 1],
            dest.at[me],
            sems,
            (j - 1,),
            {"expert": lax.rem(me + experts - j, experts)},
        )

    acc_ref[...] = jnp.zeros_like(acc_ref)

    def up(first, last, at):
        span = slice(first * cap, last * cap)

        def one(step, carry):
            next_weights(step + at * chunks)
            slot = lax.rem(step + at * chunks, 2)
            rows = all_x[first:last].reshape((last - first) * cap, width)
            gate = dot(rows, wide_buf[slot, 0])
            lift = dot(rows, wide_buf[slot, 1])
            sig = 1.0 / (1.0 + jnp.exp(-gate))
            swish = gate * sig
            hidden = (swish * lift).astype(BF16)
            z_ref[step, span] = hidden
            a_ref[step, span] = (lift * sig * (1.0 + gate * (1.0 - sig))).astype(BF16)
            b_ref[step, span] = swish.astype(BF16)
            acc_ref[span, :] += dot_nt(hidden, down_buf[slot])
            return carry

        lax.fori_loop(0, chunks, one, 0)

    def down(first, last, at):
        span = slice(first * cap, last * cap)

        def one(step, carry):
            next_weights(step + at * chunks)
            slot = lax.rem(step + at * chunks, 2)
            dz = dot(all_g[first:last].reshape((last - first) * cap, width), down_buf[slot])
            dg = (dz * a_ref[step, span].astype(F32)).astype(BF16)
            du = (dz * b_ref[step, span].astype(F32)).astype(BF16)
            a_ref[step, span] = dg
            b_ref[step, span] = du
            acc_ref[span, :] += dot_nt(dg, wide_buf[slot, 0]) + dot_nt(du, wide_buf[slot, 1])
            return carry

        lax.fori_loop(0, chunks, one, 0)

    def keep_own(buffer, dest, index):
        buffer[experts - 1] = acc_ref[:cap, :].astype(BF16)
        copy = pltpu.make_async_copy(
            buffer.at[experts - 1], dest.at[me], local_sems.at[index]
        )
        copy.start()
        return copy

    weigh(0)
    up(0, 1, 0)
    own = [keep_own(send_x, flow_ref, 0)]
    acc_ref[:cap, :] = jnp.zeros((cap, width), F32)
    down(0, 1, 1)
    own.append(keep_own(send_g, drow_ref, 1))
    for j in range(1, experts):
        g_copies[j].wait()
        weigh(j)
    turned_g[...] = all_g[...].reshape(slots, width).T
    for j in range(1, experts):
        x_copies[j].wait()
    up(1, experts, 2)
    for j in range(1, experts):
        send_x[j - 1] = acc_ref[j * cap : (j + 1) * cap, :].astype(BF16)
        back(send_x, flow_ref, flow_sems, j).start()
    turned_ref[...] = all_x[...].reshape(slots, width).T
    acc_ref[cap:, :] = jnp.zeros((slots - cap, width), F32)
    down(1, experts, 3)
    for j in range(1, experts):
        send_g[j - 1] = acc_ref[j * cap : (j + 1) * cap, :].astype(BF16)
        back(send_g, drow_ref, drow_sems, j).start()

    def wide_copy(step):
        return remote(
            wide_given.at[step],
            wide_taken.at[step],
            wide_sems,
            (step,),
            {"context": 1 - core},
        )

    def down_copy(step):
        chunk = lax.rem((1 - core) * per + step, chunks)
        return remote(
            down_given.at[step],
            down_taken.at[chunk],
            down_sems,
            (chunk,),
            {"context": 1 - core},
        )

    def products(step):
        chunk = lax.rem((1 - core) * per + step, chunks)
        gate = dot(turned_ref[...], a_ref[chunk])
        lift = dot(turned_ref[...], b_ref[chunk])
        low = dot(turned_g[...], z_ref[chunk])
        top, bottom = low[:half], low[half:]
        down_given[step] = jnp.where(core == 0, bottom, top).astype(BF16)
        kept_ref[chunk] = jnp.where(core == 0, top, bottom).astype(BF16)
        down_copy(step).start()
        return gate, lift

    def give(step, carry):
        gate, lift = products(step)
        wide_given[step, 0] = gate.astype(BF16)
        wide_given[step, 1] = lift.astype(BF16)
        wide_copy(step).start()
        return carry

    lax.fori_loop(0, per, give, 0)

    def keep(step, carry):
        gate, lift = products(step)
        wide_copy(step - per).wait_recv()
        for i, value in enumerate((gate, lift)):
            at = pl.ds(pl.multiple_of((i * per + step - per) * FC, FC), FC)
            value = value + wide_taken[step - per, i].astype(F32)
            gw_ref[:, :, at] = value.reshape(slabs, rows_out, FC).astype(BF16)
        return carry

    lax.fori_loop(per, chunks, keep, 0)

    def settle(step, carry):
        other = lax.rem(core * per + step, chunks)
        copy = remote(
            down_given.at[step],
            down_taken.at[other],
            down_sems,
            (other,),
            {"context": 1 - core},
        )
        copy.wait_recv()
        value = kept_ref[other].astype(F32) + down_taken[other].astype(F32)
        for b in range(half // rows_out):
            part = value[b * rows_out : (b + 1) * rows_out]
            start = 2 * per * FC + b * deep
            if FC <= deep:
                inside = lax.rem(other, deep // FC) * FC
                at = pl.ds(pl.multiple_of(start + inside, FC), FC)
                gw_ref[other // (deep // FC), :, at] = part.astype(BF16)
            else:
                for i in range(FC // deep):
                    gw_ref[other * (FC // deep) + i, :, start : start + deep] = part[
                        :, i * deep : (i + 1) * deep
                    ].astype(BF16)
        return carry

    lax.fori_loop(0, chunks, settle, 0)

    for copy in own:
        copy.wait()
    for j in range(1, experts):
        back(send_x, flow_ref, flow_sems, j).wait()
        back(send_g, drow_ref, drow_sems, j).wait()

    def sent(step, carry):
        down_copy(step).wait_send()
        return carry

    lax.fori_loop(0, chunks, sent, 0)
    lax.fori_loop(0, per, lambda step, carry: (wide_copy(step).wait_send(), carry)[1], 0)


def run_experts(total, experts, slabs, hidden, cap, flat_t, atwo, dy, stat, wide, wd):
    rows, width = atwo.shape
    chunks = hidden // FC
    per = chunks // 2
    half = width // 2
    slots = experts * cap
    vmem = pl.BlockSpec(memory_space=pltpu.VMEM)
    anywhere = pl.BlockSpec(memory_space=pl.ANY)
    dma = pltpu.SemaphoreType.DMA
    return pl.pallas_call(
        functools.partial(expert_kernel, total),
        in_specs=[vmem] * 2 + [anywhere, vmem] + [anywhere] * 2,
        out_specs=[anywhere] * 2 + [vmem],
        out_shape=(
            jax.ShapeDtypeStruct((experts, cap, width), BF16),
            jax.ShapeDtypeStruct((experts, cap, width), BF16),
            jax.ShapeDtypeStruct((slabs, width // slabs, 3 * hidden // 2), BF16),
        ),
        scratch_shapes=[
            pltpu.VMEM((experts, cap, width), BF16),
            pltpu.VMEM((experts, cap, width), BF16),
            pltpu.VMEM((experts, cap, width), BF16),
            pltpu.VMEM((experts, cap, width), BF16),
            pltpu.VMEM((experts - 1, 8, cap), F32),
            pltpu.VMEM((experts, 8, cap), F32),
            pltpu.VMEM((slots, width), F32),
            pltpu.VMEM((chunks, slots, FC), BF16),
            pltpu.VMEM((chunks, slots, FC), BF16),
            pltpu.VMEM((chunks, slots, FC), BF16),
            pltpu.VMEM((width, slots), BF16),
            pltpu.VMEM((width, slots), BF16),
            pltpu.VMEM((chunks, half, FC), BF16),
            pltpu.VMEM((2, 2, width, FC), BF16),
            pltpu.VMEM((2, width, FC), BF16),
            pltpu.VMEM((per, 2, width, FC), BF16),
            pltpu.VMEM((per, 2, width, FC), BF16),
            pltpu.VMEM((chunks, half, FC), BF16),
            pltpu.VMEM((chunks, half, FC), BF16),
            dma((experts,)),
            dma((2, experts - 1)),
            dma((2, experts - 1)),
            dma((2, experts - 1)),
            dma((2, experts - 1)),
            dma((2,)),
            dma((2, 6)),
            dma((2, per)),
            dma((2, chunks)),
        ],
        compiler_params=pltpu.CompilerParams(
            collective_id=2, has_side_effects=True, vmem_limit_bytes=62 * MIB
        ),
        cost_estimate=cost(18 * slots * width * hidden, 30 * width * hidden),
        name="experts",
    )(flat_t, atwo, dy, stat, wide, wd)


def combine_kernel(
    experts,
    total,
    flow_ref,
    drow_ref,
    flat_ref,
    stat_ref,
    flat_t_ref,
    hres_ref,
    atwo_ref,
    dy_ref,
    o_ref,
    extra_ref,
    w_ref,
    prev_ref,
    out_ref,
    dh_ref,
    dolow_ref,
    gw_ref,
    small_ref,
    right_ref,
    picked_ref,
    summed_ref,
    sums_ref,
    columns_ref,
    dhlow_ref,
    stage_ref,
    own_sems,
    dolow_sems,
):
    step = pl.program_id(0)
    core = lax.axis_index("context")

    @pl.when(step == 0)
    def _():
        greet_all(("context",))

    def dolow_copies(block):
        rows = pl.ds(pl.multiple_of(block * TB, TB), TB)
        return (
            pltpu.make_async_copy(
                stage_ref.at[core, rows], dolow_ref.at[core, rows], own_sems.at[block]
            ),
            remote(
                stage_ref.at[1 - core, rows],
                dolow_ref.at[core, rows],
                dolow_sems,
                (block,),
                {"context": 1 - core},
            ),
        )

    slots, width = flow_ref.shape
    half = width // 2
    gain = extra_ref[GAIN_TWO : GAIN_TWO + 1].astype(F32)
    vecs = [extra_ref[VECS + j : VECS + j + 1].astype(F32) for j in range(2)]

    @pl.when(step == 0)
    def _():
        right_ref[:slots] = drow_ref[...]
        right_ref[slots:] = extra_ref[...]

    spread_out = iota((TB, slots), 1)
    hots = [
        jnp.where(flat_ref[:, k : k + 1] == spread_out, 1.0, 0.0).astype(BF16) for k in range(2)
    ]
    for k in range(2):
        picked_ref[k] = dot(hots[k], flow_ref[...])
    vec_dot = dot_nt(dy_ref[...], extra_ref[...])
    lane = iota((RC, LANES), 1)
    for start in range(0, TB, RC):
        at = slice(start, start + RC)
        dy = dy_ref[at].astype(F32)
        ntwo = hres_ref[at] * stat_ref[at, total + 4 : total + 5] * gain
        sums = vec_dot[at]
        for i, part in enumerate((ntwo, picked_ref[0, at], picked_ref[1, at])):
            sums = jnp.where(lane == i, jnp.sum(dy * part, axis=1, keepdims=True), sums)
        sums_ref[at] = sums

    sums, stats = sums_ref[...].T, stat_ref[...].T
    row = lambda i: stats[i : i + 1]
    dot_normed, dot_picked = sums[0:1], [sums[1:2], sums[2:3]]
    dot_vecs = [sums[VECS + j : VECS + j + 1] for j in range(2)]
    gates = [row(total + 5 + k) for k in range(2)]
    mixes = [[row(total + 2 * j + i) for i in range(2)] for j in range(2)]
    routes = [flat_t_ref[2 + k : 3 + k] for k in range(2)]
    copies = [jnp.where(route == experts + 1, 1.0, 0.0) for route in routes]
    consts = [
        [jnp.where(route == experts + 2 + j, 1.0, 0.0) for j in range(2)] for route in routes
    ]
    pulls = [mixes[j][0] * dot_normed + mixes[j][1] * dot_vecs[j] for j in range(2)]
    sub = iota((total, TB), 0).astype(F32)
    dpgate = jnp.zeros((total, TB), F32)
    for k in range(2):
        dgate = dot_picked[k] + copies[k] * dot_normed
        dgate = dgate + consts[k][0] * pulls[0] + consts[k][1] * pulls[1]
        dpgate = dpgate + jnp.where(sub == routes[k], dgate, 0.0)
    pgate = stats[:total]
    dlogit = pgate * (dpgate - jnp.sum(pgate * dpgate, axis=0, keepdims=True))
    weight = gates[0] * copies[0] + gates[1] * copies[1]
    dmix, shares, pieces = [], [], []
    for j in range(2):
        const = gates[0] * consts[0][j] + gates[1] * consts[1][j]
        grads = [const * dot_normed, const * dot_vecs[j]]
        inner = mixes[j][0] * grads[0] + mixes[j][1] * grads[1]
        dmix += [mixes[j][i] * (grads[i] - inner) for i in range(2)]
        weight = weight + const * mixes[j][0]
        share = const * mixes[j][1]
        shares.append(share)
        for i in range(3):
            pieces.append(share.astype(BF16).astype(F32))
            share = share - pieces[-1]
    empty = jnp.zeros((1, TB), F32)
    droute_t = jnp.concatenate([dlogit] + dmix + [empty] * (12 - total), axis=0).astype(BF16)
    rows = jnp.concatenate(
        [dlogit] + dmix + [weight] + shares + [jnp.zeros((LANES - total - 7, TB), F32)], axis=0
    )
    columns_ref[...] = rows.T
    for start in range(0, TB, RC):
        at = slice(start, start + RC)
        hres = hres_ref[at]
        ntwo = hres * stat_ref[at, total + 4 : total + 5] * gain
        out = hres + columns_ref[at, total + 4 : total + 5] * ntwo
        for k in range(2):
            out = out + stat_ref[at, total + 5 + k : total + 6 + k] * picked_ref[k, at]
        for j in range(2):
            out = out + columns_ref[at, total + 5 + j : total + 6 + j] * vecs[j]
        out_ref[at] = out.astype(BF16)

    lane = iota((TB, LANES), 1)
    droute = jnp.where(lane < total + 4, columns_ref[...], 0.0).astype(BF16)
    summed_ref[...] = dot(
        jnp.concatenate([hots[0] + hots[1], droute], axis=1), right_ref[...]
    )
    gain_row = jnp.zeros((1, width), F32)
    for start in range(0, TB, RC):
        at = slice(start, start + RC)
        hres = hres_ref[at]
        dy = dy_ref[at].astype(F32)
        scale = stat_ref[at, total + 4 : total + 5]
        dntwo = columns_ref[at, total + 4 : total + 5] * dy + summed_ref[at]
        both = hres * dntwo
        inner = jnp.sum(both * gain, axis=1, keepdims=True) * (1.0 / width)
        dh = dy + dntwo * gain * scale - hres * (scale * scale * scale * inner)
        gain_row = gain_row + jnp.sum(both * scale, axis=0, keepdims=True)
        dh_ref[at] = dh
        dhlow_ref[pl.ds(pl.multiple_of(step * TB + start, RC), RC), :] = dh.astype(BF16)
    w_out = jnp.concatenate([w_ref[0, 0], w_ref[0, 1]], axis=1)
    dolow = dot_nt(dhlow_ref[pl.ds(pl.multiple_of(step * TB, TB), TB), :], w_out).astype(BF16)
    rows_at = pl.ds(pl.multiple_of(step * TB, TB), TB)
    stage_ref[0, rows_at] = dolow[:, :half]
    stage_ref[1, rows_at] = dolow[:, half:]
    for copy in dolow_copies(step):
        copy.start()
    route_rows = dot(droute_t, atwo_ref[...])
    vec_parts = dot(
        jnp.concatenate(pieces + [empty] * 2, axis=0).astype(BF16), dy_ref[...]
    )
    vec_rows = [
        vec_parts[3 * j : 3 * j + 1] + vec_parts[3 * j + 1 : 3 * j + 2] + vec_parts[3 * j + 2 : 3 * j + 3]
        for j in range(2)
    ]
    res_rows = jnp.dot(dlogit, prev_ref[...], precision=HIGH, preferred_element_type=F32)
    res_rows = jnp.concatenate([res_rows, jnp.zeros((total, width - total), F32)], axis=1)
    small = jnp.concatenate(
        [route_rows[: total + 4], gain_row] + vec_rows + [jnp.zeros((1, width), F32), res_rows],
        axis=0,
    )

    @pl.when(step == 0)
    def _():
        small_ref[...] = small

    @pl.when(step > 0)
    def _():
        small_ref[...] += small

    @pl.when(step == pl.num_programs(0) - 1)
    def _():
        for side in range(2):
            at = slice(side * half, (side + 1) * half)
            weight = dot(o_ref[:, at].T, dhlow_ref[...]).astype(BF16)
            gw_ref[0, at] = weight[:, :half]
            gw_ref[1, at] = weight[:, half:]
        for block in range(dhlow_ref.shape[0] // TB):
            for copy in dolow_copies(block):
                copy.wait()


def combine(experts, total, flow, drow, flat, stat, flat_t, hres, atwo, dy, o, w_shared, extra, prev):
    rows, width = hres.shape
    slots = flow.shape[0]
    half = width // 2
    token = lambda i: (i, 0)
    whole = lambda i: (0, 0)
    weight = pl.BlockSpec((2, width, half), lambda i: (0, 0, 0))
    small_rows = 2 * total + 8
    return pl.pallas_call(
        functools.partial(combine_kernel, experts, total),
        grid=(rows // TB,),
        in_specs=[
            pl.BlockSpec((slots, width), whole),
            pl.BlockSpec((slots, width), whole),
            pl.BlockSpec((TB, LANES), token),
            pl.BlockSpec((TB, LANES), token),
            pl.BlockSpec((8, TB), lambda i: (0, i)),
            pl.BlockSpec((TB, width), token),
            pl.BlockSpec((TB, width), token),
            pl.BlockSpec((TB, width), token),
            pl.BlockSpec((rows, width), whole),
            pl.BlockSpec((LANES, width), whole),
            pl.BlockSpec((1, 2, width, half), lambda i: (3, 0, 0, 0)),
            pl.BlockSpec((TB, total), token),
        ],
        out_specs=[
            pl.BlockSpec((TB, width), token),
            pl.BlockSpec((TB, width), token),
            pl.BlockSpec(memory_space=pl.ANY),
            weight,
            pl.BlockSpec((small_rows, width), whole),
        ],
        out_shape=(
            jax.ShapeDtypeStruct((rows, width), BF16),
            jax.ShapeDtypeStruct((rows, width), F32),
            jax.ShapeDtypeStruct((2, rows, half), BF16),
            jax.ShapeDtypeStruct((2, width, half), BF16),
            jax.ShapeDtypeStruct((small_rows, width), F32),
        ),
        scratch_shapes=[
            pltpu.VMEM((slots + LANES, width), BF16),
            pltpu.VMEM((2, TB, width), F32),
            pltpu.VMEM((TB, width), F32),
            pltpu.VMEM((TB, LANES), F32),
            pltpu.VMEM((TB, LANES), F32),
            pltpu.VMEM((rows, width), BF16),
            pltpu.VMEM((2, rows, half), BF16),
            pltpu.SemaphoreType.DMA((rows // TB,)),
            pltpu.SemaphoreType.DMA((2, rows // TB)),
        ],
        compiler_params=pltpu.CompilerParams(
            collective_id=3, has_side_effects=True, vmem_limit_bytes=62 * MIB
        ),
        cost_estimate=cost(
            6 * rows * slots * width + 4 * rows * width * width, 30 * rows * width + 8 * width * width
        ),
        name="combine",
    )(flow, drow, flat, stat, flat_t, hres, atwo, dy, o, extra, w_shared, prev)


def tail_kernel(
    gain_at,
    sent_ref,
    aone_ref,
    w_ref,
    extra_ref,
    x_ref,
    dh_ref,
    gwo_ref,
    small_ref,
    out_ref,
    final,
    small_out_ref,
    both,
    grads,
    w_buf,
    x_buf,
    dh_buf,
    out_buf,
    core_in,
    plane_out,
    plane_in,
    slab_out,
    slab_in,
    own_ref,
    small_own,
    small_core,
    small_plane,
    small_slab,
    load_sems,
    store_sems,
    both_sems,
    core_sems,
    plane_sems,
    slab_sems,
    final_sems,
    pass_sems,
    small_core_sems,
    small_plane_sems,
    small_slab_sems,
):
    experts = lax.axis_size("expert")
    slabs = lax.axis_size("dp")
    me, core, slab = lax.axis_index("expert"), lax.axis_index("context"), lax.axis_index("dp")
    other = 1 - core
    tokens, width = x_buf.shape
    half = width // 2
    parts = 4
    block = tokens // parts

    mine = pltpu.make_async_copy(sent_ref.at[core], both.at[core], load_sems.at[0])
    mine.start()
    loads = [
        pltpu.make_async_copy(w_ref.at[pl.ds(0, 3)], w_buf, load_sems.at[1]),
        pltpu.make_async_copy(x_ref, x_buf, load_sems.at[2]),
        pltpu.make_async_copy(dh_ref, dh_buf, load_sems.at[3]),
    ]
    for copy in loads:
        copy.start()
    greet_all(("context", "expert", "dp"))
    theirs = [
        remote(
            sent_ref.at[other, which],
            both.at[core, which],
            both_sems,
            (which,),
            {"context": other},
        )
        for which in range(3)
    ]

    def core_copy(which):
        return remote(
            grads.at[other, which], core_in.at[which], core_sems, (which,), {"context": other}
        )

    for side in range(2):
        grads[side, 3] = gwo_ref[side]
    core_copy(3).start()
    for copy in theirs:
        copy.start()

    def plane_copy(j, at):
        return remote(
            plane_out.at[j - 1, at],
            plane_in.at[j - 1, at],
            plane_sems,
            (j - 1, at),
            {"expert": lax.rem(me + j, experts)},
        )

    def pass_on(which):
        core_copy(which).wait_recv()
        j = lax.rem(which + experts - me, experts)

        @pl.when(j != 0)
        def _():
            def one(k):
                at = lax.rem(slab + k + 1, slabs)
                plane_out[j - 1, at] = (
                    grads[core, which, at].astype(F32) + core_in[which, at].astype(F32)
                ).astype(BF16)
                plane_copy(j, at).start()

            loop(slabs, one)

    mine.wait()
    turned = aone_ref[...].T
    pass_on(3)
    for which in range(3):
        theirs[which].wait_recv()
        grad = jnp.concatenate([both[0, which], both[1, which]], axis=1)
        weight = dot(turned, grad)
        for side in range(2):
            grads[side, which] = (
                weight[:, side * half : (side + 1) * half]
                .reshape(slabs, width // slabs, half)
                .astype(BF16)
            )
        core_copy(which).start()
        if which > 0:
            pass_on(which - 1)
    for copy in loads:
        copy.wait()

    gain = extra_ref[GAIN_ONE : GAIN_ONE + 1].astype(F32)
    stores = []
    gain_row = jnp.zeros((1, width), F32)
    for part in range(parts):
        at = slice(part * block, (part + 1) * block)
        dnone = None
        for which in range(3):
            grad = jnp.concatenate([both[0, which, at], both[1, which, at]], axis=1)
            whole = jnp.concatenate([w_buf[which, 0], w_buf[which, 1]], axis=1)
            product = dot_nt(grad, whole)
            dnone = product if dnone is None else dnone + product
        values = x_buf[at].astype(F32)
        scale = lax.rsqrt(jnp.mean(values * values, axis=-1, keepdims=True) + EPS)
        scaled = dnone * gain
        inner = jnp.mean(values * scaled, axis=1, keepdims=True)
        out_buf[at] = dh_buf[at] + scale * scaled - values * (scale * scale * scale * inner)
        stores.append(
            pltpu.make_async_copy(out_buf.at[at], out_ref.at[at], store_sems.at[part])
        )
        stores[-1].start()
        gain_row = gain_row + jnp.sum(dnone * values * scale, axis=0, keepdims=True)
        if part == 0:
            pass_on(2)

    row = iota(small_ref.shape, 0)
    small_own[...] = small_ref[...] + jnp.where(row == gain_at, gain_row, 0.0)
    small_copy = remote(small_own, small_core, small_core_sems, (0,), {"context": other})
    small_copy.start()
    small_copy.wait()
    small_plane[me] = small_own[...] + small_core[...]
    small_plane_copies = []
    for j in range(1, experts):
        small_plane_copies.append(
            remote(
                small_plane.at[me],
                small_plane.at[me],
                small_plane_sems,
                (j,),
                {"expert": lax.rem(me + j, experts)},
            )
        )
        small_plane_copies[-1].start()

    def gathered(at):
        value = grads[core, me, at].astype(F32) + core_in[me, at].astype(F32)
        for j in range(1, experts):
            plane_copy(j, at).wait_recv()
            value = value + plane_in[j - 1, at].astype(F32)
        return value

    def slab_copy(k):
        return remote(
            slab_out.at[k],
            slab_in.at[k],
            slab_sems,
            (k,),
            {"dp": lax.rem(slab + k + 1, slabs)},
        )

    def scatter(k):
        slab_out[k] = gathered(lax.rem(slab + k + 1, slabs)).astype(BF16)
        slab_copy(k).start()

    loop(slabs - 1, scatter)

    for copy in small_plane_copies:
        copy.wait()
    value = small_plane[0]
    for j in range(1, experts):
        value = value + small_plane[j]
    small_slab[slab] = value

    def small_slab_copy(k):
        return remote(
            small_slab.at[slab],
            small_slab.at[slab],
            small_slab_sems,
            (k,),
            {"dp": lax.rem(slab + k + 1, slabs)},
        )

    loop(slabs - 1, lambda k: small_slab_copy(k).start())

    own_ref[...] = gathered(slab)

    def collect(k):
        slab_copy(k).wait_recv()
        own_ref[...] += slab_in[k].astype(F32)

    loop(slabs - 1, collect)
    final[core, me] = own_ref[...].astype(BF16)
    final_copies, pass_copies = [], []
    for j in range(1, experts):
        final_copies.append(
            remote(
                final.at[core, me],
                final.at[core, me],
                final_sems,
                (j,),
                {"expert": lax.rem(me + j, experts)},
            )
        )
        final_copies[-1].start()
    for j in range(experts):
        source = lax.rem(me + experts - j, experts)
        if j > 0:
            final_copies[j - 1].wait_recv()
        pass_copies.append(
            remote(
                final.at[core, source],
                final.at[core, source],
                pass_sems,
                (j,),
                {"context": other},
            )
        )
        pass_copies[-1].start()

    loop(slabs - 1, lambda k: small_slab_copy(k).wait())
    small_out_ref[...] = small_slab[0]

    def add_small(k):
        small_out_ref[...] += small_slab[k + 1]

    loop(slabs - 1, add_small)

    for copy in pass_copies:
        copy.wait_recv()
    for copy in stores:
        copy.wait()
    for which in range(4):
        core_copy(which).wait_send()
    for j in range(1, experts):

        def sent(k, j=j):
            plane_copy(j, k).wait_send()

        loop(slabs, sent)
    loop(slabs - 1, lambda k: slab_copy(k).wait_send())
    for copy in theirs + final_copies + pass_copies:
        copy.wait_send()


def tail(experts, slabs, gain_at, sent, aone, w_shared, extra, x, dh, gwo, small):
    tokens, width = x.shape
    half = width // 2
    rows = width // slabs
    vmem = pl.BlockSpec(memory_space=pltpu.VMEM)
    anywhere = pl.BlockSpec(memory_space=pl.ANY)
    dma = pltpu.SemaphoreType.DMA
    return pl.pallas_call(
        functools.partial(tail_kernel, gain_at),
        in_specs=[anywhere, vmem, anywhere, vmem, anywhere, anywhere] + [vmem] * 2,
        out_specs=[anywhere] + [vmem] * 2,
        out_shape=(
            jax.ShapeDtypeStruct((tokens, width), F32),
            jax.ShapeDtypeStruct((2, experts, rows, half), BF16),
            jax.ShapeDtypeStruct(small.shape, F32),
        ),
        scratch_shapes=[
            pltpu.VMEM((2, 3, tokens, half), BF16),
            pltpu.VMEM((2, 4, slabs, rows, half), BF16),
            pltpu.VMEM((3, 2, width, half), BF16),
            pltpu.VMEM((tokens, width), BF16),
            pltpu.VMEM((tokens, width), F32),
            pltpu.VMEM((tokens, width), F32),
            pltpu.VMEM((4, slabs, rows, half), BF16),
            pltpu.VMEM((experts - 1, slabs, rows, half), BF16),
            pltpu.VMEM((experts - 1, slabs, rows, half), BF16),
            pltpu.VMEM((slabs - 1, rows, half), BF16),
            pltpu.VMEM((slabs - 1, rows, half), BF16),
            pltpu.VMEM((rows, half), F32),
            pltpu.VMEM(small.shape, F32),
            pltpu.VMEM(small.shape, F32),
            pltpu.VMEM((experts,) + small.shape, F32),
            pltpu.VMEM((slabs,) + small.shape, F32),
            dma((4,)),
            dma((4,)),
            dma((2, 3)),
            dma((2, 4)),
            dma((2, experts - 1, slabs)),
            dma((2, slabs - 1)),
            dma((2, experts)),
            dma((2, experts)),
            dma((2, 1)),
            dma((2, experts)),
            dma((2, slabs - 1)),
        ],
        compiler_params=pltpu.CompilerParams(
            collective_id=0, has_side_effects=True, vmem_limit_bytes=62 * MIB
        ),
        cost_estimate=cost(12 * tokens * width * width, 40 * tokens * width),
        name="tail",
    )(sent, aone, w_shared, extra, x, dh, gwo, small)


def finish_kernel(
    total,
    place_ref,
    small_ref,
    final_ref,
    mine_ref,
    theirs_ref,
    tokens_ref,
    norm_one_ref,
    norm_two_ref,
    router_ref,
    mix_ref,
    vec_ref,
    res_ref,
    q_ref,
    k_ref,
    v_ref,
    o_ref,
    gate_ref,
    up_ref,
    gd_ref,
    tokens_out_ref,
    tokens_buf,
    final_buf,
    share_buf,
    square_buf,
    gate_buf,
    up_buf,
    gd_buf,
    turned_ref,
    load_sems,
    store_sems,
):
    rows, half = final_buf.shape[2:]
    wide = share_buf.shape[2] // 3
    deep = gd_buf.shape[0]
    core = place_ref[1]
    loads = [
        pltpu.make_async_copy(mine_ref, share_buf.at[0], load_sems.at[0]),
        pltpu.make_async_copy(theirs_ref, share_buf.at[1], load_sems.at[1]),
        pltpu.make_async_copy(final_ref, final_buf, load_sems.at[2]),
        pltpu.make_async_copy(tokens_ref, tokens_buf, load_sems.at[3]),
    ]
    for copy in loads[3:] + loads[:3]:
        copy.start()
    small = small_ref[...]
    fill = jnp.zeros((LANES - small.shape[0], small.shape[1]), F32)
    turned_ref[...] = jnp.concatenate([small, fill], axis=0).T
    own = turned_ref[pl.ds(pl.multiple_of(place_ref[0] * rows, 8), rows), :]
    own = own.T
    router_ref[...] = own[:total]
    mix_ref[...] = own[total : total + 4]
    norm_two_ref[...] = own[total + 4 : total + 5]
    vec_ref[...] = own[total + 5 : total + 7]
    norm_one_ref[...] = own[total + 7 : total + 8]
    res_ref[...] = turned_ref[:total, total + 8 : 2 * total + 8]

    stores = []

    def store(buffer, ref):
        stores.append(pltpu.make_async_copy(buffer, ref, store_sems.at[len(stores)]))
        stores[-1].start()

    def sides(buffer, size, left, right):
        buffer[:, :size] = left
        buffer[:, size:] = right

    def ordered(get):
        first, second = get(share_buf.at[0]), get(share_buf.at[1])
        swap = core != 0
        return jnp.where(swap, second, first), jnp.where(swap, first, second)

    loads[3].wait()
    store(tokens_buf, tokens_out_ref)
    for copy in loads[:2]:
        copy.wait()
    sides(gate_buf, wide, *ordered(lambda ref: ref[:, :wide].astype(F32)))
    store(gate_buf, gate_ref.at[0])
    sides(up_buf, wide, *ordered(lambda ref: ref[:, wide : 2 * wide].astype(F32)))
    store(up_buf, up_ref.at[0])

    def down(ref):
        blocks = [
            ref[:, 2 * wide + b * deep : 2 * wide + (b + 1) * deep].astype(F32)
            for b in range(half // rows)
        ]
        return jnp.concatenate(blocks, axis=0).T

    sides(gd_buf, half, *ordered(down))
    store(gd_buf, gd_ref.at[0])
    loads[2].wait()
    for which, ref in enumerate((q_ref, k_ref, v_ref, o_ref)):
        sides(
            square_buf.at[which],
            half,
            final_buf[0, which].astype(F32),
            final_buf[1, which].astype(F32),
        )
        store(square_buf.at[which], ref)
    for copy in stores:
        copy.wait()


def finish(total, place, final, small, mine, theirs, tokens):
    rows, half = final.shape[2:]
    width = 2 * half
    wide = mine.shape[1] // 3
    deep = wide * rows // half
    anywhere = pl.BlockSpec(memory_space=pl.ANY)
    vmem = pl.BlockSpec(memory_space=pltpu.VMEM)
    shape = lambda *dims: jax.ShapeDtypeStruct(dims, F32)
    return pl.pallas_call(
        functools.partial(finish_kernel, total),
        in_specs=[pl.BlockSpec(memory_space=pltpu.SMEM), vmem] + [anywhere] * 4,
        out_specs=[vmem] * 6 + [anywhere] * 8,
        out_shape=(
            shape(1, rows),
            shape(1, rows),
            shape(total, rows),
            shape(4, rows),
            shape(2, rows),
            shape(total, total),
            shape(rows, width),
            shape(rows, width),
            shape(rows, width),
            shape(rows, width),
            shape(1, rows, 2 * wide),
            shape(1, rows, 2 * wide),
            shape(1, deep, width),
            shape(*tokens.shape),
        ),
        scratch_shapes=[
            pltpu.VMEM(tokens.shape, F32),
            pltpu.VMEM(final.shape, BF16),
            pltpu.VMEM((2,) + mine.shape, BF16),
            pltpu.VMEM((4, rows, width), F32),
            pltpu.VMEM((rows, 2 * wide), F32),
            pltpu.VMEM((rows, 2 * wide), F32),
            pltpu.VMEM((deep, width), F32),
            pltpu.VMEM((width, LANES), F32),
            pltpu.SemaphoreType.DMA((4,)),
            pltpu.SemaphoreType.DMA((8,)),
        ],
        compiler_params=params(62),
        cost_estimate=cost(1e6, 20 * rows * width),
        name="finish",
    )(place, small, final, mine, theirs, tokens)


def on_device(
    tokens,
    segments,
    routes,
    prev_logits,
    ranks,
    cotangent,
    norm_one,
    w_query,
    w_key,
    w_value,
    w_out,
    norm_two,
    router,
    w_res,
    const_mix,
    const_vec,
    w_gate,
    w_up,
    w_down,
):
    experts = lax.axis_size("expert")
    dp = lax.axis_size("dp")
    total = experts + NZ
    _, rows, width = tokens.shape
    hidden = w_gate.shape[2]
    cap = (18 * rows + 8 * total - 1) // (8 * total)
    seq = 2 * rows
    core = lax.axis_index("context")
    half = width // 2

    def mine(shard, size):
        return lax.dynamic_slice_in_dim(shard, core * size, size, 1)

    def gather(shard):
        return lax.all_gather(shard, ("context", "dp"), axis=0).reshape(
            2, dp * shard.shape[0], shard.shape[1]
        )

    extra = jnp.concatenate(
        [router, const_mix, norm_one[:, None], norm_two[:, None], const_vec], axis=1
    )
    cos, sin = (jnp.asarray(table).reshape(2, rows, LANES) for table in rope_tables(seq))
    x = tokens[0]
    dy = cotangent[0]
    w_shared, extra, flat, flat_t, low, first, qkv, aone, dy_rows = spread(
        experts,
        dp,
        cap,
        w_query,
        w_key,
        w_value,
        w_out,
        extra.astype(F32).T,
        routes[0],
        ranks[0],
        segments,
        x,
        dy,
        cos,
        sin,
    )
    w_shared = w_shared.reshape(4, 2, width, half)
    extra = extra.transpose(1, 0, 2).reshape(total + 8, width).astype(BF16)
    extra = jnp.concatenate(
        [
            extra[: total + 4],
            jnp.zeros((GAIN_ONE - total - 4, width), BF16),
            extra[total + 4 :],
            jnp.zeros((LANES - GAIN_ONE - 4, width), BF16),
        ],
        axis=0,
    )
    wide_mine = [mine(w_gate[0], hidden // 2), mine(w_up[0], hidden // 2)]
    down_mine = mine(w_down[0], half)
    deep = hidden // dp
    if deep == FC:
        turned = down_mine.T.reshape(-1, width // dp, deep).transpose(1, 0, 2)
        wide_w = gather(jnp.concatenate(wide_mine + [turned.reshape(width // dp, -1)], axis=1))
        down_w = wide_w
    else:
        wide_w = gather(jnp.concatenate(wide_mine, axis=1))
        down_w = gather(down_mine).transpose(0, 2, 1)

    res = jnp.pad(w_res.astype(F32), ((0, 0), (0, LANES - total)))

    dy_rows = lax.all_to_all(dy_rows, "expert", split_axis=0, concat_axis=0, tiled=True)
    o_keep, o_give, lse = attend(first, qkv, low)
    o_give, dy_rows = lax.optimization_barrier((o_give, dy_rows))
    o_theirs = lax.ppermute(o_give, "context", [(0, 1), (1, 0)])
    hres, atwo, stat, o = middle(
        total, first, x, o_keep, o_theirs, w_shared, extra, prev_logits[0], res, routes[0]
    )
    flow_back, drow_back, grad_wide = run_experts(
        total, experts, dp, hidden, cap, flat_t, atwo, dy_rows, stat, wide_w, down_w
    )
    flow_back = flow_back.reshape(experts * cap, width)
    drow_back = drow_back.reshape(experts * cap, width)
    wide = lax.psum_scatter(
        grad_wide.reshape(width, 3 * hidden // 2), "dp", scatter_dimension=0, tiled=True
    )

    output, dh, grad_o, grad_out_w, small = combine(
        experts,
        total,
        flow_back,
        drow_back,
        flat,
        stat,
        flat_t,
        hres,
        atwo,
        dy,
        o,
        w_shared,
        extra,
        prev_logits[0],
    )
    grads_sent, output = attend_back(
        first,
        qkv,
        grad_o,
        o_keep,
        o_give,
        lse,
        low,
        cos,
        sin,
        output,
    )
    grad_tokens, final, small = tail(
        experts,
        dp,
        total + 7,
        grads_sent,
        aone,
        w_shared,
        extra,
        x,
        dh,
        grad_out_w.reshape(2, dp, width // dp, half),
        small,
    )
    wide, small = lax.optimization_barrier((wide, small))
    wide_other = lax.ppermute(wide, "context", [(0, 1), (1, 0)])
    (
        grad_norm_one,
        grad_norm_two,
        grad_router,
        grad_mix,
        grad_vec,
        grad_res,
        grad_query,
        grad_key,
        grad_value,
        grad_out,
        grad_gate,
        grad_up,
        grad_down,
        grad_tokens,
    ) = finish(
        total,
        jnp.stack([lax.axis_index("dp"), core]),
        final,
        small,
        wide,
        wide_other,
        grad_tokens,
    )
    return (
        output[None],
        grad_tokens[None],
        grad_norm_one[0],
        grad_query,
        grad_key,
        grad_value,
        grad_out,
        grad_norm_two[0],
        grad_router.T,
        grad_res,
        grad_mix.T,
        grad_vec.T,
        grad_gate,
        grad_up,
        grad_down,
    )


def solution(mesh):
    token = P(("expert", "dp"), "context", None)
    rows = P("dp", None)
    expert = P("expert", "dp", None)
    in_specs = (
        token,
        P(("expert", "dp"), "context"),
        token,
        token,
        token,
        token,
        P("dp"),
        rows,
        rows,
        rows,
        rows,
        P("dp"),
        rows,
        P(),
        rows,
        rows,
        expert,
        expert,
        expert,
    )
    out_specs = (
        token,
        token,
        P("dp"),
        rows,
        rows,
        rows,
        rows,
        P("dp"),
        rows,
        P(),
        rows,
        rows,
        expert,
        expert,
        expert,
    )
    return jax.shard_map(
        on_device, mesh=mesh, in_specs=in_specs, out_specs=out_specs, check_vma=False
    )
```

```python
import functools

import jax
import jax.numpy as jnp
import numpy as np
from jax import lax
from jax.experimental import pallas as pl
from jax.experimental.pallas import tpu as pltpu
from jax.sharding import PartitionSpec as P

HEADS = 12
HEAD_DIM = 64
WIN = 1024
NZ = 4
SEGMENTS = 5
GAIN_ONE, GAIN_TWO, VECS = 112, 113, 114
TQ = 256
TB = 256
RC = 64
FC = 512
LANES = 128
EPS = 1e-05
MASKED = -1000000000.0
HIGH = lax.Precision.HIGHEST
F32 = jnp.float32
BF16 = jnp.bfloat16
MIB = 1024 * 1024


def params(mib):
    return pltpu.CompilerParams(vmem_limit_bytes=mib * MIB)


def cost(flops, nbytes, trans=0):
    return pl.CostEstimate(flops=int(flops), bytes_accessed=int(nbytes), transcendentals=int(trans))


def dot(left, right):
    return jnp.dot(left, right, preferred_element_type=F32)


def dot_nt(left, right):
    return lax.dot_general(left, right, (((1,), (1,)), ((), ())), preferred_element_type=F32)


def dot_tn(left, right):
    return lax.dot_general(left, right, (((0,), (0,)), ((), ())), preferred_element_type=F32)


def iota(shape, axis):
    return lax.broadcasted_iota(jnp.int32, shape, axis)


def rope_tables(seq):
    half = HEAD_DIM // 2
    frequency = np.float32(10000.0) ** (
        -np.arange(half, dtype=np.float32) * np.float32(2.0) / np.float32(HEAD_DIM)
    )
    angles = np.arange(seq, dtype=np.float32)[:, None] * frequency.astype(np.float32)[None, :]
    cos = np.cos(angles.astype(np.float64)).astype(np.float32)
    sin = np.sin(angles.astype(np.float64)).astype(np.float32)
    return np.concatenate([cos] * 4, axis=1), np.concatenate([-sin, sin, -sin, sin], axis=1)


def swap_halves(chunk):
    lane = iota(chunk.shape, 1)
    return jnp.where(
        lane % HEAD_DIM < HEAD_DIM // 2, pltpu.roll(chunk, 96, 1), pltpu.roll(chunk, 32, 1)
    )


def loop(count, body):
    if count <= 4:
        for step in range(count):
            body(step)
    else:
        lax.fori_loop(0, count, lambda step, carry: (body(step), carry)[1], 0)


def remote(src, dst, sems, index, where):
    return pltpu.make_async_remote_copy(
        src_ref=src,
        dst_ref=dst,
        send_sem=sems.at[(0,) + index],
        recv_sem=sems.at[(1,) + index],
        device_id=where,
        device_id_type=pl.DeviceIdType.MESH,
    )


def greet_all(axes):
    barrier = pltpu.get_barrier_semaphore()
    total = 0
    for axis in axes:
        size = lax.axis_size(axis)
        me = lax.axis_index(axis)
        total += size - 1

        def greet(k, axis=axis, size=size, me=me):
            pl.semaphore_signal(
                barrier,
                inc=1,
                device_id={axis: lax.rem(me + k + 1, size)},
                device_id_type=pl.DeviceIdType.MESH,
            )

        loop(size - 1, greet)
    pl.semaphore_wait(barrier, total)


def place_pairs(experts, cap, routes_ref, ranks_ref, flat_ref, flat_t_ref):
    rows = routes_ref.shape[0]
    lane = iota((rows, LANES), 1)
    first, second = routes_ref[:, 0:1], routes_ref[:, 1:2]
    hot_first, hot_second = first == lane, second == lane
    hot = (hot_first.astype(F32) + hot_second.astype(F32)).astype(BF16)
    ranks = ranks_ref[...].astype(F32)
    ranks_col = jnp.broadcast_to(ranks, (LANES, rows)).T[:, 0:1]
    earlier = jnp.where(ranks < ranks_col, 1.0, 0.0).astype(BF16)
    counts = dot(earlier, hot)

    def flat(hit, route):
        slot = jnp.sum(jnp.where(hit, counts, 0.0), axis=1, keepdims=True).astype(jnp.int32)
        return jnp.where((route < experts) & (slot < cap), route * cap + slot, experts * cap)

    columns = (flat(hot_first, first), flat(hot_second, second), first, second)
    out = jnp.zeros((rows, LANES), jnp.int32)
    for i, column in enumerate(columns):
        out = jnp.where(lane == i, column, out)
    flat_ref[...] = out
    flat_t_ref[...] = out.astype(F32).T[:8]


def find_starts(segs_ref, low_ref, first_ref):
    rows = segs_ref.shape[2]
    per = rows // TQ
    segs = [segs_ref[side].astype(F32) for side in range(2)]
    starts = [jnp.zeros((1, rows), F32) for side in range(2)]
    for number in range(1, SEGMENTS):
        before = sum(
            jnp.sum(jnp.where(part < number, 1.0, 0.0), axis=1, keepdims=True) for part in segs
        )
        starts = [
            jnp.where(part == number, before, start) for part, start in zip(segs, starts)
        ]
    for side in range(2):
        place = (iota((1, rows), 1) + (side * rows - WIN + 1)).astype(F32)
        low = jnp.maximum(starts[side], place)
        for tile in range(per):
            part = low[:, tile * TQ : (tile + 1) * TQ]
            low_ref[side * per + tile] = part.astype(jnp.int32)
            first_ref[side * per + tile] = jnp.min(part).astype(jnp.int32) // TQ
    first_ref[2 * per] = lax.axis_index("context")


def hot_slots(flat_ref, cap, target):
    slot = (iota((cap, flat_ref.shape[1]), 0) + target * cap).astype(F32)
    return flat_ref[0:1, :] == slot, flat_ref[1:2, :] == slot


def spread_kernel(
    cap,
    w_query_ref,
    w_key_ref,
    w_value_ref,
    w_out_ref,
    extra_ref,
    routes_ref,
    ranks_ref,
    segs_ref,
    x_ref,
    dy_ref,
    cos_ref,
    sin_ref,
    shared_ref,
    extra_out_ref,
    flat_ref,
    flat_t_ref,
    low_ref,
    first_ref,
    qkv_ref,
    aone_ref,
    dy_rows_ref,
    out_ref,
    segs_all,
    stage_ref,
    slab_sems,
    plane_sems,
    core_sems,
    extra_sems,
    segs_sems,
    shared_sem,
    own_sems,
    qkv_sems,
):
    experts = lax.axis_size("expert")
    slabs = lax.axis_size("dp")
    me, core, slab = lax.axis_index("expert"), lax.axis_index("context"), lax.axis_index("dp")
    half = out_ref.shape[4]
    for which, ref in enumerate((w_query_ref, w_key_ref, w_value_ref, w_out_ref)):
        for side in range(2):

            @pl.when((me == which) & (core == side))
            def _():
                out_ref[which, side, slab] = ref[:, side * half : (side + 1) * half]

    extra_out_ref[slab] = extra_ref[...]
    segs_all[core] = segs_ref[...]
    greet_all(("context", "expert", "dp"))

    def slab_copy(k):
        piece = out_ref.at[me, core, slab]
        return remote(piece, piece, slab_sems, (k,), {"dp": lax.rem(slab + k + 1, slabs)})

    def extra_copy(k):
        piece = extra_out_ref.at[slab]
        return remote(piece, piece, extra_sems, (k,), {"dp": lax.rem(slab + k + 1, slabs)})

    def plane_copy(j, at):
        piece = out_ref.at[me, core, at]
        return remote(
            piece, piece, plane_sems, (j - 1, at), {"expert": lax.rem(me + j, experts)}
        )

    def core_copy(j, at):
        piece = out_ref.at[lax.rem(me + experts - j, experts), core, at]
        return remote(piece, piece, core_sems, (j, at), {"context": 1 - core})

    def share(at):
        for j in range(1, experts):
            plane_copy(j, at).start()
        core_copy(0, at).start()

    loop(slabs - 1, lambda k: extra_copy(k).start())
    loop(slabs - 1, lambda k: slab_copy(k).start())
    share(slab)
    segs_copy = remote(
        segs_all.at[core], segs_all.at[core], segs_sems, (0,), {"context": 1 - core}
    )
    segs_copy.start()
    place_pairs(experts, cap, routes_ref, ranks_ref, flat_ref, flat_t_ref)
    segs_copy.wait()
    find_starts(segs_all, low_ref, first_ref)
    loop(slabs - 1, lambda k: extra_copy(k).wait())
    at = extra_ref.shape[0] - 4
    gain = jnp.concatenate([extra_out_ref[z, at : at + 1, :] for z in range(slabs)], axis=1)
    tokens = x_ref.shape[0]
    for start in range(0, tokens, TB):
        values = x_ref[start : start + TB].astype(F32)
        scale = lax.rsqrt(jnp.mean(values * values, axis=-1, keepdims=True) + EPS)
        aone_ref[start : start + TB] = (values * scale * gain).astype(BF16)

    def forward(k):
        slab_copy(k).wait_recv()
        share(lax.rem(slab + slabs - k - 1, slabs))

    loop(slabs - 1, forward)
    for target in range(experts):
        first, second = hot_slots(flat_t_ref, cap, target)
        hot = jnp.where(first | second, 1.0, 0.0).astype(BF16)
        dy_rows_ref[target] = dot(hot, dy_ref[...]).astype(BF16)

    def relay(k):
        at = lax.rem(slab + slabs - k, slabs)
        for j in range(1, experts):
            plane_copy(j, at).wait_recv()
            core_copy(j, at).start()

    loop(slabs, relay)
    loop(slabs - 1, lambda k: slab_copy(k).wait_send())

    def arrive(at):
        for j in range(experts):
            core_copy(j, at).wait()
        for j in range(1, experts):
            plane_copy(j, at).wait_send()

    loop(slabs, arrive)
    keep = pltpu.make_async_copy(out_ref, shared_ref, shared_sem)
    keep.start()

    width = 2 * half
    wholes = [
        jnp.concatenate(
            [out_ref[which, side].reshape(width, half) for side in range(2)], axis=1
        )
        for which in range(3)
    ]
    copies = []
    for block in range(tokens // TB):
        span = slice(block * TB, (block + 1) * TB)
        cos, sin = cos_ref[core, span], sin_ref[core, span]
        for which in range(3):
            product = dot(aone_ref[span], wholes[which])
            for pair in range(width // LANES):
                chunk = product[:, pair * LANES : (pair + 1) * LANES]
                if which < 2:
                    chunk = chunk * cos + swap_halves(chunk) * sin
                if which == 0:
                    chunk = chunk * HEAD_DIM ** (-0.5)
                side, place_in = pair // (half // LANES), pair % (half // LANES)
                stage_ref[side, which, span, place_in * LANES : (place_in + 1) * LANES] = (
                    chunk.astype(BF16)
                )
        copies.append(
            pltpu.make_async_copy(
                stage_ref.at[core, :, span], qkv_ref.at[core, :, span], own_sems.at[block]
            )
        )
        copies.append(
            remote(
                stage_ref.at[1 - core, :, span],
                qkv_ref.at[core, :, span],
                qkv_sems,
                (block,),
                {"context": 1 - core},
            )
        )
        for copy in copies[-2:]:
            copy.start()
    for copy in copies:
        copy.wait()
    keep.wait()


def spread(
    experts, slabs, cap, w_query, w_key, w_value, w_out, extra, routes, ranks, segs, x, dy, cos, sin
):
    tokens = routes.shape[0]
    tiles = 2 * tokens // TQ
    rows, width = w_query.shape
    half = width // 2
    vmem = pl.BlockSpec(memory_space=pltpu.VMEM)
    anywhere = pl.BlockSpec(memory_space=pl.ANY)
    dma = pltpu.SemaphoreType.DMA
    return pl.pallas_call(
        functools.partial(spread_kernel, cap),
        in_specs=[vmem] * 12,
        out_specs=[anywhere]
        + [vmem] * 4
        + [pl.BlockSpec(memory_space=pltpu.SMEM), anywhere, vmem, vmem],
        out_shape=(
            jax.ShapeDtypeStruct((4, 2, slabs, rows, half), BF16),
            jax.ShapeDtypeStruct((slabs,) + extra.shape, F32),
            jax.ShapeDtypeStruct((tokens, LANES), jnp.int32),
            jax.ShapeDtypeStruct((8, tokens), F32),
            jax.ShapeDtypeStruct((tiles, 1, TQ), jnp.int32),
            jax.ShapeDtypeStruct((tiles + 1,), jnp.int32),
            jax.ShapeDtypeStruct((2, 3, tokens, half), BF16),
            jax.ShapeDtypeStruct((tokens, width), BF16),
            jax.ShapeDtypeStruct((experts, cap, width), BF16),
        ),
        scratch_shapes=[
            pltpu.VMEM((4, 2, slabs, rows, half), BF16),
            pltpu.VMEM((2, 1, tokens), jnp.int32),
            pltpu.VMEM((2, 3, tokens, half), BF16),
            dma((2, slabs - 1)),
            dma((2, experts - 1, slabs)),
            dma((2, experts, slabs)),
            dma((2, slabs - 1)),
            dma((2, 1)),
            dma,
            dma((tokens // TB,)),
            dma((2, tokens // TB)),
        ],
        compiler_params=pltpu.CompilerParams(
            collective_id=1, has_side_effects=True, vmem_limit_bytes=62 * MIB
        ),
        cost_estimate=cost(1e6, 16 * width * width),
        name="spread",
    )(w_query, w_key, w_value, w_out, extra, routes, ranks, segs, x, dy, cos, sin)


def head_masks():
    lane = iota((TQ, LANES), 1)
    low = jnp.where(lane < HEAD_DIM, 1.0, 0.0).astype(BF16)
    return low, (1.0 - low.astype(F32)).astype(BF16)


def spans(tile, first, body):
    for count in range(1, WIN // TQ + 2):

        @pl.when(tile - first + 1 == count)
        def _():
            body(count)


def masked(scores, low, start, count):
    shape = (TQ, 2 * TQ)
    sub, lane = iota(shape, 0), lax.rem(iota(shape, 1), TQ)
    low = jnp.concatenate([low, low], axis=1)
    parts = []
    for t in range(count):
        mark = sub >= low - (start + t * TQ)
        if t == count - 1:
            mark = mark & (sub <= lane)
        parts.append(jnp.where(mark, scores[t * TQ : (t + 1) * TQ], MASKED))
    return parts


def own_blocks(both):
    return jnp.concatenate([both[:HEAD_DIM, :TQ], both[HEAD_DIM:LANES, TQ:]], axis=0)


def attend_kernel(
    first_ref, q_ref, k_ref, v_ref, lo_ref, keep_ref, give_ref, lse_ref, keys_ref, vt_ref
):
    rows = q_ref.shape[2]
    per = rows // TQ
    masks = head_masks()
    for side in range(2):
        at = slice(side * rows, (side + 1) * rows)
        keys_ref[at, :] = k_ref[side, 0]
        vt_ref[:LANES, at] = v_ref[side, 0].T
        vt_ref[LANES:, at] = jnp.ones((16, rows), BF16)

    def q_step(qi, carry):
        at = pl.ds(pl.multiple_of(lax.rem(qi, per) * TQ, TQ), TQ)
        query = q_ref[qi // per, 0, at, :]
        low = lo_ref[qi]

        def run(count):
            start = pl.multiple_of((qi - count + 1) * TQ, TQ)
            span = pl.ds(start, count * TQ)
            both = jnp.concatenate([query * mask for mask in masks], axis=0)
            scores = masked(dot_nt(keys_ref[span, :], both), low, start, count)
            peak = functools.reduce(
                jnp.maximum, [jnp.max(part, axis=0, keepdims=True) for part in scores]
            )
            probs = jnp.concatenate([jnp.exp(part - peak).astype(BF16) for part in scores], axis=0)
            mixed = dot(vt_ref[:, span], probs)
            total = mixed[LANES : LANES + 1]
            lse_ref[0, qi, 0:1, :] = peak + jnp.log(total)
            out = own_blocks(mixed[:LANES] / total).T.astype(BF16)

            @pl.when(qi // per == first_ref[2 * per])
            def _():
                keep_ref[at, :] = out

            @pl.when(qi // per != first_ref[2 * per])
            def _():
                give_ref[at, :] = out

        spans(qi, first_ref[qi], run)
        return carry

    lax.fori_loop(0, 2 * per, q_step, 0)


def part_spec(which, rows):
    return pl.BlockSpec((2, 1, rows, LANES), lambda p, first, which=which: (0, which, 0, p))


def attend(first, qkv, low):
    _, _, rows, half = qkv.shape
    pairs = half // LANES
    tiles = 2 * rows // TQ
    return pl.pallas_call(
        attend_kernel,
        grid_spec=pltpu.PrefetchScalarGridSpec(
            num_scalar_prefetch=1,
            grid=(pairs,),
            in_specs=[
                part_spec(0, rows),
                part_spec(1, rows),
                part_spec(2, rows),
                pl.BlockSpec((tiles, 1, TQ), lambda p, first: (0, 0, 0)),
            ],
            out_specs=[
                pl.BlockSpec((rows, LANES), lambda p, first: (0, p)),
                pl.BlockSpec((rows, LANES), lambda p, first: (0, p)),
                pl.BlockSpec((1, tiles, 8, 2 * TQ), lambda p, first: (p, 0, 0, 0)),
            ],
            scratch_shapes=[
                pltpu.VMEM((2 * rows, LANES), BF16),
                pltpu.VMEM((LANES + 16, 2 * rows), BF16),
            ],
        ),
        out_shape=(
            jax.ShapeDtypeStruct((rows, half), BF16),
            jax.ShapeDtypeStruct((rows, half), BF16),
            jax.ShapeDtypeStruct((pairs, tiles, 8, 2 * TQ), F32),
        ),
        compiler_params=params(62),
        cost_estimate=cost(40e9, 16 * rows * half, 12e6),
        name="attend",
    )(first, qkv, qkv, qkv, low)


def attend_back_kernel(
    first_ref,
    q_ref,
    k_ref,
    v_ref,
    do_ref,
    keep_ref,
    give_ref,
    lse_ref,
    lo_ref,
    cos_ref,
    sin_ref,
    layer_ref,
    g_ref,
    layer_out_ref,
    keys_ref,
    values_ref,
    kt_ref,
    delta_ref,
    dk_ref,
    dv_ref,
):
    rows = q_ref.shape[2]
    per = rows // TQ
    masks = head_masks()
    for side in range(2):
        at = slice(side * rows, (side + 1) * rows)
        keys_ref[at, :] = k_ref[side, 0]
        values_ref[at, :] = v_ref[side, 0]
        kt_ref[:, at] = k_ref[side, 0].T
    layer_out_ref[...] = layer_ref[...]
    dk_ref[...] = jnp.zeros_like(dk_ref)
    dv_ref[...] = jnp.zeros_like(dv_ref)

    def prepare(tile, carry):
        at = pl.ds(pl.multiple_of(lax.rem(tile, per) * TQ, TQ), TQ)
        out = jnp.where(tile // per == first_ref[2 * per], keep_ref[at, :], give_ref[at, :])
        both = out.astype(F32) * do_ref[tile // per, at, :].astype(F32)
        both = both.T
        delta_ref[tile, 0:1, :TQ] = jnp.sum(both[:HEAD_DIM], axis=0, keepdims=True)
        delta_ref[tile, 0:1, TQ:] = jnp.sum(both[HEAD_DIM:], axis=0, keepdims=True)
        return carry

    lax.fori_loop(0, 2 * per, prepare, 0)

    def q_step(qi, carry):
        at = pl.ds(pl.multiple_of(lax.rem(qi, per) * TQ, TQ), TQ)
        query = q_ref[qi // per, 0, at, :]
        grad = do_ref[qi // per, at, :]
        low = lo_ref[qi]

        def run(count):
            start = pl.multiple_of((qi - count + 1) * TQ, TQ)
            span = pl.ds(start, count * TQ)
            queries = jnp.concatenate([query * mask for mask in masks], axis=0)
            grads = jnp.concatenate([grad * mask for mask in masks], axis=0)
            lse, delta = lse_ref[0, qi, 0:1, :], delta_ref[qi, 0:1, :]
            scores = masked(dot_nt(keys_ref[span, :], queries), low, start, count)
            grad_probs = dot_nt(values_ref[span, :], grads)
            probs = [jnp.exp(part - lse) for part in scores]
            grad_scores = jnp.concatenate(
                [
                    (part * (grad_probs[t * TQ : (t + 1) * TQ] - delta)).astype(BF16)
                    for t, part in enumerate(probs)
                ],
                axis=0,
            )
            probs = jnp.concatenate([part.astype(BF16) for part in probs], axis=0)
            dv_ref[span, :] += dot(probs, grads)
            dk_ref[span, :] += dot(grad_scores, queries)
            turned = own_blocks(dot(kt_ref[:, span], grad_scores))
            grad_query = turned.T * HEAD_DIM ** (-0.5)
            cos, sin = cos_ref[qi // per, at, :], sin_ref[qi // per, at, :]
            g_ref[qi // per, 0, at, :] = (
                grad_query * cos - swap_halves(grad_query) * sin
            ).astype(BF16)

        spans(qi, first_ref[qi], run)
        return carry

    lax.fori_loop(0, 2 * per, q_step, 0)

    def finish(tile, carry):
        at = pl.ds(pl.multiple_of(lax.rem(tile, per) * TQ, TQ), TQ)
        span = pl.ds(pl.multiple_of(tile * TQ, TQ), TQ)
        cos, sin = cos_ref[tile // per, at, :], sin_ref[tile // per, at, :]
        grad_key = dk_ref[span, :]
        g_ref[tile // per, 1, at, :] = (grad_key * cos - swap_halves(grad_key) * sin).astype(BF16)
        g_ref[tile // per, 2, at, :] = dv_ref[span, :].astype(BF16)
        return carry

    lax.fori_loop(0, 2 * per, finish, 0)


def attend_back(first, qkv, grad_o, keep, give, lse, low, cos, sin, layer):
    _, _, rows, half = qkv.shape
    pairs = half // LANES
    tiles = 2 * rows // TQ
    side = pl.BlockSpec((2, rows, LANES), lambda p, first: (0, 0, p))
    table = pl.BlockSpec((2, rows, LANES), lambda p, first: (0, 0, 0))
    return pl.pallas_call(
        attend_back_kernel,
        grid_spec=pltpu.PrefetchScalarGridSpec(
            num_scalar_prefetch=1,
            grid=(pairs,),
            in_specs=[
                part_spec(0, rows),
                part_spec(1, rows),
                part_spec(2, rows),
                side,
                pl.BlockSpec((rows, LANES), lambda p, first: (0, p)),
                pl.BlockSpec((rows, LANES), lambda p, first: (0, p)),
                pl.BlockSpec((1, tiles, 8, 2 * TQ), lambda p, first: (p, 0, 0, 0)),
                pl.BlockSpec((tiles, 1, TQ), lambda p, first: (0, 0, 0)),
                table,
                table,
                pl.BlockSpec((rows, 2 * LANES), lambda p, first: (0, p)),
            ],
            out_specs=[
                pl.BlockSpec((2, 3, rows, LANES), lambda p, first: (0, 0, 0, p)),
                pl.BlockSpec((rows, 2 * LANES), lambda p, first: (0, p)),
            ],
            scratch_shapes=[
                pltpu.VMEM((2 * rows, LANES), BF16),
                pltpu.VMEM((2 * rows, LANES), BF16),
                pltpu.VMEM((LANES, 2 * rows), BF16),
                pltpu.VMEM((tiles, 8, 2 * TQ), F32),
                pltpu.VMEM((2 * rows, LANES), F32),
                pltpu.VMEM((2 * rows, LANES), F32),
            ],
        ),
        out_shape=(
            jax.ShapeDtypeStruct((2, 3, rows, half), BF16),
            jax.ShapeDtypeStruct(layer.shape, BF16),
        ),
        compiler_params=params(62),
        cost_estimate=cost(100e9, 32 * rows * half, 12e6),
        name="attend_back",
    )(first, qkv, qkv, qkv, grad_o, keep, give, lse, low, cos, sin, layer)


def middle_kernel(
    total,
    first_ref,
    x_ref,
    mine_ref,
    theirs_ref,
    w_ref,
    extra_ref,
    prev_ref,
    res_ref,
    routes_ref,
    hres_ref,
    atwo_ref,
    stat_ref,
    attended_ref,
):
    mine, theirs = mine_ref[...], theirs_ref[...]
    swap = first_ref[first_ref.shape[0] - 1] != 0
    attended = jnp.concatenate(
        [jnp.where(swap, theirs, mine), jnp.where(swap, mine, theirs)], axis=1
    )
    attended_ref[...] = attended
    hres = x_ref[...].astype(F32) + dot(
        attended, jnp.concatenate([w_ref[0, 0], w_ref[0, 1]], axis=1)
    )
    hres_ref[...] = hres
    scale = lax.rsqrt(jnp.mean(hres * hres, axis=-1, keepdims=True) + EPS)
    extra = extra_ref[...]
    gain = extra[GAIN_TWO : GAIN_TWO + 1].astype(F32)
    atwo = (hres * scale * gain).astype(BF16)
    atwo_ref[...] = atwo
    logits = dot_nt(atwo, extra)
    for j in range(total):
        logits = logits + prev_ref[:, j : j + 1] * res_ref[j : j + 1, :]
    lane = iota(logits.shape, 1)

    def soft(inside):
        peak = jnp.max(jnp.where(inside, logits, -jnp.inf), axis=1, keepdims=True)
        powers = jnp.where(inside, jnp.exp(jnp.where(inside, logits - peak, 0.0)), 0.0)
        return powers / jnp.sum(powers, axis=1, keepdims=True)

    probs = soft(lane < total)
    stat = probs
    for j in range(2):
        start = total + 2 * j
        stat = stat + soft((lane >= start) & (lane < start + 2))
    stat = jnp.where(lane == total + 4, scale, stat)
    for k in range(2):
        gate = jnp.sum(
            jnp.where(lane == routes_ref[:, k : k + 1], probs, 0.0), axis=1, keepdims=True
        )
        stat = jnp.where(lane == total + 5 + k, gate, stat)
    stat_ref[...] = stat


def middle(total, first, x, o, theirs, w_shared, extra, prev, res, routes):
    rows, width = x.shape
    token = lambda i: (i, 0)
    whole = lambda i: (0, 0)
    return pl.pallas_call(
        functools.partial(middle_kernel, total),
        grid=(rows // TB,),
        in_specs=[
            pl.BlockSpec(memory_space=pltpu.SMEM),
            pl.BlockSpec((TB, width), token),
            pl.BlockSpec((TB, width // 2), token),
            pl.BlockSpec((TB, width // 2), token),
            pl.BlockSpec((1, 2, width, width // 2), lambda i: (3, 0, 0, 0)),
            pl.BlockSpec((LANES, width), whole),
            pl.BlockSpec((TB, total), token),
            pl.BlockSpec((total, LANES), whole),
            pl.BlockSpec((TB, 2), token),
        ],
        out_specs=[
            pl.BlockSpec((TB, width), token),
            pl.BlockSpec((TB, width), token),
            pl.BlockSpec((TB, LANES), token),
            pl.BlockSpec((TB, width), token),
        ],
        out_shape=(
            jax.ShapeDtypeStruct((rows, width), F32),
            jax.ShapeDtypeStruct((rows, width), BF16),
            jax.ShapeDtypeStruct((rows, LANES), F32),
            jax.ShapeDtypeStruct((rows, width), BF16),
        ),
        compiler_params=params(62),
        cost_estimate=cost(2 * rows * width * width, 2 * width * width + 10 * rows * width),
        name="middle",
    )(first, x, o, theirs, w_shared, extra, prev, res, routes)


def expert_kernel(
    total,
    flat_ref,
    atwo_ref,
    dy_ref,
    stat_ref,
    wide_ref,
    wd_ref,
    flow_ref,
    drow_ref,
    gw_ref,
    send_x,
    send_g,
    all_x,
    all_g,
    send_gate,
    all_gate,
    acc_ref,
    z_ref,
    a_ref,
    b_ref,
    turned_ref,
    turned_g,
    kept_ref,
    wide_buf,
    down_buf,
    wide_given,
    wide_taken,
    down_given,
    down_taken,
    dy_sems,
    x_sems,
    g_sems,
    flow_sems,
    drow_sems,
    local_sems,
    weight_sems,
    wide_sems,
    down_sems,
):
    experts, cap, width = all_x.shape
    slots = experts * cap
    chunks = z_ref.shape[0]
    per = chunks // 2
    half = width // 2
    slabs, rows_out = gw_ref.shape[:2]
    deep = chunks * FC // slabs
    me, core = lax.axis_index("expert"), lax.axis_index("context")

    def down_pieces(chunk):
        if deep == FC:
            rows = pl.ds(pl.multiple_of(chunk * rows_out, rows_out), rows_out)
            return [
                (
                    wd_ref.at[side, rows, 2 * per * FC + b * deep : 2 * per * FC + (b + 1) * deep],
                    side * half + b * rows_out,
                    rows_out,
                )
                for side in range(2)
                for b in range(half // rows_out)
            ]
        at = pl.ds(pl.multiple_of(chunk * FC, FC), FC)
        return [(wd_ref.at[side, :, at], side * half, half) for side in range(2)]

    def weights(step):
        chunk, slot = lax.rem(step, chunks), lax.rem(step, 2)
        gate_at = pl.ds(pl.multiple_of(lax.rem(chunk, per) * FC, FC), FC)
        up_at = pl.ds(pl.multiple_of((per + lax.rem(chunk, per)) * FC, FC), FC)
        return (
            pltpu.make_async_copy(
                wide_ref.at[chunk // per, :, gate_at], wide_buf.at[slot, 0], weight_sems.at[slot, 0]
            ),
            pltpu.make_async_copy(
                wide_ref.at[chunk // per, :, up_at], wide_buf.at[slot, 1], weight_sems.at[slot, 1]
            ),
        ) + tuple(
            pltpu.make_async_copy(
                source, down_buf.at[slot, at : at + size, :], weight_sems.at[slot, 2 + i]
            )
            for i, (source, at, size) in enumerate(down_pieces(chunk))
        )

    def next_weights(step):
        @pl.when(step + 1 < 6 * chunks)
        def _():
            for copy in weights(step + 1):
                copy.start()

        for copy in weights(step):
            copy.wait()

    for copy in weights(0):
        copy.start()
    greet_all(("context", "expert"))

    for j in range(experts):
        pltpu.make_async_copy(
            dy_ref.at[lax.rem(me + experts - j, experts)], all_g.at[j], dy_sems.at[j]
        ).start()
    gates = stat_ref[...].T
    x_copies, g_copies = {}, {}
    for j in list(range(1, experts)) + [0]:
        target = lax.rem(me + j, experts)
        first, second = hot_slots(flat_ref, cap, target)
        rows = dot(jnp.where(first | second, 1.0, 0.0).astype(BF16), atwo_ref[...]).astype(BF16)
        gate = jnp.sum(
            jnp.where(first, gates[total + 5 : total + 6], 0.0)
            + jnp.where(second, gates[total + 6 : total + 7], 0.0),
            axis=1,
            keepdims=True,
        )
        gate = jnp.broadcast_to(gate, (cap, LANES)).T[:8]
        if j == 0:
            all_x[0] = rows
            all_gate[0] = gate
        else:
            send_gate[j - 1] = gate
            send_x[j - 1] = rows
            g_copies[j] = remote(
                send_gate.at[j - 1], all_gate.at[j], g_sems, (j - 1,), {"expert": target}
            )
            x_copies[j] = remote(
                send_x.at[j - 1], all_x.at[j], x_sems, (j - 1,), {"expert": target}
            )
            g_copies[j].start()
            x_copies[j].start()

    def weigh(j):
        pltpu.make_async_copy(
            dy_ref.at[lax.rem(me + experts - j, experts)], all_g.at[j], dy_sems.at[j]
        ).wait()
        gate = jnp.broadcast_to(all_gate[j, 0:1, :], (LANES, cap)).T[:, 0:1]
        all_g[j] = (all_g[j].astype(F32) * gate).astype(BF16)

    def back(buffer, dest, sems, j):
        return remote(
            buffer.at[j - 1],
            dest.at[me],
            sems,
            (j - 1,),
            {"expert": lax.rem(me + experts - j, experts)},
        )

    acc_ref[...] = jnp.zeros_like(acc_ref)

    def up(first, last, at):
        span = slice(first * cap, last * cap)

        def one(step, carry):
            next_weights(step + at * chunks)
            slot = lax.rem(step + at * chunks, 2)
            rows = all_x[first:last].reshape((last - first) * cap, width)
            gate = dot(rows, wide_buf[slot, 0])
            lift = dot(rows, wide_buf[slot, 1])
            sig = 1.0 / (1.0 + jnp.exp(-gate))
            swish = gate * sig
            hidden = (swish * lift).astype(BF16)
            z_ref[step, span] = hidden
            a_ref[step, span] = (lift * sig * (1.0 + gate * (1.0 - sig))).astype(BF16)
            b_ref[step, span] = swish.astype(BF16)
            acc_ref[span, :] += dot_nt(hidden, down_buf[slot])
            return carry

        lax.fori_loop(0, chunks, one, 0)

    def down(first, last, at):
        span = slice(first * cap, last * cap)

        def one(step, carry):
            next_weights(step + at * chunks)
            slot = lax.rem(step + at * chunks, 2)
            dz = dot(all_g[first:last].reshape((last - first) * cap, width), down_buf[slot])
            dg = (dz * a_ref[step, span].astype(F32)).astype(BF16)
            du = (dz * b_ref[step, span].astype(F32)).astype(BF16)
            a_ref[step, span] = dg
            b_ref[step, span] = du
            acc_ref[span, :] += dot_nt(dg, wide_buf[slot, 0]) + dot_nt(du, wide_buf[slot, 1])
            return carry

        lax.fori_loop(0, chunks, one, 0)

    def keep_own(buffer, dest, index):
        buffer[experts - 1] = acc_ref[:cap, :].astype(BF16)
        copy = pltpu.make_async_copy(
            buffer.at[experts - 1], dest.at[me], local_sems.at[index]
        )
        copy.start()
        return copy

    weigh(0)
    up(0, 1, 0)
    own = [keep_own(send_x, flow_ref, 0)]
    acc_ref[:cap, :] = jnp.zeros((cap, width), F32)
    down(0, 1, 1)
    own.append(keep_own(send_g, drow_ref, 1))
    for j in range(1, experts):
        g_copies[j].wait()
        weigh(j)
    turned_g[...] = all_g[...].reshape(slots, width).T
    groups = ((1, 2), (2, experts))

    def return_rows(buffer, dest, sems, first, last):
        for j in range(first, last):
            buffer[j - 1] = acc_ref[j * cap : (j + 1) * cap, :].astype(BF16)
            back(buffer, dest, sems, j).start()

    for i, (first_at, last_at) in enumerate(groups):
        for j in range(first_at, last_at):
            x_copies[j].wait()
        up(first_at, last_at, 2 + i)
        return_rows(send_x, flow_ref, flow_sems, first_at, last_at)
    turned_ref[...] = all_x[...].reshape(slots, width).T
    acc_ref[cap:, :] = jnp.zeros((slots - cap, width), F32)
    for i, (first_at, last_at) in enumerate(groups):
        down(first_at, last_at, 4 + i)
        return_rows(send_g, drow_ref, drow_sems, first_at, last_at)

    def wide_copy(step):
        return remote(
            wide_given.at[step],
            wide_taken.at[step],
            wide_sems,
            (step,),
            {"context": 1 - core},
        )

    def down_copy(step):
        chunk = lax.rem((1 - core) * per + step, chunks)
        return remote(
            down_given.at[step],
            down_taken.at[chunk],
            down_sems,
            (chunk,),
            {"context": 1 - core},
        )

    def products(step):
        chunk = lax.rem((1 - core) * per + step, chunks)
        gate = dot(turned_ref[...], a_ref[chunk])
        lift = dot(turned_ref[...], b_ref[chunk])
        low = dot(turned_g[...], z_ref[chunk])
        top, bottom = low[:half], low[half:]
        down_given[step] = jnp.where(core == 0, bottom, top).astype(BF16)
        kept_ref[chunk] = jnp.where(core == 0, top, bottom).astype(BF16)
        down_copy(step).start()
        return gate, lift

    def give(step, carry):
        gate, lift = products(step)
        wide_given[step, 0] = gate.astype(BF16)
        wide_given[step, 1] = lift.astype(BF16)
        wide_copy(step).start()
        return carry

    lax.fori_loop(0, per, give, 0)

    def keep(step, carry):
        gate, lift = products(step)
        wide_copy(step - per).wait_recv()
        for i, value in enumerate((gate, lift)):
            at = pl.ds(pl.multiple_of((i * per + step - per) * FC, FC), FC)
            value = value + wide_taken[step - per, i].astype(F32)
            gw_ref[:, :, at] = value.reshape(slabs, rows_out, FC).astype(BF16)
        return carry

    lax.fori_loop(per, chunks, keep, 0)

    def settle(step, carry):
        other = lax.rem(core * per + step, chunks)
        copy = remote(
            down_given.at[step],
            down_taken.at[other],
            down_sems,
            (other,),
            {"context": 1 - core},
        )
        copy.wait_recv()
        value = kept_ref[other].astype(F32) + down_taken[other].astype(F32)
        for b in range(half // rows_out):
            part = value[b * rows_out : (b + 1) * rows_out]
            start = 2 * per * FC + b * deep
            if FC <= deep:
                inside = lax.rem(other, deep // FC) * FC
                at = pl.ds(pl.multiple_of(start + inside, FC), FC)
                gw_ref[other // (deep // FC), :, at] = part.astype(BF16)
            else:
                for i in range(FC // deep):
                    gw_ref[other * (FC // deep) + i, :, start : start + deep] = part[
                        :, i * deep : (i + 1) * deep
                    ].astype(BF16)
        return carry

    lax.fori_loop(0, chunks, settle, 0)

    for copy in own:
        copy.wait()
    for j in range(1, experts):
        back(send_x, flow_ref, flow_sems, j).wait()
        back(send_g, drow_ref, drow_sems, j).wait()

    def sent(step, carry):
        down_copy(step).wait_send()
        return carry

    lax.fori_loop(0, chunks, sent, 0)
    lax.fori_loop(0, per, lambda step, carry: (wide_copy(step).wait_send(), carry)[1], 0)


def run_experts(total, experts, slabs, hidden, cap, flat_t, atwo, dy, stat, wide, wd):
    rows, width = atwo.shape
    chunks = hidden // FC
    per = chunks // 2
    half = width // 2
    slots = experts * cap
    vmem = pl.BlockSpec(memory_space=pltpu.VMEM)
    anywhere = pl.BlockSpec(memory_space=pl.ANY)
    dma = pltpu.SemaphoreType.DMA
    return pl.pallas_call(
        functools.partial(expert_kernel, total),
        in_specs=[vmem] * 2 + [anywhere, vmem] + [anywhere] * 2,
        out_specs=[anywhere] * 2 + [vmem],
        out_shape=(
            jax.ShapeDtypeStruct((experts, cap, width), BF16),
            jax.ShapeDtypeStruct((experts, cap, width), BF16),
            jax.ShapeDtypeStruct((slabs, width // slabs, 3 * hidden // 2), BF16),
        ),
        scratch_shapes=[
            pltpu.VMEM((experts, cap, width), BF16),
            pltpu.VMEM((experts, cap, width), BF16),
            pltpu.VMEM((experts, cap, width), BF16),
            pltpu.VMEM((experts, cap, width), BF16),
            pltpu.VMEM((experts - 1, 8, cap), F32),
            pltpu.VMEM((experts, 8, cap), F32),
            pltpu.VMEM((slots, width), F32),
            pltpu.VMEM((chunks, slots, FC), BF16),
            pltpu.VMEM((chunks, slots, FC), BF16),
            pltpu.VMEM((chunks, slots, FC), BF16),
            pltpu.VMEM((width, slots), BF16),
            pltpu.VMEM((width, slots), BF16),
            pltpu.VMEM((chunks, half, FC), BF16),
            pltpu.VMEM((2, 2, width, FC), BF16),
            pltpu.VMEM((2, width, FC), BF16),
            pltpu.VMEM((per, 2, width, FC), BF16),
            pltpu.VMEM((per, 2, width, FC), BF16),
            pltpu.VMEM((chunks, half, FC), BF16),
            pltpu.VMEM((chunks, half, FC), BF16),
            dma((experts,)),
            dma((2, experts - 1)),
            dma((2, experts - 1)),
            dma((2, experts - 1)),
            dma((2, experts - 1)),
            dma((2,)),
            dma((2, 6)),
            dma((2, per)),
            dma((2, chunks)),
        ],
        compiler_params=pltpu.CompilerParams(
            collective_id=2, has_side_effects=True, vmem_limit_bytes=62 * MIB
        ),
        cost_estimate=cost(18 * slots * width * hidden, 30 * width * hidden),
        name="experts",
    )(flat_t, atwo, dy, stat, wide, wd)


def combine_kernel(
    experts,
    total,
    flow_ref,
    drow_ref,
    flat_ref,
    stat_ref,
    flat_t_ref,
    hres_ref,
    atwo_ref,
    dy_ref,
    o_ref,
    extra_ref,
    w_ref,
    prev_ref,
    out_ref,
    dh_ref,
    dolow_ref,
    gw_ref,
    small_ref,
    right_ref,
    picked_ref,
    summed_ref,
    sums_ref,
    columns_ref,
    dhlow_ref,
    stage_ref,
    own_sems,
    dolow_sems,
):
    step = pl.program_id(0)
    core = lax.axis_index("context")

    @pl.when(step == 0)
    def _():
        greet_all(("context",))

    def dolow_copies(block):
        rows = pl.ds(pl.multiple_of(block * TB, TB), TB)
        return (
            pltpu.make_async_copy(
                stage_ref.at[core, rows], dolow_ref.at[core, rows], own_sems.at[block]
            ),
            remote(
                stage_ref.at[1 - core, rows],
                dolow_ref.at[core, rows],
                dolow_sems,
                (block,),
                {"context": 1 - core},
            ),
        )

    slots, width = flow_ref.shape
    half = width // 2
    gain = extra_ref[GAIN_TWO : GAIN_TWO + 1].astype(F32)
    vecs = [extra_ref[VECS + j : VECS + j + 1].astype(F32) for j in range(2)]

    @pl.when(step == 0)
    def _():
        right_ref[:slots] = drow_ref[...]
        right_ref[slots:] = extra_ref[...]

    spread_out = iota((TB, slots), 1)
    hots = [
        jnp.where(flat_ref[:, k : k + 1] == spread_out, 1.0, 0.0).astype(BF16) for k in range(2)
    ]
    for k in range(2):
        picked_ref[k] = dot(hots[k], flow_ref[...])
    vec_dot = dot_nt(dy_ref[...], extra_ref[...])
    lane = iota((RC, LANES), 1)
    for start in range(0, TB, RC):
        at = slice(start, start + RC)
        dy = dy_ref[at].astype(F32)
        ntwo = hres_ref[at] * stat_ref[at, total + 4 : total + 5] * gain
        sums = vec_dot[at]
        for i, part in enumerate((ntwo, picked_ref[0, at], picked_ref[1, at])):
            sums = jnp.where(lane == i, jnp.sum(dy * part, axis=1, keepdims=True), sums)
        sums_ref[at] = sums

    sums, stats = sums_ref[...].T, stat_ref[...].T
    row = lambda i: stats[i : i + 1]
    dot_normed, dot_picked = sums[0:1], [sums[1:2], sums[2:3]]
    dot_vecs = [sums[VECS + j : VECS + j + 1] for j in range(2)]
    gates = [row(total + 5 + k) for k in range(2)]
    mixes = [[row(total + 2 * j + i) for i in range(2)] for j in range(2)]
    routes = [flat_t_ref[2 + k : 3 + k] for k in range(2)]
    copies = [jnp.where(route == experts + 1, 1.0, 0.0) for route in routes]
    consts = [
        [jnp.where(route == experts + 2 + j, 1.0, 0.0) for j in range(2)] for route in routes
    ]
    pulls = [mixes[j][0] * dot_normed + mixes[j][1] * dot_vecs[j] for j in range(2)]
    sub = iota((total, TB), 0).astype(F32)
    dpgate = jnp.zeros((total, TB), F32)
    for k in range(2):
        dgate = dot_picked[k] + copies[k] * dot_normed
        dgate = dgate + consts[k][0] * pulls[0] + consts[k][1] * pulls[1]
        dpgate = dpgate + jnp.where(sub == routes[k], dgate, 0.0)
    pgate = stats[:total]
    dlogit = pgate * (dpgate - jnp.sum(pgate * dpgate, axis=0, keepdims=True))
    weight = gates[0] * copies[0] + gates[1] * copies[1]
    dmix, shares, pieces = [], [], []
    for j in range(2):
        const = gates[0] * consts[0][j] + gates[1] * consts[1][j]
        grads = [const * dot_normed, const * dot_vecs[j]]
        inner = mixes[j][0] * grads[0] + mixes[j][1] * grads[1]
        dmix += [mixes[j][i] * (grads[i] - inner) for i in range(2)]
        weight = weight + const * mixes[j][0]
        share = const * mixes[j][1]
        shares.append(share)
        for i in range(3):
            pieces.append(share.astype(BF16).astype(F32))
            share = share - pieces[-1]
    empty = jnp.zeros((1, TB), F32)
    droute_t = jnp.concatenate([dlogit] + dmix + [empty] * (12 - total), axis=0).astype(BF16)
    rows = jnp.concatenate(
        [dlogit] + dmix + [weight] + shares + [jnp.zeros((LANES - total - 7, TB), F32)], axis=0
    )
    columns_ref[...] = rows.T
    for start in range(0, TB, RC):
        at = slice(start, start + RC)
        hres = hres_ref[at]
        ntwo = hres * stat_ref[at, total + 4 : total + 5] * gain
        out = hres + columns_ref[at, total + 4 : total + 5] * ntwo
        for k in range(2):
            out = out + stat_ref[at, total + 5 + k : total + 6 + k] * picked_ref[k, at]
        for j in range(2):
            out = out + columns_ref[at, total + 5 + j : total + 6 + j] * vecs[j]
        out_ref[at] = out.astype(BF16)

    lane = iota((TB, LANES), 1)
    droute = jnp.where(lane < total + 4, columns_ref[...], 0.0).astype(BF16)
    summed_ref[...] = dot(
        jnp.concatenate([hots[0] + hots[1], droute], axis=1), right_ref[...]
    )
    gain_row = jnp.zeros((1, width), F32)
    for start in range(0, TB, RC):
        at = slice(start, start + RC)
        hres = hres_ref[at]
        dy = dy_ref[at].astype(F32)
        scale = stat_ref[at, total + 4 : total + 5]
        dntwo = columns_ref[at, total + 4 : total + 5] * dy + summed_ref[at]
        both = hres * dntwo
        inner = jnp.sum(both * gain, axis=1, keepdims=True) * (1.0 / width)
        dh = dy + dntwo * gain * scale - hres * (scale * scale * scale * inner)
        gain_row = gain_row + jnp.sum(both * scale, axis=0, keepdims=True)
        dh_ref[at] = dh
        dhlow_ref[pl.ds(pl.multiple_of(step * TB + start, RC), RC), :] = dh.astype(BF16)
    w_out = jnp.concatenate([w_ref[0, 0], w_ref[0, 1]], axis=1)
    dolow = dot_nt(dhlow_ref[pl.ds(pl.multiple_of(step * TB, TB), TB), :], w_out).astype(BF16)
    rows_at = pl.ds(pl.multiple_of(step * TB, TB), TB)
    stage_ref[0, rows_at] = dolow[:, :half]
    stage_ref[1, rows_at] = dolow[:, half:]
    for copy in dolow_copies(step):
        copy.start()
    route_rows = dot(droute_t, atwo_ref[...])
    vec_parts = dot(
        jnp.concatenate(pieces + [empty] * 2, axis=0).astype(BF16), dy_ref[...]
    )
    vec_rows = [
        vec_parts[3 * j : 3 * j + 1] + vec_parts[3 * j + 1 : 3 * j + 2] + vec_parts[3 * j + 2 : 3 * j + 3]
        for j in range(2)
    ]
    res_rows = jnp.dot(dlogit, prev_ref[...], precision=HIGH, preferred_element_type=F32)
    res_rows = jnp.concatenate([res_rows, jnp.zeros((total, width - total), F32)], axis=1)
    small = jnp.concatenate(
        [route_rows[: total + 4], gain_row] + vec_rows + [jnp.zeros((1, width), F32), res_rows],
        axis=0,
    )

    @pl.when(step == 0)
    def _():
        small_ref[...] = small

    @pl.when(step > 0)
    def _():
        small_ref[...] += small

    @pl.when(step == pl.num_programs(0) - 1)
    def _():
        for side in range(2):
            at = slice(side * half, (side + 1) * half)
            weight = dot(o_ref[:, at].T, dhlow_ref[...]).astype(BF16)
            gw_ref[0, at] = weight[:, :half]
            gw_ref[1, at] = weight[:, half:]
        for block in range(dhlow_ref.shape[0] // TB):
            for copy in dolow_copies(block):
                copy.wait()


def combine(experts, total, flow, drow, flat, stat, flat_t, hres, atwo, dy, o, w_shared, extra, prev):
    rows, width = hres.shape
    slots = flow.shape[0]
    half = width // 2
    token = lambda i: (i, 0)
    whole = lambda i: (0, 0)
    weight = pl.BlockSpec((2, width, half), lambda i: (0, 0, 0))
    small_rows = 2 * total + 8
    return pl.pallas_call(
        functools.partial(combine_kernel, experts, total),
        grid=(rows // TB,),
        in_specs=[
            pl.BlockSpec((slots, width), whole),
            pl.BlockSpec((slots, width), whole),
            pl.BlockSpec((TB, LANES), token),
            pl.BlockSpec((TB, LANES), token),
            pl.BlockSpec((8, TB), lambda i: (0, i)),
            pl.BlockSpec((TB, width), token),
            pl.BlockSpec((TB, width), token),
            pl.BlockSpec((TB, width), token),
            pl.BlockSpec((rows, width), whole),
            pl.BlockSpec((LANES, width), whole),
            pl.BlockSpec((1, 2, width, half), lambda i: (3, 0, 0, 0)),
            pl.BlockSpec((TB, total), token),
        ],
        out_specs=[
            pl.BlockSpec((TB, width), token),
            pl.BlockSpec((TB, width), token),
            pl.BlockSpec(memory_space=pl.ANY),
            weight,
            pl.BlockSpec((small_rows, width), whole),
        ],
        out_shape=(
            jax.ShapeDtypeStruct((rows, width), BF16),
            jax.ShapeDtypeStruct((rows, width), F32),
            jax.ShapeDtypeStruct((2, rows, half), BF16),
            jax.ShapeDtypeStruct((2, width, half), BF16),
            jax.ShapeDtypeStruct((small_rows, width), F32),
        ),
        scratch_shapes=[
            pltpu.VMEM((slots + LANES, width), BF16),
            pltpu.VMEM((2, TB, width), F32),
            pltpu.VMEM((TB, width), F32),
            pltpu.VMEM((TB, LANES), F32),
            pltpu.VMEM((TB, LANES), F32),
            pltpu.VMEM((rows, width), BF16),
            pltpu.VMEM((2, rows, half), BF16),
            pltpu.SemaphoreType.DMA((rows // TB,)),
            pltpu.SemaphoreType.DMA((2, rows // TB)),
        ],
        compiler_params=pltpu.CompilerParams(
            collective_id=3, has_side_effects=True, vmem_limit_bytes=62 * MIB
        ),
        cost_estimate=cost(
            6 * rows * slots * width + 4 * rows * width * width, 30 * rows * width + 8 * width * width
        ),
        name="combine",
    )(flow, drow, flat, stat, flat_t, hres, atwo, dy, o, extra, w_shared, prev)


def tail_kernel(
    gain_at,
    sent_ref,
    aone_ref,
    w_ref,
    extra_ref,
    x_ref,
    dh_ref,
    gwo_ref,
    small_ref,
    out_ref,
    final,
    small_out_ref,
    both,
    grads,
    w_buf,
    x_buf,
    dh_buf,
    out_buf,
    core_in,
    plane_out,
    plane_in,
    slab_out,
    slab_in,
    own_ref,
    small_own,
    small_core,
    small_plane,
    small_slab,
    load_sems,
    store_sems,
    both_sems,
    core_sems,
    plane_sems,
    slab_sems,
    final_sems,
    pass_sems,
    small_core_sems,
    small_plane_sems,
    small_slab_sems,
):
    experts = lax.axis_size("expert")
    slabs = lax.axis_size("dp")
    me, core, slab = lax.axis_index("expert"), lax.axis_index("context"), lax.axis_index("dp")
    other = 1 - core
    tokens, width = x_buf.shape
    half = width // 2
    parts = 4
    block = tokens // parts

    mine = pltpu.make_async_copy(sent_ref.at[core], both.at[core], load_sems.at[0])
    mine.start()
    loads = [
        pltpu.make_async_copy(w_ref.at[pl.ds(0, 3)], w_buf, load_sems.at[1]),
        pltpu.make_async_copy(x_ref, x_buf, load_sems.at[2]),
        pltpu.make_async_copy(dh_ref, dh_buf, load_sems.at[3]),
    ]
    for copy in loads:
        copy.start()
    greet_all(("context", "expert", "dp"))
    theirs = [
        remote(
            sent_ref.at[other, which],
            both.at[core, which],
            both_sems,
            (which,),
            {"context": other},
        )
        for which in range(3)
    ]

    def core_copy(which):
        return remote(
            grads.at[other, which], core_in.at[which], core_sems, (which,), {"context": other}
        )

    for side in range(2):
        grads[side, 3] = gwo_ref[side]
    core_copy(3).start()
    for copy in theirs:
        copy.start()

    def plane_copy(j, at):
        return remote(
            plane_out.at[j - 1, at],
            plane_in.at[j - 1, at],
            plane_sems,
            (j - 1, at),
            {"expert": lax.rem(me + j, experts)},
        )

    def pass_on(which):
        core_copy(which).wait_recv()
        j = lax.rem(which + experts - me, experts)

        @pl.when(j != 0)
        def _():
            def one(k):
                at = lax.rem(slab + k + 1, slabs)
                plane_out[j - 1, at] = (
                    grads[core, which, at].astype(F32) + core_in[which, at].astype(F32)
                ).astype(BF16)
                plane_copy(j, at).start()

            loop(slabs, one)

    mine.wait()
    turned = aone_ref[...].T
    pass_on(3)
    for which in range(3):
        theirs[which].wait_recv()
        grad = jnp.concatenate([both[0, which], both[1, which]], axis=1)
        weight = dot(turned, grad)
        for side in range(2):
            grads[side, which] = (
                weight[:, side * half : (side + 1) * half]
                .reshape(slabs, width // slabs, half)
                .astype(BF16)
            )
        core_copy(which).start()
        if which > 0:
            pass_on(which - 1)
    for copy in loads:
        copy.wait()

    gain = extra_ref[GAIN_ONE : GAIN_ONE + 1].astype(F32)
    stores = []
    gain_row = jnp.zeros((1, width), F32)
    for part in range(parts):
        at = slice(part * block, (part + 1) * block)
        dnone = None
        for which in range(3):
            grad = jnp.concatenate([both[0, which, at], both[1, which, at]], axis=1)
            whole = jnp.concatenate([w_buf[which, 0], w_buf[which, 1]], axis=1)
            product = dot_nt(grad, whole)
            dnone = product if dnone is None else dnone + product
        values = x_buf[at].astype(F32)
        scale = lax.rsqrt(jnp.mean(values * values, axis=-1, keepdims=True) + EPS)
        scaled = dnone * gain
        inner = jnp.mean(values * scaled, axis=1, keepdims=True)
        out_buf[at] = dh_buf[at] + scale * scaled - values * (scale * scale * scale * inner)
        stores.append(
            pltpu.make_async_copy(out_buf.at[at], out_ref.at[at], store_sems.at[part])
        )
        stores[-1].start()
        gain_row = gain_row + jnp.sum(dnone * values * scale, axis=0, keepdims=True)
        if part == 0:
            pass_on(2)

    row = iota(small_ref.shape, 0)
    small_own[...] = small_ref[...] + jnp.where(row == gain_at, gain_row, 0.0)
    small_copy = remote(small_own, small_core, small_core_sems, (0,), {"context": other})
    small_copy.start()
    small_copy.wait()
    small_plane[me] = small_own[...] + small_core[...]
    small_plane_copies = []
    for j in range(1, experts):
        small_plane_copies.append(
            remote(
                small_plane.at[me],
                small_plane.at[me],
                small_plane_sems,
                (j,),
                {"expert": lax.rem(me + j, experts)},
            )
        )
        small_plane_copies[-1].start()

    def gathered(at):
        value = grads[core, me, at].astype(F32) + core_in[me, at].astype(F32)
        for j in range(1, experts):
            plane_copy(j, at).wait_recv()
            value = value + plane_in[j - 1, at].astype(F32)
        return value

    def slab_copy(k):
        return remote(
            slab_out.at[k],
            slab_in.at[k],
            slab_sems,
            (k,),
            {"dp": lax.rem(slab + k + 1, slabs)},
        )

    def scatter(k):
        slab_out[k] = gathered(lax.rem(slab + k + 1, slabs)).astype(BF16)
        slab_copy(k).start()

    loop(slabs - 1, scatter)

    for copy in small_plane_copies:
        copy.wait()
    value = small_plane[0]
    for j in range(1, experts):
        value = value + small_plane[j]
    small_slab[slab] = value

    def small_slab_copy(k):
        return remote(
            small_slab.at[slab],
            small_slab.at[slab],
            small_slab_sems,
            (k,),
            {"dp": lax.rem(slab + k + 1, slabs)},
        )

    loop(slabs - 1, lambda k: small_slab_copy(k).start())

    own_ref[...] = gathered(slab)

    def collect(k):
        slab_copy(k).wait_recv()
        own_ref[...] += slab_in[k].astype(F32)

    loop(slabs - 1, collect)
    final[core, me] = own_ref[...].astype(BF16)
    final_copies, pass_copies = [], []
    for j in range(1, experts):
        final_copies.append(
            remote(
                final.at[core, me],
                final.at[core, me],
                final_sems,
                (j,),
                {"expert": lax.rem(me + j, experts)},
            )
        )
        final_copies[-1].start()
    for j in range(experts):
        source = lax.rem(me + experts - j, experts)
        if j > 0:
            final_copies[j - 1].wait_recv()
        pass_copies.append(
            remote(
                final.at[core, source],
                final.at[core, source],
                pass_sems,
                (j,),
                {"context": other},
            )
        )
        pass_copies[-1].start()

    loop(slabs - 1, lambda k: small_slab_copy(k).wait())
    small_out_ref[...] = small_slab[0]

    def add_small(k):
        small_out_ref[...] += small_slab[k + 1]

    loop(slabs - 1, add_small)

    for copy in pass_copies:
        copy.wait_recv()
    for copy in stores:
        copy.wait()
    for which in range(4):
        core_copy(which).wait_send()
    for j in range(1, experts):

        def sent(k, j=j):
            plane_copy(j, k).wait_send()

        loop(slabs, sent)
    loop(slabs - 1, lambda k: slab_copy(k).wait_send())
    for copy in theirs + final_copies + pass_copies:
        copy.wait_send()


def tail(experts, slabs, gain_at, sent, aone, w_shared, extra, x, dh, gwo, small):
    tokens, width = x.shape
    half = width // 2
    rows = width // slabs
    vmem = pl.BlockSpec(memory_space=pltpu.VMEM)
    anywhere = pl.BlockSpec(memory_space=pl.ANY)
    dma = pltpu.SemaphoreType.DMA
    return pl.pallas_call(
        functools.partial(tail_kernel, gain_at),
        in_specs=[anywhere, vmem, anywhere, vmem, anywhere, anywhere] + [vmem] * 2,
        out_specs=[anywhere] + [vmem] * 2,
        out_shape=(
            jax.ShapeDtypeStruct((tokens, width), F32),
            jax.ShapeDtypeStruct((2, experts, rows, half), BF16),
            jax.ShapeDtypeStruct(small.shape, F32),
        ),
        scratch_shapes=[
            pltpu.VMEM((2, 3, tokens, half), BF16),
            pltpu.VMEM((2, 4, slabs, rows, half), BF16),
            pltpu.VMEM((3, 2, width, half), BF16),
            pltpu.VMEM((tokens, width), BF16),
            pltpu.VMEM((tokens, width), F32),
            pltpu.VMEM((tokens, width), F32),
            pltpu.VMEM((4, slabs, rows, half), BF16),
            pltpu.VMEM((experts - 1, slabs, rows, half), BF16),
            pltpu.VMEM((experts - 1, slabs, rows, half), BF16),
            pltpu.VMEM((slabs - 1, rows, half), BF16),
            pltpu.VMEM((slabs - 1, rows, half), BF16),
            pltpu.VMEM((rows, half), F32),
            pltpu.VMEM(small.shape, F32),
            pltpu.VMEM(small.shape, F32),
            pltpu.VMEM((experts,) + small.shape, F32),
            pltpu.VMEM((slabs,) + small.shape, F32),
            dma((4,)),
            dma((4,)),
            dma((2, 3)),
            dma((2, 4)),
            dma((2, experts - 1, slabs)),
            dma((2, slabs - 1)),
            dma((2, experts)),
            dma((2, experts)),
            dma((2, 1)),
            dma((2, experts)),
            dma((2, slabs - 1)),
        ],
        compiler_params=pltpu.CompilerParams(
            collective_id=0, has_side_effects=True, vmem_limit_bytes=62 * MIB
        ),
        cost_estimate=cost(12 * tokens * width * width, 40 * tokens * width),
        name="tail",
    )(sent, aone, w_shared, extra, x, dh, gwo, small)


def finish_kernel(
    total,
    place_ref,
    small_ref,
    final_ref,
    mine_ref,
    theirs_ref,
    tokens_ref,
    norm_one_ref,
    norm_two_ref,
    router_ref,
    mix_ref,
    vec_ref,
    res_ref,
    q_ref,
    k_ref,
    v_ref,
    o_ref,
    gate_ref,
    up_ref,
    gd_ref,
    tokens_out_ref,
    tokens_buf,
    final_buf,
    share_buf,
    square_buf,
    gate_buf,
    up_buf,
    gd_buf,
    turned_ref,
    load_sems,
    store_sems,
):
    rows, half = final_buf.shape[2:]
    wide = share_buf.shape[2] // 3
    deep = gd_buf.shape[0]
    core = place_ref[1]
    loads = [
        pltpu.make_async_copy(mine_ref, share_buf.at[0], load_sems.at[0]),
        pltpu.make_async_copy(theirs_ref, share_buf.at[1], load_sems.at[1]),
        pltpu.make_async_copy(final_ref, final_buf, load_sems.at[2]),
        pltpu.make_async_copy(tokens_ref, tokens_buf, load_sems.at[3]),
    ]
    for copy in loads[3:] + loads[:3]:
        copy.start()
    small = small_ref[...]
    fill = jnp.zeros((LANES - small.shape[0], small.shape[1]), F32)
    turned_ref[...] = jnp.concatenate([small, fill], axis=0).T
    own = turned_ref[pl.ds(pl.multiple_of(place_ref[0] * rows, 8), rows), :]
    own = own.T
    router_ref[...] = own[:total]
    mix_ref[...] = own[total : total + 4]
    norm_two_ref[...] = own[total + 4 : total + 5]
    vec_ref[...] = own[total + 5 : total + 7]
    norm_one_ref[...] = own[total + 7 : total + 8]
    res_ref[...] = turned_ref[:total, total + 8 : 2 * total + 8]

    stores = []

    def store(buffer, ref):
        stores.append(pltpu.make_async_copy(buffer, ref, store_sems.at[len(stores)]))
        stores[-1].start()

    def sides(buffer, size, left, right):
        buffer[:, :size] = left
        buffer[:, size:] = right

    def ordered(get):
        first, second = get(share_buf.at[0]), get(share_buf.at[1])
        swap = core != 0
        return jnp.where(swap, second, first), jnp.where(swap, first, second)

    loads[3].wait()
    store(tokens_buf, tokens_out_ref)
    for copy in loads[:2]:
        copy.wait()
    sides(gate_buf, wide, *ordered(lambda ref: ref[:, :wide].astype(F32)))
    store(gate_buf, gate_ref.at[0])
    sides(up_buf, wide, *ordered(lambda ref: ref[:, wide : 2 * wide].astype(F32)))
    store(up_buf, up_ref.at[0])

    def down(ref):
        blocks = [
            ref[:, 2 * wide + b * deep : 2 * wide + (b + 1) * deep].astype(F32)
            for b in range(half // rows)
        ]
        return jnp.concatenate(blocks, axis=0).T

    sides(gd_buf, half, *ordered(down))
    store(gd_buf, gd_ref.at[0])
    loads[2].wait()
    for which, ref in enumerate((q_ref, k_ref, v_ref, o_ref)):
        sides(
            square_buf.at[which],
            half,
            final_buf[0, which].astype(F32),
            final_buf[1, which].astype(F32),
        )
        store(square_buf.at[which], ref)
    for copy in stores:
        copy.wait()


def finish(total, place, final, small, mine, theirs, tokens):
    rows, half = final.shape[2:]
    width = 2 * half
    wide = mine.shape[1] // 3
    deep = wide * rows // half
    anywhere = pl.BlockSpec(memory_space=pl.ANY)
    vmem = pl.BlockSpec(memory_space=pltpu.VMEM)
    shape = lambda *dims: jax.ShapeDtypeStruct(dims, F32)
    return pl.pallas_call(
        functools.partial(finish_kernel, total),
        in_specs=[pl.BlockSpec(memory_space=pltpu.SMEM), vmem] + [anywhere] * 4,
        out_specs=[vmem] * 6 + [anywhere] * 8,
        out_shape=(
            shape(1, rows),
            shape(1, rows),
            shape(total, rows),
            shape(4, rows),
            shape(2, rows),
            shape(total, total),
            shape(rows, width),
            shape(rows, width),
            shape(rows, width),
            shape(rows, width),
            shape(1, rows, 2 * wide),
            shape(1, rows, 2 * wide),
            shape(1, deep, width),
            shape(*tokens.shape),
        ),
        scratch_shapes=[
            pltpu.VMEM(tokens.shape, F32),
            pltpu.VMEM(final.shape, BF16),
            pltpu.VMEM((2,) + mine.shape, BF16),
            pltpu.VMEM((4, rows, width), F32),
            pltpu.VMEM((rows, 2 * wide), F32),
            pltpu.VMEM((rows, 2 * wide), F32),
            pltpu.VMEM((deep, width), F32),
            pltpu.VMEM((width, LANES), F32),
            pltpu.SemaphoreType.DMA((4,)),
            pltpu.SemaphoreType.DMA((8,)),
        ],
        compiler_params=params(62),
        cost_estimate=cost(1e6, 20 * rows * width),
        name="finish",
    )(place, small, final, mine, theirs, tokens)


def on_device(
    tokens,
    segments,
    routes,
    prev_logits,
    ranks,
    cotangent,
    norm_one,
    w_query,
    w_key,
    w_value,
    w_out,
    norm_two,
    router,
    w_res,
    const_mix,
    const_vec,
    w_gate,
    w_up,
    w_down,
):
    experts = lax.axis_size("expert")
    dp = lax.axis_size("dp")
    total = experts + NZ
    _, rows, width = tokens.shape
    hidden = w_gate.shape[2]
    cap = (18 * rows + 8 * total - 1) // (8 * total)
    seq = 2 * rows
    core = lax.axis_index("context")
    half = width // 2

    def mine(shard, size):
        return lax.dynamic_slice_in_dim(shard, core * size, size, 1)

    def gather(shard):
        return lax.all_gather(shard, ("context", "dp"), axis=0).reshape(
            2, dp * shard.shape[0], shard.shape[1]
        )

    extra = jnp.concatenate(
        [router, const_mix, norm_one[:, None], norm_two[:, None], const_vec], axis=1
    )
    cos, sin = (jnp.asarray(table).reshape(2, rows, LANES) for table in rope_tables(seq))
    x = tokens[0]
    dy = cotangent[0]
    w_shared, extra, flat, flat_t, low, first, qkv, aone, dy_rows = spread(
        experts,
        dp,
        cap,
        w_query,
        w_key,
        w_value,
        w_out,
        extra.astype(F32).T,
        routes[0],
        ranks[0],
        segments,
        x,
        dy,
        cos,
        sin,
    )
    w_shared = w_shared.reshape(4, 2, width, half)
    extra = extra.transpose(1, 0, 2).reshape(total + 8, width).astype(BF16)
    extra = jnp.concatenate(
        [
            extra[: total + 4],
            jnp.zeros((GAIN_ONE - total - 4, width), BF16),
            extra[total + 4 :],
            jnp.zeros((LANES - GAIN_ONE - 4, width), BF16),
        ],
        axis=0,
    )
    wide_mine = [mine(w_gate[0], hidden // 2), mine(w_up[0], hidden // 2)]
    down_mine = mine(w_down[0], half)
    deep = hidden // dp
    if deep == FC:
        turned = down_mine.T.reshape(-1, width // dp, deep).transpose(1, 0, 2)
        wide_w = gather(jnp.concatenate(wide_mine + [turned.reshape(width // dp, -1)], axis=1))
        down_w = wide_w
    else:
        wide_w = gather(jnp.concatenate(wide_mine, axis=1))
        down_w = gather(down_mine).transpose(0, 2, 1)

    res = jnp.pad(w_res.astype(F32), ((0, 0), (0, LANES - total)))

    dy_rows = lax.all_to_all(dy_rows, "expert", split_axis=0, concat_axis=0, tiled=True)
    o_keep, o_give, lse = attend(first, qkv, low)
    o_give, dy_rows = lax.optimization_barrier((o_give, dy_rows))
    o_theirs = lax.ppermute(o_give, "context", [(0, 1), (1, 0)])
    hres, atwo, stat, o = middle(
        total, first, x, o_keep, o_theirs, w_shared, extra, prev_logits[0], res, routes[0]
    )
    flow_back, drow_back, grad_wide = run_experts(
        total, experts, dp, hidden, cap, flat_t, atwo, dy_rows, stat, wide_w, down_w
    )
    flow_back = flow_back.reshape(experts * cap, width)
    drow_back = drow_back.reshape(experts * cap, width)
    wide = lax.psum_scatter(
        grad_wide.reshape(width, 3 * hidden // 2), "dp", scatter_dimension=0, tiled=True
    )

    output, dh, grad_o, grad_out_w, small = combine(
        experts,
        total,
        flow_back,
        drow_back,
        flat,
        stat,
        flat_t,
        hres,
        atwo,
        dy,
        o,
        w_shared,
        extra,
        prev_logits[0],
    )
    grads_sent, output = attend_back(
        first,
        qkv,
        grad_o,
        o_keep,
        o_give,
        lse,
        low,
        cos,
        sin,
        output,
    )
    grad_tokens, final, small = tail(
        experts,
        dp,
        total + 7,
        grads_sent,
        aone,
        w_shared,
        extra,
        x,
        dh,
        grad_out_w.reshape(2, dp, width // dp, half),
        small,
    )
    wide, small = lax.optimization_barrier((wide, small))
    wide_other = lax.ppermute(wide, "context", [(0, 1), (1, 0)])
    (
        grad_norm_one,
        grad_norm_two,
        grad_router,
        grad_mix,
        grad_vec,
        grad_res,
        grad_query,
        grad_key,
        grad_value,
        grad_out,
        grad_gate,
        grad_up,
        grad_down,
        grad_tokens,
    ) = finish(
        total,
        jnp.stack([lax.axis_index("dp"), core]),
        final,
        small,
        wide,
        wide_other,
        grad_tokens,
    )
    return (
        output[None],
        grad_tokens[None],
        grad_norm_one[0],
        grad_query,
        grad_key,
        grad_value,
        grad_out,
        grad_norm_two[0],
        grad_router.T,
        grad_res,
        grad_mix.T,
        grad_vec.T,
        grad_gate,
        grad_up,
        grad_down,
    )


def solution(mesh):
    token = P(("expert", "dp"), "context", None)
    rows = P("dp", None)
    expert = P("expert", "dp", None)
    in_specs = (
        token,
        P(("expert", "dp"), "context"),
        token,
        token,
        token,
        token,
        P("dp"),
        rows,
        rows,
        rows,
        rows,
        P("dp"),
        rows,
        P(),
        rows,
        rows,
        expert,
        expert,
        expert,
    )
    out_specs = (
        token,
        token,
        P("dp"),
        rows,
        rows,
        rows,
        rows,
        P("dp"),
        rows,
        P(),
        rows,
        rows,
        expert,
        expert,
        expert,
    )
    return jax.shard_map(
        on_device, mesh=mesh, in_specs=in_specs, out_specs=out_specs, check_vma=False
    )
```

```python
import functools

import jax
import jax.numpy as jnp
import numpy as np
from jax import lax
from jax.experimental import pallas as pl
from jax.experimental.pallas import tpu as pltpu
from jax.sharding import PartitionSpec as P

HEADS = 12
HEAD_DIM = 64
WIN = 1024
NZ = 4
SEGMENTS = 5
GAIN_ONE, GAIN_TWO, VECS = 112, 113, 114
TQ = 256
TB = 256
RC = 64
FC = 512
LANES = 128
EPS = 1e-05
MASKED = -1000000000.0
HIGH = lax.Precision.HIGHEST
F32 = jnp.float32
BF16 = jnp.bfloat16
MIB = 1024 * 1024


def params(mib):
    return pltpu.CompilerParams(vmem_limit_bytes=mib * MIB)


def cost(flops, nbytes, trans=0):
    return pl.CostEstimate(flops=int(flops), bytes_accessed=int(nbytes), transcendentals=int(trans))


def dot(left, right):
    return jnp.dot(left, right, preferred_element_type=F32)


def dot_nt(left, right):
    return lax.dot_general(left, right, (((1,), (1,)), ((), ())), preferred_element_type=F32)


def dot_tn(left, right):
    return lax.dot_general(left, right, (((0,), (0,)), ((), ())), preferred_element_type=F32)


def iota(shape, axis):
    return lax.broadcasted_iota(jnp.int32, shape, axis)


def rope_tables(seq):
    half = HEAD_DIM // 2
    frequency = np.float32(10000.0) ** (
        -np.arange(half, dtype=np.float32) * np.float32(2.0) / np.float32(HEAD_DIM)
    )
    angles = np.arange(seq, dtype=np.float32)[:, None] * frequency.astype(np.float32)[None, :]
    cos = np.cos(angles.astype(np.float64)).astype(np.float32)
    sin = np.sin(angles.astype(np.float64)).astype(np.float32)
    return np.concatenate([cos] * 4, axis=1), np.concatenate([-sin, sin, -sin, sin], axis=1)


def swap_halves(chunk):
    lane = iota(chunk.shape, 1)
    return jnp.where(
        lane % HEAD_DIM < HEAD_DIM // 2, pltpu.roll(chunk, 96, 1), pltpu.roll(chunk, 32, 1)
    )


def loop(count, body):
    if count <= 4:
        for step in range(count):
            body(step)
    else:
        lax.fori_loop(0, count, lambda step, carry: (body(step), carry)[1], 0)


def remote(src, dst, sems, index, where):
    return pltpu.make_async_remote_copy(
        src_ref=src,
        dst_ref=dst,
        send_sem=sems.at[(0,) + index],
        recv_sem=sems.at[(1,) + index],
        device_id=where,
        device_id_type=pl.DeviceIdType.MESH,
    )


def greet_all(axes):
    barrier = pltpu.get_barrier_semaphore()
    total = 0
    for axis in axes:
        size = lax.axis_size(axis)
        me = lax.axis_index(axis)
        total += size - 1

        def greet(k, axis=axis, size=size, me=me):
            pl.semaphore_signal(
                barrier,
                inc=1,
                device_id={axis: lax.rem(me + k + 1, size)},
                device_id_type=pl.DeviceIdType.MESH,
            )

        loop(size - 1, greet)
    pl.semaphore_wait(barrier, total)


def place_pairs(experts, cap, routes_ref, ranks_ref, flat_ref, flat_t_ref):
    rows = routes_ref.shape[0]
    lane = iota((rows, LANES), 1)
    first, second = routes_ref[:, 0:1], routes_ref[:, 1:2]
    hot_first, hot_second = first == lane, second == lane
    hot = (hot_first.astype(F32) + hot_second.astype(F32)).astype(BF16)
    ranks = ranks_ref[...].astype(F32)
    ranks_col = jnp.broadcast_to(ranks, (LANES, rows)).T[:, 0:1]
    earlier = jnp.where(ranks < ranks_col, 1.0, 0.0).astype(BF16)
    counts = dot(earlier, hot)

    def flat(hit, route):
        slot = jnp.sum(jnp.where(hit, counts, 0.0), axis=1, keepdims=True).astype(jnp.int32)
        return jnp.where((route < experts) & (slot < cap), route * cap + slot, experts * cap)

    columns = (flat(hot_first, first), flat(hot_second, second), first, second)
    out = jnp.zeros((rows, LANES), jnp.int32)
    for i, column in enumerate(columns):
        out = jnp.where(lane == i, column, out)
    flat_ref[...] = out
    flat_t_ref[...] = out.astype(F32).T[:8]


def find_starts(segs_ref, low_ref, first_ref):
    rows = segs_ref.shape[2]
    per = rows // TQ
    segs = [segs_ref[side].astype(F32) for side in range(2)]
    starts = [jnp.zeros((1, rows), F32) for side in range(2)]
    for number in range(1, SEGMENTS):
        before = sum(
            jnp.sum(jnp.where(part < number, 1.0, 0.0), axis=1, keepdims=True) for part in segs
        )
        starts = [
            jnp.where(part == number, before, start) for part, start in zip(segs, starts)
        ]
    for side in range(2):
        place = (iota((1, rows), 1) + (side * rows - WIN + 1)).astype(F32)
        low = jnp.maximum(starts[side], place)
        for tile in range(per):
            part = low[:, tile * TQ : (tile + 1) * TQ]
            low_ref[side * per + tile] = part.astype(jnp.int32)
            first_ref[side * per + tile] = jnp.min(part).astype(jnp.int32) // TQ
    first_ref[2 * per] = lax.axis_index("context")


def hot_slots(flat_ref, cap, target):
    slot = (iota((cap, flat_ref.shape[1]), 0) + target * cap).astype(F32)
    return flat_ref[0:1, :] == slot, flat_ref[1:2, :] == slot


def spread_kernel(
    cap,
    w_query_ref,
    w_key_ref,
    w_value_ref,
    w_out_ref,
    extra_ref,
    routes_ref,
    ranks_ref,
    segs_ref,
    x_ref,
    dy_ref,
    cos_ref,
    sin_ref,
    shared_ref,
    extra_out_ref,
    flat_ref,
    flat_t_ref,
    low_ref,
    first_ref,
    qkv_ref,
    aone_ref,
    dy_rows_ref,
    out_ref,
    segs_all,
    stage_ref,
    slab_sems,
    plane_sems,
    core_sems,
    extra_sems,
    segs_sems,
    shared_sem,
    own_sems,
    qkv_sems,
):
    experts = lax.axis_size("expert")
    slabs = lax.axis_size("dp")
    me, core, slab = lax.axis_index("expert"), lax.axis_index("context"), lax.axis_index("dp")
    half = out_ref.shape[4]
    for which, ref in enumerate((w_query_ref, w_key_ref, w_value_ref, w_out_ref)):
        for side in range(2):

            @pl.when((me == which) & (core == side))
            def _():
                out_ref[which, side, slab] = ref[:, side * half : (side + 1) * half]

    extra_out_ref[slab] = extra_ref[...]
    segs_all[core] = segs_ref[...]
    greet_all(("context", "expert", "dp"))

    def slab_copy(k):
        piece = out_ref.at[me, core, slab]
        return remote(piece, piece, slab_sems, (k,), {"dp": lax.rem(slab + k + 1, slabs)})

    def extra_copy(k):
        piece = extra_out_ref.at[slab]
        return remote(piece, piece, extra_sems, (k,), {"dp": lax.rem(slab + k + 1, slabs)})

    def plane_copy(j, at):
        piece = out_ref.at[me, core, at]
        return remote(
            piece, piece, plane_sems, (j - 1, at), {"expert": lax.rem(me + j, experts)}
        )

    def core_copy(j, at):
        piece = out_ref.at[lax.rem(me + experts - j, experts), core, at]
        return remote(piece, piece, core_sems, (j, at), {"context": 1 - core})

    def share(at):
        for j in range(1, experts):
            plane_copy(j, at).start()
        core_copy(0, at).start()

    loop(slabs - 1, lambda k: extra_copy(k).start())
    loop(slabs - 1, lambda k: slab_copy(k).start())
    share(slab)
    segs_copy = remote(
        segs_all.at[core], segs_all.at[core], segs_sems, (0,), {"context": 1 - core}
    )
    segs_copy.start()
    place_pairs(experts, cap, routes_ref, ranks_ref, flat_ref, flat_t_ref)
    segs_copy.wait()
    find_starts(segs_all, low_ref, first_ref)
    loop(slabs - 1, lambda k: extra_copy(k).wait())
    at = extra_ref.shape[0] - 4
    gain = jnp.concatenate([extra_out_ref[z, at : at + 1, :] for z in range(slabs)], axis=1)
    tokens = x_ref.shape[0]
    for start in range(0, tokens, TB):
        values = x_ref[start : start + TB].astype(F32)
        scale = lax.rsqrt(jnp.mean(values * values, axis=-1, keepdims=True) + EPS)
        aone_ref[start : start + TB] = (values * scale * gain).astype(BF16)

    def forward(k):
        slab_copy(k).wait_recv()
        share(lax.rem(slab + slabs - k - 1, slabs))

    loop(slabs - 1, forward)
    for target in range(experts):
        first, second = hot_slots(flat_t_ref, cap, target)
        hot = jnp.where(first | second, 1.0, 0.0).astype(BF16)
        dy_rows_ref[target] = dot(hot, dy_ref[...]).astype(BF16)

    def relay(k):
        at = lax.rem(slab + slabs - k, slabs)
        for j in range(1, experts):
            plane_copy(j, at).wait_recv()
            core_copy(j, at).start()

    loop(slabs, relay)
    loop(slabs - 1, lambda k: slab_copy(k).wait_send())

    def arrive(at):
        for j in range(experts):
            core_copy(j, at).wait()
        for j in range(1, experts):
            plane_copy(j, at).wait_send()

    loop(slabs, arrive)
    keep = pltpu.make_async_copy(out_ref, shared_ref, shared_sem)
    keep.start()

    width = 2 * half
    wholes = [
        jnp.concatenate(
            [out_ref[which, side].reshape(width, half) for side in range(2)], axis=1
        )
        for which in range(3)
    ]
    copies = []
    for block in range(tokens // TB):
        span = slice(block * TB, (block + 1) * TB)
        cos, sin = cos_ref[core, span], sin_ref[core, span]
        for which in range(3):
            product = dot(aone_ref[span], wholes[which])
            for pair in range(width // LANES):
                chunk = product[:, pair * LANES : (pair + 1) * LANES]
                if which < 2:
                    chunk = chunk * cos + swap_halves(chunk) * sin
                if which == 0:
                    chunk = chunk * HEAD_DIM ** (-0.5)
                side, place_in = pair // (half // LANES), pair % (half // LANES)
                stage_ref[side, which, span, place_in * LANES : (place_in + 1) * LANES] = (
                    chunk.astype(BF16)
                )
        copies.append(
            pltpu.make_async_copy(
                stage_ref.at[core, :, span], qkv_ref.at[core, :, span], own_sems.at[block]
            )
        )
        copies.append(
            remote(
                stage_ref.at[1 - core, :, span],
                qkv_ref.at[core, :, span],
                qkv_sems,
                (block,),
                {"context": 1 - core},
            )
        )
        for copy in copies[-2:]:
            copy.start()
    for copy in copies:
        copy.wait()
    keep.wait()


def spread(
    experts, slabs, cap, w_query, w_key, w_value, w_out, extra, routes, ranks, segs, x, dy, cos, sin
):
    tokens = routes.shape[0]
    tiles = 2 * tokens // TQ
    rows, width = w_query.shape
    half = width // 2
    vmem = pl.BlockSpec(memory_space=pltpu.VMEM)
    anywhere = pl.BlockSpec(memory_space=pl.ANY)
    dma = pltpu.SemaphoreType.DMA
    return pl.pallas_call(
        functools.partial(spread_kernel, cap),
        in_specs=[vmem] * 12,
        out_specs=[anywhere]
        + [vmem] * 4
        + [pl.BlockSpec(memory_space=pltpu.SMEM), anywhere, vmem, vmem],
        out_shape=(
            jax.ShapeDtypeStruct((4, 2, slabs, rows, half), BF16),
            jax.ShapeDtypeStruct((slabs,) + extra.shape, F32),
            jax.ShapeDtypeStruct((tokens, LANES), jnp.int32),
            jax.ShapeDtypeStruct((8, tokens), F32),
            jax.ShapeDtypeStruct((tiles, 1, TQ), jnp.int32),
            jax.ShapeDtypeStruct((tiles + 1,), jnp.int32),
            jax.ShapeDtypeStruct((2, 3, tokens, half), BF16),
            jax.ShapeDtypeStruct((tokens, width), BF16),
            jax.ShapeDtypeStruct((experts, cap, width), BF16),
        ),
        scratch_shapes=[
            pltpu.VMEM((4, 2, slabs, rows, half), BF16),
            pltpu.VMEM((2, 1, tokens), jnp.int32),
            pltpu.VMEM((2, 3, tokens, half), BF16),
            dma((2, slabs - 1)),
            dma((2, experts - 1, slabs)),
            dma((2, experts, slabs)),
            dma((2, slabs - 1)),
            dma((2, 1)),
            dma,
            dma((tokens // TB,)),
            dma((2, tokens // TB)),
        ],
        compiler_params=pltpu.CompilerParams(
            collective_id=1, has_side_effects=True, vmem_limit_bytes=62 * MIB
        ),
        cost_estimate=cost(1e6, 16 * width * width),
        name="spread",
    )(w_query, w_key, w_value, w_out, extra, routes, ranks, segs, x, dy, cos, sin)


def head_masks():
    lane = iota((TQ, LANES), 1)
    low = jnp.where(lane < HEAD_DIM, 1.0, 0.0).astype(BF16)
    return low, (1.0 - low.astype(F32)).astype(BF16)


def spans(tile, first, body):
    for count in range(1, WIN // TQ + 2):

        @pl.when(tile - first + 1 == count)
        def _():
            body(count)


def masked(scores, low, start, count):
    shape = (TQ, 2 * TQ)
    sub, lane = iota(shape, 0), lax.rem(iota(shape, 1), TQ)
    low = jnp.concatenate([low, low], axis=1)
    parts = []
    for t in range(count):
        mark = sub >= low - (start + t * TQ)
        if t == count - 1:
            mark = mark & (sub <= lane)
        parts.append(jnp.where(mark, scores[t * TQ : (t + 1) * TQ], MASKED))
    return parts


def own_blocks(both):
    return jnp.concatenate([both[:HEAD_DIM, :TQ], both[HEAD_DIM:LANES, TQ:]], axis=0)


def attend_kernel(
    first_ref, q_ref, k_ref, v_ref, lo_ref, keep_ref, give_ref, lse_ref, keys_ref, vt_ref
):
    rows = q_ref.shape[2]
    per = rows // TQ
    masks = head_masks()
    for side in range(2):
        at = slice(side * rows, (side + 1) * rows)
        keys_ref[at, :] = k_ref[side, 0]
        vt_ref[:LANES, at] = v_ref[side, 0].T
        vt_ref[LANES:, at] = jnp.ones((16, rows), BF16)

    def q_step(qi, carry):
        at = pl.ds(pl.multiple_of(lax.rem(qi, per) * TQ, TQ), TQ)
        query = q_ref[qi // per, 0, at, :]
        low = lo_ref[qi]

        def run(count):
            start = pl.multiple_of((qi - count + 1) * TQ, TQ)
            span = pl.ds(start, count * TQ)
            both = jnp.concatenate([query * mask for mask in masks], axis=0)
            scores = masked(dot_nt(keys_ref[span, :], both), low, start, count)
            peak = functools.reduce(
                jnp.maximum, [jnp.max(part, axis=0, keepdims=True) for part in scores]
            )
            probs = jnp.concatenate([jnp.exp(part - peak).astype(BF16) for part in scores], axis=0)
            mixed = dot(vt_ref[:, span], probs)
            total = mixed[LANES : LANES + 1]
            lse_ref[0, qi, 0:1, :] = peak + jnp.log(total)
            out = own_blocks(mixed[:LANES] / total).T.astype(BF16)

            @pl.when(qi // per == first_ref[2 * per])
            def _():
                keep_ref[at, :] = out

            @pl.when(qi // per != first_ref[2 * per])
            def _():
                give_ref[at, :] = out

        spans(qi, first_ref[qi], run)
        return carry

    lax.fori_loop(0, 2 * per, q_step, 0)


def part_spec(which, rows):
    return pl.BlockSpec((2, 1, rows, LANES), lambda p, first, which=which: (0, which, 0, p))


def attend(first, qkv, low):
    _, _, rows, half = qkv.shape
    pairs = half // LANES
    tiles = 2 * rows // TQ
    return pl.pallas_call(
        attend_kernel,
        grid_spec=pltpu.PrefetchScalarGridSpec(
            num_scalar_prefetch=1,
            grid=(pairs,),
            in_specs=[
                part_spec(0, rows),
                part_spec(1, rows),
                part_spec(2, rows),
                pl.BlockSpec((tiles, 1, TQ), lambda p, first: (0, 0, 0)),
            ],
            out_specs=[
                pl.BlockSpec((rows, LANES), lambda p, first: (0, p)),
                pl.BlockSpec((rows, LANES), lambda p, first: (0, p)),
                pl.BlockSpec((1, tiles, 8, 2 * TQ), lambda p, first: (p, 0, 0, 0)),
            ],
            scratch_shapes=[
                pltpu.VMEM((2 * rows, LANES), BF16),
                pltpu.VMEM((LANES + 16, 2 * rows), BF16),
            ],
        ),
        out_shape=(
            jax.ShapeDtypeStruct((rows, half), BF16),
            jax.ShapeDtypeStruct((rows, half), BF16),
            jax.ShapeDtypeStruct((pairs, tiles, 8, 2 * TQ), F32),
        ),
        compiler_params=params(62),
        cost_estimate=cost(40e9, 16 * rows * half, 12e6),
        name="attend",
    )(first, qkv, qkv, qkv, low)


def attend_back_kernel(
    first_ref,
    q_ref,
    k_ref,
    v_ref,
    do_ref,
    keep_ref,
    give_ref,
    lse_ref,
    lo_ref,
    cos_ref,
    sin_ref,
    layer_ref,
    g_ref,
    layer_out_ref,
    keys_ref,
    values_ref,
    kt_ref,
    delta_ref,
    dk_ref,
    dv_ref,
):
    rows = q_ref.shape[2]
    per = rows // TQ
    masks = head_masks()
    for side in range(2):
        at = slice(side * rows, (side + 1) * rows)
        keys_ref[at, :] = k_ref[side, 0]
        values_ref[at, :] = v_ref[side, 0]
        kt_ref[:, at] = k_ref[side, 0].T
    layer_out_ref[...] = layer_ref[...]
    dk_ref[...] = jnp.zeros_like(dk_ref)
    dv_ref[...] = jnp.zeros_like(dv_ref)

    def prepare(tile, carry):
        at = pl.ds(pl.multiple_of(lax.rem(tile, per) * TQ, TQ), TQ)
        out = jnp.where(tile // per == first_ref[2 * per], keep_ref[at, :], give_ref[at, :])
        both = out.astype(F32) * do_ref[tile // per, at, :].astype(F32)
        both = both.T
        delta_ref[tile, 0:1, :TQ] = jnp.sum(both[:HEAD_DIM], axis=0, keepdims=True)
        delta_ref[tile, 0:1, TQ:] = jnp.sum(both[HEAD_DIM:], axis=0, keepdims=True)
        return carry

    lax.fori_loop(0, 2 * per, prepare, 0)

    def q_step(qi, carry):
        at = pl.ds(pl.multiple_of(lax.rem(qi, per) * TQ, TQ), TQ)
        query = q_ref[qi // per, 0, at, :]
        grad = do_ref[qi // per, at, :]
        low = lo_ref[qi]

        def run(count):
            start = pl.multiple_of((qi - count + 1) * TQ, TQ)
            span = pl.ds(start, count * TQ)
            queries = jnp.concatenate([query * mask for mask in masks], axis=0)
            grads = jnp.concatenate([grad * mask for mask in masks], axis=0)
            lse, delta = lse_ref[0, qi, 0:1, :], delta_ref[qi, 0:1, :]
            scores = masked(dot_nt(keys_ref[span, :], queries), low, start, count)
            grad_probs = dot_nt(values_ref[span, :], grads)
            probs = [jnp.exp(part - lse) for part in scores]
            grad_scores = jnp.concatenate(
                [
                    (part * (grad_probs[t * TQ : (t + 1) * TQ] - delta)).astype(BF16)
                    for t, part in enumerate(probs)
                ],
                axis=0,
            )
            probs = jnp.concatenate([part.astype(BF16) for part in probs], axis=0)
            dv_ref[span, :] += dot(probs, grads)
            dk_ref[span, :] += dot(grad_scores, queries)
            turned = own_blocks(dot(kt_ref[:, span], grad_scores))
            grad_query = turned.T * HEAD_DIM ** (-0.5)
            cos, sin = cos_ref[qi // per, at, :], sin_ref[qi // per, at, :]
            g_ref[qi // per, 0, at, :] = (
                grad_query * cos - swap_halves(grad_query) * sin
            ).astype(BF16)

        spans(qi, first_ref[qi], run)
        return carry

    lax.fori_loop(0, 2 * per, q_step, 0)

    def finish(tile, carry):
        at = pl.ds(pl.multiple_of(lax.rem(tile, per) * TQ, TQ), TQ)
        span = pl.ds(pl.multiple_of(tile * TQ, TQ), TQ)
        cos, sin = cos_ref[tile // per, at, :], sin_ref[tile // per, at, :]
        grad_key = dk_ref[span, :]
        g_ref[tile // per, 1, at, :] = (grad_key * cos - swap_halves(grad_key) * sin).astype(BF16)
        g_ref[tile // per, 2, at, :] = dv_ref[span, :].astype(BF16)
        return carry

    lax.fori_loop(0, 2 * per, finish, 0)


def attend_back(first, qkv, grad_o, keep, give, lse, low, cos, sin, layer):
    _, _, rows, half = qkv.shape
    pairs = half // LANES
    tiles = 2 * rows // TQ
    side = pl.BlockSpec((2, rows, LANES), lambda p, first: (0, 0, p))
    table = pl.BlockSpec((2, rows, LANES), lambda p, first: (0, 0, 0))
    return pl.pallas_call(
        attend_back_kernel,
        grid_spec=pltpu.PrefetchScalarGridSpec(
            num_scalar_prefetch=1,
            grid=(pairs,),
            in_specs=[
                part_spec(0, rows),
                part_spec(1, rows),
                part_spec(2, rows),
                side,
                pl.BlockSpec((rows, LANES), lambda p, first: (0, p)),
                pl.BlockSpec((rows, LANES), lambda p, first: (0, p)),
                pl.BlockSpec((1, tiles, 8, 2 * TQ), lambda p, first: (p, 0, 0, 0)),
                pl.BlockSpec((tiles, 1, TQ), lambda p, first: (0, 0, 0)),
                table,
                table,
                pl.BlockSpec((rows, 2 * LANES), lambda p, first: (0, p)),
            ],
            out_specs=[
                pl.BlockSpec((2, 3, rows, LANES), lambda p, first: (0, 0, 0, p)),
                pl.BlockSpec((rows, 2 * LANES), lambda p, first: (0, p)),
            ],
            scratch_shapes=[
                pltpu.VMEM((2 * rows, LANES), BF16),
                pltpu.VMEM((2 * rows, LANES), BF16),
                pltpu.VMEM((LANES, 2 * rows), BF16),
                pltpu.VMEM((tiles, 8, 2 * TQ), F32),
                pltpu.VMEM((2 * rows, LANES), F32),
                pltpu.VMEM((2 * rows, LANES), F32),
            ],
        ),
        out_shape=(
            jax.ShapeDtypeStruct((2, 3, rows, half), BF16),
            jax.ShapeDtypeStruct(layer.shape, BF16),
        ),
        compiler_params=params(62),
        cost_estimate=cost(100e9, 32 * rows * half, 12e6),
        name="attend_back",
    )(first, qkv, qkv, qkv, grad_o, keep, give, lse, low, cos, sin, layer)


def middle_kernel(
    total,
    first_ref,
    x_ref,
    mine_ref,
    theirs_ref,
    w_ref,
    extra_ref,
    prev_ref,
    res_ref,
    routes_ref,
    hres_ref,
    atwo_ref,
    stat_ref,
    attended_ref,
):
    mine, theirs = mine_ref[...], theirs_ref[...]
    swap = first_ref[first_ref.shape[0] - 1] != 0
    attended = jnp.concatenate(
        [jnp.where(swap, theirs, mine), jnp.where(swap, mine, theirs)], axis=1
    )
    attended_ref[...] = attended
    hres = x_ref[...].astype(F32) + dot(
        attended, jnp.concatenate([w_ref[0, 0], w_ref[0, 1]], axis=1)
    )
    hres_ref[...] = hres
    scale = lax.rsqrt(jnp.mean(hres * hres, axis=-1, keepdims=True) + EPS)
    extra = extra_ref[...]
    gain = extra[GAIN_TWO : GAIN_TWO + 1].astype(F32)
    atwo = (hres * scale * gain).astype(BF16)
    atwo_ref[...] = atwo
    logits = dot_nt(atwo, extra)
    for j in range(total):
        logits = logits + prev_ref[:, j : j + 1] * res_ref[j : j + 1, :]
    lane = iota(logits.shape, 1)

    def soft(inside):
        peak = jnp.max(jnp.where(inside, logits, -jnp.inf), axis=1, keepdims=True)
        powers = jnp.where(inside, jnp.exp(jnp.where(inside, logits - peak, 0.0)), 0.0)
        return powers / jnp.sum(powers, axis=1, keepdims=True)

    probs = soft(lane < total)
    stat = probs
    for j in range(2):
        start = total + 2 * j
        stat = stat + soft((lane >= start) & (lane < start + 2))
    stat = jnp.where(lane == total + 4, scale, stat)
    for k in range(2):
        gate = jnp.sum(
            jnp.where(lane == routes_ref[:, k : k + 1], probs, 0.0), axis=1, keepdims=True
        )
        stat = jnp.where(lane == total + 5 + k, gate, stat)
    stat_ref[...] = stat


def middle(total, first, x, o, theirs, w_shared, extra, prev, res, routes):
    rows, width = x.shape
    token = lambda i: (i, 0)
    whole = lambda i: (0, 0)
    return pl.pallas_call(
        functools.partial(middle_kernel, total),
        grid=(rows // TB,),
        in_specs=[
            pl.BlockSpec(memory_space=pltpu.SMEM),
            pl.BlockSpec((TB, width), token),
            pl.BlockSpec((TB, width // 2), token),
            pl.BlockSpec((TB, width // 2), token),
            pl.BlockSpec((1, 2, width, width // 2), lambda i: (3, 0, 0, 0)),
            pl.BlockSpec((LANES, width), whole),
            pl.BlockSpec((TB, total), token),
            pl.BlockSpec((total, LANES), whole),
            pl.BlockSpec((TB, 2), token),
        ],
        out_specs=[
            pl.BlockSpec((TB, width), token),
            pl.BlockSpec((TB, width), token),
            pl.BlockSpec((TB, LANES), token),
            pl.BlockSpec((TB, width), token),
        ],
        out_shape=(
            jax.ShapeDtypeStruct((rows, width), F32),
            jax.ShapeDtypeStruct((rows, width), BF16),
            jax.ShapeDtypeStruct((rows, LANES), F32),
            jax.ShapeDtypeStruct((rows, width), BF16),
        ),
        compiler_params=params(62),
        cost_estimate=cost(2 * rows * width * width, 2 * width * width + 10 * rows * width),
        name="middle",
    )(first, x, o, theirs, w_shared, extra, prev, res, routes)


def expert_kernel(
    total,
    flat_ref,
    atwo_ref,
    dy_ref,
    stat_ref,
    wide_ref,
    wd_ref,
    flow_ref,
    drow_ref,
    gw_ref,
    send_x,
    send_g,
    all_x,
    all_g,
    send_gate,
    all_gate,
    acc_ref,
    z_ref,
    a_ref,
    b_ref,
    turned_ref,
    turned_g,
    kept_ref,
    wide_buf,
    down_buf,
    wide_given,
    wide_taken,
    down_given,
    down_taken,
    dy_sems,
    x_sems,
    g_sems,
    flow_sems,
    drow_sems,
    local_sems,
    weight_sems,
    wide_sems,
    down_sems,
):
    experts, cap, width = all_x.shape
    slots = experts * cap
    chunks = z_ref.shape[0]
    per = chunks // 2
    half = width // 2
    slabs, rows_out = gw_ref.shape[:2]
    deep = chunks * FC // slabs
    me, core = lax.axis_index("expert"), lax.axis_index("context")

    def down_pieces(chunk):
        if deep == FC:
            rows = pl.ds(pl.multiple_of(chunk * rows_out, rows_out), rows_out)
            return [
                (
                    wd_ref.at[side, rows, 2 * per * FC + b * deep : 2 * per * FC + (b + 1) * deep],
                    side * half + b * rows_out,
                    rows_out,
                )
                for side in range(2)
                for b in range(half // rows_out)
            ]
        at = pl.ds(pl.multiple_of(chunk * FC, FC), FC)
        return [(wd_ref.at[side, :, at], side * half, half) for side in range(2)]

    def weights(step):
        chunk, slot = lax.rem(step, chunks), lax.rem(step, 2)
        gate_at = pl.ds(pl.multiple_of(lax.rem(chunk, per) * FC, FC), FC)
        up_at = pl.ds(pl.multiple_of((per + lax.rem(chunk, per)) * FC, FC), FC)
        return (
            pltpu.make_async_copy(
                wide_ref.at[chunk // per, :, gate_at], wide_buf.at[slot, 0], weight_sems.at[slot, 0]
            ),
            pltpu.make_async_copy(
                wide_ref.at[chunk // per, :, up_at], wide_buf.at[slot, 1], weight_sems.at[slot, 1]
            ),
        ) + tuple(
            pltpu.make_async_copy(
                source, down_buf.at[slot, at : at + size, :], weight_sems.at[slot, 2 + i]
            )
            for i, (source, at, size) in enumerate(down_pieces(chunk))
        )

    def next_weights(step):
        @pl.when(step + 1 < 2 * experts * chunks)
        def _():
            for copy in weights(step + 1):
                copy.start()

        for copy in weights(step):
            copy.wait()

    for copy in weights(0):
        copy.start()
    greet_all(("context", "expert"))

    for j in range(experts):
        pltpu.make_async_copy(
            dy_ref.at[lax.rem(me + experts - j, experts)], all_g.at[j], dy_sems.at[j]
        ).start()
    gates = stat_ref[...].T
    x_copies, g_copies = {}, {}
    for j in list(range(1, experts)) + [0]:
        target = lax.rem(me + j, experts)
        first, second = hot_slots(flat_ref, cap, target)
        rows = dot(jnp.where(first | second, 1.0, 0.0).astype(BF16), atwo_ref[...]).astype(BF16)
        gate = jnp.sum(
            jnp.where(first, gates[total + 5 : total + 6], 0.0)
            + jnp.where(second, gates[total + 6 : total + 7], 0.0),
            axis=1,
            keepdims=True,
        )
        gate = jnp.broadcast_to(gate, (cap, LANES)).T[:8]
        if j == 0:
            all_x[0] = rows
            all_gate[0] = gate
        else:
            send_gate[j - 1] = gate
            send_x[j - 1] = rows
            g_copies[j] = remote(
                send_gate.at[j - 1], all_gate.at[j], g_sems, (j - 1,), {"expert": target}
            )
            x_copies[j] = remote(
                send_x.at[j - 1], all_x.at[j], x_sems, (j - 1,), {"expert": target}
            )
            g_copies[j].start()
            x_copies[j].start()

    def weigh(j):
        pltpu.make_async_copy(
            dy_ref.at[lax.rem(me + experts - j, experts)], all_g.at[j], dy_sems.at[j]
        ).wait()
        gate = jnp.broadcast_to(all_gate[j, 0:1, :], (LANES, cap)).T[:, 0:1]
        all_g[j] = (all_g[j].astype(F32) * gate).astype(BF16)

    def back(buffer, dest, sems, j):
        return remote(
            buffer.at[j - 1],
            dest.at[me],
            sems,
            (j - 1,),
            {"expert": lax.rem(me + experts - j, experts)},
        )

    acc_ref[...] = jnp.zeros_like(acc_ref)

    def up(first, last, at):
        span = slice(first * cap, last * cap)

        def one(step, carry):
            next_weights(step + at * chunks)
            slot = lax.rem(step + at * chunks, 2)
            rows = all_x[first:last].reshape((last - first) * cap, width)
            gate = dot(rows, wide_buf[slot, 0])
            lift = dot(rows, wide_buf[slot, 1])
            sig = 1.0 / (1.0 + jnp.exp(-gate))
            swish = gate * sig
            hidden = (swish * lift).astype(BF16)
            z_ref[step, span] = hidden
            a_ref[step, span] = (lift * sig * (1.0 + gate * (1.0 - sig))).astype(BF16)
            b_ref[step, span] = swish.astype(BF16)
            acc_ref[span, :] += dot_nt(hidden, down_buf[slot])
            return carry

        lax.fori_loop(0, chunks, one, 0)

    def down(first, last, at):
        span = slice(first * cap, last * cap)

        def one(step, carry):
            next_weights(step + at * chunks)
            slot = lax.rem(step + at * chunks, 2)
            dz = dot(all_g[first:last].reshape((last - first) * cap, width), down_buf[slot])
            dg = (dz * a_ref[step, span].astype(F32)).astype(BF16)
            du = (dz * b_ref[step, span].astype(F32)).astype(BF16)
            a_ref[step, span] = dg
            b_ref[step, span] = du
            acc_ref[span, :] += dot_nt(dg, wide_buf[slot, 0]) + dot_nt(du, wide_buf[slot, 1])
            return carry

        lax.fori_loop(0, chunks, one, 0)

    def keep_own(buffer, dest, index):
        buffer[experts - 1] = acc_ref[:cap, :].astype(BF16)
        copy = pltpu.make_async_copy(
            buffer.at[experts - 1], dest.at[me], local_sems.at[index]
        )
        copy.start()
        return copy

    weigh(0)
    up(0, 1, 0)
    own = [keep_own(send_x, flow_ref, 0)]
    acc_ref[:cap, :] = jnp.zeros((cap, width), F32)
    down(0, 1, 1)
    own.append(keep_own(send_g, drow_ref, 1))
    for j in range(1, experts):
        g_copies[j].wait()
        weigh(j)
    turned_g[...] = all_g[...].reshape(slots, width).T
    groups = [(j, j + 1) for j in range(1, experts)]

    def return_rows(buffer, dest, sems, first, last):
        for j in range(first, last):
            buffer[j - 1] = acc_ref[j * cap : (j + 1) * cap, :].astype(BF16)
            back(buffer, dest, sems, j).start()

    for i, (first_at, last_at) in enumerate(groups):
        for j in range(first_at, last_at):
            x_copies[j].wait()
        up(first_at, last_at, 2 + i)
        return_rows(send_x, flow_ref, flow_sems, first_at, last_at)
    turned_ref[...] = all_x[...].reshape(slots, width).T
    acc_ref[cap:, :] = jnp.zeros((slots - cap, width), F32)
    for i, (first_at, last_at) in enumerate(groups):
        down(first_at, last_at, 2 + len(groups) + i)
        return_rows(send_g, drow_ref, drow_sems, first_at, last_at)

    def wide_copy(step):
        return remote(
            wide_given.at[step],
            wide_taken.at[step],
            wide_sems,
            (step,),
            {"context": 1 - core},
        )

    def down_copy(step):
        chunk = lax.rem((1 - core) * per + step, chunks)
        return remote(
            down_given.at[step],
            down_taken.at[chunk],
            down_sems,
            (chunk,),
            {"context": 1 - core},
        )

    def products(step):
        chunk = lax.rem((1 - core) * per + step, chunks)
        gate = dot(turned_ref[...], a_ref[chunk])
        lift = dot(turned_ref[...], b_ref[chunk])
        low = dot(turned_g[...], z_ref[chunk])
        top, bottom = low[:half], low[half:]
        down_given[step] = jnp.where(core == 0, bottom, top).astype(BF16)
        kept_ref[chunk] = jnp.where(core == 0, top, bottom).astype(BF16)
        down_copy(step).start()
        return gate, lift

    def give(step, carry):
        gate, lift = products(step)
        wide_given[step, 0] = gate.astype(BF16)
        wide_given[step, 1] = lift.astype(BF16)
        wide_copy(step).start()
        return carry

    lax.fori_loop(0, per, give, 0)

    def keep(step, carry):
        gate, lift = products(step)
        wide_copy(step - per).wait_recv()
        for i, value in enumerate((gate, lift)):
            at = pl.ds(pl.multiple_of((i * per + step - per) * FC, FC), FC)
            value = value + wide_taken[step - per, i].astype(F32)
            gw_ref[:, :, at] = value.reshape(slabs, rows_out, FC).astype(BF16)
        return carry

    lax.fori_loop(per, chunks, keep, 0)

    def settle(step, carry):
        other = lax.rem(core * per + step, chunks)
        copy = remote(
            down_given.at[step],
            down_taken.at[other],
            down_sems,
            (other,),
            {"context": 1 - core},
        )
        copy.wait_recv()
        value = kept_ref[other].astype(F32) + down_taken[other].astype(F32)
        for b in range(half // rows_out):
            part = value[b * rows_out : (b + 1) * rows_out]
            start = 2 * per * FC + b * deep
            if FC <= deep:
                inside = lax.rem(other, deep // FC) * FC
                at = pl.ds(pl.multiple_of(start + inside, FC), FC)
                gw_ref[other // (deep // FC), :, at] = part.astype(BF16)
            else:
                for i in range(FC // deep):
                    gw_ref[other * (FC // deep) + i, :, start : start + deep] = part[
                        :, i * deep : (i + 1) * deep
                    ].astype(BF16)
        return carry

    lax.fori_loop(0, chunks, settle, 0)

    for copy in own:
        copy.wait()
    for j in range(1, experts):
        back(send_x, flow_ref, flow_sems, j).wait()
        back(send_g, drow_ref, drow_sems, j).wait()

    def sent(step, carry):
        down_copy(step).wait_send()
        return carry

    lax.fori_loop(0, chunks, sent, 0)
    lax.fori_loop(0, per, lambda step, carry: (wide_copy(step).wait_send(), carry)[1], 0)


def run_experts(total, experts, slabs, hidden, cap, flat_t, atwo, dy, stat, wide, wd):
    rows, width = atwo.shape
    chunks = hidden // FC
    per = chunks // 2
    half = width // 2
    slots = experts * cap
    vmem = pl.BlockSpec(memory_space=pltpu.VMEM)
    anywhere = pl.BlockSpec(memory_space=pl.ANY)
    dma = pltpu.SemaphoreType.DMA
    return pl.pallas_call(
        functools.partial(expert_kernel, total),
        in_specs=[vmem] * 2 + [anywhere, vmem] + [anywhere] * 2,
        out_specs=[anywhere] * 2 + [vmem],
        out_shape=(
            jax.ShapeDtypeStruct((experts, cap, width), BF16),
            jax.ShapeDtypeStruct((experts, cap, width), BF16),
            jax.ShapeDtypeStruct((slabs, width // slabs, 3 * hidden // 2), BF16),
        ),
        scratch_shapes=[
            pltpu.VMEM((experts, cap, width), BF16),
            pltpu.VMEM((experts, cap, width), BF16),
            pltpu.VMEM((experts, cap, width), BF16),
            pltpu.VMEM((experts, cap, width), BF16),
            pltpu.VMEM((experts - 1, 8, cap), F32),
            pltpu.VMEM((experts, 8, cap), F32),
            pltpu.VMEM((slots, width), F32),
            pltpu.VMEM((chunks, slots, FC), BF16),
            pltpu.VMEM((chunks, slots, FC), BF16),
            pltpu.VMEM((chunks, slots, FC), BF16),
            pltpu.VMEM((width, slots), BF16),
            pltpu.VMEM((width, slots), BF16),
            pltpu.VMEM((chunks, half, FC), BF16),
            pltpu.VMEM((2, 2, width, FC), BF16),
            pltpu.VMEM((2, width, FC), BF16),
            pltpu.VMEM((per, 2, width, FC), BF16),
            pltpu.VMEM((per, 2, width, FC), BF16),
            pltpu.VMEM((chunks, half, FC), BF16),
            pltpu.VMEM((chunks, half, FC), BF16),
            dma((experts,)),
            dma((2, experts - 1)),
            dma((2, experts - 1)),
            dma((2, experts - 1)),
            dma((2, experts - 1)),
            dma((2,)),
            dma((2, 6)),
            dma((2, per)),
            dma((2, chunks)),
        ],
        compiler_params=pltpu.CompilerParams(
            collective_id=2, has_side_effects=True, vmem_limit_bytes=62 * MIB
        ),
        cost_estimate=cost(18 * slots * width * hidden, 30 * width * hidden),
        name="experts",
    )(flat_t, atwo, dy, stat, wide, wd)


def combine_kernel(
    experts,
    total,
    flow_ref,
    drow_ref,
    flat_ref,
    stat_ref,
    flat_t_ref,
    hres_ref,
    atwo_ref,
    dy_ref,
    o_ref,
    extra_ref,
    w_ref,
    prev_ref,
    out_ref,
    dh_ref,
    dolow_ref,
    gw_ref,
    small_ref,
    right_ref,
    picked_ref,
    summed_ref,
    sums_ref,
    columns_ref,
    dhlow_ref,
    stage_ref,
    own_sems,
    dolow_sems,
):
    step = pl.program_id(0)
    core = lax.axis_index("context")

    @pl.when(step == 0)
    def _():
        greet_all(("context",))

    def dolow_copies(block):
        rows = pl.ds(pl.multiple_of(block * TB, TB), TB)
        return (
            pltpu.make_async_copy(
                stage_ref.at[core, rows], dolow_ref.at[core, rows], own_sems.at[block]
            ),
            remote(
                stage_ref.at[1 - core, rows],
                dolow_ref.at[core, rows],
                dolow_sems,
                (block,),
                {"context": 1 - core},
            ),
        )

    slots, width = flow_ref.shape
    half = width // 2
    gain = extra_ref[GAIN_TWO : GAIN_TWO + 1].astype(F32)
    vecs = [extra_ref[VECS + j : VECS + j + 1].astype(F32) for j in range(2)]

    @pl.when(step == 0)
    def _():
        right_ref[:slots] = drow_ref[...]
        right_ref[slots:] = extra_ref[...]

    spread_out = iota((TB, slots), 1)
    hots = [
        jnp.where(flat_ref[:, k : k + 1] == spread_out, 1.0, 0.0).astype(BF16) for k in range(2)
    ]
    for k in range(2):
        picked_ref[k] = dot(hots[k], flow_ref[...])
    vec_dot = dot_nt(dy_ref[...], extra_ref[...])
    lane = iota((RC, LANES), 1)
    for start in range(0, TB, RC):
        at = slice(start, start + RC)
        dy = dy_ref[at].astype(F32)
        ntwo = hres_ref[at] * stat_ref[at, total + 4 : total + 5] * gain
        sums = vec_dot[at]
        for i, part in enumerate((ntwo, picked_ref[0, at], picked_ref[1, at])):
            sums = jnp.where(lane == i, jnp.sum(dy * part, axis=1, keepdims=True), sums)
        sums_ref[at] = sums

    sums, stats = sums_ref[...].T, stat_ref[...].T
    row = lambda i: stats[i : i + 1]
    dot_normed, dot_picked = sums[0:1], [sums[1:2], sums[2:3]]
    dot_vecs = [sums[VECS + j : VECS + j + 1] for j in range(2)]
    gates = [row(total + 5 + k) for k in range(2)]
    mixes = [[row(total + 2 * j + i) for i in range(2)] for j in range(2)]
    routes = [flat_t_ref[2 + k : 3 + k] for k in range(2)]
    copies = [jnp.where(route == experts + 1, 1.0, 0.0) for route in routes]
    consts = [
        [jnp.where(route == experts + 2 + j, 1.0, 0.0) for j in range(2)] for route in routes
    ]
    pulls = [mixes[j][0] * dot_normed + mixes[j][1] * dot_vecs[j] for j in range(2)]
    sub = iota((total, TB), 0).astype(F32)
    dpgate = jnp.zeros((total, TB), F32)
    for k in range(2):
        dgate = dot_picked[k] + copies[k] * dot_normed
        dgate = dgate + consts[k][0] * pulls[0] + consts[k][1] * pulls[1]
        dpgate = dpgate + jnp.where(sub == routes[k], dgate, 0.0)
    pgate = stats[:total]
    dlogit = pgate * (dpgate - jnp.sum(pgate * dpgate, axis=0, keepdims=True))
    weight = gates[0] * copies[0] + gates[1] * copies[1]
    dmix, shares, pieces = [], [], []
    for j in range(2):
        const = gates[0] * consts[0][j] + gates[1] * consts[1][j]
        grads = [const * dot_normed, const * dot_vecs[j]]
        inner = mixes[j][0] * grads[0] + mixes[j][1] * grads[1]
        dmix += [mixes[j][i] * (grads[i] - inner) for i in range(2)]
        weight = weight + const * mixes[j][0]
        share = const * mixes[j][1]
        shares.append(share)
        for i in range(3):
            pieces.append(share.astype(BF16).astype(F32))
            share = share - pieces[-1]
    empty = jnp.zeros((1, TB), F32)
    droute_t = jnp.concatenate([dlogit] + dmix + [empty] * (12 - total), axis=0).astype(BF16)
    rows = jnp.concatenate(
        [dlogit] + dmix + [weight] + shares + [jnp.zeros((LANES - total - 7, TB), F32)], axis=0
    )
    columns_ref[...] = rows.T
    for start in range(0, TB, RC):
        at = slice(start, start + RC)
        hres = hres_ref[at]
        ntwo = hres * stat_ref[at, total + 4 : total + 5] * gain
        out = hres + columns_ref[at, total + 4 : total + 5] * ntwo
        for k in range(2):
            out = out + stat_ref[at, total + 5 + k : total + 6 + k] * picked_ref[k, at]
        for j in range(2):
            out = out + columns_ref[at, total + 5 + j : total + 6 + j] * vecs[j]
        out_ref[at] = out.astype(BF16)

    lane = iota((TB, LANES), 1)
    droute = jnp.where(lane < total + 4, columns_ref[...], 0.0).astype(BF16)
    summed_ref[...] = dot(
        jnp.concatenate([hots[0] + hots[1], droute], axis=1), right_ref[...]
    )
    gain_row = jnp.zeros((1, width), F32)
    for start in range(0, TB, RC):
        at = slice(start, start + RC)
        hres = hres_ref[at]
        dy = dy_ref[at].astype(F32)
        scale = stat_ref[at, total + 4 : total + 5]
        dntwo = columns_ref[at, total + 4 : total + 5] * dy + summed_ref[at]
        both = hres * dntwo
        inner = jnp.sum(both * gain, axis=1, keepdims=True) * (1.0 / width)
        dh = dy + dntwo * gain * scale - hres * (scale * scale * scale * inner)
        gain_row = gain_row + jnp.sum(both * scale, axis=0, keepdims=True)
        dh_ref[at] = dh
        dhlow_ref[pl.ds(pl.multiple_of(step * TB + start, RC), RC), :] = dh.astype(BF16)
    w_out = jnp.concatenate([w_ref[0, 0], w_ref[0, 1]], axis=1)
    dolow = dot_nt(dhlow_ref[pl.ds(pl.multiple_of(step * TB, TB), TB), :], w_out).astype(BF16)
    rows_at = pl.ds(pl.multiple_of(step * TB, TB), TB)
    stage_ref[0, rows_at] = dolow[:, :half]
    stage_ref[1, rows_at] = dolow[:, half:]
    for copy in dolow_copies(step):
        copy.start()
    route_rows = dot(droute_t, atwo_ref[...])
    vec_parts = dot(
        jnp.concatenate(pieces + [empty] * 2, axis=0).astype(BF16), dy_ref[...]
    )
    vec_rows = [
        vec_parts[3 * j : 3 * j + 1] + vec_parts[3 * j + 1 : 3 * j + 2] + vec_parts[3 * j + 2 : 3 * j + 3]
        for j in range(2)
    ]
    res_rows = jnp.dot(dlogit, prev_ref[...], precision=HIGH, preferred_element_type=F32)
    res_rows = jnp.concatenate([res_rows, jnp.zeros((total, width - total), F32)], axis=1)
    small = jnp.concatenate(
        [route_rows[: total + 4], gain_row] + vec_rows + [jnp.zeros((1, width), F32), res_rows],
        axis=0,
    )

    @pl.when(step == 0)
    def _():
        small_ref[...] = small

    @pl.when(step > 0)
    def _():
        small_ref[...] += small

    @pl.when(step == pl.num_programs(0) - 1)
    def _():
        for side in range(2):
            at = slice(side * half, (side + 1) * half)
            weight = dot(o_ref[:, at].T, dhlow_ref[...]).astype(BF16)
            gw_ref[0, at] = weight[:, :half]
            gw_ref[1, at] = weight[:, half:]
        for block in range(dhlow_ref.shape[0] // TB):
            for copy in dolow_copies(block):
                copy.wait()


def combine(experts, total, flow, drow, flat, stat, flat_t, hres, atwo, dy, o, w_shared, extra, prev):
    rows, width = hres.shape
    slots = flow.shape[0]
    half = width // 2
    token = lambda i: (i, 0)
    whole = lambda i: (0, 0)
    weight = pl.BlockSpec((2, width, half), lambda i: (0, 0, 0))
    small_rows = 2 * total + 8
    return pl.pallas_call(
        functools.partial(combine_kernel, experts, total),
        grid=(rows // TB,),
        in_specs=[
            pl.BlockSpec((slots, width), whole),
            pl.BlockSpec((slots, width), whole),
            pl.BlockSpec((TB, LANES), token),
            pl.BlockSpec((TB, LANES), token),
            pl.BlockSpec((8, TB), lambda i: (0, i)),
            pl.BlockSpec((TB, width), token),
            pl.BlockSpec((TB, width), token),
            pl.BlockSpec((TB, width), token),
            pl.BlockSpec((rows, width), whole),
            pl.BlockSpec((LANES, width), whole),
            pl.BlockSpec((1, 2, width, half), lambda i: (3, 0, 0, 0)),
            pl.BlockSpec((TB, total), token),
        ],
        out_specs=[
            pl.BlockSpec((TB, width), token),
            pl.BlockSpec((TB, width), token),
            pl.BlockSpec(memory_space=pl.ANY),
            weight,
            pl.BlockSpec((small_rows, width), whole),
        ],
        out_shape=(
            jax.ShapeDtypeStruct((rows, width), BF16),
            jax.ShapeDtypeStruct((rows, width), F32),
            jax.ShapeDtypeStruct((2, rows, half), BF16),
            jax.ShapeDtypeStruct((2, width, half), BF16),
            jax.ShapeDtypeStruct((small_rows, width), F32),
        ),
        scratch_shapes=[
            pltpu.VMEM((slots + LANES, width), BF16),
            pltpu.VMEM((2, TB, width), F32),
            pltpu.VMEM((TB, width), F32),
            pltpu.VMEM((TB, LANES), F32),
            pltpu.VMEM((TB, LANES), F32),
            pltpu.VMEM((rows, width), BF16),
            pltpu.VMEM((2, rows, half), BF16),
            pltpu.SemaphoreType.DMA((rows // TB,)),
            pltpu.SemaphoreType.DMA((2, rows // TB)),
        ],
        compiler_params=pltpu.CompilerParams(
            collective_id=3, has_side_effects=True, vmem_limit_bytes=62 * MIB
        ),
        cost_estimate=cost(
            6 * rows * slots * width + 4 * rows * width * width, 30 * rows * width + 8 * width * width
        ),
        name="combine",
    )(flow, drow, flat, stat, flat_t, hres, atwo, dy, o, extra, w_shared, prev)


def tail_kernel(
    gain_at,
    sent_ref,
    aone_ref,
    w_ref,
    extra_ref,
    x_ref,
    dh_ref,
    gwo_ref,
    small_ref,
    out_ref,
    final,
    small_out_ref,
    both,
    grads,
    w_buf,
    x_buf,
    dh_buf,
    out_buf,
    core_in,
    plane_out,
    plane_in,
    slab_out,
    slab_in,
    own_ref,
    small_own,
    small_core,
    small_plane,
    small_slab,
    load_sems,
    store_sems,
    both_sems,
    core_sems,
    plane_sems,
    slab_sems,
    final_sems,
    pass_sems,
    small_core_sems,
    small_plane_sems,
    small_slab_sems,
):
    experts = lax.axis_size("expert")
    slabs = lax.axis_size("dp")
    me, core, slab = lax.axis_index("expert"), lax.axis_index("context"), lax.axis_index("dp")
    other = 1 - core
    tokens, width = x_buf.shape
    half = width // 2
    parts = 4
    block = tokens // parts

    mine = pltpu.make_async_copy(sent_ref.at[core], both.at[core], load_sems.at[0])
    mine.start()
    loads = [
        pltpu.make_async_copy(w_ref.at[pl.ds(0, 3)], w_buf, load_sems.at[1]),
        pltpu.make_async_copy(x_ref, x_buf, load_sems.at[2]),
        pltpu.make_async_copy(dh_ref, dh_buf, load_sems.at[3]),
    ]
    for copy in loads:
        copy.start()
    greet_all(("context", "expert", "dp"))
    theirs = [
        remote(
            sent_ref.at[other, which],
            both.at[core, which],
            both_sems,
            (which,),
            {"context": other},
        )
        for which in range(3)
    ]

    def core_copy(which):
        return remote(
            grads.at[other, which], core_in.at[which], core_sems, (which,), {"context": other}
        )

    for side in range(2):
        grads[side, 3] = gwo_ref[side]
    core_copy(3).start()
    for copy in theirs:
        copy.start()

    def plane_copy(j, at):
        return remote(
            plane_out.at[j - 1, at],
            plane_in.at[j - 1, at],
            plane_sems,
            (j - 1, at),
            {"expert": lax.rem(me + j, experts)},
        )

    def pass_on(which):
        core_copy(which).wait_recv()
        j = lax.rem(which + experts - me, experts)

        @pl.when(j != 0)
        def _():
            def one(k):
                at = lax.rem(slab + k + 1, slabs)
                plane_out[j - 1, at] = (
                    grads[core, which, at].astype(F32) + core_in[which, at].astype(F32)
                ).astype(BF16)
                plane_copy(j, at).start()

            loop(slabs, one)

    mine.wait()
    turned = aone_ref[...].T
    pass_on(3)
    for which in range(3):
        theirs[which].wait_recv()
        grad = jnp.concatenate([both[0, which], both[1, which]], axis=1)
        weight = dot(turned, grad)
        for side in range(2):
            grads[side, which] = (
                weight[:, side * half : (side + 1) * half]
                .reshape(slabs, width // slabs, half)
                .astype(BF16)
            )
        core_copy(which).start()
        if which > 0:
            pass_on(which - 1)
    for copy in loads:
        copy.wait()

    gain = extra_ref[GAIN_ONE : GAIN_ONE + 1].astype(F32)
    stores = []
    gain_row = jnp.zeros((1, width), F32)
    for part in range(parts):
        at = slice(part * block, (part + 1) * block)
        dnone = None
        for which in range(3):
            grad = jnp.concatenate([both[0, which, at], both[1, which, at]], axis=1)
            whole = jnp.concatenate([w_buf[which, 0], w_buf[which, 1]], axis=1)
            product = dot_nt(grad, whole)
            dnone = product if dnone is None else dnone + product
        values = x_buf[at].astype(F32)
        scale = lax.rsqrt(jnp.mean(values * values, axis=-1, keepdims=True) + EPS)
        scaled = dnone * gain
        inner = jnp.mean(values * scaled, axis=1, keepdims=True)
        out_buf[at] = dh_buf[at] + scale * scaled - values * (scale * scale * scale * inner)
        stores.append(
            pltpu.make_async_copy(out_buf.at[at], out_ref.at[at], store_sems.at[part])
        )
        stores[-1].start()
        gain_row = gain_row + jnp.sum(dnone * values * scale, axis=0, keepdims=True)
        if part == 0:
            pass_on(2)

    row = iota(small_ref.shape, 0)
    small_own[...] = small_ref[...] + jnp.where(row == gain_at, gain_row, 0.0)
    small_copy = remote(small_own, small_core, small_core_sems, (0,), {"context": other})
    small_copy.start()
    small_copy.wait()
    small_plane[me] = small_own[...] + small_core[...]
    small_plane_copies = []
    for j in range(1, experts):
        small_plane_copies.append(
            remote(
                small_plane.at[me],
                small_plane.at[me],
                small_plane_sems,
                (j,),
                {"expert": lax.rem(me + j, experts)},
            )
        )
        small_plane_copies[-1].start()

    def gathered(at):
        value = grads[core, me, at].astype(F32) + core_in[me, at].astype(F32)
        for j in range(1, experts):
            plane_copy(j, at).wait_recv()
            value = value + plane_in[j - 1, at].astype(F32)
        return value

    def slab_copy(k):
        return remote(
            slab_out.at[k],
            slab_in.at[k],
            slab_sems,
            (k,),
            {"dp": lax.rem(slab + k + 1, slabs)},
        )

    def scatter(k):
        slab_out[k] = gathered(lax.rem(slab + k + 1, slabs)).astype(BF16)
        slab_copy(k).start()

    loop(slabs - 1, scatter)

    for copy in small_plane_copies:
        copy.wait()
    value = small_plane[0]
    for j in range(1, experts):
        value = value + small_plane[j]
    small_slab[slab] = value

    def small_slab_copy(k):
        return remote(
            small_slab.at[slab],
            small_slab.at[slab],
            small_slab_sems,
            (k,),
            {"dp": lax.rem(slab + k + 1, slabs)},
        )

    loop(slabs - 1, lambda k: small_slab_copy(k).start())

    own_ref[...] = gathered(slab)

    def collect(k):
        slab_copy(k).wait_recv()
        own_ref[...] += slab_in[k].astype(F32)

    loop(slabs - 1, collect)
    final[core, me] = own_ref[...].astype(BF16)
    final_copies, pass_copies = [], []
    for j in range(1, experts):
        final_copies.append(
            remote(
                final.at[core, me],
                final.at[core, me],
                final_sems,
                (j,),
                {"expert": lax.rem(me + j, experts)},
            )
        )
        final_copies[-1].start()
    for j in range(experts):
        source = lax.rem(me + experts - j, experts)
        if j > 0:
            final_copies[j - 1].wait_recv()
        pass_copies.append(
            remote(
                final.at[core, source],
                final.at[core, source],
                pass_sems,
                (j,),
                {"context": other},
            )
        )
        pass_copies[-1].start()

    loop(slabs - 1, lambda k: small_slab_copy(k).wait())
    small_out_ref[...] = small_slab[0]

    def add_small(k):
        small_out_ref[...] += small_slab[k + 1]

    loop(slabs - 1, add_small)

    for copy in pass_copies:
        copy.wait_recv()
    for copy in stores:
        copy.wait()
    for which in range(4):
        core_copy(which).wait_send()
    for j in range(1, experts):

        def sent(k, j=j):
            plane_copy(j, k).wait_send()

        loop(slabs, sent)
    loop(slabs - 1, lambda k: slab_copy(k).wait_send())
    for copy in theirs + final_copies + pass_copies:
        copy.wait_send()


def tail(experts, slabs, gain_at, sent, aone, w_shared, extra, x, dh, gwo, small):
    tokens, width = x.shape
    half = width // 2
    rows = width // slabs
    vmem = pl.BlockSpec(memory_space=pltpu.VMEM)
    anywhere = pl.BlockSpec(memory_space=pl.ANY)
    dma = pltpu.SemaphoreType.DMA
    return pl.pallas_call(
        functools.partial(tail_kernel, gain_at),
        in_specs=[anywhere, vmem, anywhere, vmem, anywhere, anywhere] + [vmem] * 2,
        out_specs=[anywhere] + [vmem] * 2,
        out_shape=(
            jax.ShapeDtypeStruct((tokens, width), F32),
            jax.ShapeDtypeStruct((2, experts, rows, half), BF16),
            jax.ShapeDtypeStruct(small.shape, F32),
        ),
        scratch_shapes=[
            pltpu.VMEM((2, 3, tokens, half), BF16),
            pltpu.VMEM((2, 4, slabs, rows, half), BF16),
            pltpu.VMEM((3, 2, width, half), BF16),
            pltpu.VMEM((tokens, width), BF16),
            pltpu.VMEM((tokens, width), F32),
            pltpu.VMEM((tokens, width), F32),
            pltpu.VMEM((4, slabs, rows, half), BF16),
            pltpu.VMEM((experts - 1, slabs, rows, half), BF16),
            pltpu.VMEM((experts - 1, slabs, rows, half), BF16),
            pltpu.VMEM((slabs - 1, rows, half), BF16),
            pltpu.VMEM((slabs - 1, rows, half), BF16),
            pltpu.VMEM((rows, half), F32),
            pltpu.VMEM(small.shape, F32),
            pltpu.VMEM(small.shape, F32),
            pltpu.VMEM((experts,) + small.shape, F32),
            pltpu.VMEM((slabs,) + small.shape, F32),
            dma((4,)),
            dma((4,)),
            dma((2, 3)),
            dma((2, 4)),
            dma((2, experts - 1, slabs)),
            dma((2, slabs - 1)),
            dma((2, experts)),
            dma((2, experts)),
            dma((2, 1)),
            dma((2, experts)),
            dma((2, slabs - 1)),
        ],
        compiler_params=pltpu.CompilerParams(
            collective_id=0, has_side_effects=True, vmem_limit_bytes=62 * MIB
        ),
        cost_estimate=cost(12 * tokens * width * width, 40 * tokens * width),
        name="tail",
    )(sent, aone, w_shared, extra, x, dh, gwo, small)


def finish_kernel(
    total,
    place_ref,
    small_ref,
    final_ref,
    mine_ref,
    theirs_ref,
    tokens_ref,
    norm_one_ref,
    norm_two_ref,
    router_ref,
    mix_ref,
    vec_ref,
    res_ref,
    q_ref,
    k_ref,
    v_ref,
    o_ref,
    gate_ref,
    up_ref,
    gd_ref,
    tokens_out_ref,
    tokens_buf,
    final_buf,
    share_buf,
    square_buf,
    gate_buf,
    up_buf,
    gd_buf,
    turned_ref,
    load_sems,
    store_sems,
):
    rows, half = final_buf.shape[2:]
    wide = share_buf.shape[2] // 3
    deep = gd_buf.shape[0]
    core = place_ref[1]
    loads = [
        pltpu.make_async_copy(mine_ref, share_buf.at[0], load_sems.at[0]),
        pltpu.make_async_copy(theirs_ref, share_buf.at[1], load_sems.at[1]),
        pltpu.make_async_copy(final_ref, final_buf, load_sems.at[2]),
        pltpu.make_async_copy(tokens_ref, tokens_buf, load_sems.at[3]),
    ]
    for copy in loads[3:] + loads[:3]:
        copy.start()
    small = small_ref[...]
    fill = jnp.zeros((LANES - small.shape[0], small.shape[1]), F32)
    turned_ref[...] = jnp.concatenate([small, fill], axis=0).T
    own = turned_ref[pl.ds(pl.multiple_of(place_ref[0] * rows, 8), rows), :]
    own = own.T
    router_ref[...] = own[:total]
    mix_ref[...] = own[total : total + 4]
    norm_two_ref[...] = own[total + 4 : total + 5]
    vec_ref[...] = own[total + 5 : total + 7]
    norm_one_ref[...] = own[total + 7 : total + 8]
    res_ref[...] = turned_ref[:total, total + 8 : 2 * total + 8]

    stores = []

    def store(buffer, ref):
        stores.append(pltpu.make_async_copy(buffer, ref, store_sems.at[len(stores)]))
        stores[-1].start()

    def sides(buffer, size, left, right):
        buffer[:, :size] = left
        buffer[:, size:] = right

    def ordered(get):
        first, second = get(share_buf.at[0]), get(share_buf.at[1])
        swap = core != 0
        return jnp.where(swap, second, first), jnp.where(swap, first, second)

    loads[3].wait()
    store(tokens_buf, tokens_out_ref)
    for copy in loads[:2]:
        copy.wait()
    sides(gate_buf, wide, *ordered(lambda ref: ref[:, :wide].astype(F32)))
    store(gate_buf, gate_ref.at[0])
    sides(up_buf, wide, *ordered(lambda ref: ref[:, wide : 2 * wide].astype(F32)))
    store(up_buf, up_ref.at[0])

    def down(ref):
        blocks = [
            ref[:, 2 * wide + b * deep : 2 * wide + (b + 1) * deep].astype(F32)
            for b in range(half // rows)
        ]
        return jnp.concatenate(blocks, axis=0).T

    sides(gd_buf, half, *ordered(down))
    store(gd_buf, gd_ref.at[0])
    loads[2].wait()
    for which, ref in enumerate((q_ref, k_ref, v_ref, o_ref)):
        sides(
            square_buf.at[which],
            half,
            final_buf[0, which].astype(F32),
            final_buf[1, which].astype(F32),
        )
        store(square_buf.at[which], ref)
    for copy in stores:
        copy.wait()


def finish(total, place, final, small, mine, theirs, tokens):
    rows, half = final.shape[2:]
    width = 2 * half
    wide = mine.shape[1] // 3
    deep = wide * rows // half
    anywhere = pl.BlockSpec(memory_space=pl.ANY)
    vmem = pl.BlockSpec(memory_space=pltpu.VMEM)
    shape = lambda *dims: jax.ShapeDtypeStruct(dims, F32)
    return pl.pallas_call(
        functools.partial(finish_kernel, total),
        in_specs=[pl.BlockSpec(memory_space=pltpu.SMEM), vmem] + [anywhere] * 4,
        out_specs=[vmem] * 6 + [anywhere] * 8,
        out_shape=(
            shape(1, rows),
            shape(1, rows),
            shape(total, rows),
            shape(4, rows),
            shape(2, rows),
            shape(total, total),
            shape(rows, width),
            shape(rows, width),
            shape(rows, width),
            shape(rows, width),
            shape(1, rows, 2 * wide),
            shape(1, rows, 2 * wide),
            shape(1, deep, width),
            shape(*tokens.shape),
        ),
        scratch_shapes=[
            pltpu.VMEM(tokens.shape, F32),
            pltpu.VMEM(final.shape, BF16),
            pltpu.VMEM((2,) + mine.shape, BF16),
            pltpu.VMEM((4, rows, width), F32),
            pltpu.VMEM((rows, 2 * wide), F32),
            pltpu.VMEM((rows, 2 * wide), F32),
            pltpu.VMEM((deep, width), F32),
            pltpu.VMEM((width, LANES), F32),
            pltpu.SemaphoreType.DMA((4,)),
            pltpu.SemaphoreType.DMA((8,)),
        ],
        compiler_params=params(62),
        cost_estimate=cost(1e6, 20 * rows * width),
        name="finish",
    )(place, small, final, mine, theirs, tokens)


def on_device(
    tokens,
    segments,
    routes,
    prev_logits,
    ranks,
    cotangent,
    norm_one,
    w_query,
    w_key,
    w_value,
    w_out,
    norm_two,
    router,
    w_res,
    const_mix,
    const_vec,
    w_gate,
    w_up,
    w_down,
):
    experts = lax.axis_size("expert")
    dp = lax.axis_size("dp")
    total = experts + NZ
    _, rows, width = tokens.shape
    hidden = w_gate.shape[2]
    cap = (18 * rows + 8 * total - 1) // (8 * total)
    seq = 2 * rows
    core = lax.axis_index("context")
    half = width // 2

    def mine(shard, size):
        return lax.dynamic_slice_in_dim(shard, core * size, size, 1)

    def gather(shard):
        return lax.all_gather(shard, ("context", "dp"), axis=0).reshape(
            2, dp * shard.shape[0], shard.shape[1]
        )

    extra = jnp.concatenate(
        [router, const_mix, norm_one[:, None], norm_two[:, None], const_vec], axis=1
    )
    cos, sin = (jnp.asarray(table).reshape(2, rows, LANES) for table in rope_tables(seq))
    x = tokens[0]
    dy = cotangent[0]
    w_shared, extra, flat, flat_t, low, first, qkv, aone, dy_rows = spread(
        experts,
        dp,
        cap,
        w_query,
        w_key,
        w_value,
        w_out,
        extra.astype(F32).T,
        routes[0],
        ranks[0],
        segments,
        x,
        dy,
        cos,
        sin,
    )
    w_shared = w_shared.reshape(4, 2, width, half)
    extra = extra.transpose(1, 0, 2).reshape(total + 8, width).astype(BF16)
    extra = jnp.concatenate(
        [
            extra[: total + 4],
            jnp.zeros((GAIN_ONE - total - 4, width), BF16),
            extra[total + 4 :],
            jnp.zeros((LANES - GAIN_ONE - 4, width), BF16),
        ],
        axis=0,
    )
    wide_mine = [mine(w_gate[0], hidden // 2), mine(w_up[0], hidden // 2)]
    down_mine = mine(w_down[0], half)
    deep = hidden // dp
    if deep == FC:
        turned = down_mine.T.reshape(-1, width // dp, deep).transpose(1, 0, 2)
        wide_w = gather(jnp.concatenate(wide_mine + [turned.reshape(width // dp, -1)], axis=1))
        down_w = wide_w
    else:
        wide_w = gather(jnp.concatenate(wide_mine, axis=1))
        down_w = gather(down_mine).transpose(0, 2, 1)

    res = jnp.pad(w_res.astype(F32), ((0, 0), (0, LANES - total)))

    dy_rows = lax.all_to_all(dy_rows, "expert", split_axis=0, concat_axis=0, tiled=True)
    o_keep, o_give, lse = attend(first, qkv, low)
    o_give, dy_rows = lax.optimization_barrier((o_give, dy_rows))
    o_theirs = lax.ppermute(o_give, "context", [(0, 1), (1, 0)])
    hres, atwo, stat, o = middle(
        total, first, x, o_keep, o_theirs, w_shared, extra, prev_logits[0], res, routes[0]
    )
    flow_back, drow_back, grad_wide = run_experts(
        total, experts, dp, hidden, cap, flat_t, atwo, dy_rows, stat, wide_w, down_w
    )
    flow_back = flow_back.reshape(experts * cap, width)
    drow_back = drow_back.reshape(experts * cap, width)
    wide = lax.psum_scatter(
        grad_wide.reshape(width, 3 * hidden // 2), "dp", scatter_dimension=0, tiled=True
    )

    output, dh, grad_o, grad_out_w, small = combine(
        experts,
        total,
        flow_back,
        drow_back,
        flat,
        stat,
        flat_t,
        hres,
        atwo,
        dy,
        o,
        w_shared,
        extra,
        prev_logits[0],
    )
    grads_sent, output = attend_back(
        first,
        qkv,
        grad_o,
        o_keep,
        o_give,
        lse,
        low,
        cos,
        sin,
        output,
    )
    grad_tokens, final, small = tail(
        experts,
        dp,
        total + 7,
        grads_sent,
        aone,
        w_shared,
        extra,
        x,
        dh,
        grad_out_w.reshape(2, dp, width // dp, half),
        small,
    )
    wide, small = lax.optimization_barrier((wide, small))
    wide_other = lax.ppermute(wide, "context", [(0, 1), (1, 0)])
    (
        grad_norm_one,
        grad_norm_two,
        grad_router,
        grad_mix,
        grad_vec,
        grad_res,
        grad_query,
        grad_key,
        grad_value,
        grad_out,
        grad_gate,
        grad_up,
        grad_down,
        grad_tokens,
    ) = finish(
        total,
        jnp.stack([lax.axis_index("dp"), core]),
        final,
        small,
        wide,
        wide_other,
        grad_tokens,
    )
    return (
        output[None],
        grad_tokens[None],
        grad_norm_one[0],
        grad_query,
        grad_key,
        grad_value,
        grad_out,
        grad_norm_two[0],
        grad_router.T,
        grad_res,
        grad_mix.T,
        grad_vec.T,
        grad_gate,
        grad_up,
        grad_down,
    )


def solution(mesh):
    token = P(("expert", "dp"), "context", None)
    rows = P("dp", None)
    expert = P("expert", "dp", None)
    in_specs = (
        token,
        P(("expert", "dp"), "context"),
        token,
        token,
        token,
        token,
        P("dp"),
        rows,
        rows,
        rows,
        rows,
        P("dp"),
        rows,
        P(),
        rows,
        rows,
        expert,
        expert,
        expert,
    )
    out_specs = (
        token,
        token,
        P("dp"),
        rows,
        rows,
        rows,
        rows,
        P("dp"),
        rows,
        P(),
        rows,
        rows,
        expert,
        expert,
        expert,
    )
    return jax.shard_map(
        on_device, mesh=mesh, in_specs=in_specs, out_specs=out_specs, check_vma=False
    )
```
